128 devices in a mesh: fsdp: 32 (over z, y_lo, x), tp: 4 (over y_hi, core).
Axes of the slice: x: 4, y: 4 (y_hi: 2, y_lo: 2; y = y_hi * 2 + y_lo), z: 4, core: 2. Of those that a mesh axis runs over, the one named last changes fastest.
Arguments:
- hidden_in: bfloat16 [16384, 2048], P(('fsdp', 'tp')), may hold values from -6 to 6
- out_grad: bfloat16 [16384, 2048], P(('fsdp', 'tp')), may hold values from -6 to 6
- attn_gain: bfloat16 [2048], P(('fsdp', 'tp')), may hold values from 0.5 to 1.5
- q_down: bfloat16 [2048, 1536], P(('fsdp', 'tp')), may hold values from -0.125 to 0.125
- q_gain: bfloat16 [1536], P(('fsdp', 'tp')), may hold values from 0.5 to 1.5
- kv_down: bfloat16 [2048, 576], P(('fsdp', 'tp')), may hold values from -0.125 to 0.125
- kv_gain: bfloat16 [512], P(('fsdp', 'tp')), may hold values from 0.5 to 1.5
- q_up: bfloat16 [1536, 3072], P('fsdp', 'tp'), may hold values from -0.15625 to 0.15625
- kv_up: bfloat16 [512, 4096], P('fsdp', 'tp'), may hold values from -0.25 to 0.25
- out_proj: bfloat16 [2048, 2048], P('tp', 'fsdp'), may hold values from -1.5 to 1.5
- ffn_gain: bfloat16 [2048], P(('fsdp', 'tp')), may hold values from 0.5 to 1.5
- router: bfloat16 [2048, 8], P(('fsdp', 'tp')), may hold values from -0.125 to 0.125
- routed_gate_up: bfloat16 [8, 2048, 2, 1408], P(None, 'fsdp', None, 'tp'), may hold values from -0.125 to 0.125
- routed_down: bfloat16 [8, 1408, 2048], P(None, 'tp', 'fsdp'), may hold values from -0.15625 to 0.15625
- shared_gate_up: bfloat16 [2048, 2, 2816], P('fsdp', None, 'tp'), may hold values from -0.125 to 0.125
- shared_down: bfloat16 [2816, 2048], P('tp', 'fsdp'), may hold values from -0.109375 to 0.109375
- choices: int32 [16384, 2], P('fsdp'), may hold values from 0 to 7, all different within a row; in each aligned block of 512 rows (0 to 511, 512 to 1023, ...) at most 160 rows name the same one
- seq_lens: int32 [32, 4], P('fsdp'), may hold values from 1 to 448, as said below
Outputs:
- layer_out: bfloat16 [16384, 2048], P(('fsdp', 'tp'))
- input_grad: bfloat16 [16384, 2048], P(('fsdp', 'tp'))
- attn_gain_grad: float32 [2048], P(('fsdp', 'tp'))
- q_down_grad: float32 [2048, 1536], P(('fsdp', 'tp'))
- q_gain_grad: float32 [1536], P(('fsdp', 'tp'))
- kv_down_grad: float32 [2048, 576], P(('fsdp', 'tp'))
- kv_gain_grad: float32 [512], P(('fsdp', 'tp'))
- q_up_grad: float32 [1536, 3072], P('fsdp', 'tp')
- kv_up_grad: float32 [512, 4096], P('fsdp', 'tp')
- out_proj_grad: float32 [2048, 2048], P('tp', 'fsdp')
- ffn_gain_grad: float32 [2048], P(('fsdp', 'tp'))
- router_grad: float32 [2048, 8], P(('fsdp', 'tp'))
- routed_gate_up_grad: float32 [8, 2048, 2, 1408], P(None, 'fsdp', None, 'tp')
- routed_down_grad: float32 [8, 1408, 2048], P(None, 'tp', 'fsdp')
- shared_gate_up_grad: float32 [2048, 2, 2816], P('fsdp', None, 'tp')
- shared_down_grad: float32 [2816, 2048], P('tp', 'fsdp')
The draws below stay inside these ranges and needn't reach their ends.
Inputs may be any that keep to these rules, and one draw needn't show every extreme that they name: `choices`: no expert is chosen by more than 160 of the rows of one group of 512 rows; some group reaches 160. `seq_lens`: each row sums to 512 and holds exactly one length 448.
All inputs are finite; a program needn't handle non-finite values.
Results may differ from the reference program's by a relative error of at most 0.03.
Values may be sent and summed in bfloat16 or wider, within the bound.
A program may use at most 384 MiB of HBM per device.

```python
import math
import jax
import jax.numpy as jnp
import numpy as np
from jax import lax

D = 2048
HEADS = 16
NOPE = 128
ROPE = 64
VDIM = 128
QR = 1536
KVR = 512
FFE = 1408
SFF = 2816
EXPERTS = 8
TOPK = 2
TOK_DEV = 128
CAP = 160
LONGEST = 448
TOKENS = 16384
N_FSDP = 32
N_TP = 4


def draw_seq_lens(key, part):
    key = jax.random.fold_in(key, 7)
    group_total = TOK_DEV * N_TP
    remainder = group_total - LONGEST

    def one_group(subkey):
        key_order, key_place = jax.random.split(subkey)
        shuffled = jax.random.permutation(key_order, remainder - 1) + 1
        cut_points = jnp.sort(shuffled[:2])
        pieces = jnp.stack([cut_points[0], cut_points[1] - cut_points[0], remainder - cut_points[1]]).astype(jnp.int32)
        longest = jnp.full((1,), LONGEST, jnp.int32)
        leading = jnp.concatenate([longest, pieces])
        swapped = jnp.concatenate([pieces[:1], longest, pieces[1:]])
        placed = jax.random.randint(key_place, (), 0, 2)
        return jnp.where(placed == 0, leading, swapped).astype(jnp.int32)
    return jax.vmap(one_group)(jax.random.split(key, N_FSDP))


def levels(rng, dims, cuts, smallest, high):
    level = 1.0
    for axis_at, blocks in cuts:
        heights = jax.random.uniform(jax.random.fold_in(jax.random.fold_in(rng, 6), axis_at), (blocks,), jnp.float32, smallest / len(cuts), high / len(cuts))
        level = level * jnp.repeat(jnp.exp(heights), dims[axis_at] // blocks).reshape((-1,) + (1,) * (len(dims) - 1 - axis_at))
    return level


def shared_out(stream_key, own, number, rows, count, top, reach, lean):
    ranking = jax.random.permutation(stream_key, count)
    crowded, ordinary = load_shares(count, rows * top, reach, lean, True), load_shares(count, rows * top, reach, lean, False)
    places = jnp.arange(count)

    def named(sizes, offset_by):
        used = int((sizes > 0).sum())
        fixed = max(1, used // 4)
        moved = fixed + (places - fixed + offset_by * (used - fixed)) % max(1, count - fixed)
        return jnp.zeros((count,), jnp.int32).at[ranking[jnp.where(places < fixed, places, moved)]].set(jnp.asarray(sizes, jnp.int32))

    sizes = jnp.where(number % 4 == 0, named(crowded, number // 4), named(ordinary, number - number // 4 - 1))
    mixed = jax.random.permutation(jax.random.fold_in(own, 3), count)
    donor, taker = mixed[0:count // 2 * 2:2], mixed[1:count // 2 * 2:2]
    slack = jnp.minimum(sizes[donor] - 1, reach - sizes[taker]) // 2
    slack = jnp.where((donor == ranking[0]) | (taker == ranking[0]) | (sizes[taker] == 0), 0, jnp.maximum(slack, 0))
    moved = jax.random.randint(jax.random.fold_in(own, 4), (count // 2,), 0, 1 << 20) % (slack + 1)
    sizes = sizes.at[donor].add(-moved).at[taker].add(moved)
    members = jnp.searchsorted(jnp.cumsum(sizes), jnp.arange(rows * top), side="right").astype(jnp.int32)
    grid = members.reshape(top, rows).T
    grid = grid[jax.random.permutation(jax.random.fold_in(own, 1), rows)]
    offset_by = jax.random.randint(jax.random.fold_in(own, 2), (rows, 1), 0, top)
    return jnp.take_along_axis(grid, (jnp.arange(top)[None, :] + offset_by) % top, axis=1)


def load_shares(amount, total, most, skew, full):
    weights = [(1 << 20) // math.isqrt(standing ** skew) + 1 for standing in range(1, amount + 1)]
    largest = most if full else min(most, max(-(-total // amount), total * weights[0] // sum(weights)))
    least = 1 if total - largest >= amount - 1 else 0
    given, surplus = [largest] + [least] * (amount - 1), total - largest - least * (amount - 1)
    while surplus > 0:
        free = [i for i in range(1, amount) if given[i] < largest] or [i for i in range(1, amount) if given[i] < most]
        pool, remaining = sum([weights[i] for i in free]), surplus
        for i in free:
            extra = min(most - given[i], max(1, remaining * weights[i] // pool), surplus)
            given[i] = given[i] + extra
            surplus = surplus - extra
    return np.array(given)


def normal_values(key, extent, scale, most, cuts=(), held_as=jnp.bfloat16):
    entries = scale * jax.random.normal(key, extent, jnp.float32)
    if cuts:
        entries = entries * levels(key, extent, cuts, -0.22, 0.18)
    return jnp.clip(entries, -most, most).astype(held_as)


def setup_inputs(seed: int = 0) -> dict:
    key_of = jax.random.split(jax.random.key(seed), 19)
    hidden_in = normal_values(key_of[0], (TOKENS, D), 1.0, 6.0, ((0, 128),))
    out_grad = normal_values(key_of[1], (TOKENS, D), 1.0, 6.0, ((0, 128),))
    attn_gain = jnp.clip(1.0 + 0.1 * jax.random.normal(key_of[2], (D,), jnp.float32), 0.5, 1.5).astype(jnp.bfloat16)
    q_down = normal_values(key_of[3], (D, QR), D ** -0.5, 0.125, ((0, 128),))
    q_gain = jnp.clip(1.0 + 0.1 * jax.random.normal(key_of[4], (QR,), jnp.float32), 0.5, 1.5).astype(jnp.bfloat16)
    kv_down = normal_values(key_of[5], (D, KVR + ROPE), D ** -0.5, 0.125, ((0, 128),))
    kv_gain = jnp.clip(1.0 + 0.1 * jax.random.normal(key_of[6], (KVR,), jnp.float32), 0.5, 1.5).astype(jnp.bfloat16)
    q_up = normal_values(key_of[7], (QR, HEADS * (NOPE + ROPE)), QR ** -0.5, 0.15625, ((0, 32), (1, 4)))
    kv_up = normal_values(key_of[8], (KVR, HEADS * (NOPE + VDIM)), KVR ** -0.5, 0.25, ((0, 32), (1, 4)))
    out_proj = normal_values(key_of[9], (HEADS * VDIM, D), (max(HEADS * VDIM // 128, 4)) ** -0.5, 1.5, ((0, 4), (1, 32)))
    ffn_gain = jnp.clip(1.0 + 0.1 * jax.random.normal(key_of[10], (D,), jnp.float32), 0.5, 1.5).astype(jnp.bfloat16)
    router = normal_values(key_of[11], (D, EXPERTS), D ** -0.5, 0.125, ((0, 128),))
    routed_gate_up = normal_values(key_of[12], (EXPERTS, D, 2, FFE), D ** -0.5, 0.125, ((1, 32), (3, 4)))
    routed_down = normal_values(key_of[13], (EXPERTS, FFE, D), FFE ** -0.5, 0.15625, ((1, 4), (2, 32)))
    shared_gate_up = normal_values(key_of[14], (D, 2, SFF), D ** -0.5, 0.125, ((0, 32), (2, 4)))
    shared_down = normal_values(key_of[15], (SFF, D), SFF ** -0.5, 0.109375, ((0, 4), (1, 32)))
    choices_keys = jax.random.split(jax.random.fold_in(key_of[16], 1), TOKENS // (TOK_DEV * N_TP))
    choices_turns = jax.random.permutation(jax.random.fold_in(key_of[16], 3), TOKENS // (TOK_DEV * N_TP))
    choices = jax.vmap(lambda own, number: shared_out(jax.random.fold_in(key_of[16], 2), own, number, TOK_DEV * N_TP, EXPERTS, TOPK, CAP, 1))(choices_keys, choices_turns).reshape((TOKENS, TOPK))
    seq_lens = draw_seq_lens(jax.random.fold_in(key_of[18], 71), 0)
    return dict(hidden_in=hidden_in, out_grad=out_grad, attn_gain=attn_gain, q_down=q_down, q_gain=q_gain, kv_down=kv_down, kv_gain=kv_gain, q_up=q_up, kv_up=kv_up, out_proj=out_proj, ffn_gain=ffn_gain, router=router, routed_gate_up=routed_gate_up, routed_down=routed_down, shared_gate_up=shared_gate_up, shared_down=shared_down, choices=choices, seq_lens=seq_lens)


theta_base = 50000.0
norm_eps = 1e-06
route_scale = 2.446
masked_score = -1e+30

@jax.custom_vjp
def low(v):
    return lax.optimization_barrier(v.astype(jnp.bfloat16)).astype(jnp.float32)

@jax.custom_vjp
def low_back(v):
    return v

def low_keep(v):
    return (low(v), None)

def low_pass(kept, grad):
    return (grad,)

def back_keep(v):
    return (v, None)

def back_low(kept, grad):
    return (low(grad),)
low.defvjp(low_keep, low_pass)
low_back.defvjp(back_keep, back_low)

def product(first_op, second_op):
    return jnp.dot(first_op, second_op, precision=lax.Precision.HIGHEST, preferred_element_type=jnp.float32)

def scaled_norm(values, weight):
    return values * lax.rsqrt(lax.optimization_barrier(jnp.mean(values * values, axis=-1, keepdims=True)) + norm_eps) * weight

def rotary_tables(position):
    half_size = ROPE // 2
    inverse = theta_base ** (-(2.0 * jnp.arange(half_size, dtype=jnp.float32)) / ROPE)
    angles = position.astype(jnp.float32)[:, None] * inverse[None, :]
    return (jnp.cos(angles), jnp.sin(angles))

def rotary(values, cosine, sine_table):
    half_size = values.shape[-1] // 2
    front_half = values[..., :half_size]
    back_half = values[..., half_size:]
    return jnp.concatenate([front_half * cosine - back_half * sine_table, back_half * cosine + front_half * sine_table], axis=-1)

def packing(lengths, total_rows):
    positions = jnp.arange(total_rows, dtype=jnp.int32)
    endings = jnp.cumsum(lengths).astype(jnp.int32)
    segment = lax.optimization_barrier(jnp.sum((positions[:, None] >= endings[None, :]).astype(jnp.int32), axis=1))
    starting = endings - lengths
    owner_mask = segment[:, None] == jnp.arange(lengths.shape[0], dtype=jnp.int32)[None, :]
    first_row = lax.optimization_barrier(jnp.sum(jnp.where(owner_mask, starting[None, :], 0), axis=1))
    return (segment, positions - first_row)

def attention_mask(segment):
    places = jnp.arange(segment.shape[0], dtype=jnp.int32)
    return (segment[:, None] == segment[None, :]) & (places[None, :] <= places[:, None])

def dispatch(picked, experts, capacity):
    flat_picks = picked.reshape(-1)
    onehot = (flat_picks[:, None] == jnp.arange(experts, dtype=jnp.int32)[None, :]).astype(jnp.int32)
    earlier = jnp.cumsum(onehot, axis=0) - onehot
    within = lax.optimization_barrier(jnp.sum(earlier * onehot, axis=1))
    target = flat_picks * capacity + within
    row_of = jnp.arange(flat_picks.shape[0], dtype=jnp.int32) // picked.shape[1]
    source = jnp.zeros((experts * capacity,), jnp.int32).at[target].set(row_of)
    return (target.reshape(picked.shape), source)

def swiglu(stacked):
    return jax.nn.silu(stacked[..., 0, :]) * stacked[..., 1, :]

def gate_values(logits, chosen_mask):
    scores = jax.nn.sigmoid(logits)
    picked = lax.optimization_barrier(jnp.sum(chosen_mask * scores[:, None, :], axis=-1))
    return route_scale * picked / lax.optimization_barrier(jnp.sum(picked, axis=-1, keepdims=True))

def group_layer(weights, block_rows, picked, lengths):
    attn_gain, q_down, q_gain, kv_down, kv_gain, q_up, kv_up, out_proj, ffn_gain, router, routed_gate_up, routed_down, shared_gate_up, shared_down = weights
    group_rows = TOK_DEV * N_TP
    segment, position = packing(lengths, group_rows)
    cosine, sine_table = rotary_tables(position)
    attn_in = low(scaled_norm(block_rows, attn_gain))
    query_raw = low_back(product(attn_in, q_down))
    keyval_raw = low_back(product(attn_in, kv_down))
    query_latent = low(scaled_norm(query_raw, q_gain))
    keyval_latent = low(scaled_norm(keyval_raw[:, :KVR], kv_gain))
    key_rotated = low(rotary(keyval_raw[:, KVR:], cosine, sine_table))
    query_all = low_back(product(query_latent, q_up)).reshape(group_rows, HEADS, NOPE + ROPE)
    query_rot = rotary(query_all[..., NOPE:], cosine[:, None, :], sine_table[:, None, :])
    query_heads = low(jnp.concatenate([query_all[..., :NOPE], query_rot], axis=-1))
    keyval_all = low_back(product(keyval_latent, kv_up)).reshape(group_rows, HEADS, NOPE + VDIM)
    rope_part = jnp.broadcast_to(key_rotated[:, None, :], (group_rows, HEADS, ROPE))
    key_heads = low(jnp.concatenate([keyval_all[..., :NOPE], rope_part], axis=-1))
    value_heads = low(keyval_all[..., NOPE:])
    raw_scores = low_back(jnp.einsum('qhd,khd->hqk', query_heads, key_heads, precision=lax.Precision.HIGHEST))
    scaled = jnp.where(attention_mask(segment)[None], raw_scores * (NOPE + ROPE) ** (-0.5), masked_score)
    exp_scores = jnp.exp(scaled - lax.optimization_barrier(jnp.max(scaled, axis=-1, keepdims=True)))
    attn_probs = exp_scores / lax.optimization_barrier(jnp.sum(exp_scores, axis=-1, keepdims=True))
    mixed = jnp.einsum('hqk,khd->qhd', low(attn_probs), value_heads, precision=lax.Precision.HIGHEST)
    heads_out = low(low_back(mixed)).reshape(group_rows, HEADS * VDIM)
    residual = block_rows + low_back(product(heads_out, out_proj))
    ffn_input = scaled_norm(residual, ffn_gain)
    chosen_mask = (picked[:, :, None] == jnp.arange(EXPERTS, dtype=jnp.int32)[None, None, :]).astype(jnp.float32)
    gate_weights = low(gate_values(product(ffn_input, router), chosen_mask))
    moe_in = low(ffn_input)
    target, source = dispatch(picked, EXPERTS, CAP)
    expert_in = moe_in[source].reshape(EXPERTS, CAP, D)
    gate_up = low_back(jnp.einsum('ecd,edjf->ecjf', expert_in, routed_gate_up, precision=lax.Precision.HIGHEST))
    hidden_low = low(swiglu(gate_up))
    expert_out = low_back(jnp.einsum('ecf,efd->ecd', hidden_low, routed_down, precision=lax.Precision.HIGHEST))
    expert_out = expert_out.reshape(EXPERTS * CAP, D)
    routed_sum = lax.optimization_barrier(jnp.sum(gate_weights[:, :, None] * expert_out[target], axis=1))
    common_gu = low_back(jnp.einsum('rd,djf->rjf', moe_in, shared_gate_up, precision=lax.Precision.HIGHEST))
    common_out = product(low(swiglu(common_gu)), shared_down)
    return residual + common_out + routed_sum

def reference(hidden_in, out_grad, attn_gain, q_down, q_gain, kv_down, kv_gain, q_up, kv_up, out_proj, ffn_gain, router, routed_gate_up, routed_down, shared_gate_up, shared_down, choices, seq_lens):
    group_rows = TOK_DEV * N_TP
    weights = tuple((w.astype(jnp.float32) for w in (attn_gain, q_down, q_gain, kv_down, kv_gain, q_up, kv_up, out_proj, ffn_gain, router, routed_gate_up, routed_down, shared_gate_up, shared_down)))
    inputs = hidden_in.astype(jnp.float32)
    picked = choices.reshape(N_FSDP, group_rows, TOPK)

    def forward(inputs, weights):

        def one_group(carried, element):
            return (carried, jax.checkpoint(group_layer)(weights, element[0], element[1], element[2]))
        carried_out, outputs = lax.scan(one_group, jnp.zeros((), jnp.float32), (inputs.reshape(N_FSDP, group_rows, D), picked, seq_lens))
        return outputs.reshape(N_FSDP * group_rows, D)
    result, pullback = jax.vjp(forward, inputs, weights)
    grad_in, grad_weights = pullback(out_grad.astype(jnp.float32))
    return (result.astype(jnp.bfloat16), grad_in.astype(jnp.bfloat16), grad_weights[0], grad_weights[1], grad_weights[2], grad_weights[3], grad_weights[4], grad_weights[5], grad_weights[6], grad_weights[7], grad_weights[8], grad_weights[9], grad_weights[10], grad_weights[11], grad_weights[12], grad_weights[13])
```

```python
import functools

import jax
import jax.numpy as jnp
from jax import lax
from jax.experimental import pallas as pl
from jax.experimental.pallas import tpu as pltpu
from jax.sharding import PartitionSpec as P

HEADS = 16
NOPE = 128
ROPE = 64
VDIM = 128
KVR = 512
TOPK = 2

theta_base = 50000.0
norm_eps = 1e-06
route_scale = 2.446
masked_score = -1e30

MESH = pl.DeviceIdType.MESH
BF = jnp.bfloat16
F32 = jnp.float32
MIB = 1 << 20


class Spot:
    def __init__(self):
        f, t = lax.axis_index("fsdp"), lax.axis_index("tp")
        self.t = t
        self.z, self.yl, self.x = lax.div(f, 8), lax.rem(lax.div(f, 4), 2), lax.rem(f, 4)
        self.yh, self.c = lax.div(t, 2), lax.rem(t, 2)
        self.y = self.yh * 2 + self.yl

    def at(self, z=None, yl=None, x=None, yh=None, c=None):
        z = self.z if z is None else z
        yl = self.yl if yl is None else yl
        x = self.x if x is None else x
        yh = self.yh if yh is None else yh
        c = self.c if c is None else c
        return ((z * 2 + yl) * 4 + x, yh * 2 + c)

    def along_x(self, by):
        return self.at(x=lax.rem(self.x + by, 4))

    def along_z(self, by):
        return self.at(z=lax.rem(self.z + by, 4))

    def along_y(self, by):
        y = lax.rem(self.y + by, 4)
        return self.at(yl=lax.rem(y, 2), yh=lax.div(y, 2))

    def pair(self):
        return self.at(yl=1 - self.yl)

    def core(self):
        return self.at(c=1 - self.c)

    def far(self):
        return self.at(yh=1 - self.yh)

    def diagonal(self):
        return self.at(yh=1 - self.yh, c=1 - self.c)

    def rings(self):
        return [self.along_x(1), self.along_x(3), self.along_z(1), self.along_z(3)]


def greet(devices):
    barrier = pltpu.get_barrier_semaphore()
    for device in devices:
        pl.semaphore_signal(barrier, inc=1, device_id=device, device_id_type=MESH)
    pl.semaphore_wait(barrier, len(devices))


class Wire:
    def __init__(self, send, recv, here):
        self.send, self.recv, self.here = send, recv, here
        self.sent = self.kept = 0

    def copy(self, source, target, device):
        made = pltpu.make_async_remote_copy(
            src_ref=source,
            dst_ref=target,
            send_sem=self.send.at[self.sent],
            recv_sem=self.recv.at[self.sent],
            device_id=device,
            device_id_type=MESH,
        )
        self.sent += 1
        made.start()
        return made

    def keep(self, source, target):
        made = pltpu.make_async_copy(source, target, self.here.at[self.kept])
        self.kept += 1
        made.start()
        return made


def wait_all(copies):
    for made in copies:
        made.wait()


def together(*parts):
    left = list(parts)
    while left:
        for part in list(left):
            if next(part, "over") == "over":
                left.remove(part)
        yield


def finish(part):
    for _ in part:
        pass


def add_into(target, *terms):
    lead, (rows, columns) = target.shape[:-2], target.shape[-2:]
    step = rows if rows * columns <= 49152 else 16
    pieces = rows // step
    count = pieces
    for size in lead:
        count *= size

    def body(i, carry):
        at = [pl.ds(pl.multiple_of(lax.rem(i, pieces) * step, 16), step)]
        i = lax.div(i, pieces)
        for size in reversed(lead):
            at.insert(0, lax.rem(i, size))
            i = lax.div(i, size)
        at = tuple(at)
        total = terms[0][at].astype(F32)
        for term in terms[1:]:
            total = total + term[at].astype(F32)
        target[at] = total.astype(target.dtype)
        return carry

    lax.fori_loop(0, count, body, 0)


def gather_ring(wire, pos, plus, minus, units):
    prev, following = lax.rem(pos + 3, 4), lax.rem(pos + 1, 4)
    right = [wire.copy(view(pos), view(pos), plus) for view, _ in units]
    left = [wire.copy(view(pos), view(pos), minus) for view, _ in units]
    yield
    wait_all(right)
    onward = [wire.copy(view(prev), view(prev), plus) for view, half in units if half == 0]
    wait_all(left)
    onward += [wire.copy(view(following), view(following), minus) for view, half in units if half == 1]
    yield
    wait_all(onward)


def sum_ring(wire, pos, plus, minus, units):
    prev, following, across = lax.rem(pos + 3, 4), lax.rem(pos + 1, 4), lax.rem(pos + 2, 4)
    first, direct, last = [], [], []
    for half, view, between, own, through, from_left, from_right, loads in units:
        first.append(wire.copy(view(across), through, plus if half == 0 else minus))
    for half, view, between, own, through, from_left, from_right, loads in units:
        if half == 0:
            direct.append(wire.copy(view(prev), from_right, minus))
        else:
            direct.append(wire.copy(view(following), from_left, plus))
    yield
    for made, (half, view, between, own, through, from_left, from_right, loads) in zip(first, units):
        wait_all(loads)
        made.wait()
        add_into(between, between, through)
        if half == 0:
            last.append(wire.copy(between, from_left, plus))
        else:
            last.append(wire.copy(between, from_right, minus))
    yield
    for one, two, (half, view, between, own, through, from_left, from_right, loads) in zip(direct, last, units):
        one.wait()
        two.wait()
        add_into(own, own, from_left, from_right)


def gather_tp(wire, spot, out, source):
    across = wire.copy(source, out.at[spot.t], spot.far())
    own = wire.keep(source, out.at[spot.t])
    other = wire.copy(source, out.at[spot.t], spot.core())
    yield
    across.wait()
    there = (1 - spot.yh) * 2 + spot.c
    last = wire.copy(out.at[there], out.at[there], spot.core())
    yield
    own.wait()
    other.wait()
    last.wait()


def gather_y(wire, spot, out, source):
    def view(rows):
        return lambda y: out.at[lax.rem(y, 2), lax.div(y, 2), spot.c, rows]

    rows = source.shape[0] // 2
    own = wire.keep(source, out.at[spot.yl, spot.yh, spot.c])
    other = [wire.copy(source, out.at[spot.yl, spot.yh, spot.c], spot.core())]
    own.wait()
    units = [(view(pl.ds(0, rows)), 0), (view(pl.ds(rows, rows)), 1)]
    yield from gather_ring(wire, spot.y, spot.along_y(1), spot.along_y(3), units)
    for by in (1, 2, 3):
        y = lax.rem(spot.y + by, 4)
        part = out.at[lax.rem(y, 2), lax.div(y, 2), spot.c]
        other.append(wire.copy(part, part, spot.core()))
    yield
    wait_all(other)


def sum_tp(wire, spot, source, out, got, held, last):
    cores = [wire.copy(source.at[yh * 2 + 1 - spot.c], got.at[yh], spot.core()) for yh in (0, 1)]
    yield
    wait_all(cores)
    there = 1 - spot.yh
    add_into(held, source.at[there * 2 + spot.c], got.at[there])
    across = wire.copy(held, last, spot.far())
    yield
    across.wait()
    add_into(out, source.at[spot.t], got.at[spot.yh], last)


def sum_y(wire, spot, source, out, got, held, through, from_left, from_right):
    cores = [wire.copy(source.at[y % 2, y // 2, 1 - spot.c], got.at[y], spot.core()) for y in range(4)]
    yield
    for y, made in enumerate(cores):
        made.wait()
        add_into(held.at[y], source.at[y % 2, y // 2, spot.c], got.at[y])
    rows = out.shape[0] // 2
    following, prev = lax.rem(spot.y + 1, 4), lax.rem(spot.y + 3, 4)
    units = []
    for half in (0, 1):
        part = pl.ds(half * rows, rows)
        units.append(
            (
                half,
                lambda y, part=part: held.at[y, part],
                held.at[following if half == 0 else prev, part],
                held.at[spot.y, part],
                through.at[part],
                from_left.at[part],
                from_right.at[part],
                [],
            )
        )
    yield from sum_ring(wire, spot.y, spot.along_y(1), spot.along_y(3), units)
    add_into(out, held.at[spot.y])


def sum_unit(wire, spot, half, part, order, scratch):
    following, prev = (lambda p: lax.rem(p + 1, 4)), (lambda p: lax.rem(p + 3, 4))
    (between, own, through, from_left, from_right), (between2, own2, through2, from_left2, from_right2) = scratch
    near = following if half == 0 else prev
    if order == "zx":
        view, pos, pos2 = (lambda i: part.at[:, i]), spot.z, spot.x
        view2 = lambda i: own.at[:, :, i]
    else:
        view, pos, pos2 = (lambda i: part.at[:, :, :, i]), spot.x, spot.z
        view2 = lambda i: own.at[:, i]

    def loads():
        return [wire.keep(view(near(pos)), between), wire.keep(view(pos), own)]

    def loads2():
        return [wire.keep(view2(near(pos2)), between2), wire.keep(view2(pos2), own2)]

    one = lambda: (half, view, between, own, through, from_left, from_right, loads())
    two = lambda: (half, view2, between2, own2, through2, from_left2, from_right2, loads2())
    return one, two, own2


def sum_stream(wire, spot, order, units):
    x = (spot.x, spot.along_x(1), spot.along_x(3))
    z = (spot.z, spot.along_z(1), spot.along_z(3))
    axes = (z, x) if order == "zx" else (x, z)
    yield from sum_ring(wire, *axes[0], [one() for one, _, _ in units])
    yield from sum_ring(wire, *axes[1], [two() for _, two, _ in units])


def unit_scratch(planes, order, rows, columns):
    first = (planes, 2, 4, rows, columns) if order == "zx" else (planes, 4, 2, rows, columns)
    second = (planes, 2, rows, columns)
    return [pltpu.VMEM(first, BF)] * 5 + [pltpu.VMEM(second, BF)] * 5


def call(kernel, number, outs, ins, scratch, copies, keeps, operands, vmem):
    space = {"hbm": pltpu.HBM, "vmem": pltpu.VMEM}
    return pl.pallas_call(
        kernel,
        out_shape=[jax.ShapeDtypeStruct(shape, dtype) for shape, dtype, _ in outs],
        in_specs=[pl.BlockSpec(memory_space=space[kind]) for kind in ins],
        out_specs=[pl.BlockSpec(memory_space=space[kind]) for _, _, kind in outs],
        scratch_shapes=list(scratch)
        + [
            pltpu.SemaphoreType.DMA((max(copies, 1),)),
            pltpu.SemaphoreType.DMA((max(copies, 1),)),
            pltpu.SemaphoreType.DMA((max(keeps, 1),)),
        ],
        compiler_params=pltpu.CompilerParams(
            collective_id=number, has_side_effects=True, vmem_limit_bytes=vmem * MIB
        ),
    )(*operands)


def head_gather_kernel(
    downs, q_up, kv_up, out_t, hidden, grad,
    all_downs, all_q, all_kv, all_out, all_hidden, all_grad,
    rows, send, recv, here,
):
    spot, wire = Spot(), Wire(send, recv, here)
    greet(spot.rings() + [spot.along_y(1), spot.along_y(3), spot.core(), spot.far(), spot.diagonal()])

    def weights():
        mine = rows.at[pl.ds(pl.multiple_of(spot.t * 16, 16), 16)]
        swaps = [wire.keep(downs.at[spot.t], mine)]
        for yh, c, device in (
            (spot.yh, 1 - spot.c, spot.core()),
            (1 - spot.yh, spot.c, spot.far()),
            (1 - spot.yh, 1 - spot.c, spot.diagonal()),
        ):
            swaps.append(wire.copy(downs.at[yh * 2 + c], mine, device))
        moves = []
        for source, target in ((q_up, all_q), (kv_up, all_kv), (out_t, all_out)):
            place = target.at[spot.z, spot.yl, spot.x]
            moves += [wire.copy(source, place, spot.pair()), wire.keep(source, place)]
        yield
        wait_all(swaps)
        place = all_downs.at[spot.z, spot.yl, spot.x]
        moves += [wire.copy(rows, place, spot.pair()), wire.keep(rows, place)]
        yield
        wait_all(moves)
        x = (spot.x, spot.along_x(1), spot.along_x(3))
        z = (spot.z, spot.along_z(1), spot.along_z(3))

        low, high = pl.ds(0, 32), pl.ds(32, 32)

        def x_then_z(*parts):
            yield from gather_ring(wire, *x, [((lambda i, r=r, cut=cut: r.at[spot.z, :, i, cut]), half) for r, half, cut in parts])
            yield from gather_ring(wire, *z, [((lambda i, r=r, cut=cut: r.at[i, :, :, cut]), half) for r, half, cut in parts])

        def z_then_x(*parts):
            yield from gather_ring(wire, *z, [((lambda i, r=r, cut=cut: r.at[i, :, spot.x, cut]), half) for r, half, cut in parts])
            yield from gather_ring(wire, *x, [((lambda i, r=r, cut=cut: r.at[:, :, i, cut]), half) for r, half, cut in parts])

        every = slice(None)
        yield from together(
            x_then_z((all_q, 0, every), (all_out, 1, every)),
            z_then_x((all_downs, 0, low), (all_kv, 0, every), (all_downs, 1, high)),
        )

    finish(together(weights(), gather_tp(wire, spot, all_hidden, hidden), gather_y(wire, spot, all_grad, grad)))


def head_gather(downs, q_up, kv_up, out_t, hidden, grad):
    rows, width = hidden.shape

    def spread(array):
        return ((4, 2, 4) + array.shape[-2:], BF, "hbm")

    outs = [
        ((4, 2, 4, 64, downs.shape[-1]), BF, "hbm"),
        spread(q_up), spread(kv_up), spread(out_t),
        ((4, rows, width), BF, "hbm"),
        ((2, 2, 2, rows, width), BF, "hbm"),
    ]
    return call(
        head_gather_kernel, 0, outs, ["hbm"] * 6, [pltpu.VMEM((64, downs.shape[-1]), BF)],
        64, 16, (downs, q_up, kv_up, out_t, hidden, grad), 16,
    )


def tp_gather_kernel(source, out, send, recv, here):
    spot, wire = Spot(), Wire(send, recv, here)
    greet([spot.core(), spot.far()])
    finish(gather_tp(wire, spot, out, source))


def tp_gather(array, number):
    return call(
        tp_gather_kernel, number, [((4,) + array.shape, array.dtype, "hbm")], ["hbm"], [], 3, 1, (array,), 16
    )[0]


def y_gather_kernel(source, out, send, recv, here):
    spot, wire = Spot(), Wire(send, recv, here)
    greet([spot.core(), spot.along_y(1), spot.along_y(3)])
    finish(gather_y(wire, spot, out, source))


def y_gather(array, number):
    return call(
        y_gather_kernel, number, [((2, 2, 2) + array.shape, array.dtype, "hbm")], ["hbm"], [], 12, 1, (array,), 16
    )[0]


def tp_sum_kernel(source, out, got, held, last, send, recv, here):
    spot, wire = Spot(), Wire(send, recv, here)
    greet([spot.core(), spot.far()])
    finish(sum_tp(wire, spot, source, out, got, held, last))


def tp_sum_scratch(rows, columns):
    return [pltpu.VMEM((2, rows, columns), BF), pltpu.VMEM((rows, columns), BF), pltpu.VMEM((rows, columns), BF)]


def tp_sum(array, number):
    _, rows, columns = array.shape
    return call(
        tp_sum_kernel, number, [((rows, columns), F32, "vmem")], ["vmem"], tp_sum_scratch(rows, columns),
        3, 1, (array,), 32,
    )[0]


def tp_swap_kernel(source, out, send, recv, here):
    spot, wire = Spot(), Wire(send, recv, here)
    greet([spot.core(), spot.far(), spot.diagonal()])
    moves = [wire.keep(source.at[spot.t], out.at[spot.t])]
    for yh, c, device in (
        (spot.yh, 1 - spot.c, spot.core()),
        (1 - spot.yh, spot.c, spot.far()),
        (1 - spot.yh, 1 - spot.c, spot.diagonal()),
    ):
        moves.append(wire.copy(source.at[yh * 2 + c], out.at[spot.t], device))
    wait_all(moves)


def tp_swap(array, number):
    return call(tp_swap_kernel, number, [(array.shape, array.dtype, "hbm")], ["hbm"], [], 3, 1, (array,), 16)[0]


def ffn_gather_kernel(gu, dn, sgu, sdn, all_gu, all_dn, all_sgu, all_sdn, send, recv, here):
    spot, wire = Spot(), Wire(send, recv, here)
    greet(spot.rings() + [spot.pair()])
    moves = []
    for source, target in ((gu, all_gu), (dn, all_dn), (sgu, all_sgu), (sdn, all_sdn)):
        place = target.at[:, spot.z, spot.yl, spot.x]
        moves += [wire.copy(source.at[1 - spot.yl], place, spot.pair()), wire.keep(source.at[spot.yl], place)]
    wait_all(moves)
    x = (spot.x, spot.along_x(1), spot.along_x(3))
    z = (spot.z, spot.along_z(1), spot.along_z(3))

    def x_then_z(*parts):
        yield from gather_ring(wire, *x, [((lambda i, r=r, cut=cut: r.at[cut, spot.z, :, i]), half) for r, half, cut in parts])
        yield from gather_ring(wire, *z, [((lambda i, r=r, cut=cut: r.at[cut, i]), half) for r, half, cut in parts])

    def z_then_x(*parts):
        yield from gather_ring(wire, *z, [((lambda i, r=r, cut=cut: r.at[cut, i, :, spot.x]), half) for r, half, cut in parts])
        yield from gather_ring(wire, *x, [((lambda i, r=r, cut=cut: r.at[cut, :, :, i]), half) for r, half, cut in parts])

    finish(
        together(
            x_then_z((all_gu, 0, pl.ds(0, 4)), (all_gu, 1, pl.ds(4, 4))),
            z_then_x((all_dn, 0, pl.ds(0, 4)), (all_sgu, 1, pl.ds(0, 2)), (all_sdn, 1, pl.ds(0, 1))),
        )
    )


def ffn_gather(*arrays):
    outs = [((a.shape[1], 4, 2, 4) + a.shape[2:], BF, "hbm") for a in arrays]
    return call(ffn_gather_kernel, 4, outs, ["hbm"] * 4, [], 40, 4, arrays, 16)


def ffn_sum_kernel(gu, dn, sgu, sdn, moe, back, o_gu, o_dn, o_sgu, o_sdn, o_moe, o_back, *rest):
    scratch, (send, recv, here) = list(rest[:-3]), rest[-3:]
    spot, wire = Spot(), Wire(send, recv, here)
    greet(spot.rings() + [spot.along_y(1), spot.along_y(3), spot.core()])

    def take(count):
        taken, scratch[:] = scratch[:count], scratch[count:]
        return taken

    def unit(half, part, order):
        return sum_unit(wire, spot, half, part, order, (take(5), take(5)))

    one = [unit(0, gu.at[pl.ds(0, 4)], "zx"), unit(1, gu.at[pl.ds(4, 4)], "zx")]
    two = [unit(0, dn, "xz"), unit(1, sgu, "xz"), unit(1, sdn, "xz")]
    tokens = [take(5), take(5)]

    def weights():
        yield from together(sum_stream(wire, spot, "zx", one), sum_stream(wire, spot, "xz", two))
        moves = []
        places = (
            (one[0][2], o_gu.at[spot.yl, pl.ds(0, 4)]),
            (one[1][2], o_gu.at[spot.yl, pl.ds(4, 4)]),
            (two[0][2], o_dn.at[spot.yl]),
            (two[1][2], o_sgu.at[spot.yl]),
            (two[2][2], o_sdn.at[spot.yl]),
        )
        for total, place in places:
            moves += [wire.copy(total.at[:, 1 - spot.yl], place, spot.pair()), wire.keep(total.at[:, spot.yl], place)]
        yield
        wait_all(moves)

    finish(
        together(
            weights(),
            sum_y(wire, spot, back, o_back, *tokens[0]),
            sum_y(wire, spot, moe, o_moe, *tokens[1]),
        )
    )


def ffn_sum(gu, dn, sgu, sdn, moe, back):
    outs = [((2, a.shape[0]) + a.shape[4:], BF, "hbm") for a in (gu, dn, sgu, sdn)]
    scratch = []
    for planes, order in ((4, "zx"), (4, "zx"), (4, "xz"), (2, "xz"), (1, "xz")):
        scratch += unit_scratch(planes, order, gu.shape[4], gu.shape[5])
    for tokens in (back, moe):
        rows, columns = tokens.shape[3:]
        outs.append(((rows, columns), F32, "vmem"))
        scratch += [pltpu.VMEM((4, rows, columns), BF)] * 2 + [pltpu.VMEM((rows, columns), BF)] * 3
    outs = outs[:4] + [outs[5], outs[4]]
    return call(
        ffn_sum_kernel, 5, outs, ["hbm"] * 4 + ["vmem"] * 2, scratch, 64, 32, (gu, dn, sgu, sdn, moe, back), 62
    )


def head_sum_kernel(downs, q_up, kv_up, out_t, part, o_downs, o_q, o_kv, o_out, o_part, *rest):
    scratch, (send, recv, here) = list(rest[:-3]), rest[-3:]
    spot, wire = Spot(), Wire(send, recv, here)
    greet(spot.rings() + [spot.pair(), spot.core(), spot.far(), spot.diagonal()])

    def take(count):
        taken, scratch[:] = scratch[:count], scratch[count:]
        return taken

    def unit(half, ref, order):
        return sum_unit(wire, spot, half, ref, order, (take(5), take(5)))

    one = [unit(0, q_up, "zx"), unit(1, out_t, "zx")]
    two = [unit(0, downs, "xz"), unit(1, kv_up, "xz")]
    (got_q, got_out, got_downs, got_kv, rows), tokens = take(5), take(3)

    def weights():
        yield from together(sum_stream(wire, spot, "zx", one), sum_stream(wire, spot, "xz", two))
        finals = (
            (two[0][2], got_downs, rows),
            (one[0][2], got_q, o_q),
            (one[1][2], got_out, o_out),
            (two[1][2], got_kv, o_kv),
        )
        moves = [wire.copy(total.at[:, 1 - spot.yl], got, spot.pair()) for total, got, _ in finals]
        yield
        swaps = []
        for made, (total, got, out) in zip(moves, finals):
            made.wait()
            add_into(out, total.at[0, spot.yl], got.at[0])
            if not swaps:
                cut = lambda t: rows.at[pl.ds(pl.multiple_of(t * 16, 16), 16)]
                swaps.append(wire.keep(cut(spot.t), o_downs.at[spot.t]))
                for yh, c, device in (
                    (spot.yh, 1 - spot.c, spot.core()),
                    (1 - spot.yh, spot.c, spot.far()),
                    (1 - spot.yh, 1 - spot.c, spot.diagonal()),
                ):
                    swaps.append(wire.copy(cut(yh * 2 + c), o_downs.at[spot.t], device))
        yield
        wait_all(swaps)

    finish(together(weights(), sum_tp(wire, spot, part, o_part, *tokens)))


def head_sum(downs, q_up, kv_up, out_t, part):
    scratch, ends = [], []
    for a, order in ((q_up, "zx"), (out_t, "zx"), (downs, "xz"), (kv_up, "xz")):
        scratch += unit_scratch(1, order, *a.shape[-2:])
        ends.append(pltpu.VMEM((1,) + a.shape[-2:], BF))
    scratch += ends + [pltpu.VMEM(downs.shape[-2:], BF)] + tp_sum_scratch(*part.shape[1:])
    outs = [((4, 16, downs.shape[-1]), BF, "hbm")]
    outs += [(a.shape[-2:], F32, "vmem") for a in (q_up, kv_up, out_t)]
    outs.append((part.shape[1:], F32, "vmem"))
    return call(
        head_sum_kernel, 9, outs, ["hbm"] * 4 + ["vmem"], scratch, 48, 24, (downs, q_up, kv_up, out_t, part), 40
    )


def rotary_tables(position):
    half_size = ROPE // 2
    inverse = theta_base ** (-(2.0 * jnp.arange(half_size, dtype=F32)) / ROPE)
    angles = position.astype(F32)[:, None] * inverse[None, :]
    return (jnp.cos(angles), jnp.sin(angles))


def rotary(values, cosine, sine_table):
    half_size = values.shape[-1] // 2
    front_half = values[..., :half_size]
    back_half = values[..., half_size:]
    return jnp.concatenate(
        [
            front_half * cosine - back_half * sine_table,
            back_half * cosine + front_half * sine_table,
        ],
        axis=-1,
    )


def unrotary(values, cosine, sine_table):
    return rotary(values, cosine, -sine_table)


def packing(lengths, total_rows):
    positions = jnp.arange(total_rows, dtype=jnp.int32)
    endings = jnp.cumsum(lengths)
    segment = jnp.sum((positions[:, None] >= endings[None, :]).astype(jnp.int32), axis=1)
    starting = endings - lengths
    owner_mask = segment[:, None] == jnp.arange(lengths.shape[0], dtype=jnp.int32)[None, :]
    first_row = jnp.sum(jnp.where(owner_mask, starting[None, :], 0), axis=1)
    return (segment, positions - first_row)


def attention_mask(segment):
    places = jnp.arange(segment.shape[0], dtype=jnp.int32)
    return (segment[:, None] == segment[None, :]) & (places[None, :] <= places[:, None])


def normalized(values):
    scale = lax.rsqrt(jnp.mean(values * values, axis=-1, keepdims=True) + norm_eps)
    return values * scale, scale


def norm_back(grad, gain, hat, scale):
    weighted = grad * gain
    return scale * (weighted - hat * jnp.mean(weighted * hat, axis=-1, keepdims=True))


def swiglu(gate, up):
    return jax.nn.silu(gate) * up


def gate_values(logits, chosen_mask):
    scores = jax.nn.sigmoid(logits)
    picked = jnp.sum(chosen_mask * scores[:, None, :], axis=-1)
    return route_scale * picked / jnp.sum(picked, axis=-1, keepdims=True)


def masked_scores(query_heads, key_heads, allowed):
    raw_scores = jnp.einsum("qhd,khd->hqk", query_heads, key_heads, preferred_element_type=F32)
    return jnp.where(allowed[None], raw_scores * (NOPE + ROPE) ** (-0.5), masked_score)


def mm(spec, a, b):
    return jnp.einsum(spec, a, b, preferred_element_type=F32)


def per_device(
    hidden_in,
    out_grad,
    attn_gain,
    q_down,
    q_gain,
    kv_down,
    kv_gain,
    q_up,
    kv_up,
    out_proj,
    ffn_gain,
    router,
    routed_gate_up,
    routed_down,
    shared_gate_up,
    shared_down,
    choices,
    seq_lens,
):
    local_rows, width = hidden_in.shape
    group_rows = choices.shape[0]
    tp_count = lax.axis_size("tp")
    tp_index = lax.axis_index("tp")
    y_lo = lax.rem(lax.div(lax.axis_index("fsdp"), 4), 2)
    head_count = HEADS // tp_count
    experts = router.shape[1]
    held = experts // 2
    capacity = 5 * group_rows * TOPK // (4 * experts)
    units = routed_gate_up.shape[3]
    row_shard = routed_gate_up.shape[1]
    q_cols, kv_cols = q_down.shape[1] // tp_count, kv_down.shape[1] // tp_count
    raw_cols = q_cols + kv_cols
    raw_pad = -raw_cols % 128
    small_at = raw_cols + raw_pad

    def own(array):
        return lax.dynamic_slice_in_dim(array, tp_index * local_rows, local_rows)

    down_rows = q_down.shape[0]
    columns = jnp.concatenate(
        [q_down.reshape(down_rows, tp_count, q_cols), kv_down.reshape(down_rows, tp_count, kv_cols)], axis=-1
    ).transpose(1, 0, 2)
    small = jnp.concatenate(
        [
            router,
            attn_gain[:, None],
            ffn_gain[:, None],
            jnp.pad(q_gain, (0, down_rows - q_gain.shape[0]))[:, None],
            jnp.pad(kv_gain, (0, down_rows - kv_gain.shape[0]))[:, None],
        ],
        axis=1,
    )
    small = jnp.pad(small, ((0, 0), (0, 128 - small.shape[1])))
    downs = jnp.concatenate(
        [
            jnp.pad(columns, ((0, 0), (0, 0), (0, raw_pad))),
            jnp.broadcast_to(small[None], (tp_count,) + small.shape),
        ],
        axis=-1,
    )
    send_gu = routed_gate_up.transpose(0, 2, 1, 3).reshape(2, held * 2, row_shard, units)
    send_dn = routed_down.transpose(0, 2, 1).reshape(2, held, row_shard, units)
    send_sgu = shared_gate_up.reshape(row_shard, 2, 2, units).transpose(2, 1, 0, 3)
    send_sdn = shared_down.T.reshape(row_shard, 2, units).transpose(1, 0, 2)[:, None]

    all_downs, all_q, all_kv, all_out, group_hidden, all_grad = head_gather(
        downs, q_up, kv_up, out_proj.T, hidden_in, out_grad
    )
    wide_gu, wide_dn, wide_sgu, wide_sdn = ffn_gather(send_gu, send_dn, send_sgu, send_sdn)
    all_downs = all_downs.reshape(width, -1)
    down_weight = all_downs[:, :raw_cols]
    up_query = all_q.reshape(-1, q_up.shape[1])
    up_keyval = all_kv.reshape(-1, kv_up.shape[1])
    out_weight = all_out.reshape(width, -1)
    gains = all_downs[:, small_at:].astype(F32)
    router_full = gains[:, :experts]
    again, fgain = gains[:, experts], gains[:, experts + 1]
    devices = width // down_rows
    qgain = gains[:, experts + 2].reshape(devices, down_rows)[:, : q_gain.shape[0]].reshape(-1)
    kvgain = gains[:, experts + 3].reshape(devices, down_rows)[:, : kv_gain.shape[0]].reshape(-1)
    wide_gu = wide_gu.reshape(held, 2, width, units)
    wide_dn = wide_dn.reshape(held, width, units)
    wide_sgu = wide_sgu.reshape(2, width, units)
    wide_sdn = wide_sdn.reshape(width, units)

    segment, position = packing(seq_lens[0], group_rows)
    cosine, sine_table = rotary_tables(position)
    own_cos, own_sin = own(cosine), own(sine_table)
    input_hat, input_scale = normalized(group_hidden.reshape(group_rows, width).astype(F32))
    attn_in = (input_hat * again).astype(BF)
    raw_part = mm("rd,dc->rc", attn_in, down_weight).astype(BF)
    raw = tp_gather(jnp.pad(raw_part, ((0, 0), (0, raw_pad))), 1)
    query_raw = raw[..., :q_cols].transpose(1, 0, 2).reshape(group_rows, -1).astype(F32)
    keyval_raw = raw[..., q_cols:raw_cols].transpose(1, 0, 2).reshape(group_rows, -1).astype(F32)
    query_hat, query_scale = normalized(query_raw)
    keyval_hat, keyval_scale = normalized(keyval_raw[:, :KVR])
    group_query = (query_hat * qgain).astype(BF)
    group_keyval = (keyval_hat * kvgain).astype(BF)
    group_rope = rotary(keyval_raw[:, KVR:], cosine, sine_table).astype(BF)
    query_all = mm("rl,lc->rc", group_query, up_query).reshape(group_rows, head_count, NOPE + ROPE)
    query_rot = rotary(query_all[..., NOPE:], cosine[:, None, :], sine_table[:, None, :])
    query_heads = jnp.concatenate([query_all[..., :NOPE], query_rot], axis=-1).astype(BF)
    keyval_all = mm("rl,lc->rc", group_keyval, up_keyval).reshape(group_rows, head_count, NOPE + VDIM)
    rope_part = jnp.broadcast_to(group_rope[:, None, :], (group_rows, head_count, ROPE))
    key_heads = jnp.concatenate([keyval_all[..., :NOPE].astype(BF), rope_part], axis=-1)
    value_heads = keyval_all[..., NOPE:].astype(BF)
    allowed = attention_mask(segment)
    scaled = masked_scores(query_heads, key_heads, allowed)
    row_peak = jnp.max(scaled, axis=-1, keepdims=True)
    exp_scores = jnp.exp(scaled - row_peak)
    totals = jnp.sum(exp_scores, axis=-1, keepdims=True)
    attn_probs = exp_scores / totals
    log_norm = row_peak + jnp.log(totals)
    heads_out = mm("hqk,khd->qhd", attn_probs.astype(BF), value_heads)
    heads_out = heads_out.reshape(group_rows, head_count * VDIM).astype(BF)
    attn_part = mm("rf,df->rd", heads_out, out_weight).astype(BF)
    attn_out = tp_sum(attn_part.reshape(tp_count, local_rows, width), 2)

    residual = hidden_in.astype(F32) + attn_out
    ffn_hat, ffn_scale = normalized(residual)
    ffn_input = ffn_hat * fgain
    logits = jnp.dot(ffn_input, router_full, precision=lax.Precision.HIGHEST, preferred_element_type=F32)
    expert_ids = jnp.arange(experts, dtype=jnp.int32)
    chosen_mask = (own(choices)[:, :, None] == expert_ids[None, None, :]).astype(F32)
    gate_low = lax.optimization_barrier(gate_values(logits, chosen_mask).astype(BF)).astype(F32)
    gate_dense = jnp.sum(chosen_mask * gate_low[:, :, None], axis=1)
    sent = jnp.concatenate([ffn_input, gate_dense, jnp.sum(chosen_mask, axis=1)], axis=1).astype(BF)
    sent = jnp.pad(sent, ((0, 0), (0, 128 - 2 * experts)))
    tokens = y_gather(sent, 3).reshape(2, group_rows, -1)

    moe_in = tokens[..., :width]
    grad_rows = all_grad.reshape(2, group_rows, width)
    extra = tokens[..., width:].astype(F32)
    gate_mine = lax.dynamic_slice_in_dim(extra, y_lo * held, held, axis=2).transpose(0, 2, 1)
    mask_mine = lax.dynamic_slice_in_dim(extra, experts + y_lo * held, held, axis=2).transpose(0, 2, 1)
    place = jnp.cumsum(mask_mine, axis=2) - mask_mine
    place = jnp.where(mask_mine > 0, place, -1.0).astype(jnp.int32)
    slots = place[:, :, None, :] == jnp.arange(capacity, dtype=jnp.int32)[None, None, :, None]
    onehot = slots.astype(BF)
    gate_slot = jnp.sum(jnp.where(slots, gate_mine[:, :, None, :], 0.0), axis=-1)
    gate_slot = gate_slot.transpose(1, 0, 2).reshape(held, 2 * capacity, 1)
    expert_in = mm("gest,gtd->egsd", onehot, moe_in).astype(BF).reshape(held, 2 * capacity, width)
    expert_dy = mm("gest,gtd->egsd", onehot, grad_rows).reshape(held, 2 * capacity, width)
    expert_grad = (gate_slot * expert_dy).astype(BF)
    gate = mm("ecd,edf->ecf", expert_in, wide_gu[:, 0])
    up = mm("ecd,edf->ecf", expert_in, wide_gu[:, 1])
    hidden_act, act_pull = jax.vjp(swiglu, gate, up)
    hidden_low = hidden_act.astype(BF)
    rows_out = mm("ecf,edf->ecd", hidden_low, wide_dn)
    grad_hidden = mm("ecd,edf->ecf", expert_grad, wide_dn)
    grad_gate, grad_up = (v.astype(BF) for v in act_pull(grad_hidden))
    sum_dn = mm("ecd,ecf->edf", expert_grad, hidden_low).astype(BF)
    sum_gu = jnp.stack(
        [mm("ecd,ecf->edf", expert_in, grad_gate).astype(BF), mm("ecd,ecf->edf", expert_in, grad_up).astype(BF)],
        axis=1,
    )
    back_rows = mm("ecf,edf->ecd", grad_gate, wide_gu[:, 0]) + mm("ecf,edf->ecd", grad_up, wide_gu[:, 1])
    gate_back = jnp.sum(rows_out * expert_dy, axis=-1).reshape(held, 2, capacity)
    slot_shape = (held, 2, capacity, width)
    weighted_out = (gate_slot * rows_out).astype(BF).reshape(slot_shape)
    routed_sum = mm("gest,egsd->gtd", onehot, weighted_out)
    routed_back = mm("gest,egsd->gtd", onehot, back_rows.astype(BF).reshape(slot_shape))
    dense_back = jnp.sum(jnp.where(slots, gate_back.transpose(1, 0, 2)[..., None], 0.0), axis=2)
    flat_in, flat_dy = moe_in.reshape(-1, width), grad_rows.reshape(-1, width)
    common_gate, common_up = mm("rd,df->rf", flat_in, wide_sgu[0]), mm("rd,df->rf", flat_in, wide_sgu[1])
    common_act, common_pull = jax.vjp(swiglu, common_gate, common_up)
    common_low = common_act.astype(BF)
    moe_part = mm("rf,df->rd", common_low, wide_sdn) + routed_sum.reshape(-1, width)
    common_dhid = mm("rd,df->rf", flat_dy, wide_sdn)
    common_dgate, common_dup = (v.astype(BF) for v in common_pull(common_dhid))
    sum_sdn = mm("rd,rf->df", flat_dy, common_low).astype(BF)
    sum_sgu = jnp.stack(
        [mm("rd,rf->df", flat_in, common_dgate).astype(BF), mm("rd,rf->df", flat_in, common_dup).astype(BF)]
    )
    moe_back = mm("rf,df->rd", common_dgate, wide_sgu[0]) + mm("rf,df->rd", common_dup, wide_sgu[1])
    moe_back = moe_back + routed_back.reshape(-1, width)
    dense_back = lax.dynamic_update_slice(
        jnp.zeros((2, group_rows, 128), F32), dense_back.transpose(0, 2, 1), (0, 0, y_lo * held)
    )
    back_part = jnp.concatenate([moe_back.astype(BF), dense_back.reshape(-1, 128).astype(BF)], axis=1)
    ring = (2, 2, 2, local_rows)
    blocks = (4, 2, 4, row_shard, units)
    own_gu, own_dn, own_sgu, own_sdn, moe_own, back_own = ffn_sum(
        sum_gu.reshape((held * 2,) + blocks),
        sum_dn.reshape((held,) + blocks),
        sum_sgu.reshape((2,) + blocks),
        sum_sdn.reshape((1,) + blocks),
        moe_part.astype(BF).reshape(ring + (width,)),
        back_part.reshape(ring + (width + 128,)),
    )

    layer_out = (residual + moe_own).astype(BF)
    grad_gates = jnp.sum(chosen_mask * back_own[:, None, width : width + experts], axis=-1)
    gate_pull = jax.vjp(lambda v: gate_values(v, chosen_mask), logits)[1]
    grad_logits = gate_pull(grad_gates)[0]
    grad_ffn = back_own[:, :width] + jnp.dot(
        grad_logits, router_full.T, precision=lax.Precision.HIGHEST, preferred_element_type=F32
    )
    grad_router = jnp.dot(
        ffn_input.T, grad_logits, precision=lax.Precision.HIGHEST, preferred_element_type=F32
    )
    grad_fgain = jnp.sum(grad_ffn * ffn_hat, axis=0)
    grad_resid = out_grad.astype(F32) + norm_back(grad_ffn, fgain, ffn_hat, ffn_scale)

    group_dh = tp_gather(grad_resid.astype(BF), 6).reshape(group_rows, width)
    grad_out_weight = mm("rd,rf->df", group_dh, heads_out).astype(BF)
    grad_heads = mm("rd,df->rf", group_dh, out_weight)
    grad_heads = grad_heads.reshape(group_rows, head_count, VDIM).astype(BF)
    again_probs = jnp.exp(masked_scores(query_heads, key_heads, allowed) - log_norm)
    grad_values = mm("hqk,qhd->khd", again_probs.astype(BF), grad_heads)
    grad_probs = mm("qhd,khd->hqk", grad_heads, value_heads)
    row_dot = jnp.sum(again_probs * grad_probs, axis=-1, keepdims=True)
    grad_scores = (again_probs * (grad_probs - row_dot) * (NOPE + ROPE) ** (-0.5)).astype(BF)
    grad_query = mm("hqk,khd->qhd", grad_scores, key_heads)
    grad_key = mm("hqk,qhd->khd", grad_scores, query_heads)
    grad_qrot = unrotary(grad_query[..., NOPE:], cosine[:, None, :], sine_table[:, None, :])
    grad_qall = jnp.concatenate([grad_query[..., :NOPE], grad_qrot], axis=-1).reshape(group_rows, -1).astype(BF)
    grad_kvall = jnp.concatenate([grad_key[..., :NOPE], grad_values], axis=-1).reshape(group_rows, -1).astype(BF)
    grad_krope = jnp.sum(grad_key[..., NOPE:], axis=1)
    grad_up_query = mm("rl,rc->lc", group_query, grad_qall).astype(BF)
    grad_up_keyval = mm("rl,rc->lc", group_keyval, grad_kvall).astype(BF)
    grad_latents = jnp.concatenate(
        [
            mm("rc,lc->rl", grad_qall, up_query),
            mm("rc,lc->rl", grad_kvall, up_keyval),
            grad_krope,
            jnp.zeros((group_rows, -grad_krope.shape[1] % 128), F32),
        ],
        axis=1,
    ).astype(BF)
    latents = tp_sum(grad_latents.reshape(tp_count, local_rows, -1), 7)
    q_rank = query_raw.shape[1]
    grad_qlatent, grad_kvlatent = latents[:, :q_rank], latents[:, q_rank : q_rank + KVR]
    grad_krotated = latents[:, q_rank + KVR : q_rank + KVR + ROPE]
    own_qhat, own_kvhat = own(query_hat), own(keyval_hat)
    grad_qgain = jnp.sum(grad_qlatent * own_qhat, axis=0)
    grad_kvgain = jnp.sum(grad_kvlatent * own_kvhat, axis=0)
    grad_qraw = norm_back(grad_qlatent, qgain, own_qhat, own(query_scale)).astype(BF)
    grad_kvnorm = norm_back(grad_kvlatent, kvgain, own_kvhat, own(keyval_scale))
    grad_kvrope = unrotary(grad_krotated, own_cos, own_sin)
    grad_kvraw = jnp.concatenate([grad_kvnorm, grad_kvrope], axis=-1).astype(BF)
    raw_back = jnp.concatenate(
        [grad_qraw.reshape(local_rows, tp_count, q_cols), grad_kvraw.reshape(local_rows, tp_count, kv_cols)], axis=-1
    ).transpose(1, 0, 2)
    raw_back = tp_swap(jnp.pad(raw_back, ((0, 0), (0, 0), (0, raw_pad))), 8)
    raw_back = raw_back.reshape(group_rows, -1)[:, :raw_cols]
    grad_down = mm("rd,rc->dc", attn_in, raw_back)
    attn_back = mm("rc,dc->rd", raw_back, down_weight)
    grad_again = jnp.sum(attn_back * input_hat, axis=0)

    def by_device(vector):
        each = vector.reshape(devices, -1)
        return jnp.pad(each, ((0, 0), (0, down_rows - each.shape[1]))).reshape(-1, 1)

    small_grads = jnp.concatenate(
        [grad_router, grad_again[:, None], grad_fgain[:, None], by_device(grad_qgain), by_device(grad_kvgain)], axis=1
    )
    small_grads = jnp.pad(small_grads, ((0, 0), (0, 128 - small_grads.shape[1])))
    grad_downs = jnp.concatenate([jnp.pad(grad_down, ((0, 0), (0, raw_pad))), small_grads], axis=1).astype(BF)

    def spread(array, like):
        return array.reshape((1, 4, 2, 4) + like.shape)

    got_downs, sum_up_query, sum_up_keyval, sum_out, attn_back_own = head_sum(
        grad_downs.reshape(1, 4, 2, 4, row_shard, -1),
        spread(grad_up_query, q_up),
        spread(grad_up_keyval, kv_up),
        spread(grad_out_weight, out_proj.T),
        attn_back.astype(BF).reshape(tp_count, local_rows, width),
    )
    input_grad = grad_resid + norm_back(attn_back_own, again, own(input_hat), own(input_scale))
    got_downs = got_downs.astype(F32)
    sum_qdown = got_downs[..., :q_cols].transpose(1, 0, 2).reshape(down_rows, -1)
    sum_kvdown = got_downs[..., q_cols:raw_cols].transpose(1, 0, 2).reshape(down_rows, -1)
    small_sum = jnp.sum(got_downs[..., small_at:], axis=0)
    sum_wide_gu = own_gu.reshape(experts, 2, row_shard, units).transpose(0, 2, 1, 3).astype(F32)
    sum_wide_down = own_dn.reshape(experts, row_shard, units).transpose(0, 2, 1).astype(F32)
    sum_common_gu = own_sgu.transpose(2, 1, 0, 3).reshape(row_shard, 2, 2 * units).astype(F32)
    sum_common_down = own_sdn[:, 0].transpose(1, 0, 2).reshape(row_shard, 2 * units).T.astype(F32)
    return (
        layer_out,
        input_grad.astype(BF),
        small_sum[:, experts],
        sum_qdown,
        small_sum[: q_gain.shape[0], experts + 2],
        sum_kvdown,
        small_sum[: kv_gain.shape[0], experts + 3],
        sum_up_query,
        sum_up_keyval,
        sum_out.T,
        small_sum[:, experts + 1],
        small_sum[:, :experts],
        sum_wide_gu,
        sum_wide_down,
        sum_common_gu,
        sum_common_down,
    )


def solution(mesh):
    return jax.shard_map(
        per_device,
        mesh=mesh,
        in_specs=(
            P(("fsdp", "tp"), None),
            P(("fsdp", "tp"), None),
            P(("fsdp", "tp")),
            P(("fsdp", "tp"), None),
            P(("fsdp", "tp")),
            P(("fsdp", "tp"), None),
            P(("fsdp", "tp")),
            P("fsdp", "tp"),
            P("fsdp", "tp"),
            P("tp", "fsdp"),
            P(("fsdp", "tp")),
            P(("fsdp", "tp"), None),
            P(None, "fsdp", None, "tp"),
            P(None, "tp", "fsdp"),
            P("fsdp", None, "tp"),
            P("tp", "fsdp"),
            P("fsdp", None),
            P("fsdp", None),
        ),
        out_specs=(
            P(("fsdp", "tp"), None),
            P(("fsdp", "tp"), None),
            P(("fsdp", "tp")),
            P(("fsdp", "tp"), None),
            P(("fsdp", "tp")),
            P(("fsdp", "tp"), None),
            P(("fsdp", "tp")),
            P("fsdp", "tp"),
            P("fsdp", "tp"),
            P("tp", "fsdp"),
            P(("fsdp", "tp")),
            P(("fsdp", "tp"), None),
            P(None, "fsdp", None, "tp"),
            P(None, "tp", "fsdp"),
            P("fsdp", None, "tp"),
            P("tp", "fsdp"),
        ),
        check_vma=False,
    )
```

```python
import functools

import jax
import jax.numpy as jnp
from jax import lax
from jax.experimental import pallas as pl
from jax.experimental.pallas import tpu as pltpu
from jax.sharding import PartitionSpec as P

HEADS = 16
NOPE = 128
ROPE = 64
VDIM = 128
KVR = 512
TOPK = 2

theta_base = 50000.0
norm_eps = 1e-06
route_scale = 2.446
masked_score = -1e30

MESH = pl.DeviceIdType.MESH
BF = jnp.bfloat16
F32 = jnp.float32
MIB = 1 << 20


class Spot:
    def __init__(self):
        f, t = lax.axis_index("fsdp"), lax.axis_index("tp")
        self.t = t
        self.z, self.yl, self.x = lax.div(f, 8), lax.rem(lax.div(f, 4), 2), lax.rem(f, 4)
        self.yh, self.c = lax.div(t, 2), lax.rem(t, 2)
        self.y = self.yh * 2 + self.yl

    def at(self, z=None, yl=None, x=None, yh=None, c=None):
        z = self.z if z is None else z
        yl = self.yl if yl is None else yl
        x = self.x if x is None else x
        yh = self.yh if yh is None else yh
        c = self.c if c is None else c
        return ((z * 2 + yl) * 4 + x, yh * 2 + c)

    def along_x(self, by):
        return self.at(x=lax.rem(self.x + by, 4))

    def along_z(self, by):
        return self.at(z=lax.rem(self.z + by, 4))

    def along_y(self, by):
        y = lax.rem(self.y + by, 4)
        return self.at(yl=lax.rem(y, 2), yh=lax.div(y, 2))

    def pair(self):
        return self.at(yl=1 - self.yl)

    def core(self):
        return self.at(c=1 - self.c)

    def far(self):
        return self.at(yh=1 - self.yh)

    def diagonal(self):
        return self.at(yh=1 - self.yh, c=1 - self.c)

    def rings(self):
        return [self.along_x(1), self.along_x(3), self.along_z(1), self.along_z(3)]


def greet(devices):
    barrier = pltpu.get_barrier_semaphore()
    for device in devices:
        pl.semaphore_signal(barrier, inc=1, device_id=device, device_id_type=MESH)
    pl.semaphore_wait(barrier, len(devices))


class Wire:
    def __init__(self, send, recv, here):
        self.send, self.recv, self.here = send, recv, here
        self.sent = self.kept = 0

    def copy(self, source, target, device):
        made = pltpu.make_async_remote_copy(
            src_ref=source,
            dst_ref=target,
            send_sem=self.send.at[self.sent],
            recv_sem=self.recv.at[self.sent],
            device_id=device,
            device_id_type=MESH,
        )
        self.sent += 1
        made.start()
        return made

    def keep(self, source, target):
        made = pltpu.make_async_copy(source, target, self.here.at[self.kept])
        self.kept += 1
        made.start()
        return made


def wait_all(copies):
    for made in copies:
        made.wait()


def together(*parts):
    left = list(parts)
    while left:
        for part in list(left):
            if next(part, "over") == "over":
                left.remove(part)
        yield


def finish(part):
    for _ in part:
        pass


def add_into(target, *terms):
    lead, (rows, columns) = target.shape[:-2], target.shape[-2:]
    step = rows if rows * columns <= 49152 else 16
    pieces = rows // step
    count = pieces
    for size in lead:
        count *= size

    def body(i, carry):
        at = [pl.ds(pl.multiple_of(lax.rem(i, pieces) * step, 16), step)]
        i = lax.div(i, pieces)
        for size in reversed(lead):
            at.insert(0, lax.rem(i, size))
            i = lax.div(i, size)
        at = tuple(at)
        total = terms[0][at].astype(F32)
        for term in terms[1:]:
            total = total + term[at].astype(F32)
        target[at] = total.astype(target.dtype)
        return carry

    lax.fori_loop(0, count, body, 0)


def gather_ring(wire, pos, plus, minus, units):
    prev, following = lax.rem(pos + 3, 4), lax.rem(pos + 1, 4)
    right = [wire.copy(view(pos), view(pos), plus) for view, _ in units]
    left = [wire.copy(view(pos), view(pos), minus) for view, _ in units]
    yield
    wait_all(right)
    onward = [wire.copy(view(prev), view(prev), plus) for view, half in units if half == 0]
    wait_all(left)
    onward += [wire.copy(view(following), view(following), minus) for view, half in units if half == 1]
    yield
    wait_all(onward)


def sum_ring(wire, pos, plus, minus, units):
    prev, following, across = lax.rem(pos + 3, 4), lax.rem(pos + 1, 4), lax.rem(pos + 2, 4)
    first, direct, last = [], [], []
    for half, view, between, own, through, from_left, from_right, loads in units:
        first.append(wire.copy(view(across), through, plus if half == 0 else minus))
    for half, view, between, own, through, from_left, from_right, loads in units:
        if half == 0:
            direct.append(wire.copy(view(prev), from_right, minus))
        else:
            direct.append(wire.copy(view(following), from_left, plus))
    yield
    for made, (half, view, between, own, through, from_left, from_right, loads) in zip(first, units):
        wait_all(loads)
        made.wait()
        add_into(between, between, through)
        if half == 0:
            last.append(wire.copy(between, from_left, plus))
        else:
            last.append(wire.copy(between, from_right, minus))
    yield
    for one, two, (half, view, between, own, through, from_left, from_right, loads) in zip(direct, last, units):
        one.wait()
        two.wait()
        add_into(own, own, from_left, from_right)


def gather_tp(wire, spot, out, source):
    across = wire.copy(source, out.at[spot.t], spot.far())
    own = wire.keep(source, out.at[spot.t])
    other = wire.copy(source, out.at[spot.t], spot.core())
    yield
    across.wait()
    there = (1 - spot.yh) * 2 + spot.c
    last = wire.copy(out.at[there], out.at[there], spot.core())
    yield
    own.wait()
    other.wait()
    last.wait()


def gather_y(wire, spot, out, source):
    def view(rows):
        return lambda y: out.at[lax.rem(y, 2), lax.div(y, 2), spot.c, rows]

    rows = source.shape[0] // 2
    own = wire.keep(source, out.at[spot.yl, spot.yh, spot.c])
    other = [wire.copy(source, out.at[spot.yl, spot.yh, spot.c], spot.core())]
    own.wait()
    units = [(view(pl.ds(0, rows)), 0), (view(pl.ds(rows, rows)), 1)]
    yield from gather_ring(wire, spot.y, spot.along_y(1), spot.along_y(3), units)
    for by in (1, 2, 3):
        y = lax.rem(spot.y + by, 4)
        part = out.at[lax.rem(y, 2), lax.div(y, 2), spot.c]
        other.append(wire.copy(part, part, spot.core()))
    yield
    wait_all(other)


def sum_tp(wire, spot, source, out, got, held, last):
    cores = [wire.copy(source.at[yh * 2 + 1 - spot.c], got.at[yh], spot.core()) for yh in (0, 1)]
    yield
    wait_all(cores)
    there = 1 - spot.yh
    add_into(held, source.at[there * 2 + spot.c], got.at[there])
    across = wire.copy(held, last, spot.far())
    yield
    across.wait()
    add_into(out, source.at[spot.t], got.at[spot.yh], last)


def sum_y(wire, spot, source, out, got, held, through, from_left, from_right):
    cores = [wire.copy(source.at[y % 2, y // 2, 1 - spot.c], got.at[y], spot.core()) for y in range(4)]
    yield
    for y, made in enumerate(cores):
        made.wait()
        add_into(held.at[y], source.at[y % 2, y // 2, spot.c], got.at[y])
    rows = out.shape[0] // 2
    following, prev = lax.rem(spot.y + 1, 4), lax.rem(spot.y + 3, 4)
    units = []
    for half in (0, 1):
        part = pl.ds(half * rows, rows)
        units.append(
            (
                half,
                lambda y, part=part: held.at[y, part],
                held.at[following if half == 0 else prev, part],
                held.at[spot.y, part],
                through.at[part],
                from_left.at[part],
                from_right.at[part],
                [],
            )
        )
    yield from sum_ring(wire, spot.y, spot.along_y(1), spot.along_y(3), units)
    add_into(out, held.at[spot.y])


def sum_unit(wire, spot, half, part, order, scratch):
    following, prev = (lambda p: lax.rem(p + 1, 4)), (lambda p: lax.rem(p + 3, 4))
    (between, own, through, from_left, from_right), (between2, own2, through2, from_left2, from_right2) = scratch
    near = following if half == 0 else prev
    if order == "zx":
        view, pos, pos2 = (lambda i: part.at[:, i]), spot.z, spot.x
        view2 = lambda i: own.at[:, :, i]
    else:
        view, pos, pos2 = (lambda i: part.at[:, :, :, i]), spot.x, spot.z
        view2 = lambda i: own.at[:, i]

    def loads():
        return [wire.keep(view(near(pos)), between), wire.keep(view(pos), own)]

    def loads2():
        return [wire.keep(view2(near(pos2)), between2), wire.keep(view2(pos2), own2)]

    one = lambda: (half, view, between, own, through, from_left, from_right, loads())
    two = lambda: (half, view2, between2, own2, through2, from_left2, from_right2, loads2())
    return one, two, own2


def sum_stream(wire, spot, order, units):
    x = (spot.x, spot.along_x(1), spot.along_x(3))
    z = (spot.z, spot.along_z(1), spot.along_z(3))
    axes = (z, x) if order == "zx" else (x, z)
    yield from sum_ring(wire, *axes[0], [one() for one, _, _ in units])
    yield from sum_ring(wire, *axes[1], [two() for _, two, _ in units])


def unit_scratch(planes, order, rows, columns):
    first = (planes, 2, 4, rows, columns) if order == "zx" else (planes, 4, 2, rows, columns)
    second = (planes, 2, rows, columns)
    return [pltpu.VMEM(first, BF)] * 5 + [pltpu.VMEM(second, BF)] * 5


def call(kernel, number, outs, ins, scratch, copies, keeps, operands, vmem):
    space = {"hbm": pltpu.HBM, "vmem": pltpu.VMEM}
    return pl.pallas_call(
        kernel,
        out_shape=[jax.ShapeDtypeStruct(shape, dtype) for shape, dtype, _ in outs],
        in_specs=[pl.BlockSpec(memory_space=space[kind]) for kind in ins],
        out_specs=[pl.BlockSpec(memory_space=space[kind]) for _, _, kind in outs],
        scratch_shapes=list(scratch)
        + [
            pltpu.SemaphoreType.DMA((max(copies, 1),)),
            pltpu.SemaphoreType.DMA((max(copies, 1),)),
            pltpu.SemaphoreType.DMA((max(keeps, 1),)),
        ],
        compiler_params=pltpu.CompilerParams(
            collective_id=number, has_side_effects=True, vmem_limit_bytes=vmem * MIB
        ),
    )(*operands)


def tp_gather_kernel(source, out, send, recv, here):
    spot, wire = Spot(), Wire(send, recv, here)
    greet([spot.core(), spot.far()])
    finish(gather_tp(wire, spot, out, source))


def tp_gather(array, number):
    return call(
        tp_gather_kernel, number, [((4,) + array.shape, array.dtype, "hbm")], ["hbm"], [], 3, 1, (array,), 16
    )[0]


def tp_sum_kernel(source, out, got, held, last, send, recv, here):
    spot, wire = Spot(), Wire(send, recv, here)
    greet([spot.core(), spot.far()])
    finish(sum_tp(wire, spot, source, out, got, held, last))


def tp_sum_scratch(rows, columns):
    return [pltpu.VMEM((2, rows, columns), BF), pltpu.VMEM((rows, columns), BF), pltpu.VMEM((rows, columns), BF)]


def tp_sum(array, number):
    _, rows, columns = array.shape
    return call(
        tp_sum_kernel, number, [((rows, columns), F32, "vmem")], ["vmem"], tp_sum_scratch(rows, columns),
        3, 1, (array,), 32,
    )[0]


def tp_swap_kernel(source, out, send, recv, here):
    spot, wire = Spot(), Wire(send, recv, here)
    greet([spot.core(), spot.far(), spot.diagonal()])
    moves = [wire.keep(source.at[spot.t], out.at[spot.t])]
    for yh, c, device in (
        (spot.yh, 1 - spot.c, spot.core()),
        (1 - spot.yh, spot.c, spot.far()),
        (1 - spot.yh, 1 - spot.c, spot.diagonal()),
    ):
        moves.append(wire.copy(source.at[yh * 2 + c], out.at[spot.t], device))
    wait_all(moves)


def tp_swap(array, number):
    return call(tp_swap_kernel, number, [(array.shape, array.dtype, "hbm")], ["hbm"], [], 3, 1, (array,), 16)[0]


def ffn_sum_kernel(gu, dn, sgu, sdn, moe, back, o_gu, o_dn, o_sgu, o_sdn, o_moe, o_back, *rest):
    scratch, (send, recv, here) = list(rest[:-3]), rest[-3:]
    spot, wire = Spot(), Wire(send, recv, here)
    greet(spot.rings() + [spot.along_y(1), spot.along_y(3), spot.core()])

    def take(count):
        taken, scratch[:] = scratch[:count], scratch[count:]
        return taken

    def unit(half, part, order):
        return sum_unit(wire, spot, half, part, order, (take(5), take(5)))

    one = [unit(0, gu.at[pl.ds(0, 4)], "zx"), unit(1, gu.at[pl.ds(4, 4)], "zx")]
    two = [unit(0, dn, "xz"), unit(1, sgu, "xz"), unit(1, sdn, "xz")]
    tokens = [take(5), take(5)]

    def weights():
        yield from together(sum_stream(wire, spot, "zx", one), sum_stream(wire, spot, "xz", two))
        moves = []
        places = (
            (one[0][2], o_gu.at[spot.yl, pl.ds(0, 4)]),
            (one[1][2], o_gu.at[spot.yl, pl.ds(4, 4)]),
            (two[0][2], o_dn.at[spot.yl]),
            (two[1][2], o_sgu.at[spot.yl]),
            (two[2][2], o_sdn.at[spot.yl]),
        )
        for total, place in places:
            moves += [wire.copy(total.at[:, 1 - spot.yl], place, spot.pair()), wire.keep(total.at[:, spot.yl], place)]
        yield
        wait_all(moves)

    finish(
        together(
            weights(),
            sum_y(wire, spot, back, o_back, *tokens[0]),
            sum_y(wire, spot, moe, o_moe, *tokens[1]),
        )
    )


def ffn_sum(gu, dn, sgu, sdn, moe, back):
    outs = [((2, a.shape[0]) + a.shape[4:], BF, "hbm") for a in (gu, dn, sgu, sdn)]
    scratch = []
    for planes, order in ((4, "zx"), (4, "zx"), (4, "xz"), (2, "xz"), (1, "xz")):
        scratch += unit_scratch(planes, order, gu.shape[4], gu.shape[5])
    for tokens in (back, moe):
        rows, columns = tokens.shape[3:]
        outs.append(((rows, columns), F32, "vmem"))
        scratch += [pltpu.VMEM((4, rows, columns), BF)] * 2 + [pltpu.VMEM((rows, columns), BF)] * 3
    outs = outs[:4] + [outs[5], outs[4]]
    return call(
        ffn_sum_kernel, 5, outs, ["hbm"] * 4 + ["vmem"] * 2, scratch, 64, 32, (gu, dn, sgu, sdn, moe, back), 62
    )


def head_sum_kernel(downs, q_up, kv_up, out_t, part, o_downs, o_q, o_kv, o_out, o_part, *rest):
    scratch, (send, recv, here) = list(rest[:-3]), rest[-3:]
    spot, wire = Spot(), Wire(send, recv, here)
    greet(spot.rings() + [spot.pair(), spot.core(), spot.far(), spot.diagonal()])

    def take(count):
        taken, scratch[:] = scratch[:count], scratch[count:]
        return taken

    def unit(half, ref, order):
        return sum_unit(wire, spot, half, ref, order, (take(5), take(5)))

    one = [unit(0, q_up, "zx"), unit(1, out_t, "zx")]
    two = [unit(0, downs, "xz"), unit(1, kv_up, "xz")]
    (got_q, got_out, got_downs, got_kv, rows), tokens = take(5), take(3)

    def weights():
        yield from together(sum_stream(wire, spot, "zx", one), sum_stream(wire, spot, "xz", two))
        finals = (
            (two[0][2], got_downs, rows),
            (one[0][2], got_q, o_q),
            (one[1][2], got_out, o_out),
            (two[1][2], got_kv, o_kv),
        )
        moves = [wire.copy(total.at[:, 1 - spot.yl], got, spot.pair()) for total, got, _ in finals]
        yield
        swaps = []
        for made, (total, got, out) in zip(moves, finals):
            made.wait()
            add_into(out, total.at[0, spot.yl], got.at[0])
            if not swaps:
                cut = lambda t: rows.at[pl.ds(pl.multiple_of(t * 16, 16), 16)]
                swaps.append(wire.keep(cut(spot.t), o_downs.at[spot.t]))
                for yh, c, device in (
                    (spot.yh, 1 - spot.c, spot.core()),
                    (1 - spot.yh, spot.c, spot.far()),
                    (1 - spot.yh, 1 - spot.c, spot.diagonal()),
                ):
                    swaps.append(wire.copy(cut(yh * 2 + c), o_downs.at[spot.t], device))
        yield
        wait_all(swaps)

    finish(together(weights(), sum_tp(wire, spot, part, o_part, *tokens)))


def head_sum(downs, q_up, kv_up, out_t, part):
    scratch, ends = [], []
    for a, order in ((q_up, "zx"), (out_t, "zx"), (downs, "xz"), (kv_up, "xz")):
        scratch += unit_scratch(1, order, *a.shape[-2:])
        ends.append(pltpu.VMEM((1,) + a.shape[-2:], BF))
    scratch += ends + [pltpu.VMEM(downs.shape[-2:], BF)] + tp_sum_scratch(*part.shape[1:])
    outs = [((4, 16, downs.shape[-1]), BF, "hbm")]
    outs += [(a.shape[-2:], F32, "vmem") for a in (q_up, kv_up, out_t)]
    outs.append((part.shape[1:], F32, "vmem"))
    return call(
        head_sum_kernel, 9, outs, ["hbm"] * 4 + ["vmem"], scratch, 48, 24, (downs, q_up, kv_up, out_t, part), 40
    )


def dot(a, b, dims="nn", precision=None):
    left, right = {"nn": (1, 0), "nt": (1, 1), "tn": (0, 0)}[dims]
    return lax.dot_general(
        a, b, (((left,), (right,)), ((), ())), precision=precision, preferred_element_type=F32
    )


def loop(count, body):
    def step(i, carry):
        body(i)
        return carry

    lax.fori_loop(0, count, step, 0)


def at_tile(i, size):
    return pl.ds(pl.multiple_of(i * size, size), size)


def flat(block):
    return block.reshape(-1, block.shape[-1])


def lane_grid(rows, columns):
    return (
        lax.broadcasted_iota(jnp.int32, (rows, columns), 0),
        lax.broadcasted_iota(jnp.int32, (rows, columns), 1),
    )


def head_lanes(values, head):
    lanes = lax.broadcasted_iota(jnp.int32, (1, values.shape[1]), 1)
    return values * (lax.div(lanes, 32) == head).astype(F32).astype(values.dtype)


def all_sum_small(wire, spot, buffers, own):
    steps = (
        [spot.core()],
        [spot.far()],
        [spot.pair()],
        [spot.along_x(1), spot.along_x(2), spot.along_x(3)],
        [spot.along_z(1), spot.along_z(2), spot.along_z(3)],
    )
    for step, devices in enumerate(steps):
        moves = [wire.copy(own.at[step], buffers.at[step, i], device) for i, device in enumerate(devices)]
        yield
        wait_all(moves)
        total = own[step]
        for i in range(len(devices)):
            total = total + buffers[step, i]
        own[step + 1] = total


def ffn_stream(wire, spot, sources, targets):
    moves = []
    for source, target in zip(sources, targets):
        place = target.at[:, spot.z, spot.yl, spot.x]
        moves += [wire.copy(source.at[1 - spot.yl], place, spot.pair()), wire.keep(source.at[spot.yl], place)]
    yield
    wait_all(moves)
    x = (spot.x, spot.along_x(1), spot.along_x(3))
    z = (spot.z, spot.along_z(1), spot.along_z(3))
    gu, dn, sgu, sdn = targets

    def x_then_z(*parts):
        yield from gather_ring(wire, *x, [((lambda i, r=r, cut=cut: r.at[cut, spot.z, :, i]), half) for r, half, cut in parts])
        yield from gather_ring(wire, *z, [((lambda i, r=r, cut=cut: r.at[cut, i]), half) for r, half, cut in parts])

    def z_then_x(*parts):
        yield from gather_ring(wire, *z, [((lambda i, r=r, cut=cut: r.at[cut, i, :, spot.x]), half) for r, half, cut in parts])
        yield from gather_ring(wire, *x, [((lambda i, r=r, cut=cut: r.at[cut, :, :, i]), half) for r, half, cut in parts])

    yield from together(
        x_then_z((gu, 0, pl.ds(0, 4)), (gu, 1, pl.ds(4, 4))),
        z_then_x((dn, 0, pl.ds(0, 4)), (sgu, 1, pl.ds(0, 2)), (sdn, 1, pl.ds(0, 1))),
    )


def front_kernel(
    downs, q_up, kv_up, out_t, hidden, grad, gu, dn, sgu, sdn, small, cosine, sine, seg_col, seg_row, pick_a, pick_b,
    pick_sent,
    o_downs, o_q, o_kv, o_out, o_grad, o_gu, o_dn, o_sgu, o_sdn, o_tokens,
    o_hidden, o_hat, o_raw, o_qhat, o_kvhat, o_query, o_keyval, o_rope, o_norm, o_heads, o_resid, o_logits, o_small,
    rows, s_downs, s_q, s_kv, s_out, s_hidden, s_hat, s_part, s_raw, s_qlat, s_kvlat, s_query, s_keyval, s_rope,
    s_norm, s_heads, s_attn, s_sum, s_resid, s_sent, s_small, s_buf, t_got, t_held, t_last,
    send, recv, here,
):
    spot, wire = Spot(), Wire(send, recv, here)
    greet(
        spot.rings()
        + [spot.along_x(2), spot.along_z(2), spot.along_y(1), spot.along_y(3)]
        + [spot.core(), spot.far(), spot.diagonal()]
    )
    groups, width = 4 * hidden.shape[0], hidden.shape[1]
    own_rows = hidden.shape[0]

    def weights():
        mine = rows.at[pl.ds(pl.multiple_of(spot.t * 16, 16), 16)]
        swaps = [wire.keep(downs.at[spot.t], mine)]
        for yh, c, device in (
            (spot.yh, 1 - spot.c, spot.core()),
            (1 - spot.yh, spot.c, spot.far()),
            (1 - spot.yh, 1 - spot.c, spot.diagonal()),
        ):
            swaps.append(wire.copy(downs.at[yh * 2 + c], mine, device))
        moves = []
        for source, target in ((q_up, s_q), (kv_up, s_kv), (out_t, s_out)):
            place = target.at[spot.z, spot.yl, spot.x]
            moves += [wire.copy(source, place, spot.pair()), wire.keep(source, place)]
        yield
        wait_all(swaps)
        place = s_downs.at[spot.z, spot.yl, spot.x]
        moves += [wire.copy(rows, place, spot.pair()), wire.keep(rows, place)]
        yield
        wait_all(moves)
        x = (spot.x, spot.along_x(1), spot.along_x(3))
        z = (spot.z, spot.along_z(1), spot.along_z(3))
        low, high, every = pl.ds(0, 32), pl.ds(32, 32), slice(None)

        def x_then_z(*parts):
            yield from gather_ring(wire, *x, [((lambda i, r=r, cut=cut: r.at[spot.z, :, i, cut]), half) for r, half, cut in parts])
            yield from gather_ring(wire, *z, [((lambda i, r=r, cut=cut: r.at[i, :, :, cut]), half) for r, half, cut in parts])

        def z_then_x(*parts):
            yield from gather_ring(wire, *z, [((lambda i, r=r, cut=cut: r.at[i, :, spot.x, cut]), half) for r, half, cut in parts])
            yield from gather_ring(wire, *x, [((lambda i, r=r, cut=cut: r.at[:, :, i, cut]), half) for r, half, cut in parts])

        yield from together(
            x_then_z((s_q, 0, every), (s_out, 1, every)),
            z_then_x((s_downs, 0, low), (s_kv, 0, every), (s_downs, 1, high)),
        )

    hiddens = gather_tp(wire, spot, s_hidden, hidden)
    next(hiddens)
    heads = weights()
    next(heads)
    s_small[0] = small[...]
    smalls = all_sum_small(wire, spot, s_buf, s_small)
    next(smalls)
    next(hiddens)
    next(heads)
    next(smalls)
    finish(hiddens)
    ffn = ffn_stream(wire, spot, (gu, dn, sgu, sdn), (o_gu, o_dn, o_sgu, o_sdn))
    next(ffn)
    grads = gather_y(wire, spot, o_grad, grad)
    next(grads)
    next(heads)
    finish(smalls)
    gains = s_small[5].astype(F32)
    attn_gain, ffn_gain = gains[8:9], gains[9:10]
    latent_gain = gains[10:11]
    keeps = [wire.keep(s_hidden, o_hidden)]

    def norm_rows(i):
        block, part = lax.div(i, 8), at_tile(lax.rem(i, 8), 16)
        values = s_hidden[block, part].astype(F32)
        scale = lax.rsqrt(jnp.mean(values * values, axis=-1, keepdims=True) + norm_eps)
        s_hat[at_tile(i, 16)] = (values * scale * attn_gain).astype(BF)

    loop(groups // 16, norm_rows)
    finish(heads)
    next(grads)
    next(ffn)
    keeps += [wire.keep(a, b) for a, b in ((s_downs, o_downs), (s_q, o_q), (s_kv, o_kv), (s_out, o_out), (s_hat, o_hat))]

    def down(i):
        j, k = lax.div(i, 2), lax.rem(i, 2)
        lanes = at_tile(j, 128)
        s_part[at_tile(k, 256), lanes] = dot(s_hat[at_tile(k, 256)], flat(s_downs[:, :, :, :, lanes])).astype(BF)

    loop(10, down)
    finish(gather_tp(wire, spot, s_raw, s_part))
    finish(grads)
    next(ffn)
    keeps.append(wire.keep(s_raw, o_raw))

    row, lane = lane_grid(128, 128)
    low_pick = (row == lax.rem(lane, 16)) & (lax.rem(lane, 32) < 16)
    high_pick = (row == lax.rem(lane, 16)) & (lax.rem(lane, 32) >= 16)
    low_pick, high_pick = low_pick.astype(F32).astype(BF), high_pick.astype(F32).astype(BF)

    def latents(i):
        part = at_tile(i, 32)
        raw = [s_raw[t, part, 0:384].astype(F32) for t in range(4)]
        total = sum(jnp.sum(v * v, axis=-1, keepdims=True) for v in raw)
        scale = lax.rsqrt(total / 1536.0 + norm_eps)
        for t in range(4):
            s_qlat[part, t * 384 : t * 384 + 384] = (raw[t] * scale * latent_gain[:, t * 384 : t * 384 + 384]).astype(BF)
        raw = [s_raw[t, part, 384:512].astype(F32) for t in range(4)]
        total = sum(jnp.sum(v * v, axis=-1, keepdims=True) for v in raw)
        scale = lax.rsqrt(total / 512.0 + norm_eps)
        for t in range(4):
            gain = latent_gain[:, 1536 + t * 128 : 1664 + t * 128]
            s_kvlat[part, t * 128 : t * 128 + 128] = (raw[t] * scale * gain).astype(BF)
        front = dot(s_raw[0, part, 512:640], low_pick) + dot(s_raw[1, part, 512:640], high_pick)
        back = dot(s_raw[2, part, 512:640], low_pick) + dot(s_raw[3, part, 512:640], high_pick)
        c, s = cosine[part], sine[part]
        s_rope[part, 0:128] = (front * c - back * s).astype(BF)
        s_rope[part, 128:256] = (back * c + front * s).astype(BF)

    loop(groups // 32, latents)

    def query(i):
        part = at_tile(i, 256)
        for j in range(2):
            lanes = pl.ds(j * 256, 256)
            s_query[part, lanes] = dot(s_qlat[part], flat(s_q[:, :, :, :, lanes])).astype(BF)
        both = dot(s_qlat[part], flat(s_q[:, :, :, :, 512:768]))
        front, back = both[:, 0:128], both[:, 128:256]
        c, s = cosine[part], sine[part]
        s_query[part, 512:640] = (front * c - back * s).astype(BF)
        s_query[part, 640:768] = (back * c + front * s).astype(BF)
        for j in range(4):
            lanes = pl.ds(j * 256, 256)
            s_keyval[part, lanes] = dot(s_kvlat[part], flat(s_kv[:, :, :, :, lanes])).astype(BF)

    loop(2, query)

    def attend(i):
        part = at_tile(i, 256)
        places = lax.broadcasted_iota(jnp.int32, (256, groups), 0) + i * 256
        keys = lax.broadcasted_iota(jnp.int32, (256, groups), 1)
        allowed = (seg_col[part] == seg_row[...]) & (keys <= places)
        norms = jnp.zeros((256, 128), F32)
        for head in range(4):
            scores = dot(s_query[part, head * 128 : head * 128 + 128], s_keyval[:, head * 256 : head * 256 + 128], "nt")
            scores += dot(head_lanes(s_query[part, 512:640], head), s_rope[:, 0:128], "nt")
            scores += dot(head_lanes(s_query[part, 640:768], head), s_rope[:, 128:256], "nt")
            scores = jnp.where(allowed, scores * (NOPE + ROPE) ** (-0.5), masked_score)
            peak = jnp.max(scores, axis=-1, keepdims=True)
            raised = jnp.exp(scores - peak)
            total = jnp.sum(raised, axis=-1, keepdims=True)
            probs = (raised / total).astype(BF)
            out = dot(probs, s_keyval[:, head * 256 + 128 : head * 256 + 256])
            s_heads[part, head * 128 : head * 128 + 128] = out.astype(BF)
            lanes = lax.broadcasted_iota(jnp.int32, (256, 128), 1)
            norms = jnp.where(lanes == head, peak + jnp.log(total), norms)
        s_norm[part] = norms

    loop(2, attend)
    next(ffn)
    keeps += [
        wire.keep(a, b)
        for a, b in (
            (s_qlat, o_qhat), (s_kvlat, o_kvhat), (s_query, o_query), (s_keyval, o_keyval), (s_rope, o_rope),
            (s_norm, o_norm), (s_heads, o_heads),
        )
    ]

    def project(i):
        block, z = lax.div(i, 4), lax.rem(i, 4)
        s_attn[block, :, at_tile(z, 512)] = dot(s_heads[at_tile(block, own_rows)], flat(s_out[z]), "nt").astype(BF)

    loop(16, project)
    finish(sum_tp(wire, spot, s_attn, s_sum, t_got, t_held, t_last))

    def residual(i):
        part = at_tile(i, 16)
        values = s_hidden[spot.t, part].astype(F32) + s_sum[part]
        s_resid[part] = values
        scale = lax.rsqrt(jnp.mean(values * values, axis=-1, keepdims=True) + norm_eps)
        normed = values * scale * ffn_gain
        s_sent[part, 0:width] = normed.astype(BF)
        s_sum[part] = normed

    loop(own_rows // 16, residual)
    logits = dot(s_sum[...], gains, "nt", lax.Precision.HIGHEST)
    o_logits[...] = logits
    scores = jax.nn.sigmoid(logits)
    first = jnp.sum(pick_a[...] * scores, axis=-1, keepdims=True)
    second = jnp.sum(pick_b[...] * scores, axis=-1, keepdims=True)
    both = first + second
    dense = pick_a[...] * (route_scale * first / both) + pick_b[...] * (route_scale * second / both)
    s_sent[:, width : width + 128] = jnp.zeros((own_rows, 128), BF)
    s_sent[:, width : width + 16] = (dense + pick_sent[...]).astype(BF)
    o_small[...] = s_small[5]
    keeps.append(wire.keep(s_resid, o_resid))
    next(ffn)
    finish(gather_y(wire, spot, o_tokens, s_sent))
    finish(ffn)
    wait_all(keeps)


def front(downs, q_up, kv_up, out_t, hidden, grad, ffn, small, cosine, sine, seg_col, seg_row, picks):
    rows, width = hidden.shape
    group, columns = 4 * rows, downs.shape[-1]

    def spread(array):
        return (4, 2, 4) + array.shape[-2:]

    down_spread = (4, 2, 4, 64, columns)
    weights = [down_spread, spread(q_up), spread(kv_up), spread(out_t)]
    outs = [(shape, BF, "hbm") for shape in weights]
    outs.append(((2, 2, 2, rows, width), BF, "hbm"))
    outs += [((a.shape[1], 4, 2, 4) + a.shape[2:], BF, "hbm") for a in ffn]
    outs.append(((2, 2, 2, rows, width + 128), BF, "hbm"))
    saved = [
        ((4, rows, width), BF), ((group, width), BF), ((4, group, columns), BF), ((group, 1536), BF),
        ((group, 512), BF), ((group, 768), BF), ((group, 1024), BF), ((group, 256), BF), ((group, 128), F32),
        ((group, 512), BF), ((rows, width), F32),
    ]
    outs += [(shape, dtype, "hbm") for shape, dtype in saved]
    outs += [((rows, 16), F32, "vmem"), (small.shape, small.dtype, "vmem")]
    scratch = [pltpu.VMEM((64, columns), BF)] + [pltpu.VMEM(shape, BF) for shape in weights]
    scratch += [
        pltpu.VMEM((4, rows, width), BF),
        pltpu.VMEM((group, width), BF),
        pltpu.VMEM((group, columns), BF),
        pltpu.VMEM((4, group, columns), BF),
        pltpu.VMEM((group, 1536), BF),
        pltpu.VMEM((group, 512), BF),
        pltpu.VMEM((group, 768), BF),
        pltpu.VMEM((group, 1024), BF),
        pltpu.VMEM((group, 256), BF),
        pltpu.VMEM((group, 128), F32),
        pltpu.VMEM((group, 512), BF),
        pltpu.VMEM((4, rows, width), BF),
        pltpu.VMEM((rows, width), F32),
        pltpu.VMEM((rows, width), F32),
        pltpu.VMEM((rows, width + 128), BF),
        pltpu.VMEM((6,) + small.shape, small.dtype),
        pltpu.VMEM((5, 3) + small.shape, small.dtype),
    ] + tp_sum_scratch(rows, width)
    return call(
        front_kernel, 0, outs, ["hbm"] * 10 + ["vmem"] * 8, scratch, 120, 40,
        (downs, q_up, kv_up, out_t, hidden, grad) + tuple(ffn) + (small, cosine, sine, seg_col, seg_row) + tuple(picks),
        60,
    )


def rotary_tables(position):
    half_size = ROPE // 2
    inverse = theta_base ** (-(2.0 * jnp.arange(half_size, dtype=F32)) / ROPE)
    angles = position.astype(F32)[:, None] * inverse[None, :]
    return (jnp.cos(angles), jnp.sin(angles))


def rotary(values, cosine, sine_table):
    half_size = values.shape[-1] // 2
    front_half = values[..., :half_size]
    back_half = values[..., half_size:]
    return jnp.concatenate(
        [
            front_half * cosine - back_half * sine_table,
            back_half * cosine + front_half * sine_table,
        ],
        axis=-1,
    )


def unrotary(values, cosine, sine_table):
    return rotary(values, cosine, -sine_table)


def packing(lengths, total_rows):
    positions = jnp.arange(total_rows, dtype=jnp.int32)
    endings = jnp.cumsum(lengths)
    segment = jnp.sum((positions[:, None] >= endings[None, :]).astype(jnp.int32), axis=1)
    starting = endings - lengths
    owner_mask = segment[:, None] == jnp.arange(lengths.shape[0], dtype=jnp.int32)[None, :]
    first_row = jnp.sum(jnp.where(owner_mask, starting[None, :], 0), axis=1)
    return (segment, positions - first_row)


def attention_mask(segment):
    places = jnp.arange(segment.shape[0], dtype=jnp.int32)
    return (segment[:, None] == segment[None, :]) & (places[None, :] <= places[:, None])


def normalized(values):
    scale = lax.rsqrt(jnp.mean(values * values, axis=-1, keepdims=True) + norm_eps)
    return values * scale, scale


def norm_back(grad, gain, hat, scale):
    weighted = grad * gain
    return scale * (weighted - hat * jnp.mean(weighted * hat, axis=-1, keepdims=True))


def swiglu(gate, up):
    return jax.nn.silu(gate) * up


def gate_values(logits, chosen_mask):
    scores = jax.nn.sigmoid(logits)
    picked = jnp.sum(chosen_mask * scores[:, None, :], axis=-1)
    return route_scale * picked / jnp.sum(picked, axis=-1, keepdims=True)


def masked_scores(query_heads, key_heads, allowed):
    raw_scores = jnp.einsum("qhd,khd->hqk", query_heads, key_heads, preferred_element_type=F32)
    return jnp.where(allowed[None], raw_scores * (NOPE + ROPE) ** (-0.5), masked_score)


def mm(spec, a, b):
    return jnp.einsum(spec, a, b, preferred_element_type=F32)


def per_device(
    hidden_in,
    out_grad,
    attn_gain,
    q_down,
    q_gain,
    kv_down,
    kv_gain,
    q_up,
    kv_up,
    out_proj,
    ffn_gain,
    router,
    routed_gate_up,
    routed_down,
    shared_gate_up,
    shared_down,
    choices,
    seq_lens,
):
    local_rows, width = hidden_in.shape
    group_rows = choices.shape[0]
    tp_count = lax.axis_size("tp")
    tp_index = lax.axis_index("tp")
    y_lo = lax.rem(lax.div(lax.axis_index("fsdp"), 4), 2)
    head_count = HEADS // tp_count
    experts = router.shape[1]
    held = experts // 2
    capacity = 5 * group_rows * TOPK // (4 * experts)
    units = routed_gate_up.shape[3]
    row_shard = routed_gate_up.shape[1]
    q_cols = q_down.shape[1] // tp_count
    raw_cols = q_cols + kv_down.shape[1] // tp_count
    raw_pad = -raw_cols % 128
    small_at = raw_cols + raw_pad

    def own(array):
        return lax.dynamic_slice_in_dim(array, tp_index * local_rows, local_rows)

    down_rows = q_down.shape[0]
    devices = width // down_rows
    device = lax.axis_index("fsdp") * tp_count + tp_index
    rope_cols = ROPE // tp_count
    columns = jnp.concatenate(
        [
            q_down.reshape(down_rows, tp_count, q_cols),
            kv_down[:, :KVR].reshape(down_rows, tp_count, KVR // tp_count),
            kv_down[:, KVR:].reshape(down_rows, tp_count, rope_cols),
        ],
        axis=-1,
    ).transpose(1, 0, 2)
    downs = jnp.pad(columns, ((0, 0), (0, 0), (0, raw_pad)))
    half = ROPE // 2
    q_rows = q_up.reshape(-1, head_count, NOPE + ROPE)
    q_sent = jnp.concatenate(
        [
            q_rows[..., :NOPE].reshape(-1, head_count * NOPE),
            q_rows[..., NOPE : NOPE + half].reshape(-1, head_count * half),
            q_rows[..., NOPE + half :].reshape(-1, head_count * half),
        ],
        axis=1,
    )
    small = jnp.zeros((16, width), BF)
    vectors = jnp.concatenate([router.T, attn_gain[None], ffn_gain[None]], axis=0)
    small = lax.dynamic_update_slice(small, vectors, (0, device * down_rows))
    small = lax.dynamic_update_slice(small, q_gain[None], (experts + 2, device * q_gain.shape[0]))
    kv_at = q_down.shape[1] + device * kv_gain.shape[0]
    small = lax.dynamic_update_slice(small, kv_gain[None], (experts + 2, kv_at))
    send_gu = routed_gate_up.transpose(0, 2, 1, 3).reshape(2, held * 2, row_shard, units)
    send_dn = routed_down.transpose(0, 2, 1).reshape(2, held, row_shard, units)
    send_sgu = shared_gate_up.reshape(row_shard, 2, 2, units).transpose(2, 1, 0, 3)
    send_sdn = shared_down.T.reshape(row_shard, 2, units).transpose(1, 0, 2)[:, None]

    segment, position = packing(seq_lens[0], group_rows)
    cosine, sine_table = rotary_tables(position)
    own_cos, own_sin = own(cosine), own(sine_table)
    picked = own(choices)
    lanes = jnp.arange(2 * experts, dtype=jnp.int32)
    pick_a, pick_b = ((picked[:, k : k + 1] == lanes[None]).astype(F32) for k in range(TOPK))
    pick_sent = sum((picked[:, k : k + 1] + experts == lanes[None]).astype(F32) for k in range(TOPK))

    (
        all_downs, all_q, all_kv, all_out, all_grad, wide_gu, wide_dn, wide_sgu, wide_sdn, tokens,
        group_hidden, attn_in, raw, group_query, group_keyval, query, keyval, rope, norms, heads_out, residual, logits,
        gains,
    ) = front(
        downs, q_sent, kv_up, out_proj.T, hidden_in, out_grad, (send_gu, send_dn, send_sgu, send_sdn), small,
        jnp.tile(cosine, (1, head_count)), jnp.tile(sine_table, (1, head_count)),
        segment[:, None], segment[None, :], (pick_a, pick_b, pick_sent),
    )
    down_weight = all_downs.reshape(width, -1)[:, :raw_cols]
    up_query = all_q.reshape(-1, q_up.shape[1])
    up_keyval = all_kv.reshape(-1, kv_up.shape[1])
    out_weight = all_out.reshape(width, -1)
    gains = gains.astype(F32)
    router_full = gains[:experts].T
    again, fgain = gains[experts], gains[experts + 1]
    qgain, kvgain = gains[experts + 2, : q_down.shape[1]], gains[experts + 2, q_down.shape[1] :]
    wide_gu = wide_gu.reshape(held, 2, width, units)
    wide_dn = wide_dn.reshape(held, width, units)
    wide_sgu = wide_sgu.reshape(2, width, units)
    wide_sdn = wide_sdn.reshape(width, units)
    input_hat, input_scale = normalized(group_hidden.reshape(group_rows, width).astype(F32))
    query_raw = raw[..., :q_cols].transpose(1, 0, 2).reshape(group_rows, -1).astype(F32)
    keyval_raw = raw[..., q_cols : q_cols + KVR // tp_count].transpose(1, 0, 2).reshape(group_rows, -1).astype(F32)
    query_hat, query_scale = normalized(query_raw)
    keyval_hat, keyval_scale = normalized(keyval_raw)
    nope_cols, half_cols = head_count * NOPE, head_count * half

    def by_head(values):
        return jnp.concatenate(
            [
                values[..., :nope_cols].reshape(values.shape[:-1] + (head_count, NOPE)),
                values[..., nope_cols : nope_cols + half_cols].reshape(values.shape[:-1] + (head_count, half)),
                values[..., nope_cols + half_cols :].reshape(values.shape[:-1] + (head_count, half)),
            ],
            axis=-1,
        )

    query_heads = by_head(query)
    keyval_heads = keyval.reshape(group_rows, head_count, NOPE + VDIM)
    group_rope = jnp.concatenate([rope[:, :half], rope[:, half_cols : half_cols + half]], axis=-1)
    rope_part = jnp.broadcast_to(group_rope[:, None, :], (group_rows, head_count, ROPE))
    key_heads = jnp.concatenate([keyval_heads[..., :NOPE], rope_part], axis=-1)
    value_heads = keyval_heads[..., NOPE:]
    log_norm = norms[:, :head_count].T[..., None]
    allowed = attention_mask(segment)
    logits = logits[:, :experts]
    chosen_mask = jnp.stack([pick_a[:, :experts], pick_b[:, :experts]], axis=1)
    ffn_hat, ffn_scale = normalized(residual)
    ffn_input = ffn_hat * fgain
    tokens = tokens.reshape(2, group_rows, -1)

    moe_in = tokens[..., :width]
    grad_rows = all_grad.reshape(2, group_rows, width)
    extra = tokens[..., width:].astype(F32)
    gate_mine = lax.dynamic_slice_in_dim(extra, y_lo * held, held, axis=2).transpose(0, 2, 1)
    mask_mine = lax.dynamic_slice_in_dim(extra, experts + y_lo * held, held, axis=2).transpose(0, 2, 1)
    place = jnp.cumsum(mask_mine, axis=2) - mask_mine
    place = jnp.where(mask_mine > 0, place, -1.0).astype(jnp.int32)
    slots = place[:, :, None, :] == jnp.arange(capacity, dtype=jnp.int32)[None, None, :, None]
    onehot = slots.astype(BF)
    gate_slot = jnp.sum(jnp.where(slots, gate_mine[:, :, None, :], 0.0), axis=-1)
    gate_slot = gate_slot.transpose(1, 0, 2).reshape(held, 2 * capacity, 1)
    expert_in = mm("gest,gtd->egsd", onehot, moe_in).astype(BF).reshape(held, 2 * capacity, width)
    expert_dy = mm("gest,gtd->egsd", onehot, grad_rows).reshape(held, 2 * capacity, width)
    expert_grad = (gate_slot * expert_dy).astype(BF)
    gate = mm("ecd,edf->ecf", expert_in, wide_gu[:, 0])
    up = mm("ecd,edf->ecf", expert_in, wide_gu[:, 1])
    hidden_act, act_pull = jax.vjp(swiglu, gate, up)
    hidden_low = hidden_act.astype(BF)
    rows_out = mm("ecf,edf->ecd", hidden_low, wide_dn)
    grad_hidden = mm("ecd,edf->ecf", expert_grad, wide_dn)
    grad_gate, grad_up = (v.astype(BF) for v in act_pull(grad_hidden))
    sum_dn = mm("ecd,ecf->edf", expert_grad, hidden_low).astype(BF)
    sum_gu = jnp.stack(
        [mm("ecd,ecf->edf", expert_in, grad_gate).astype(BF), mm("ecd,ecf->edf", expert_in, grad_up).astype(BF)],
        axis=1,
    )
    back_rows = mm("ecf,edf->ecd", grad_gate, wide_gu[:, 0]) + mm("ecf,edf->ecd", grad_up, wide_gu[:, 1])
    gate_back = jnp.sum(rows_out * expert_dy, axis=-1).reshape(held, 2, capacity)
    slot_shape = (held, 2, capacity, width)
    weighted_out = (gate_slot * rows_out).astype(BF).reshape(slot_shape)
    routed_sum = mm("gest,egsd->gtd", onehot, weighted_out)
    routed_back = mm("gest,egsd->gtd", onehot, back_rows.astype(BF).reshape(slot_shape))
    dense_back = jnp.sum(jnp.where(slots, gate_back.transpose(1, 0, 2)[..., None], 0.0), axis=2)
    flat_in, flat_dy = moe_in.reshape(-1, width), grad_rows.reshape(-1, width)
    common_gate, common_up = mm("rd,df->rf", flat_in, wide_sgu[0]), mm("rd,df->rf", flat_in, wide_sgu[1])
    common_act, common_pull = jax.vjp(swiglu, common_gate, common_up)
    common_low = common_act.astype(BF)
    moe_part = mm("rf,df->rd", common_low, wide_sdn) + routed_sum.reshape(-1, width)
    common_dhid = mm("rd,df->rf", flat_dy, wide_sdn)
    common_dgate, common_dup = (v.astype(BF) for v in common_pull(common_dhid))
    sum_sdn = mm("rd,rf->df", flat_dy, common_low).astype(BF)
    sum_sgu = jnp.stack(
        [mm("rd,rf->df", flat_in, common_dgate).astype(BF), mm("rd,rf->df", flat_in, common_dup).astype(BF)]
    )
    moe_back = mm("rf,df->rd", common_dgate, wide_sgu[0]) + mm("rf,df->rd", common_dup, wide_sgu[1])
    moe_back = moe_back + routed_back.reshape(-1, width)
    dense_back = lax.dynamic_update_slice(
        jnp.zeros((2, group_rows, 128), F32), dense_back.transpose(0, 2, 1), (0, 0, y_lo * held)
    )
    back_part = jnp.concatenate([moe_back.astype(BF), dense_back.reshape(-1, 128).astype(BF)], axis=1)
    ring = (2, 2, 2, local_rows)
    blocks = (4, 2, 4, row_shard, units)
    own_gu, own_dn, own_sgu, own_sdn, moe_own, back_own = ffn_sum(
        sum_gu.reshape((held * 2,) + blocks),
        sum_dn.reshape((held,) + blocks),
        sum_sgu.reshape((2,) + blocks),
        sum_sdn.reshape((1,) + blocks),
        moe_part.astype(BF).reshape(ring + (width,)),
        back_part.reshape(ring + (width + 128,)),
    )

    layer_out = (residual + moe_own).astype(BF)
    grad_gates = jnp.sum(chosen_mask * back_own[:, None, width : width + experts], axis=-1)
    gate_pull = jax.vjp(lambda v: gate_values(v, chosen_mask), logits)[1]
    grad_logits = gate_pull(grad_gates)[0]
    grad_ffn = back_own[:, :width] + jnp.dot(
        grad_logits, router_full.T, precision=lax.Precision.HIGHEST, preferred_element_type=F32
    )
    grad_router = jnp.dot(
        ffn_input.T, grad_logits, precision=lax.Precision.HIGHEST, preferred_element_type=F32
    )
    grad_fgain = jnp.sum(grad_ffn * ffn_hat, axis=0)
    grad_resid = out_grad.astype(F32) + norm_back(grad_ffn, fgain, ffn_hat, ffn_scale)

    group_dh = tp_gather(grad_resid.astype(BF), 6).reshape(group_rows, width)
    grad_out_weight = mm("rd,rf->df", group_dh, heads_out).astype(BF)
    grad_heads = mm("rd,df->rf", group_dh, out_weight)
    grad_heads = grad_heads.reshape(group_rows, head_count, VDIM).astype(BF)
    again_probs = jnp.exp(masked_scores(query_heads, key_heads, allowed) - log_norm)
    grad_values = mm("hqk,qhd->khd", again_probs.astype(BF), grad_heads)
    grad_probs = mm("qhd,khd->hqk", grad_heads, value_heads)
    row_dot = jnp.sum(again_probs * grad_probs, axis=-1, keepdims=True)
    grad_scores = (again_probs * (grad_probs - row_dot) * (NOPE + ROPE) ** (-0.5)).astype(BF)
    grad_query = mm("hqk,khd->qhd", grad_scores, key_heads)
    grad_key = mm("hqk,qhd->khd", grad_scores, query_heads)
    grad_qrot = unrotary(grad_query[..., NOPE:], cosine[:, None, :], sine_table[:, None, :])
    grad_qall = jnp.concatenate(
        [
            grad_query[..., :NOPE].reshape(group_rows, -1),
            grad_qrot[..., :half].reshape(group_rows, -1),
            grad_qrot[..., half:].reshape(group_rows, -1),
        ],
        axis=-1,
    ).astype(BF)
    grad_kvall = jnp.concatenate([grad_key[..., :NOPE], grad_values], axis=-1).reshape(group_rows, -1).astype(BF)
    grad_krope = jnp.sum(grad_key[..., NOPE:], axis=1)
    grad_up_query = mm("rl,rc->lc", group_query, grad_qall).astype(BF)
    grad_up_keyval = mm("rl,rc->lc", group_keyval, grad_kvall).astype(BF)
    grad_latents = jnp.concatenate(
        [
            mm("rc,lc->rl", grad_qall, up_query),
            mm("rc,lc->rl", grad_kvall, up_keyval),
            grad_krope,
            jnp.zeros((group_rows, -grad_krope.shape[1] % 128), F32),
        ],
        axis=1,
    ).astype(BF)
    latents = tp_sum(grad_latents.reshape(tp_count, local_rows, -1), 7)
    q_rank = query_raw.shape[1]
    grad_qlatent, grad_kvlatent = latents[:, :q_rank], latents[:, q_rank : q_rank + KVR]
    grad_krotated = latents[:, q_rank + KVR : q_rank + KVR + ROPE]
    own_qhat, own_kvhat = own(query_hat), own(keyval_hat)
    grad_qgain = jnp.sum(grad_qlatent * own_qhat, axis=0)
    grad_kvgain = jnp.sum(grad_kvlatent * own_kvhat, axis=0)
    grad_qraw = norm_back(grad_qlatent, qgain, own_qhat, own(query_scale)).astype(BF)
    grad_kvnorm = norm_back(grad_kvlatent, kvgain, own_kvhat, own(keyval_scale))
    grad_kvrope = unrotary(grad_krotated, own_cos, own_sin)
    grad_kvraw = jnp.concatenate([grad_kvnorm, grad_kvrope], axis=-1).astype(BF)
    raw_back = jnp.concatenate(
        [
            grad_qraw.reshape(local_rows, tp_count, q_cols),
            grad_kvraw[:, :KVR].reshape(local_rows, tp_count, -1),
            grad_kvraw[:, KVR:].reshape(local_rows, tp_count, -1),
        ],
        axis=-1,
    ).transpose(1, 0, 2)
    raw_back = tp_swap(jnp.pad(raw_back, ((0, 0), (0, 0), (0, raw_pad))), 8)
    raw_back = raw_back.reshape(group_rows, -1)[:, :raw_cols]
    grad_down = mm("rd,rc->dc", attn_in, raw_back)
    attn_back = mm("rc,dc->rd", raw_back, down_weight)
    grad_again = jnp.sum(attn_back * input_hat, axis=0)

    def by_device(vector):
        each = vector.reshape(devices, -1)
        return jnp.pad(each, ((0, 0), (0, down_rows - each.shape[1]))).reshape(-1, 1)

    small_grads = jnp.concatenate(
        [grad_router, grad_again[:, None], grad_fgain[:, None], by_device(grad_qgain), by_device(grad_kvgain)], axis=1
    )
    small_grads = jnp.pad(small_grads, ((0, 0), (0, 128 - small_grads.shape[1])))
    grad_downs = jnp.concatenate([jnp.pad(grad_down, ((0, 0), (0, raw_pad))), small_grads], axis=1).astype(BF)

    def spread(array, like):
        return array.reshape((1, 4, 2, 4) + like.shape)

    got_downs, sum_up_query, sum_up_keyval, sum_out, attn_back_own = head_sum(
        grad_downs.reshape(1, 4, 2, 4, row_shard, -1),
        spread(grad_up_query, q_up),
        spread(grad_up_keyval, kv_up),
        spread(grad_out_weight, out_proj.T),
        attn_back.astype(BF).reshape(tp_count, local_rows, width),
    )
    input_grad = grad_resid + norm_back(attn_back_own, again, own(input_hat), own(input_scale))
    got_downs = got_downs.astype(F32)
    sum_qdown = got_downs[..., :q_cols].transpose(1, 0, 2).reshape(down_rows, -1)
    kv_at = q_cols + KVR // tp_count
    sum_kvdown = jnp.concatenate(
        [
            got_downs[..., q_cols:kv_at].transpose(1, 0, 2).reshape(down_rows, -1),
            got_downs[..., kv_at:raw_cols].transpose(1, 0, 2).reshape(down_rows, -1),
        ],
        axis=-1,
    )
    sum_up_query = by_head(sum_up_query).reshape(sum_up_query.shape)
    small_sum = jnp.sum(got_downs[..., small_at:], axis=0)
    sum_wide_gu = own_gu.reshape(experts, 2, row_shard, units).transpose(0, 2, 1, 3).astype(F32)
    sum_wide_down = own_dn.reshape(experts, row_shard, units).transpose(0, 2, 1).astype(F32)
    sum_common_gu = own_sgu.transpose(2, 1, 0, 3).reshape(row_shard, 2, 2 * units).astype(F32)
    sum_common_down = own_sdn[:, 0].transpose(1, 0, 2).reshape(row_shard, 2 * units).T.astype(F32)
    return (
        layer_out,
        input_grad.astype(BF),
        small_sum[:, experts],
        sum_qdown,
        small_sum[: q_gain.shape[0], experts + 2],
        sum_kvdown,
        small_sum[: kv_gain.shape[0], experts + 3],
        sum_up_query,
        sum_up_keyval,
        sum_out.T,
        small_sum[:, experts + 1],
        small_sum[:, :experts],
        sum_wide_gu,
        sum_wide_down,
        sum_common_gu,
        sum_common_down,
    )


def solution(mesh):
    return jax.shard_map(
        per_device,
        mesh=mesh,
        in_specs=(
            P(("fsdp", "tp"), None),
            P(("fsdp", "tp"), None),
            P(("fsdp", "tp")),
            P(("fsdp", "tp"), None),
            P(("fsdp", "tp")),
            P(("fsdp", "tp"), None),
            P(("fsdp", "tp")),
            P("fsdp", "tp"),
            P("fsdp", "tp"),
            P("tp", "fsdp"),
            P(("fsdp", "tp")),
            P(("fsdp", "tp"), None),
            P(None, "fsdp", None, "tp"),
            P(None, "tp", "fsdp"),
            P("fsdp", None, "tp"),
            P("tp", "fsdp"),
            P("fsdp", None),
            P("fsdp", None),
        ),
        out_specs=(
            P(("fsdp", "tp"), None),
            P(("fsdp", "tp"), None),
            P(("fsdp", "tp")),
            P(("fsdp", "tp"), None),
            P(("fsdp", "tp")),
            P(("fsdp", "tp"), None),
            P(("fsdp", "tp")),
            P("fsdp", "tp"),
            P("fsdp", "tp"),
            P("tp", "fsdp"),
            P(("fsdp", "tp")),
            P(("fsdp", "tp"), None),
            P(None, "fsdp", None, "tp"),
            P(None, "tp", "fsdp"),
            P("fsdp", None, "tp"),
            P("tp", "fsdp"),
        ),
        check_vma=False,
    )
```

```python
import functools

import jax
import jax.numpy as jnp
from jax import lax
from jax.experimental import pallas as pl
from jax.experimental.pallas import tpu as pltpu
from jax.sharding import PartitionSpec as P

HEADS = 16
NOPE = 128
ROPE = 64
VDIM = 128
KVR = 512
TOPK = 2

theta_base = 50000.0
norm_eps = 1e-06
route_scale = 2.446
masked_score = -1e30

MESH = pl.DeviceIdType.MESH
BF = jnp.bfloat16
F32 = jnp.float32
MIB = 1 << 20


class Spot:
    def __init__(self):
        f, t = lax.axis_index("fsdp"), lax.axis_index("tp")
        self.t = t
        self.z, self.yl, self.x = lax.div(f, 8), lax.rem(lax.div(f, 4), 2), lax.rem(f, 4)
        self.yh, self.c = lax.div(t, 2), lax.rem(t, 2)
        self.y = self.yh * 2 + self.yl

    def at(self, z=None, yl=None, x=None, yh=None, c=None):
        z = self.z if z is None else z
        yl = self.yl if yl is None else yl
        x = self.x if x is None else x
        yh = self.yh if yh is None else yh
        c = self.c if c is None else c
        return ((z * 2 + yl) * 4 + x, yh * 2 + c)

    def along_x(self, by):
        return self.at(x=lax.rem(self.x + by, 4))

    def along_z(self, by):
        return self.at(z=lax.rem(self.z + by, 4))

    def along_y(self, by):
        y = lax.rem(self.y + by, 4)
        return self.at(yl=lax.rem(y, 2), yh=lax.div(y, 2))

    def pair(self):
        return self.at(yl=1 - self.yl)

    def core(self):
        return self.at(c=1 - self.c)

    def far(self):
        return self.at(yh=1 - self.yh)

    def diagonal(self):
        return self.at(yh=1 - self.yh, c=1 - self.c)

    def rings(self):
        return [self.along_x(1), self.along_x(3), self.along_z(1), self.along_z(3)]


def greet(devices):
    barrier = pltpu.get_barrier_semaphore()
    for device in devices:
        pl.semaphore_signal(barrier, inc=1, device_id=device, device_id_type=MESH)
    pl.semaphore_wait(barrier, len(devices))


class Wire:
    def __init__(self, send, recv, here):
        self.send, self.recv, self.here = send, recv, here
        self.sent = self.kept = 0

    def copy(self, source, target, device):
        made = pltpu.make_async_remote_copy(
            src_ref=source,
            dst_ref=target,
            send_sem=self.send.at[self.sent],
            recv_sem=self.recv.at[self.sent],
            device_id=device,
            device_id_type=MESH,
        )
        self.sent += 1
        made.start()
        return made

    def keep(self, source, target):
        made = pltpu.make_async_copy(source, target, self.here.at[self.kept])
        self.kept += 1
        made.start()
        return made


def wait_all(copies):
    for made in copies:
        made.wait()


def together(*parts):
    left = list(parts)
    while left:
        for part in list(left):
            if next(part, "over") == "over":
                left.remove(part)
        yield


def finish(part):
    for _ in part:
        pass


def add_into(target, *terms):
    lead, (rows, columns) = target.shape[:-2], target.shape[-2:]
    step = rows if rows * columns <= 49152 else 16
    pieces = rows // step
    count = pieces
    for size in lead:
        count *= size

    def body(i, carry):
        at = [pl.ds(pl.multiple_of(lax.rem(i, pieces) * step, 16), step)]
        i = lax.div(i, pieces)
        for size in reversed(lead):
            at.insert(0, lax.rem(i, size))
            i = lax.div(i, size)
        at = tuple(at)
        total = terms[0][at].astype(F32)
        for term in terms[1:]:
            total = total + term[at].astype(F32)
        target[at] = total.astype(target.dtype)
        return carry

    lax.fori_loop(0, count, body, 0)


def gather_ring(wire, pos, plus, minus, units):
    prev, following = lax.rem(pos + 3, 4), lax.rem(pos + 1, 4)
    mine = [unit[2] if len(unit) > 2 else unit[0](pos) for unit in units]
    right = [wire.copy(own, unit[0](pos), plus) for own, unit in zip(mine, units)]
    left = [wire.copy(own, unit[0](pos), minus) for own, unit in zip(mine, units)]
    yield
    wait_all(right)
    onward = [wire.copy(unit[0](prev), unit[0](prev), plus) for unit in units if unit[1] == 0]
    wait_all(left)
    onward += [wire.copy(unit[0](following), unit[0](following), minus) for unit in units if unit[1] == 1]
    yield
    wait_all(onward)


def sum_ring(wire, pos, plus, minus, units, staged=False):
    prev, following, across = lax.rem(pos + 3, 4), lax.rem(pos + 1, 4), lax.rem(pos + 2, 4)
    first, direct, last = [], [], []
    for half, view, between, own, through, from_left, from_right, loads in units:
        first.append(wire.copy(view(across), through, plus if half == 0 else minus))
    for half, view, between, own, through, from_left, from_right, loads in units:
        if half == 0:
            direct.append(wire.copy(view(prev), from_right, minus))
        else:
            direct.append(wire.copy(view(following), from_left, plus))
    yield
    for made, (half, view, between, own, through, from_left, from_right, loads) in zip(first, units):
        wait_all(loads)
        made.wait()
        add_into(between, between, through)
        if half == 0:
            last.append(wire.copy(between, from_left, plus))
        else:
            last.append(wire.copy(between, from_right, minus))
    yield
    for one, two, (half, view, between, own, through, from_left, from_right, loads) in zip(direct, last, units):
        one.wait()
        two.wait()
        if staged:
            wait_all([wire.keep(from_left, through), wire.keep(from_right, between)])
            add_into(own, own, through, between)
        else:
            add_into(own, own, from_left, from_right)


def gather_tp(wire, spot, out, source):
    across = wire.copy(source, out.at[spot.t], spot.far())
    own = wire.keep(source, out.at[spot.t])
    other = wire.copy(source, out.at[spot.t], spot.core())
    yield
    across.wait()
    there = (1 - spot.yh) * 2 + spot.c
    last = wire.copy(out.at[there], out.at[there], spot.core())
    yield
    own.wait()
    other.wait()
    last.wait()


def gather_y(wire, spot, out, source):
    def view(rows):
        return lambda y: out.at[lax.rem(y, 2), lax.div(y, 2), spot.c, rows]

    rows = source.shape[0] // 2
    own = wire.keep(source, out.at[spot.yl, spot.yh, spot.c])
    other = [own, wire.copy(source, out.at[spot.yl, spot.yh, spot.c], spot.core())]
    cuts = (pl.ds(0, rows), pl.ds(rows, rows))
    units = [(view(cut), half, source.at[cut]) for half, cut in enumerate(cuts)]
    yield from gather_ring(wire, spot.y, spot.along_y(1), spot.along_y(3), units)
    for by in (1, 2, 3):
        y = lax.rem(spot.y + by, 4)
        part = out.at[lax.rem(y, 2), lax.div(y, 2), spot.c]
        other.append(wire.copy(part, part, spot.core()))
    yield
    wait_all(other)


def sum_tp(wire, spot, source, out, got, held, last):
    cores = [wire.copy(source.at[yh * 2 + 1 - spot.c], got.at[yh], spot.core()) for yh in (0, 1)]
    yield
    wait_all(cores)
    there = 1 - spot.yh
    add_into(held, source.at[there * 2 + spot.c], got.at[there])
    across = wire.copy(held, last, spot.far())
    yield
    across.wait()
    add_into(out, source.at[spot.t], got.at[spot.yh], last)


def sum_y(wire, spot, source, out, got, held, through, from_left, from_right):
    cores = [wire.copy(source.at[y % 2, y // 2, 1 - spot.c], got.at[y], spot.core()) for y in range(4)]
    loads = [wire.keep(source.at[y % 2, y // 2, spot.c], held.at[y]) for y in range(4)]
    yield
    for y, made in enumerate(cores):
        made.wait()
        loads[y].wait()
        add_into(held.at[y], held.at[y], got.at[y])
    rows = out.shape[0] // 2
    following, prev = lax.rem(spot.y + 1, 4), lax.rem(spot.y + 3, 4)
    units = []
    for half in (0, 1):
        part = pl.ds(half * rows, rows)
        units.append(
            (
                half,
                lambda y, part=part: held.at[y, part],
                held.at[following if half == 0 else prev, part],
                held.at[spot.y, part],
                through.at[part],
                from_left.at[part],
                from_right.at[part],
                [],
            )
        )
    yield from sum_ring(wire, spot.y, spot.along_y(1), spot.along_y(3), units)
    add_into(out, held.at[spot.y])


def sum_unit(wire, spot, half, part, order, scratch):
    following, prev = (lambda p: lax.rem(p + 1, 4)), (lambda p: lax.rem(p + 3, 4))
    (between, own, through, from_left, from_right), (between2, own2, through2, from_left2, from_right2) = scratch
    near = following if half == 0 else prev
    if order == "zx":
        view, pos, pos2 = (lambda i: part.at[:, i]), spot.z, spot.x
        view2 = lambda i: own.at[:, :, i]
    else:
        view, pos, pos2 = (lambda i: part.at[:, :, :, i]), spot.x, spot.z
        view2 = lambda i: own.at[:, i]

    def loads():
        return [wire.keep(view(near(pos)), between), wire.keep(view(pos), own)]

    def loads2():
        return [wire.keep(view2(near(pos2)), between2), wire.keep(view2(pos2), own2)]

    one = lambda: (half, view, between, own, through, from_left, from_right, loads())
    two = lambda: (half, view2, between2, own2, through2, from_left2, from_right2, loads2())
    return one, two, own2


def sum_stream(wire, spot, order, units, staged=False):
    x = (spot.x, spot.along_x(1), spot.along_x(3))
    z = (spot.z, spot.along_z(1), spot.along_z(3))
    axes = (z, x) if order == "zx" else (x, z)
    yield from sum_ring(wire, *axes[0], [one() for one, _, _ in units], staged)
    yield from sum_ring(wire, *axes[1], [two() for _, two, _ in units], staged)


def unit_scratch(planes, order, rows, columns):
    first = (planes, 2, 4, rows, columns) if order == "zx" else (planes, 4, 2, rows, columns)
    second = (planes, 2, rows, columns)
    return [pltpu.VMEM(first, BF)] * 5 + [pltpu.VMEM(second, BF)] * 5


def call(kernel, number, outs, ins, scratch, copies, keeps, operands, vmem):
    space = {"hbm": pltpu.HBM, "vmem": pltpu.VMEM}
    return pl.pallas_call(
        kernel,
        out_shape=[jax.ShapeDtypeStruct(shape, dtype) for shape, dtype, _ in outs],
        in_specs=[pl.BlockSpec(memory_space=space[kind]) for kind in ins],
        out_specs=[pl.BlockSpec(memory_space=space[kind]) for _, _, kind in outs],
        scratch_shapes=list(scratch)
        + [
            pltpu.SemaphoreType.DMA((max(copies, 1),)),
            pltpu.SemaphoreType.DMA((max(copies, 1),)),
            pltpu.SemaphoreType.DMA((max(keeps, 1),)),
        ],
        compiler_params=pltpu.CompilerParams(
            collective_id=number, has_side_effects=True, vmem_limit_bytes=vmem * MIB
        ),
    )(*operands)


def tp_sum_scratch(rows, columns):
    return [pltpu.VMEM((2, rows, columns), BF), pltpu.VMEM((rows, columns), BF), pltpu.VMEM((rows, columns), BF)]


def dot(a, b, dims="nn", precision=None):
    left, right = {"nn": (1, 0), "nt": (1, 1), "tn": (0, 0)}[dims]
    return lax.dot_general(
        a, b, (((left,), (right,)), ((), ())), precision=precision, preferred_element_type=F32
    )


def loop(count, body):
    def step(i, carry):
        body(i)
        return carry

    lax.fori_loop(0, count, step, 0)


def at_tile(i, size):
    return pl.ds(pl.multiple_of(i * size, size), size)


def flat(block):
    return block.reshape(-1, block.shape[-1])


def lane_grid(rows, columns):
    return (
        lax.broadcasted_iota(jnp.int32, (rows, columns), 0),
        lax.broadcasted_iota(jnp.int32, (rows, columns), 1),
    )


def head_lanes(values, head):
    lanes = lax.broadcasted_iota(jnp.int32, (1, values.shape[1]), 1)
    return values * (lax.div(lanes, 32) == head).astype(F32).astype(values.dtype)


def all_sum_small(wire, spot, buffers, own):
    steps = (
        [spot.core()],
        [spot.far()],
        [spot.pair()],
        [spot.along_x(1), spot.along_x(2), spot.along_x(3)],
        [spot.along_z(1), spot.along_z(2), spot.along_z(3)],
    )
    for step, devices in enumerate(steps):
        moves = [wire.copy(own.at[step], buffers.at[step, i], device) for i, device in enumerate(devices)]
        yield
        wait_all(moves)
        total = own[step]
        for i in range(len(devices)):
            total = total + buffers[step, i]
        own[step + 1] = total


def ffn_stream(wire, spot, sources, targets):
    moves = []
    for source, target in zip(sources, targets):
        place = target.at[:, spot.z, spot.yl, spot.x]
        moves += [wire.copy(source.at[1 - spot.yl], place, spot.pair()), wire.keep(source.at[spot.yl], place)]
    yield
    wait_all(moves)
    x = (spot.x, spot.along_x(1), spot.along_x(3))
    z = (spot.z, spot.along_z(1), spot.along_z(3))
    gu, dn, sgu, sdn = targets

    def x_then_z(*parts):
        yield from gather_ring(wire, *x, [((lambda i, r=r, cut=cut: r.at[cut, spot.z, :, i]), half) for r, half, cut in parts])
        yield from gather_ring(wire, *z, [((lambda i, r=r, cut=cut: r.at[cut, i]), half) for r, half, cut in parts])

    def z_then_x(*parts):
        yield from gather_ring(wire, *z, [((lambda i, r=r, cut=cut: r.at[cut, i, :, spot.x]), half) for r, half, cut in parts])
        yield from gather_ring(wire, *x, [((lambda i, r=r, cut=cut: r.at[cut, :, :, i]), half) for r, half, cut in parts])

    yield from together(
        x_then_z((gu, 0, pl.ds(0, 4)), (gu, 1, pl.ds(4, 4))),
        z_then_x((dn, 0, pl.ds(0, 4)), (sgu, 1, pl.ds(0, 2)), (sdn, 1, pl.ds(0, 1))),
    )


def front_kernel(
    downs, q_up, kv_up, out_t, hidden, grad, gu, dn, sgu, sdn, small, cosine, sine, seg_col, seg_row, pick_a, pick_b,
    pick_sent,
    o_downs, o_q, o_kv, o_out, o_grad, o_gu, o_dn, o_sgu, o_sdn, o_tokens,
    o_hat, o_raw, o_qhat, o_kvhat, o_query, o_keyval, o_rope, o_norm, o_heads, o_resid, o_logits, o_small,
    rows, s_downs, s_q, s_kv, s_out, s_hidden, s_hat, s_part, s_raw, s_qlat, s_kvlat, s_query, s_keyval, s_rope,
    s_norm, s_heads, s_attn, s_sum, s_resid, s_sent, s_small, s_buf, t_got, t_held, t_last,
    send, recv, here,
):
    spot, wire = Spot(), Wire(send, recv, here)
    greet(
        spot.rings()
        + [spot.along_x(2), spot.along_z(2), spot.along_y(1), spot.along_y(3)]
        + [spot.core(), spot.far(), spot.diagonal()]
    )
    groups, width = 4 * hidden.shape[0], hidden.shape[1]
    own_rows = hidden.shape[0]

    def weights():
        mine = rows.at[pl.ds(pl.multiple_of(spot.t * 16, 16), 16)]
        swaps = [wire.keep(downs.at[spot.t], mine)]
        for yh, c, device in (
            (spot.yh, 1 - spot.c, spot.core()),
            (1 - spot.yh, spot.c, spot.far()),
            (1 - spot.yh, 1 - spot.c, spot.diagonal()),
        ):
            swaps.append(wire.copy(downs.at[yh * 2 + c], mine, device))
        moves = []
        for source, target in ((q_up, s_q), (kv_up, s_kv), (out_t, s_out)):
            place = target.at[spot.z, spot.yl, spot.x]
            moves += [wire.copy(source, place, spot.pair()), wire.keep(source, place)]
        yield
        wait_all(swaps)
        place = s_downs.at[spot.z, spot.yl, spot.x]
        moves += [wire.copy(rows, place, spot.pair()), wire.keep(rows, place)]
        yield
        wait_all(moves)
        x = (spot.x, spot.along_x(1), spot.along_x(3))
        z = (spot.z, spot.along_z(1), spot.along_z(3))
        low, high, every = pl.ds(0, 32), pl.ds(32, 32), slice(None)

        def x_then_z(*parts):
            yield from gather_ring(wire, *x, [((lambda i, r=r, cut=cut: r.at[spot.z, :, i, cut]), half) for r, half, cut in parts])
            yield from gather_ring(wire, *z, [((lambda i, r=r, cut=cut: r.at[i, :, :, cut]), half) for r, half, cut in parts])

        def z_then_x(*parts):
            yield from gather_ring(wire, *z, [((lambda i, r=r, cut=cut: r.at[i, :, spot.x, cut]), half) for r, half, cut in parts])
            yield from gather_ring(wire, *x, [((lambda i, r=r, cut=cut: r.at[:, :, i, cut]), half) for r, half, cut in parts])

        yield from together(
            x_then_z((s_q, 0, every), (s_out, 1, every)),
            z_then_x((s_downs, 0, low), (s_kv, 0, every), (s_downs, 1, high)),
        )

    hiddens = gather_tp(wire, spot, s_hidden, hidden)
    next(hiddens)
    heads = weights()
    next(heads)
    s_small[0] = small[...]
    smalls = all_sum_small(wire, spot, s_buf, s_small)
    next(smalls)
    next(hiddens)
    next(heads)
    next(smalls)
    finish(hiddens)
    ffn = ffn_stream(wire, spot, (gu, dn, sgu, sdn), (o_gu, o_dn, o_sgu, o_sdn))
    next(ffn)
    next(heads)
    finish(smalls)
    gains = s_small[5].astype(F32)
    attn_gain, ffn_gain = gains[8:9], gains[9:10]
    latent_gain = gains[10:11]
    keeps = []

    def norm_rows(i):
        block, part = lax.div(i, 8), at_tile(lax.rem(i, 8), 16)
        values = s_hidden[block, part].astype(F32)
        scale = lax.rsqrt(jnp.mean(values * values, axis=-1, keepdims=True) + norm_eps)
        s_hat[at_tile(i, 16)] = (values * scale * attn_gain).astype(BF)

    loop(groups // 16, norm_rows)
    finish(heads)
    next(ffn)
    keeps += [wire.keep(a, b) for a, b in ((s_downs, o_downs), (s_q, o_q), (s_kv, o_kv), (s_out, o_out), (s_hat, o_hat))]

    def down(i):
        j, k = lax.div(i, 2), lax.rem(i, 2)
        lanes = at_tile(j, 128)
        s_part[at_tile(k, 256), lanes] = dot(s_hat[at_tile(k, 256)], flat(s_downs[:, :, :, :, lanes])).astype(BF)

    loop(10, down)
    finish(gather_tp(wire, spot, s_raw, s_part))
    grads = gather_y(wire, spot, o_grad, grad)
    next(grads)
    next(ffn)
    keeps.append(wire.keep(s_raw, o_raw))

    row, lane = lane_grid(128, 128)
    low_pick = (row == lax.rem(lane, 16)) & (lax.rem(lane, 32) < 16)
    high_pick = (row == lax.rem(lane, 16)) & (lax.rem(lane, 32) >= 16)
    low_pick, high_pick = low_pick.astype(F32).astype(BF), high_pick.astype(F32).astype(BF)

    def latents(i):
        part = at_tile(i, 32)
        raw = [s_raw[t, part, 0:384].astype(F32) for t in range(4)]
        total = sum(jnp.sum(v * v, axis=-1, keepdims=True) for v in raw)
        scale = lax.rsqrt(total / 1536.0 + norm_eps)
        for t in range(4):
            s_qlat[part, t * 384 : t * 384 + 384] = (raw[t] * scale * latent_gain[:, t * 384 : t * 384 + 384]).astype(BF)
        raw = [s_raw[t, part, 384:512].astype(F32) for t in range(4)]
        total = sum(jnp.sum(v * v, axis=-1, keepdims=True) for v in raw)
        scale = lax.rsqrt(total / 512.0 + norm_eps)
        for t in range(4):
            gain = latent_gain[:, 1536 + t * 128 : 1664 + t * 128]
            s_kvlat[part, t * 128 : t * 128 + 128] = (raw[t] * scale * gain).astype(BF)
        front = dot(s_raw[0, part, 512:640], low_pick) + dot(s_raw[1, part, 512:640], high_pick)
        back = dot(s_raw[2, part, 512:640], low_pick) + dot(s_raw[3, part, 512:640], high_pick)
        c, s = cosine[part], sine[part]
        s_rope[part, 0:128] = (front * c - back * s).astype(BF)
        s_rope[part, 128:256] = (back * c + front * s).astype(BF)

    loop(groups // 32, latents)

    def query(i):
        part = at_tile(i, 256)
        for j in range(2):
            lanes = pl.ds(j * 256, 256)
            s_query[part, lanes] = dot(s_qlat[part], flat(s_q[:, :, :, :, lanes])).astype(BF)
        both = dot(s_qlat[part], flat(s_q[:, :, :, :, 512:768]))
        front, back = both[:, 0:128], both[:, 128:256]
        c, s = cosine[part], sine[part]
        s_query[part, 512:640] = (front * c - back * s).astype(BF)
        s_query[part, 640:768] = (back * c + front * s).astype(BF)
        for j in range(4):
            lanes = pl.ds(j * 256, 256)
            s_keyval[part, lanes] = dot(s_kvlat[part], flat(s_kv[:, :, :, :, lanes])).astype(BF)

    loop(2, query)

    def attend(i):
        part = at_tile(i, 256)
        places = lax.broadcasted_iota(jnp.int32, (256, groups), 0) + i * 256
        keys = lax.broadcasted_iota(jnp.int32, (256, groups), 1)
        allowed = (seg_col[part] == seg_row[...]) & (keys <= places)
        norms = jnp.zeros((256, 128), F32)
        for head in range(4):
            scores = dot(s_query[part, head * 128 : head * 128 + 128], s_keyval[:, head * 256 : head * 256 + 128], "nt")
            scores += dot(head_lanes(s_query[part, 512:640], head), s_rope[:, 0:128], "nt")
            scores += dot(head_lanes(s_query[part, 640:768], head), s_rope[:, 128:256], "nt")
            scores = jnp.where(allowed, scores * (NOPE + ROPE) ** (-0.5), masked_score)
            peak = jnp.max(scores, axis=-1, keepdims=True)
            raised = jnp.exp(scores - peak)
            total = jnp.sum(raised, axis=-1, keepdims=True)
            probs = (raised / total).astype(BF)
            out = dot(probs, s_keyval[:, head * 256 + 128 : head * 256 + 256])
            s_heads[part, head * 128 : head * 128 + 128] = out.astype(BF)
            lanes = lax.broadcasted_iota(jnp.int32, (256, 128), 1)
            norms = jnp.where(lanes == head, peak + jnp.log(total), norms)
        s_norm[part] = norms

    loop(2, attend)
    next(ffn)
    next(grads)
    keeps += [
        wire.keep(a, b)
        for a, b in (
            (s_qlat, o_qhat), (s_kvlat, o_kvhat), (s_query, o_query), (s_keyval, o_keyval), (s_rope, o_rope),
            (s_norm, o_norm), (s_heads, o_heads),
        )
    ]

    def project(i):
        block, z = lax.div(i, 4), lax.rem(i, 4)
        s_attn[block, :, at_tile(z, 512)] = dot(s_heads[at_tile(block, own_rows)], flat(s_out[z]), "nt").astype(BF)

    loop(16, project)
    finish(sum_tp(wire, spot, s_attn, s_sum, t_got, t_held, t_last))

    def residual(i):
        part = at_tile(i, 16)
        values = s_hidden[spot.t, part].astype(F32) + s_sum[part]
        s_resid[part] = values
        scale = lax.rsqrt(jnp.mean(values * values, axis=-1, keepdims=True) + norm_eps)
        normed = values * scale * ffn_gain
        s_sent[part, 0:width] = normed.astype(BF)
        s_sum[part] = normed

    loop(own_rows // 16, residual)
    logits = dot(s_sum[...], gains, "nt", lax.Precision.HIGHEST)
    o_logits[...] = logits
    scores = jax.nn.sigmoid(logits)
    first = jnp.sum(pick_a[...] * scores, axis=-1, keepdims=True)
    second = jnp.sum(pick_b[...] * scores, axis=-1, keepdims=True)
    both = first + second
    dense = pick_a[...] * (route_scale * first / both) + pick_b[...] * (route_scale * second / both)
    s_sent[:, width : width + 128] = jnp.zeros((own_rows, 128), BF)
    s_sent[:, width : width + 16] = (dense + pick_sent[...]).astype(BF)
    o_small[...] = s_small[5]
    keeps.append(wire.keep(s_resid, o_resid))
    finish(together(gather_y(wire, spot, o_tokens, s_sent), grads))
    finish(ffn)
    wait_all(keeps)


def front(downs, q_up, kv_up, out_t, hidden, grad, ffn, small, cosine, sine, seg_col, seg_row, picks):
    rows, width = hidden.shape
    group, columns = 4 * rows, downs.shape[-1]

    def spread(array):
        return (4, 2, 4) + array.shape[-2:]

    down_spread = (4, 2, 4, 64, columns)
    weights = [down_spread, spread(q_up), spread(kv_up), spread(out_t)]
    outs = [(shape, BF, "hbm") for shape in weights]
    outs.append(((2, 2, 2, rows, width), BF, "hbm"))
    outs += [((a.shape[1], 4, 2, 4) + a.shape[2:], BF, "hbm") for a in ffn]
    outs.append(((2, 2, 2, rows, width + 128), BF, "hbm"))
    saved = [
        ((group, width), BF), ((4, group, columns), BF), ((group, 1536), BF),
        ((group, 512), BF), ((group, 768), BF), ((group, 1024), BF), ((group, 256), BF), ((group, 128), F32),
        ((group, 512), BF), ((rows, width), F32),
    ]
    outs += [(shape, dtype, "hbm") for shape, dtype in saved]
    outs += [((rows, 16), F32, "vmem"), (small.shape, small.dtype, "vmem")]
    scratch = [pltpu.VMEM((64, columns), BF)] + [pltpu.VMEM(shape, BF) for shape in weights]
    scratch += [
        pltpu.VMEM((4, rows, width), BF),
        pltpu.VMEM((group, width), BF),
        pltpu.VMEM((group, columns), BF),
        pltpu.VMEM((4, group, columns), BF),
        pltpu.VMEM((group, 1536), BF),
        pltpu.VMEM((group, 512), BF),
        pltpu.VMEM((group, 768), BF),
        pltpu.VMEM((group, 1024), BF),
        pltpu.VMEM((group, 256), BF),
        pltpu.VMEM((group, 128), F32),
        pltpu.VMEM((group, 512), BF),
        pltpu.VMEM((4, rows, width), BF),
        pltpu.VMEM((rows, width), F32),
        pltpu.VMEM((rows, width), F32),
        pltpu.VMEM((rows, width + 128), BF),
        pltpu.VMEM((6,) + small.shape, small.dtype),
        pltpu.VMEM((5, 3) + small.shape, small.dtype),
    ] + tp_sum_scratch(rows, width)
    return call(
        front_kernel, 0, outs, ["hbm"] * 10 + ["vmem"] * 8, scratch, 120, 40,
        (downs, q_up, kv_up, out_t, hidden, grad) + tuple(ffn) + (small, cosine, sine, seg_col, seg_row) + tuple(picks),
        60,
    )


def back_kernel(
    gu, dn, sgu, sdn, part, attn_in, heads, out_w, up_q, up_kv, downs, query, keyval, rope, norms, qlat, kvlat, raw,
    resid, logits, pick_a, pick_b, grad, gains, cosine, sine, seg_col, seg_row,
    o_gu, o_dn, o_sgu, o_sdn, o_gout, o_gq, o_gkv, o_gdown, o_attn, o_resid, o_small,
    *rest,
):
    landing, rest = list(rest[:20]), rest[20:]
    scratch, (send, recv, here) = list(rest[:-3]), rest[-3:]
    spot, wire = Spot(), Wire(send, recv, here)
    greet(spot.rings() + [spot.along_y(1), spot.along_y(3), spot.core(), spot.far(), spot.diagonal()])
    own_rows, width = grad.shape
    groups = 4 * own_rows

    def take(count):
        taken, scratch[:] = scratch[:count], scratch[count:]
        return taken

    def unit(half, ref, order):
        rings = [take(3) + [landing.pop(0), landing.pop(0)] for _ in range(2)]
        return sum_unit(wire, spot, half, ref, order, rings)

    one = [unit(0, gu.at[pl.ds(0, 4)], "zx"), unit(1, gu.at[pl.ds(4, 4)], "zx")]
    two = [unit(0, dn, "xz"), unit(1, sgu, "xz"), unit(1, sdn, "xz")]

    def weights():
        yield from together(
            sum_stream(wire, spot, "zx", one, True), sum_stream(wire, spot, "xz", two, True)
        )
        moves = []
        places = (
            (one[0][2], o_gu.at[spot.yl, pl.ds(0, 4)]),
            (one[1][2], o_gu.at[spot.yl, pl.ds(4, 4)]),
            (two[0][2], o_dn.at[spot.yl]),
            (two[1][2], o_sgu.at[spot.yl]),
            (two[2][2], o_sdn.at[spot.yl]),
        )
        for total, place in places:
            moves += [wire.copy(total.at[:, 1 - spot.yl], place, spot.pair()), wire.keep(total.at[:, spot.yl], place)]
        yield
        wait_all(moves)

    tokens = take(5)
    (s_back, s_heads, s_wide, s_upq, s_upkv, s_query, s_keyval, s_rope, s_norms, s_qlat, s_kvlat, s_raw) = take(12)
    (s_normed, s_dres, s_dh, s_dhall, s_dheads, s_dq, s_dkv, s_accq, s_acck, s_dkn, s_dv, s_lat) = take(12)
    (s_swap, s_got, s_stage, s_attn, s_small) = take(5)
    t_scratch = take(3)
    s_part = tokens[1]
    sums = sum_y(wire, spot, part, s_back, *tokens)
    next(sums)
    ffn = weights()
    next(ffn)
    loads = [wire.keep(a, b) for a, b in ((heads, s_heads), (out_w, s_wide.at[:, pl.ds(0, 512)]))]
    others = [
        wire.keep(a, b)
        for a, b in (
            (query, s_query), (keyval, s_keyval), (rope, s_rope), (norms, s_norms), (qlat, s_qlat), (kvlat, s_kvlat),
            (up_q, s_upq), (up_kv, s_upkv), (raw.at[:, pl.ds(pl.multiple_of(spot.t * own_rows, 128), own_rows)], s_raw),
        )
    ]
    finish(sums)

    rows_f32 = gains[...].astype(F32)
    ffn_gain = rows_f32[9:10]
    dense = s_back[:, width : width + 16]
    scores = jax.nn.sigmoid(logits[...])
    first = jnp.sum(pick_a[...] * scores, axis=-1, keepdims=True)
    second = jnp.sum(pick_b[...] * scores, axis=-1, keepdims=True)
    both = first + second
    apart = jnp.sum((pick_a[...] - pick_b[...]) * dense, axis=-1, keepdims=True) * route_scale / both
    d_scores = (pick_a[...] * (second / both) - pick_b[...] * (first / both)) * apart
    d_logits = d_scores * scores * (1.0 - scores)
    s_normed[...] = dot(d_logits, rows_f32, "nn", lax.Precision.HIGHEST)
    s_small[0:1] = jnp.zeros((1, width), F32)

    def own_row(i):
        rows = at_tile(i, 16)
        values = resid[rows]
        scale = lax.rsqrt(jnp.mean(values * values, axis=-1, keepdims=True) + norm_eps)
        hat = values * scale
        grad_ffn = s_normed[rows] + s_back[rows, 0:width]
        s_small[0:1] += jnp.sum(grad_ffn * hat, axis=0, keepdims=True)
        weighted = grad_ffn * ffn_gain
        inner = scale * (weighted - hat * jnp.mean(weighted * hat, axis=-1, keepdims=True))
        total = grad[rows].astype(F32) + inner
        s_dres[rows] = total
        s_dh[rows] = total.astype(BF)
        s_normed[rows] = hat * ffn_gain

    loop(own_rows // 16, own_row)
    keeps = [wire.keep(s_dres, o_resid)]
    swap = gather_tp(wire, spot, s_dhall, s_dh)
    next(swap)
    next(swap)
    o_small[...] = dot(d_logits, s_normed[...], "tn", lax.Precision.HIGHEST)
    o_small[9:10] = s_small[0:1]
    finish(swap)

    wait_all(loads)

    def out_grads(i):
        lanes = at_tile(i, 512)
        s_stage[lanes, 0:512] = dot(flat(s_dhall[:, :, lanes]), s_heads[...], "tn").astype(BF)

    loop(4, out_grads)
    staged = wire.keep(s_stage.at[:, pl.ds(0, 512)], o_gout)

    def head_grads(i):
        s_dheads[at_tile(i, own_rows)] = dot(s_dhall[i], s_wide[:, 0:512]).astype(BF)

    loop(4, head_grads)
    wait_all(others)
    late = [wire.keep(attn_in.at[pl.ds(t * own_rows, own_rows)], s_dhall.at[t]) for t in range(4)]
    late.append(wire.keep(downs, s_wide))
    s_accq[...] = jnp.zeros_like(s_accq)
    s_acck[...] = jnp.zeros_like(s_acck)

    for head in range(4):
        nope, value = pl.ds(head * 256, 128), pl.ds(head * 256 + 128, 128)
        at = pl.ds(head * 128, 128)
        s_dkn[...] = jnp.zeros_like(s_dkn)
        s_dv[...] = jnp.zeros_like(s_dv)

        def attend(i, head=head, nope=nope, value=value, at=at):
            tile = at_tile(i, 256)
            places = lax.broadcasted_iota(jnp.int32, (256, groups), 0) + i * 256
            keys = lax.broadcasted_iota(jnp.int32, (256, groups), 1)
            allowed = (seg_col[tile] == seg_row[...]) & (keys <= places)
            front, back = head_lanes(s_query[tile, 512:640], head), head_lanes(s_query[tile, 640:768], head)
            scores = dot(s_query[tile, at], s_keyval[:, nope], "nt")
            scores += dot(front, s_rope[:, 0:128], "nt")
            scores += dot(back, s_rope[:, 128:256], "nt")
            scores = jnp.where(allowed, scores * (NOPE + ROPE) ** (-0.5), masked_score)
            probs = jnp.exp(scores - s_norms[tile, head : head + 1])
            d_head = s_dheads[tile, at]
            s_dv[...] += dot(probs.astype(BF), d_head, "tn")
            d_probs = dot(d_head, s_keyval[:, value], "nt")
            row_dot = jnp.sum(probs * d_probs, axis=-1, keepdims=True)
            d_scores = (probs * (d_probs - row_dot) * (NOPE + ROPE) ** (-0.5)).astype(BF)
            s_dq[tile, at] = dot(d_scores, s_keyval[:, nope]).astype(BF)
            s_accq[tile, 0:128] += head_lanes(dot(d_scores, s_rope[:, 0:128]), head)
            s_accq[tile, 128:256] += head_lanes(dot(d_scores, s_rope[:, 128:256]), head)
            s_dkn[...] += dot(d_scores, s_query[tile, at], "tn")
            s_acck[:, 0:128] += dot(d_scores, front, "tn")
            s_acck[:, 128:256] += dot(d_scores, back, "tn")

        loop(2, attend)
        s_dkv[:, nope] = s_dkn[...].astype(BF)
        s_dkv[:, value] = s_dv[...].astype(BF)
    next(ffn)

    row, lane = lane_grid(128, 128)
    fold_front = ((lane < 32) & (lane == lax.rem(row, 32))).astype(F32)
    fold_back = ((lane >= 32) & (lane < 64) & (lane - 32 == lax.rem(row, 32))).astype(F32)

    def unrotate(i):
        rows = at_tile(i, own_rows)
        c, s = cosine[rows], sine[rows]
        front, back = s_accq[rows, 0:128], s_accq[rows, 128:256]
        s_dq[rows, 512:640] = (front * c + back * s).astype(BF)
        s_dq[rows, 640:768] = (back * c - front * s).astype(BF)
        front, back = s_acck[rows, 0:128], s_acck[rows, 128:256]
        folded = dot(front * c + back * s, fold_front, "nn", lax.Precision.HIGHEST)
        folded += dot(back * c - front * s, fold_back, "nn", lax.Precision.HIGHEST)
        s_part[i, :, 2048:2176] = folded.astype(BF)
        for j in range(3):
            lanes = slice(j * 512, j * 512 + 512)
            s_part[i, :, lanes] = dot(s_dq[rows], s_upq[lanes], "nt").astype(BF)
        s_part[i, :, 1536:2048] = dot(s_dkv[rows], s_upkv[...], "nt").astype(BF)

    loop(4, unrotate)
    latents = sum_tp(wire, spot, s_part, s_lat, *t_scratch)
    next(latents)
    staged.wait()

    def q_grads(i):
        lanes = at_tile(i, 256)
        s_stage[lanes] = dot(s_qlat[:, lanes], s_dq[...], "tn").astype(BF)

    loop(6, q_grads)
    staged = wire.keep(s_stage.at[pl.ds(0, 1536)], o_gq)
    next(latents)

    def kv_grads(i):
        lanes = at_tile(i, 256)
        s_attn[lanes, 0:1024] = dot(s_kvlat[:, lanes], s_dkv[...], "tn").astype(BF)

    loop(2, kv_grads)
    staged_kv = wire.keep(s_attn.at[:, pl.ds(0, 1024)], o_gkv)
    finish(latents)

    gain = rows_f32[10:11]
    s_small[...] = jnp.zeros_like(s_small)

    def latent_row(i):
        rows = at_tile(i, 32)
        for cut, columns, start in ((slice(0, 384), 384, 0), (slice(384, 512), 128, 1536)):
            size = 4.0 * columns
            values = [s_raw[t, rows, cut].astype(F32) for t in range(4)]
            scale = lax.rsqrt(sum(jnp.sum(v * v, axis=-1, keepdims=True) for v in values) / size + norm_eps)
            hats = [v * scale for v in values]
            grads, weighted = [], []
            for t in range(4):
                at = slice(start + t * columns, start + (t + 1) * columns)
                grads.append(s_lat[rows, at])
                weighted.append(grads[t] * gain[:, at])
                s_small[0:1, at] += jnp.sum(grads[t] * hats[t], axis=0, keepdims=True)
            inner = sum(jnp.sum(w * h, axis=-1, keepdims=True) for w, h in zip(weighted, hats)) / size
            for t in range(4):
                s_swap[t, rows, cut] = (scale * (weighted[t] - hats[t] * inner)).astype(BF)
        folded = s_lat[rows, 2048:2176].astype(BF)
        for t in range(4):
            pick = ((row == t * 16 + lane) & (lane < 16)).astype(F32).astype(BF)
            s_swap[t, rows, 512:640] = dot(folded, pick).astype(BF)

    loop(own_rows // 32, latent_row)
    moves = [wire.keep(s_swap.at[spot.t], s_got.at[spot.t])]
    for yh, c, device in (
        (spot.yh, 1 - spot.c, spot.core()),
        (1 - spot.yh, spot.c, spot.far()),
        (1 - spot.yh, 1 - spot.c, spot.diagonal()),
    ):
        moves.append(wire.copy(s_swap.at[yh * 2 + c], s_got.at[spot.t], device))
    o_small[10:11] = s_small[0:1]
    s_small[0:1] = jnp.zeros((1, width), F32)
    wait_all(moves)
    wait_all(late)
    staged.wait()
    staged_kv.wait()
    next(ffn)

    def down_grads(i):
        lanes = at_tile(i, 512)
        s_stage[lanes, 0:640] = dot(flat(s_dhall[:, :, lanes]), flat(s_got[...]), "tn").astype(BF)

    loop(4, down_grads)
    staged = wire.keep(s_stage.at[:, pl.ds(0, 640)], o_gdown)

    def attn_grads(i):
        rows, lanes = lax.div(i, 4), at_tile(lax.rem(i, 4), 512)
        back = dot(s_got[rows], s_wide[lanes], "nt")
        s_attn[at_tile(rows, own_rows), lanes] = back.astype(BF)
        s_small[0:1, lanes] += jnp.sum(back * s_dhall[rows, :, lanes].astype(F32), axis=0, keepdims=True)

    loop(16, attn_grads)
    o_small[8:9] = s_small[0:1] / rows_f32[8:9]
    keeps.append(wire.keep(s_attn, o_attn))
    finish(ffn)
    staged.wait()
    wait_all(keeps)


def back(ffn_grads, part, saved, resid, logits, picks, grad, gains, cosine, sine, seg_col, seg_row):
    rows, width = grad.shape
    group = 4 * rows
    outs = [((2, a.shape[0]) + a.shape[4:], BF, "hbm") for a in ffn_grads]
    outs += [((2048, 512), BF, "hbm"), ((1536, 768), BF, "hbm"), ((512, 1024), BF, "hbm"), ((2048, 640), BF, "hbm")]
    outs += [((group, width), BF, "hbm"), ((rows, width), F32, "hbm"), ((16, width), F32, "vmem")]
    scratch = []
    tile = ffn_grads[0].shape[4:]
    for planes, order in ((4, "zx"), (4, "zx"), (4, "xz"), (2, "xz"), (1, "xz")):
        first = (planes, 2, 4) + tile if order == "zx" else (planes, 4, 2) + tile
        second = (planes, 2) + tile
        outs += [(first, BF, "hbm")] * 2 + [(second, BF, "hbm")] * 2
        scratch += [pltpu.VMEM(first, BF)] * 3 + [pltpu.VMEM(second, BF)] * 3
    columns = part.shape[-1]
    scratch += [pltpu.VMEM((4, rows, columns), BF)] * 2 + [pltpu.VMEM((rows, columns), BF)] * 3
    sizes = [
        ((rows, columns), F32), ((group, 512), BF), ((width, 640), BF), ((1536, 768), BF), ((512, 1024), BF),
        ((group, 768), BF), ((group, 1024), BF), ((group, 256), BF), ((group, 128), F32), ((group, 1536), BF),
        ((group, 512), BF), ((4, rows, 640), BF),
        ((rows, width), F32), ((rows, width), F32), ((rows, width), BF), ((4, rows, width), BF), ((group, 512), BF),
        ((group, 768), BF), ((group, 1024), BF), ((group, 256), F32), ((group, 256), F32), ((group, 128), F32),
        ((group, 128), F32), ((rows, columns), F32),
        ((4, rows, 640), BF), ((4, rows, 640), BF), ((width, 768), BF), ((group, width), BF), ((8, width), F32),
    ]
    scratch += [pltpu.VMEM(*size) for size in sizes] + tp_sum_scratch(rows, columns)
    return call(
        back_kernel, 1, outs, ["hbm"] * 18 + ["vmem"] * 10, scratch, 100, 90,
        tuple(ffn_grads) + (part,) + tuple(saved) + (resid, logits) + tuple(picks)
        + (grad, gains, cosine, sine, seg_col, seg_row),
        62,
    )[:11]


def last_kernel(downs, q_up, kv_up, out_t, part, moe, small, o_downs, o_q, o_kv, o_out, o_part, o_moe, o_small, *rest):
    scratch, (send, recv, here) = list(rest[:-3]), rest[-3:]
    spot, wire = Spot(), Wire(send, recv, here)
    greet(
        spot.rings()
        + [spot.along_x(2), spot.along_z(2), spot.along_y(1), spot.along_y(3)]
        + [spot.core(), spot.far(), spot.diagonal()]
    )

    def take(count):
        taken, scratch[:] = scratch[:count], scratch[count:]
        return taken

    def unit(half, ref, order):
        return sum_unit(wire, spot, half, ref, order, (take(5), take(5)))

    one = [unit(0, q_up, "zx"), unit(1, out_t, "zx")]
    two = [unit(0, downs, "xz"), unit(1, kv_up, "xz")]
    (got_q, got_out, got_downs, got_kv, rows), tokens, ring = take(5), take(3), take(5)
    s_small, s_buf = take(2)
    s_small[0] = small[...]

    def weights():
        yield from together(sum_stream(wire, spot, "zx", one), sum_stream(wire, spot, "xz", two))
        finals = (
            (two[0][2], got_downs, rows),
            (one[0][2], got_q, o_q),
            (one[1][2], got_out, o_out),
            (two[1][2], got_kv, o_kv),
        )
        moves = [wire.copy(total.at[:, 1 - spot.yl], got, spot.pair()) for total, got, _ in finals]
        yield
        swaps = []
        for made, (total, got, out) in zip(moves, finals):
            made.wait()
            add_into(out, total.at[0, spot.yl], got.at[0])
            if not swaps:
                cut = lambda t: rows.at[pl.ds(pl.multiple_of(t * 16, 16), 16)]
                swaps.append(wire.keep(cut(spot.t), o_downs.at[spot.t]))
                for yh, c, device in (
                    (spot.yh, 1 - spot.c, spot.core()),
                    (1 - spot.yh, spot.c, spot.far()),
                    (1 - spot.yh, 1 - spot.c, spot.diagonal()),
                ):
                    swaps.append(wire.copy(cut(yh * 2 + c), o_downs.at[spot.t], device))
        yield
        wait_all(swaps)

    finish(
        together(
            weights(),
            sum_tp(wire, spot, part, o_part, *tokens),
            all_sum_small(wire, spot, s_buf, s_small),
            sum_y(wire, spot, moe, o_moe, *ring),
        )
    )
    o_small[...] = s_small[5]


def last(downs, q_up, kv_up, out_t, part, moe, small):
    scratch, ends = [], []
    for a, order in ((q_up, "zx"), (out_t, "zx"), (downs, "xz"), (kv_up, "xz")):
        scratch += unit_scratch(1, order, *a.shape[-2:])
        ends.append(pltpu.VMEM((1,) + a.shape[-2:], BF))
    rows, columns = part.shape[1:]
    scratch += ends + [pltpu.VMEM(downs.shape[-2:], BF)] + tp_sum_scratch(rows, columns)
    scratch += [pltpu.VMEM((4, rows, columns), BF)] * 2 + [pltpu.VMEM((rows, columns), BF)] * 3
    scratch += [pltpu.VMEM((6,) + small.shape, F32), pltpu.VMEM((5, 3) + small.shape, F32)]
    outs = [((4, 16, downs.shape[-1]), BF, "hbm")]
    outs += [(a.shape[-2:], F32, "vmem") for a in (q_up, kv_up, out_t)]
    outs += [((rows, columns), F32, "vmem")] * 2 + [(small.shape, F32, "vmem")]
    return call(
        last_kernel, 2, outs, ["hbm"] * 4 + ["vmem", "hbm", "vmem"], scratch, 64, 32,
        (downs, q_up, kv_up, out_t, part, moe, small), 50,
    )


def rotary_tables(position):
    half_size = ROPE // 2
    inverse = theta_base ** (-(2.0 * jnp.arange(half_size, dtype=F32)) / ROPE)
    angles = position.astype(F32)[:, None] * inverse[None, :]
    return (jnp.cos(angles), jnp.sin(angles))


def packing(lengths, total_rows):
    positions = jnp.arange(total_rows, dtype=jnp.int32)
    endings = jnp.cumsum(lengths)
    segment = jnp.sum((positions[:, None] >= endings[None, :]).astype(jnp.int32), axis=1)
    starting = endings - lengths
    owner_mask = segment[:, None] == jnp.arange(lengths.shape[0], dtype=jnp.int32)[None, :]
    first_row = jnp.sum(jnp.where(owner_mask, starting[None, :], 0), axis=1)
    return (segment, positions - first_row)


def normalized(values):
    scale = lax.rsqrt(jnp.mean(values * values, axis=-1, keepdims=True) + norm_eps)
    return values * scale, scale


def norm_back(grad, gain, hat, scale):
    weighted = grad * gain
    return scale * (weighted - hat * jnp.mean(weighted * hat, axis=-1, keepdims=True))


def swiglu(gate, up):
    return jax.nn.silu(gate) * up


def mm(spec, a, b):
    return jnp.einsum(spec, a, b, preferred_element_type=F32)


def per_device(
    hidden_in,
    out_grad,
    attn_gain,
    q_down,
    q_gain,
    kv_down,
    kv_gain,
    q_up,
    kv_up,
    out_proj,
    ffn_gain,
    router,
    routed_gate_up,
    routed_down,
    shared_gate_up,
    shared_down,
    choices,
    seq_lens,
):
    local_rows, width = hidden_in.shape
    group_rows = choices.shape[0]
    tp_count = lax.axis_size("tp")
    tp_index = lax.axis_index("tp")
    y_lo = lax.rem(lax.div(lax.axis_index("fsdp"), 4), 2)
    head_count = HEADS // tp_count
    experts = router.shape[1]
    held = experts // 2
    capacity = 5 * group_rows * TOPK // (4 * experts)
    units = routed_gate_up.shape[3]
    row_shard = routed_gate_up.shape[1]
    q_cols = q_down.shape[1] // tp_count
    raw_cols = q_cols + kv_down.shape[1] // tp_count
    raw_pad = -raw_cols % 128
    small_at = raw_cols + raw_pad

    def own(array):
        return lax.dynamic_slice_in_dim(array, tp_index * local_rows, local_rows)

    down_rows = q_down.shape[0]
    devices = width // down_rows
    device = lax.axis_index("fsdp") * tp_count + tp_index
    rope_cols = ROPE // tp_count
    columns = jnp.concatenate(
        [
            q_down.reshape(down_rows, tp_count, q_cols),
            kv_down[:, :KVR].reshape(down_rows, tp_count, KVR // tp_count),
            kv_down[:, KVR:].reshape(down_rows, tp_count, rope_cols),
        ],
        axis=-1,
    ).transpose(1, 0, 2)
    downs = jnp.pad(columns, ((0, 0), (0, 0), (0, raw_pad)))
    half = ROPE // 2
    q_rows = q_up.reshape(-1, head_count, NOPE + ROPE)
    q_sent = jnp.concatenate(
        [
            q_rows[..., :NOPE].reshape(-1, head_count * NOPE),
            q_rows[..., NOPE : NOPE + half].reshape(-1, head_count * half),
            q_rows[..., NOPE + half :].reshape(-1, head_count * half),
        ],
        axis=1,
    )
    small = jnp.zeros((16, width), BF)
    vectors = jnp.concatenate([router.T, attn_gain[None], ffn_gain[None]], axis=0)
    small = lax.dynamic_update_slice(small, vectors, (0, device * down_rows))
    small = lax.dynamic_update_slice(small, q_gain[None], (experts + 2, device * q_gain.shape[0]))
    kv_at = q_down.shape[1] + device * kv_gain.shape[0]
    small = lax.dynamic_update_slice(small, kv_gain[None], (experts + 2, kv_at))
    send_gu = routed_gate_up.transpose(0, 2, 1, 3).reshape(2, held * 2, row_shard, units)
    send_dn = routed_down.transpose(0, 2, 1).reshape(2, held, row_shard, units)
    send_sgu = shared_gate_up.reshape(row_shard, 2, 2, units).transpose(2, 1, 0, 3)
    send_sdn = shared_down.T.reshape(row_shard, 2, units).transpose(1, 0, 2)[:, None]

    segment, position = packing(seq_lens[0], group_rows)
    cosine, sine_table = rotary_tables(position)
    cos_heads, sin_heads = jnp.tile(cosine, (1, head_count)), jnp.tile(sine_table, (1, head_count))
    picked = own(choices)
    lanes = jnp.arange(2 * experts, dtype=jnp.int32)
    pick_a, pick_b = ((picked[:, k : k + 1] == lanes[None]).astype(F32) for k in range(TOPK))
    pick_sent = sum((picked[:, k : k + 1] + experts == lanes[None]).astype(F32) for k in range(TOPK))

    (
        all_downs, all_q, all_kv, all_out, all_grad, wide_gu, wide_dn, wide_sgu, wide_sdn, tokens,
        attn_in, raw, group_query, group_keyval, query, keyval, rope, norms, heads_out, residual, logits,
        gains,
    ) = front(
        downs, q_sent, kv_up, out_proj.T, hidden_in, out_grad, (send_gu, send_dn, send_sgu, send_sdn), small,
        cos_heads, sin_heads, segment[:, None], segment[None, :], (pick_a, pick_b, pick_sent),
    )
    down_weight = all_downs.reshape(width, -1)
    up_query = all_q.reshape(-1, q_up.shape[1])
    up_keyval = all_kv.reshape(-1, kv_up.shape[1])
    out_weight = all_out.reshape(width, -1)
    wide_gu = wide_gu.reshape(held, 2, width, units)
    wide_dn = wide_dn.reshape(held, width, units)
    wide_sgu = wide_sgu.reshape(2, width, units)
    wide_sdn = wide_sdn.reshape(width, units)
    tokens = tokens.reshape(2, group_rows, -1)

    moe_in = tokens[..., :width]
    grad_rows = all_grad.reshape(2, group_rows, width)
    extra = tokens[..., width:].astype(F32)
    gate_mine = lax.dynamic_slice_in_dim(extra, y_lo * held, held, axis=2).transpose(0, 2, 1)
    mask_mine = lax.dynamic_slice_in_dim(extra, experts + y_lo * held, held, axis=2).transpose(0, 2, 1)
    place = jnp.cumsum(mask_mine, axis=2) - mask_mine
    place = jnp.where(mask_mine > 0, place, -1.0).astype(jnp.int32)
    slots = place[:, :, None, :] == jnp.arange(capacity, dtype=jnp.int32)[None, None, :, None]
    onehot = slots.astype(BF)
    gate_slot = jnp.sum(jnp.where(slots, gate_mine[:, :, None, :], 0.0), axis=-1)
    gate_slot = gate_slot.transpose(1, 0, 2).reshape(held, 2 * capacity, 1)
    expert_in = mm("gest,gtd->egsd", onehot, moe_in).astype(BF).reshape(held, 2 * capacity, width)
    expert_dy = mm("gest,gtd->egsd", onehot, grad_rows).reshape(held, 2 * capacity, width)
    expert_grad = (gate_slot * expert_dy).astype(BF)
    gate = mm("ecd,edf->ecf", expert_in, wide_gu[:, 0])
    up = mm("ecd,edf->ecf", expert_in, wide_gu[:, 1])
    hidden_act, act_pull = jax.vjp(swiglu, gate, up)
    hidden_low = hidden_act.astype(BF)
    rows_out = mm("ecf,edf->ecd", hidden_low, wide_dn)
    grad_hidden = mm("ecd,edf->ecf", expert_grad, wide_dn)
    grad_gate, grad_up = (v.astype(BF) for v in act_pull(grad_hidden))
    sum_dn = mm("ecd,ecf->edf", expert_grad, hidden_low).astype(BF)
    sum_gu = jnp.stack(
        [mm("ecd,ecf->edf", expert_in, grad_gate).astype(BF), mm("ecd,ecf->edf", expert_in, grad_up).astype(BF)],
        axis=1,
    )
    back_rows = mm("ecf,edf->ecd", grad_gate, wide_gu[:, 0]) + mm("ecf,edf->ecd", grad_up, wide_gu[:, 1])
    gate_back = jnp.sum(rows_out * expert_dy, axis=-1).reshape(held, 2, capacity)
    slot_shape = (held, 2, capacity, width)
    weighted_out = (gate_slot * rows_out).astype(BF).reshape(slot_shape)
    routed_sum = mm("gest,egsd->gtd", onehot, weighted_out)
    routed_back = mm("gest,egsd->gtd", onehot, back_rows.astype(BF).reshape(slot_shape))
    dense_back = jnp.sum(jnp.where(slots, gate_back.transpose(1, 0, 2)[..., None], 0.0), axis=2)
    flat_in, flat_dy = moe_in.reshape(-1, width), grad_rows.reshape(-1, width)
    common_gate, common_up = mm("rd,df->rf", flat_in, wide_sgu[0]), mm("rd,df->rf", flat_in, wide_sgu[1])
    common_act, common_pull = jax.vjp(swiglu, common_gate, common_up)
    common_low = common_act.astype(BF)
    moe_part = mm("rf,df->rd", common_low, wide_sdn) + routed_sum.reshape(-1, width)
    common_dhid = mm("rd,df->rf", flat_dy, wide_sdn)
    common_dgate, common_dup = (v.astype(BF) for v in common_pull(common_dhid))
    sum_sdn = mm("rd,rf->df", flat_dy, common_low).astype(BF)
    sum_sgu = jnp.stack(
        [mm("rd,rf->df", flat_in, common_dgate).astype(BF), mm("rd,rf->df", flat_in, common_dup).astype(BF)]
    )
    moe_back = mm("rf,df->rd", common_dgate, wide_sgu[0]) + mm("rf,df->rd", common_dup, wide_sgu[1])
    moe_back = moe_back + routed_back.reshape(-1, width)
    dense_back = lax.dynamic_update_slice(
        jnp.zeros((2, group_rows, 128), F32), dense_back.transpose(0, 2, 1), (0, 0, y_lo * held)
    )
    back_part = jnp.concatenate([moe_back.astype(BF), dense_back.reshape(-1, 128).astype(BF)], axis=1)
    ring = (2, 2, 2, local_rows)
    blocks = (4, 2, 4, row_shard, units)
    own_gu, own_dn, own_sgu, own_sdn, grad_out, grad_q, grad_kv, grad_down, attn_back, grad_resid, small_grads = back(
        (
            sum_gu.reshape((held * 2,) + blocks),
            sum_dn.reshape((held,) + blocks),
            sum_sgu.reshape((2,) + blocks),
            sum_sdn.reshape((1,) + blocks),
        ),
        back_part.reshape(ring + (width + 128,)),
        (
            attn_in, heads_out, out_weight, up_query, up_keyval, down_weight, query, keyval, rope, norms, group_query,
            group_keyval, raw,
        ),
        residual, logits, (pick_a, pick_b), out_grad, gains, cos_heads, sin_heads, segment[:, None], segment[None, :],
    )

    def spread(array, like):
        return array.reshape((1, 4, 2, 4) + like.shape[-2:])

    got_downs, sum_up_query, sum_up_keyval, sum_out, attn_back_own, moe_own, small_sum = last(
        spread(grad_down, jnp.zeros((row_shard, grad_down.shape[1]))),
        spread(grad_q, q_up),
        spread(grad_kv, kv_up),
        spread(grad_out, out_proj.T),
        attn_back.reshape(tp_count, local_rows, width),
        moe_part.astype(BF).reshape(ring + (width,)),
        small_grads,
    )
    layer_out = (residual + moe_own).astype(BF)
    own_hat, own_scale = normalized(hidden_in.astype(F32))
    input_grad = grad_resid + norm_back(attn_back_own, gains[experts].astype(F32), own_hat, own_scale)
    got_downs = got_downs.astype(F32)
    sum_qdown = got_downs[..., :q_cols].transpose(1, 0, 2).reshape(down_rows, -1)
    kv_at = q_cols + KVR // tp_count
    sum_kvdown = jnp.concatenate(
        [
            got_downs[..., q_cols:kv_at].transpose(1, 0, 2).reshape(down_rows, -1),
            got_downs[..., kv_at:raw_cols].transpose(1, 0, 2).reshape(down_rows, -1),
        ],
        axis=-1,
    )
    nope_cols, half_cols = head_count * NOPE, head_count * half
    sum_up_query = jnp.concatenate(
        [
            sum_up_query[:, :nope_cols].reshape(-1, head_count, NOPE),
            sum_up_query[:, nope_cols : nope_cols + half_cols].reshape(-1, head_count, half),
            sum_up_query[:, nope_cols + half_cols :].reshape(-1, head_count, half),
        ],
        axis=-1,
    ).reshape(q_up.shape)

    def mine(row, at, count):
        return lax.dynamic_slice(small_sum, (row, at), (1, count))[0]

    rows_at = device * down_rows
    sum_router = lax.dynamic_slice(small_sum, (0, rows_at), (experts, down_rows)).T
    sum_wide_gu = own_gu.reshape(experts, 2, row_shard, units).transpose(0, 2, 1, 3).astype(F32)
    sum_wide_down = own_dn.reshape(experts, row_shard, units).transpose(0, 2, 1).astype(F32)
    sum_common_gu = own_sgu.transpose(2, 1, 0, 3).reshape(row_shard, 2, 2 * units).astype(F32)
    sum_common_down = own_sdn[:, 0].transpose(1, 0, 2).reshape(row_shard, 2 * units).T.astype(F32)
    q_rank = q_down.shape[1]
    return (
        layer_out,
        input_grad.astype(BF),
        mine(experts, rows_at, down_rows),
        sum_qdown,
        mine(experts + 2, device * q_gain.shape[0], q_gain.shape[0]),
        sum_kvdown,
        mine(experts + 2, q_rank + device * kv_gain.shape[0], kv_gain.shape[0]),
        sum_up_query,
        sum_up_keyval,
        sum_out.T,
        mine(experts + 1, rows_at, down_rows),
        sum_router,
        sum_wide_gu,
        sum_wide_down,
        sum_common_gu,
        sum_common_down,
    )


def solution(mesh):
    return jax.shard_map(
        per_device,
        mesh=mesh,
        in_specs=(
            P(("fsdp", "tp"), None),
            P(("fsdp", "tp"), None),
            P(("fsdp", "tp")),
            P(("fsdp", "tp"), None),
            P(("fsdp", "tp")),
            P(("fsdp", "tp"), None),
            P(("fsdp", "tp")),
            P("fsdp", "tp"),
            P("fsdp", "tp"),
            P("tp", "fsdp"),
            P(("fsdp", "tp")),
            P(("fsdp", "tp"), None),
            P(None, "fsdp", None, "tp"),
            P(None, "tp", "fsdp"),
            P("fsdp", None, "tp"),
            P("tp", "fsdp"),
            P("fsdp", None),
            P("fsdp", None),
        ),
        out_specs=(
            P(("fsdp", "tp"), None),
            P(("fsdp", "tp"), None),
            P(("fsdp", "tp")),
            P(("fsdp", "tp"), None),
            P(("fsdp", "tp")),
            P(("fsdp", "tp"), None),
            P(("fsdp", "tp")),
            P("fsdp", "tp"),
            P("fsdp", "tp"),
            P("tp", "fsdp"),
            P(("fsdp", "tp")),
            P(("fsdp", "tp"), None),
            P(None, "fsdp", None, "tp"),
            P(None, "tp", "fsdp"),
            P("fsdp", None, "tp"),
            P("tp", "fsdp"),
        ),
        check_vma=False,
    )
```

```python
import functools

import jax
import jax.numpy as jnp
from jax import lax
from jax.experimental import pallas as pl
from jax.experimental.pallas import tpu as pltpu
from jax.sharding import PartitionSpec as P

HEADS = 16
NOPE = 128
ROPE = 64
VDIM = 128
KVR = 512
TOPK = 2

theta_base = 50000.0
norm_eps = 1e-06
route_scale = 2.446
masked_score = -1e30

MESH = pl.DeviceIdType.MESH
BF = jnp.bfloat16
F32 = jnp.float32
MIB = 1 << 20


class Spot:
    def __init__(self):
        f, t = lax.axis_index("fsdp"), lax.axis_index("tp")
        self.t = t
        self.z, self.yl, self.x = lax.div(f, 8), lax.rem(lax.div(f, 4), 2), lax.rem(f, 4)
        self.yh, self.c = lax.div(t, 2), lax.rem(t, 2)
        self.y = self.yh * 2 + self.yl

    def at(self, z=None, yl=None, x=None, yh=None, c=None):
        z = self.z if z is None else z
        yl = self.yl if yl is None else yl
        x = self.x if x is None else x
        yh = self.yh if yh is None else yh
        c = self.c if c is None else c
        return ((z * 2 + yl) * 4 + x, yh * 2 + c)

    def along_x(self, by):
        return self.at(x=lax.rem(self.x + by, 4))

    def along_z(self, by):
        return self.at(z=lax.rem(self.z + by, 4))

    def along_y(self, by):
        y = lax.rem(self.y + by, 4)
        return self.at(yl=lax.rem(y, 2), yh=lax.div(y, 2))

    def pair(self):
        return self.at(yl=1 - self.yl)

    def core(self):
        return self.at(c=1 - self.c)

    def far(self):
        return self.at(yh=1 - self.yh)

    def diagonal(self):
        return self.at(yh=1 - self.yh, c=1 - self.c)

    def rings(self):
        return [self.along_x(1), self.along_x(3), self.along_z(1), self.along_z(3)]


def greet(devices):
    barrier = pltpu.get_barrier_semaphore()
    for device in devices:
        pl.semaphore_signal(barrier, inc=1, device_id=device, device_id_type=MESH)
    pl.semaphore_wait(barrier, len(devices))


class Wire:
    def __init__(self, send, recv, here):
        self.send, self.recv, self.here = send, recv, here
        self.sent = self.kept = 0

    def copy(self, source, target, device):
        made = pltpu.make_async_remote_copy(
            src_ref=source,
            dst_ref=target,
            send_sem=self.send.at[self.sent],
            recv_sem=self.recv.at[self.sent],
            device_id=device,
            device_id_type=MESH,
        )
        self.sent += 1
        made.start()
        return made

    def keep(self, source, target):
        made = pltpu.make_async_copy(source, target, self.here.at[self.kept])
        self.kept += 1
        made.start()
        return made


def wait_all(copies):
    for made in copies:
        made.wait()


def together(*parts):
    left = list(parts)
    while left:
        for part in list(left):
            if next(part, "over") == "over":
                left.remove(part)
        yield


def finish(part):
    for _ in part:
        pass


def add_into(target, *terms):
    lead, (rows, columns) = target.shape[:-2], target.shape[-2:]
    step = rows if rows * columns <= 49152 else 16
    pieces = rows // step
    count = pieces
    for size in lead:
        count *= size

    def body(i, carry):
        at = [pl.ds(pl.multiple_of(lax.rem(i, pieces) * step, 16), step)]
        i = lax.div(i, pieces)
        for size in reversed(lead):
            at.insert(0, lax.rem(i, size))
            i = lax.div(i, size)
        at = tuple(at)
        total = terms[0][at].astype(F32)
        for term in terms[1:]:
            total = total + term[at].astype(F32)
        target[at] = total.astype(target.dtype)
        return carry

    lax.fori_loop(0, count, body, 0)


def gather_ring(wire, pos, plus, minus, units):
    prev, following = lax.rem(pos + 3, 4), lax.rem(pos + 1, 4)
    mine = [unit[2] if len(unit) > 2 else unit[0](pos) for unit in units]
    right = [wire.copy(own, unit[0](pos), plus) for own, unit in zip(mine, units)]
    left = [wire.copy(own, unit[0](pos), minus) for own, unit in zip(mine, units)]
    yield
    wait_all(right)
    onward = [wire.copy(unit[0](prev), unit[0](prev), plus) for unit in units if unit[1] == 0]
    wait_all(left)
    onward += [wire.copy(unit[0](following), unit[0](following), minus) for unit in units if unit[1] == 1]
    yield
    wait_all(onward)


def sum_ring(wire, pos, plus, minus, units, staged=False):
    prev, following, across = lax.rem(pos + 3, 4), lax.rem(pos + 1, 4), lax.rem(pos + 2, 4)
    first, direct, last = [], [], []
    for half, view, between, own, through, from_left, from_right, loads in units:
        first.append(wire.copy(view(across), through, plus if half == 0 else minus))
    for half, view, between, own, through, from_left, from_right, loads in units:
        if half == 0:
            direct.append(wire.copy(view(prev), from_right, minus))
        else:
            direct.append(wire.copy(view(following), from_left, plus))
    yield
    for made, (half, view, between, own, through, from_left, from_right, loads) in zip(first, units):
        wait_all(loads)
        made.wait()
        add_into(between, between, through)
        if half == 0:
            last.append(wire.copy(between, from_left, plus))
        else:
            last.append(wire.copy(between, from_right, minus))
    yield
    for one, two, (half, view, between, own, through, from_left, from_right, loads) in zip(direct, last, units):
        one.wait()
        two.wait()
        if staged:
            wait_all([wire.keep(from_left, through), wire.keep(from_right, between)])
            add_into(own, own, through, between)
        else:
            add_into(own, own, from_left, from_right)


def gather_tp(wire, spot, out, source):
    across = wire.copy(source, out.at[spot.t], spot.far())
    own = wire.keep(source, out.at[spot.t])
    other = wire.copy(source, out.at[spot.t], spot.core())
    yield
    across.wait()
    there = (1 - spot.yh) * 2 + spot.c
    last = wire.copy(out.at[there], out.at[there], spot.core())
    yield
    own.wait()
    other.wait()
    last.wait()


def gather_y(wire, spot, out, source):
    def view(rows):
        return lambda y: out.at[lax.rem(y, 2), lax.div(y, 2), spot.c, rows]

    rows = source.shape[0] // 2
    own = wire.keep(source, out.at[spot.yl, spot.yh, spot.c])
    other = [own, wire.copy(source, out.at[spot.yl, spot.yh, spot.c], spot.core())]
    cuts = (pl.ds(0, rows), pl.ds(rows, rows))
    units = [(view(cut), half, source.at[cut]) for half, cut in enumerate(cuts)]
    yield from gather_ring(wire, spot.y, spot.along_y(1), spot.along_y(3), units)
    for by in (1, 2, 3):
        y = lax.rem(spot.y + by, 4)
        part = out.at[lax.rem(y, 2), lax.div(y, 2), spot.c]
        other.append(wire.copy(part, part, spot.core()))
    yield
    wait_all(other)


def sum_tp(wire, spot, source, out, got, held, last):
    cores = [wire.copy(source.at[yh * 2 + 1 - spot.c], got.at[yh], spot.core()) for yh in (0, 1)]
    yield
    wait_all(cores)
    there = 1 - spot.yh
    add_into(held, source.at[there * 2 + spot.c], got.at[there])
    across = wire.copy(held, last, spot.far())
    yield
    across.wait()
    add_into(out, source.at[spot.t], got.at[spot.yh], last)


def sum_y(wire, spot, source, out, got, held, through, from_left, from_right):
    cores = [wire.copy(source.at[y % 2, y // 2, 1 - spot.c], got.at[y], spot.core()) for y in range(4)]
    loads = [wire.keep(source.at[y % 2, y // 2, spot.c], held.at[y]) for y in range(4)]
    yield
    for y, made in enumerate(cores):
        made.wait()
        loads[y].wait()
        add_into(held.at[y], held.at[y], got.at[y])
    rows = out.shape[0] // 2
    following, prev = lax.rem(spot.y + 1, 4), lax.rem(spot.y + 3, 4)
    units = []
    for half in (0, 1):
        part = pl.ds(half * rows, rows)
        units.append(
            (
                half,
                lambda y, part=part: held.at[y, part],
                held.at[following if half == 0 else prev, part],
                held.at[spot.y, part],
                through.at[part],
                from_left.at[part],
                from_right.at[part],
                [],
            )
        )
    yield from sum_ring(wire, spot.y, spot.along_y(1), spot.along_y(3), units)
    add_into(out, held.at[spot.y])


def sum_unit(wire, spot, half, part, order, scratch):
    following, prev = (lambda p: lax.rem(p + 1, 4)), (lambda p: lax.rem(p + 3, 4))
    (between, own, through, from_left, from_right), (between2, own2, through2, from_left2, from_right2) = scratch
    near = following if half == 0 else prev
    if order == "zx":
        view, pos, pos2 = (lambda i: part.at[:, i]), spot.z, spot.x
        view2 = lambda i: own.at[:, :, i]
    else:
        view, pos, pos2 = (lambda i: part.at[:, :, :, i]), spot.x, spot.z
        view2 = lambda i: own.at[:, i]

    def loads():
        return [wire.keep(view(near(pos)), between), wire.keep(view(pos), own)]

    def loads2():
        return [wire.keep(view2(near(pos2)), between2), wire.keep(view2(pos2), own2)]

    one = lambda: (half, view, between, own, through, from_left, from_right, loads())
    two = lambda: (half, view2, between2, own2, through2, from_left2, from_right2, loads2())
    return one, two, own2


def sum_stream(wire, spot, order, units, staged=False):
    x = (spot.x, spot.along_x(1), spot.along_x(3))
    z = (spot.z, spot.along_z(1), spot.along_z(3))
    axes = (z, x) if order == "zx" else (x, z)
    yield from sum_ring(wire, *axes[0], [one() for one, _, _ in units], staged)
    yield from sum_ring(wire, *axes[1], [two() for _, two, _ in units], staged)


def unit_scratch(planes, order, rows, columns):
    first = (planes, 2, 4, rows, columns) if order == "zx" else (planes, 4, 2, rows, columns)
    second = (planes, 2, rows, columns)
    return [pltpu.VMEM(first, BF)] * 5 + [pltpu.VMEM(second, BF)] * 5


def call(kernel, number, outs, ins, scratch, copies, keeps, operands, vmem):
    space = {"hbm": pltpu.HBM, "vmem": pltpu.VMEM}
    return pl.pallas_call(
        kernel,
        out_shape=[jax.ShapeDtypeStruct(shape, dtype) for shape, dtype, _ in outs],
        in_specs=[pl.BlockSpec(memory_space=space[kind]) for kind in ins],
        out_specs=[pl.BlockSpec(memory_space=space[kind]) for _, _, kind in outs],
        scratch_shapes=list(scratch)
        + [
            pltpu.SemaphoreType.DMA((max(copies, 1),)),
            pltpu.SemaphoreType.DMA((max(copies, 1),)),
            pltpu.SemaphoreType.DMA((max(keeps, 1),)),
        ],
        compiler_params=pltpu.CompilerParams(
            collective_id=number, has_side_effects=True, vmem_limit_bytes=vmem * MIB
        ),
    )(*operands)


def tp_sum_scratch(rows, columns):
    return [pltpu.VMEM((2, rows, columns), BF), pltpu.VMEM((rows, columns), BF), pltpu.VMEM((rows, columns), BF)]


def dot(a, b, dims="nn", precision=None):
    left, right = {"nn": (1, 0), "nt": (1, 1), "tn": (0, 0)}[dims]
    return lax.dot_general(
        a, b, (((left,), (right,)), ((), ())), precision=precision, preferred_element_type=F32
    )


def loop(count, body):
    def step(i, carry):
        body(i)
        return carry

    lax.fori_loop(0, count, step, 0)


def at_tile(i, size):
    return pl.ds(pl.multiple_of(i * size, size), size)


def flat(block):
    return block.reshape(-1, block.shape[-1])


def lane_grid(rows, columns):
    return (
        lax.broadcasted_iota(jnp.int32, (rows, columns), 0),
        lax.broadcasted_iota(jnp.int32, (rows, columns), 1),
    )


def head_lanes(values, head):
    lanes = lax.broadcasted_iota(jnp.int32, (1, values.shape[1]), 1)
    return values * (lax.div(lanes, 32) == head).astype(F32).astype(values.dtype)


def all_sum_small(wire, spot, buffers, own):
    steps = (
        [spot.core()],
        [spot.far()],
        [spot.pair()],
        [spot.along_x(1), spot.along_x(2), spot.along_x(3)],
        [spot.along_z(1), spot.along_z(2), spot.along_z(3)],
    )
    for step, devices in enumerate(steps):
        moves = [wire.copy(own.at[step], buffers.at[step, i], device) for i, device in enumerate(devices)]
        yield
        wait_all(moves)
        total = own[step]
        for i in range(len(devices)):
            total = total + buffers[step, i]
        own[step + 1] = total


def ffn_stream(wire, spot, sources, targets):
    moves = []
    for source, target in zip(sources, targets):
        place = target.at[:, spot.z, spot.yl, spot.x]
        moves += [wire.copy(source.at[1 - spot.yl], place, spot.pair()), wire.keep(source.at[spot.yl], place)]
    yield
    wait_all(moves)
    x = (spot.x, spot.along_x(1), spot.along_x(3))
    z = (spot.z, spot.along_z(1), spot.along_z(3))
    gu, dn, sgu, sdn = targets

    def x_then_z(*parts):
        yield from gather_ring(wire, *x, [((lambda i, r=r, cut=cut: r.at[cut, spot.z, :, i]), half) for r, half, cut in parts])
        yield from gather_ring(wire, *z, [((lambda i, r=r, cut=cut: r.at[cut, i]), half) for r, half, cut in parts])

    def z_then_x(*parts):
        yield from gather_ring(wire, *z, [((lambda i, r=r, cut=cut: r.at[cut, i, :, spot.x]), half) for r, half, cut in parts])
        yield from gather_ring(wire, *x, [((lambda i, r=r, cut=cut: r.at[cut, :, :, i]), half) for r, half, cut in parts])

    yield from together(
        x_then_z((gu, 0, pl.ds(0, 4)), (gu, 1, pl.ds(4, 4))),
        z_then_x((dn, 0, pl.ds(0, 4)), (sgu, 1, pl.ds(0, 2)), (sdn, 1, pl.ds(0, 1))),
    )


def front_kernel(
    downs, q_up, kv_up, out_t, hidden, grad, gu, dn, sgu, sdn, small, cosine, sine, seg_col, seg_row, pick_a, pick_b,
    pick_sent,
    o_downs, o_q, o_kv, o_out, o_grad, o_gu, o_dn, o_sgu, o_sdn, o_tokens,
    o_hat, o_raw, o_qhat, o_kvhat, o_query, o_keyval, o_rope, o_norm, o_heads, o_resid, o_logits, o_small,
    rows, s_downs, s_q, s_kv, s_out, s_hidden, s_hat, s_part, s_raw, s_qlat, s_kvlat, s_query, s_keyval, s_rope,
    s_norm, s_heads, s_attn, s_sum, s_resid, s_sent, s_small, s_buf, t_got, t_held, t_last,
    send, recv, here,
):
    spot, wire = Spot(), Wire(send, recv, here)
    greet(
        spot.rings()
        + [spot.along_x(2), spot.along_z(2), spot.along_y(1), spot.along_y(3)]
        + [spot.core(), spot.far(), spot.diagonal()]
    )
    groups, width = 4 * hidden.shape[0], hidden.shape[1]
    own_rows = hidden.shape[0]

    def weights():
        mine = rows.at[pl.ds(pl.multiple_of(spot.t * 16, 16), 16)]
        swaps = [wire.keep(downs.at[spot.t], mine)]
        for yh, c, device in (
            (spot.yh, 1 - spot.c, spot.core()),
            (1 - spot.yh, spot.c, spot.far()),
            (1 - spot.yh, 1 - spot.c, spot.diagonal()),
        ):
            swaps.append(wire.copy(downs.at[yh * 2 + c], mine, device))
        moves = []
        for source, target in ((q_up, s_q), (kv_up, s_kv), (out_t, s_out)):
            place = target.at[spot.z, spot.yl, spot.x]
            moves += [wire.copy(source, place, spot.pair()), wire.keep(source, place)]
        yield
        wait_all(swaps)
        place = s_downs.at[spot.z, spot.yl, spot.x]
        moves += [wire.copy(rows, place, spot.pair()), wire.keep(rows, place)]
        yield
        wait_all(moves)
        x = (spot.x, spot.along_x(1), spot.along_x(3))
        z = (spot.z, spot.along_z(1), spot.along_z(3))
        low, high, every = pl.ds(0, 32), pl.ds(32, 32), slice(None)

        def x_then_z(*parts):
            yield from gather_ring(wire, *x, [((lambda i, r=r, cut=cut: r.at[spot.z, :, i, cut]), half) for r, half, cut in parts])
            yield from gather_ring(wire, *z, [((lambda i, r=r, cut=cut: r.at[i, :, :, cut]), half) for r, half, cut in parts])

        def z_then_x(*parts):
            yield from gather_ring(wire, *z, [((lambda i, r=r, cut=cut: r.at[i, :, spot.x, cut]), half) for r, half, cut in parts])
            yield from gather_ring(wire, *x, [((lambda i, r=r, cut=cut: r.at[:, :, i, cut]), half) for r, half, cut in parts])

        yield from together(
            x_then_z((s_q, 0, every), (s_out, 1, every)),
            z_then_x((s_downs, 0, low), (s_kv, 0, every), (s_downs, 1, high)),
        )

    hiddens = gather_tp(wire, spot, s_hidden, hidden)
    next(hiddens)
    heads = weights()
    next(heads)
    s_small[0] = small[...]
    smalls = all_sum_small(wire, spot, s_buf, s_small)
    next(smalls)
    next(hiddens)
    next(heads)
    next(smalls)
    finish(hiddens)
    ffn = ffn_stream(wire, spot, (gu, dn, sgu, sdn), (o_gu, o_dn, o_sgu, o_sdn))
    next(ffn)
    next(heads)
    finish(smalls)
    gains = s_small[5].astype(F32)
    attn_gain, ffn_gain = gains[8:9], gains[9:10]
    latent_gain = gains[10:11]
    keeps = []

    def norm_rows(i):
        block, part = lax.div(i, 8), at_tile(lax.rem(i, 8), 16)
        values = s_hidden[block, part].astype(F32)
        scale = lax.rsqrt(jnp.mean(values * values, axis=-1, keepdims=True) + norm_eps)
        s_hat[at_tile(i, 16)] = (values * scale * attn_gain).astype(BF)

    loop(groups // 16, norm_rows)
    finish(heads)
    next(ffn)
    keeps += [wire.keep(a, b) for a, b in ((s_downs, o_downs), (s_q, o_q), (s_kv, o_kv), (s_out, o_out), (s_hat, o_hat))]

    def down(i):
        j, k = lax.div(i, 2), lax.rem(i, 2)
        lanes = at_tile(j, 128)
        s_part[at_tile(k, 256), lanes] = dot(s_hat[at_tile(k, 256)], flat(s_downs[:, :, :, :, lanes])).astype(BF)

    loop(10, down)
    finish(gather_tp(wire, spot, s_raw, s_part))
    grads = gather_y(wire, spot, o_grad, grad)
    next(grads)
    next(ffn)
    keeps.append(wire.keep(s_raw, o_raw))

    row, lane = lane_grid(128, 128)
    low_pick = (row == lax.rem(lane, 16)) & (lax.rem(lane, 32) < 16)
    high_pick = (row == lax.rem(lane, 16)) & (lax.rem(lane, 32) >= 16)
    low_pick, high_pick = low_pick.astype(F32).astype(BF), high_pick.astype(F32).astype(BF)

    def latents(i):
        part = at_tile(i, 32)
        raw = [s_raw[t, part, 0:384].astype(F32) for t in range(4)]
        total = sum(jnp.sum(v * v, axis=-1, keepdims=True) for v in raw)
        scale = lax.rsqrt(total / 1536.0 + norm_eps)
        for t in range(4):
            s_qlat[part, t * 384 : t * 384 + 384] = (raw[t] * scale * latent_gain[:, t * 384 : t * 384 + 384]).astype(BF)
        raw = [s_raw[t, part, 384:512].astype(F32) for t in range(4)]
        total = sum(jnp.sum(v * v, axis=-1, keepdims=True) for v in raw)
        scale = lax.rsqrt(total / 512.0 + norm_eps)
        for t in range(4):
            gain = latent_gain[:, 1536 + t * 128 : 1664 + t * 128]
            s_kvlat[part, t * 128 : t * 128 + 128] = (raw[t] * scale * gain).astype(BF)
        front = dot(s_raw[0, part, 512:640], low_pick) + dot(s_raw[1, part, 512:640], high_pick)
        back = dot(s_raw[2, part, 512:640], low_pick) + dot(s_raw[3, part, 512:640], high_pick)
        c, s = cosine[part], sine[part]
        s_rope[part, 0:128] = (front * c - back * s).astype(BF)
        s_rope[part, 128:256] = (back * c + front * s).astype(BF)

    loop(groups // 32, latents)

    def query(i):
        part = at_tile(i, 256)
        for j in range(2):
            lanes = pl.ds(j * 256, 256)
            s_query[part, lanes] = dot(s_qlat[part], flat(s_q[:, :, :, :, lanes])).astype(BF)
        both = dot(s_qlat[part], flat(s_q[:, :, :, :, 512:768]))
        front, back = both[:, 0:128], both[:, 128:256]
        c, s = cosine[part], sine[part]
        s_query[part, 512:640] = (front * c - back * s).astype(BF)
        s_query[part, 640:768] = (back * c + front * s).astype(BF)
        for j in range(4):
            lanes = pl.ds(j * 256, 256)
            s_keyval[part, lanes] = dot(s_kvlat[part], flat(s_kv[:, :, :, :, lanes])).astype(BF)

    loop(2, query)

    def attend(i):
        part = at_tile(i, 256)
        places = lax.broadcasted_iota(jnp.int32, (256, groups), 0) + i * 256
        keys = lax.broadcasted_iota(jnp.int32, (256, groups), 1)
        allowed = (seg_col[part] == seg_row[...]) & (keys <= places)
        norms = jnp.zeros((256, 128), F32)
        for head in range(4):
            scores = dot(s_query[part, head * 128 : head * 128 + 128], s_keyval[:, head * 256 : head * 256 + 128], "nt")
            scores += dot(head_lanes(s_query[part, 512:640], head), s_rope[:, 0:128], "nt")
            scores += dot(head_lanes(s_query[part, 640:768], head), s_rope[:, 128:256], "nt")
            scores = jnp.where(allowed, scores * (NOPE + ROPE) ** (-0.5), masked_score)
            peak = jnp.max(scores, axis=-1, keepdims=True)
            raised = jnp.exp(scores - peak)
            total = jnp.sum(raised, axis=-1, keepdims=True)
            probs = (raised / total).astype(BF)
            out = dot(probs, s_keyval[:, head * 256 + 128 : head * 256 + 256])
            s_heads[part, head * 128 : head * 128 + 128] = out.astype(BF)
            lanes = lax.broadcasted_iota(jnp.int32, (256, 128), 1)
            norms = jnp.where(lanes == head, peak + jnp.log(total), norms)
        s_norm[part] = norms

    loop(2, attend)
    next(ffn)
    next(grads)
    keeps += [
        wire.keep(a, b)
        for a, b in (
            (s_qlat, o_qhat), (s_kvlat, o_kvhat), (s_query, o_query), (s_keyval, o_keyval), (s_rope, o_rope),
            (s_norm, o_norm), (s_heads, o_heads),
        )
    ]

    def project(i):
        block, z = lax.div(i, 4), lax.rem(i, 4)
        s_attn[block, :, at_tile(z, 512)] = dot(s_heads[at_tile(block, own_rows)], flat(s_out[z]), "nt").astype(BF)

    loop(16, project)
    finish(sum_tp(wire, spot, s_attn, s_sum, t_got, t_held, t_last))

    def residual(i):
        part = at_tile(i, 16)
        values = s_hidden[spot.t, part].astype(F32) + s_sum[part]
        s_resid[part] = values
        scale = lax.rsqrt(jnp.mean(values * values, axis=-1, keepdims=True) + norm_eps)
        normed = values * scale * ffn_gain
        s_sent[part, 0:width] = normed.astype(BF)
        s_sum[part] = normed

    loop(own_rows // 16, residual)
    logits = dot(s_sum[...], gains, "nt", lax.Precision.HIGHEST)
    o_logits[...] = logits
    scores = jax.nn.sigmoid(logits)
    first = jnp.sum(pick_a[...] * scores, axis=-1, keepdims=True)
    second = jnp.sum(pick_b[...] * scores, axis=-1, keepdims=True)
    both = first + second
    dense = pick_a[...] * (route_scale * first / both) + pick_b[...] * (route_scale * second / both)
    s_sent[:, width : width + 128] = jnp.zeros((own_rows, 128), BF)
    s_sent[:, width : width + 16] = (dense + pick_sent[...]).astype(BF)
    o_small[...] = s_small[5]
    keeps.append(wire.keep(s_resid, o_resid))
    finish(together(gather_y(wire, spot, o_tokens, s_sent), grads))
    finish(ffn)
    wait_all(keeps)


def front(downs, q_up, kv_up, out_t, hidden, grad, ffn, small, cosine, sine, seg_col, seg_row, picks):
    rows, width = hidden.shape
    group, columns = 4 * rows, downs.shape[-1]

    def spread(array):
        return (4, 2, 4) + array.shape[-2:]

    down_spread = (4, 2, 4, 64, columns)
    weights = [down_spread, spread(q_up), spread(kv_up), spread(out_t)]
    outs = [(shape, BF, "hbm") for shape in weights]
    outs.append(((2, 2, 2, rows, width), BF, "hbm"))
    outs += [((a.shape[1], 4, 2, 4) + a.shape[2:], BF, "hbm") for a in ffn]
    outs.append(((2, 2, 2, rows, width + 128), BF, "hbm"))
    saved = [
        ((group, width), BF), ((4, group, columns), BF), ((group, 1536), BF),
        ((group, 512), BF), ((group, 768), BF), ((group, 1024), BF), ((group, 256), BF), ((group, 128), F32),
        ((group, 512), BF), ((rows, width), F32),
    ]
    outs += [(shape, dtype, "hbm") for shape, dtype in saved]
    outs += [((rows, 16), F32, "vmem"), (small.shape, small.dtype, "vmem")]
    scratch = [pltpu.VMEM((64, columns), BF)] + [pltpu.VMEM(shape, BF) for shape in weights]
    scratch += [
        pltpu.VMEM((4, rows, width), BF),
        pltpu.VMEM((group, width), BF),
        pltpu.VMEM((group, columns), BF),
        pltpu.VMEM((4, group, columns), BF),
        pltpu.VMEM((group, 1536), BF),
        pltpu.VMEM((group, 512), BF),
        pltpu.VMEM((group, 768), BF),
        pltpu.VMEM((group, 1024), BF),
        pltpu.VMEM((group, 256), BF),
        pltpu.VMEM((group, 128), F32),
        pltpu.VMEM((group, 512), BF),
        pltpu.VMEM((4, rows, width), BF),
        pltpu.VMEM((rows, width), F32),
        pltpu.VMEM((rows, width), F32),
        pltpu.VMEM((rows, width + 128), BF),
        pltpu.VMEM((6,) + small.shape, small.dtype),
        pltpu.VMEM((5, 3) + small.shape, small.dtype),
    ] + tp_sum_scratch(rows, width)
    return call(
        front_kernel, 0, outs, ["hbm"] * 10 + ["vmem"] * 8, scratch, 120, 40,
        (downs, q_up, kv_up, out_t, hidden, grad) + tuple(ffn) + (small, cosine, sine, seg_col, seg_row) + tuple(picks),
        60,
    )


def swiglu_back(gate, up, d_hidden):
    bell = jax.nn.sigmoid(gate)
    silu = gate * bell
    return silu * up, d_hidden * up * bell * (1.0 + gate * (1.0 - bell)), d_hidden * silu


def ffn_kernel(
    tokens, dy, gu, dn, sgu, sdn, o_moe, o_back, o_gu, o_dn, o_sgu, o_sdn,
    s_tok, s_dy, s_in, s_dyr, s_x, s_dg, s_one, s_turned, s_gate, s_gb, s_w, s_g, s_h, s_d1, s_d2, s_ch, s_c1, s_c2,
    s_moe, s_back, load, fetched, stored, done,
):
    capacity, slots, width = s_one.shape[1] // 4, s_one.shape[1], dy.shape[1]
    groups = s_tok.shape[0] // 2
    first = lax.rem(lax.div(lax.axis_index("fsdp"), 4), 2) * 4

    def fetch(planes, slot):
        return [pltpu.make_async_copy(p, s_w.at[slot, k], fetched.at[slot, k]) for k, p in enumerate(planes)]

    def store(planes, slot):
        return [pltpu.make_async_copy(s_g.at[slot, k], p, stored.at[slot, k]) for k, p in enumerate(planes)]

    def start(copies):
        for copy in copies:
            copy.start()

    def routed(e):
        return (gu.at[2 * e], gu.at[2 * e + 1], dn.at[e])

    def routed_sums(e):
        return (o_gu.at[2 * e], o_gu.at[2 * e + 1], o_dn.at[e])

    shared, shared_sums = (sgu.at[0], sgu.at[1], sdn.at[0]), (o_sgu.at[0], o_sgu.at[1], o_sdn.at[0])
    loads = [pltpu.make_async_copy(tokens, s_tok, load.at[0]), pltpu.make_async_copy(dy, s_dy, load.at[1])]
    start(loads)
    start(fetch(routed(0), 0))
    loads[0].wait()

    row, lane = lane_grid(groups, groups)
    before = (row < lane).astype(F32).astype(BF)
    after = (lane < row).astype(F32).astype(BF)
    slot_row, _ = lane_grid(capacity, groups)
    turned_row, turned_lane = lane_grid(groups, slots)
    for g in range(2):
        extra = s_tok[g * groups : (g + 1) * groups, width : width + 128].astype(F32)
        flipped = jnp.swapaxes(extra, 0, 1)
        gates = jnp.where(first == 0, flipped[0:4], flipped[4:8])
        masks = jnp.where(first == 0, flipped[8:12], flipped[12:16])
        padded = jnp.concatenate([masks, jnp.zeros((12, groups), F32)], axis=0)
        place = dot(padded.astype(BF), before)
        place = jnp.where(padded > 0, place, -1.0).astype(jnp.int32)
        for e in range(4):
            taken = place[e : e + 1] == slot_row
            rows = slice(e * capacity, (e + 1) * capacity)
            s_one[g, rows] = taken.astype(F32).astype(BF)
            s_gate[g, rows] = jnp.sum(jnp.where(taken, gates[e : e + 1], 0.0), axis=-1, keepdims=True)
        place = dot(after, extra.astype(BF))
        place = jnp.where(extra > 0, place, -1.0)
        columns = jnp.where(first == 0, place[:, 8:12], place[:, 12:16]).astype(jnp.int32)
        wanted = jnp.full((groups, slots), -2, jnp.int32)
        for e in range(4):
            wanted = jnp.where(lax.div(turned_lane, capacity) == e, columns[:, e : e + 1], wanted)
        s_turned[g] = (wanted == lax.rem(turned_lane, capacity)).astype(F32).astype(BF)
    loads[1].wait()

    def dispatch(i):
        g, lanes = lax.div(i, 4), at_tile(lax.rem(i, 4), 512)
        rows = at_tile(g, groups)
        s_in[g, :, lanes] = dot(s_one[g], s_tok[rows, lanes]).astype(BF)
        s_dyr[g, :, lanes] = dot(s_one[g], s_dy[rows, lanes]).astype(BF)

    loop(8, dispatch)

    def expert(e):
        slot = lax.rem(e, 2)
        mine = pl.ds(pl.multiple_of(e * capacity, 32), capacity)
        wait_all(fetch(routed(e), slot))

        @pl.when(e < 3)
        def _():
            start(fetch(routed(e + 1), 1 - slot))

        @pl.when(e == 3)
        def _():
            start(fetch(shared, 1 - slot))

        @pl.when(e >= 2)
        def _():
            wait_all(store(routed_sums(e - 2), slot))

        def place(i):
            lanes = at_tile(i, 512)
            for g in range(2):
                rows = slice(g * capacity, (g + 1) * capacity)
                s_x[rows, lanes] = s_in[g, mine, lanes]
                s_dg[rows, lanes] = (s_gate[g, mine] * s_dyr[g, mine, lanes].astype(F32)).astype(BF)

        loop(4, place)
        gate, up = dot(s_x[...], s_w[slot, 0]), dot(s_x[...], s_w[slot, 1])
        hidden, d_gate, d_up = swiglu_back(gate, up, dot(s_dg[...], s_w[slot, 2]))
        s_h[...], s_d1[...], s_d2[...] = hidden.astype(BF), d_gate.astype(BF), d_up.astype(BF)

        def sums(i):
            lanes = at_tile(i, 512)
            s_g[slot, 0, lanes] = dot(s_x[:, lanes], s_d1[...], "tn").astype(BF)
            s_g[slot, 1, lanes] = dot(s_x[:, lanes], s_d2[...], "tn").astype(BF)
            s_g[slot, 2, lanes] = dot(s_dg[:, lanes], s_h[...], "tn").astype(BF)

        loop(4, sums)
        start(store(routed_sums(e), slot))
        s_gb[...] = jnp.zeros_like(s_gb)

        def outward(i):
            lanes = at_tile(i, 512)
            out = dot(s_h[...], s_w[slot, 2, lanes], "nt")
            back = dot(s_d1[...], s_w[slot, 0, lanes], "nt") + dot(s_d2[...], s_w[slot, 1, lanes], "nt")
            for g in range(2):
                rows = slice(g * capacity, (g + 1) * capacity)
                s_gb[rows] += jnp.sum(out[rows] * s_dyr[g, mine, lanes].astype(F32), axis=-1, keepdims=True)
                s_dyr[g, mine, lanes] = (s_gate[g, mine] * out[rows]).astype(BF)
                s_in[g, mine, lanes] = back[rows].astype(BF)

        loop(4, outward)
        extra_lane = lax.broadcasted_iota(jnp.int32, (capacity, 128), 1)
        for g in range(2):
            rows = slice(g * capacity, (g + 1) * capacity)
            s_in[g, mine, width : width + 128] = jnp.where(extra_lane == first + e, s_gb[rows], 0.0).astype(BF)

    loop(4, expert)

    wait_all(fetch(shared, 0))
    wait_all(store(routed_sums(2), 0))

    def common(i):
        rows = at_tile(i, 256)
        inputs = s_tok[rows, 0:width]
        gate, up = dot(inputs, s_w[0, 0]), dot(inputs, s_w[0, 1])
        hidden, d_gate, d_up = swiglu_back(gate, up, dot(s_dy[rows], s_w[0, 2]))
        s_ch[rows], s_c1[rows], s_c2[rows] = hidden.astype(BF), d_gate.astype(BF), d_up.astype(BF)

    loop(2 * groups // 256, common)

    def common_sums(i):
        lanes = at_tile(i, 512)
        s_g[0, 0, lanes] = dot(s_tok[:, lanes], s_c1[...], "tn").astype(BF)
        s_g[0, 1, lanes] = dot(s_tok[:, lanes], s_c2[...], "tn").astype(BF)
        s_g[0, 2, lanes] = dot(s_dy[:, lanes], s_ch[...], "tn").astype(BF)

    loop(4, common_sums)
    start(store(shared_sums, 0))

    def combine(i):
        g, lanes = lax.div(i, 4), at_tile(lax.rem(i, 4), 512)
        rows = at_tile(g, groups)
        out = dot(s_ch[rows], s_w[0, 2, lanes], "nt") + dot(s_turned[g], s_dyr[g, :, lanes])
        s_moe[rows, lanes] = out.astype(BF)
        back = dot(s_c1[rows], s_w[0, 0, lanes], "nt") + dot(s_c2[rows], s_w[0, 1, lanes], "nt")
        s_back[rows, lanes] = (back + dot(s_turned[g], s_in[g, :, lanes])).astype(BF)

    loop(8, combine)
    for g in range(2):
        rows = slice(g * groups, (g + 1) * groups)
        s_back[rows, width : width + 128] = dot(s_turned[g], s_in[g, :, width : width + 128]).astype(BF)
    ends = [pltpu.make_async_copy(s_moe, o_moe, done.at[0]), pltpu.make_async_copy(s_back, o_back, done.at[1])]
    start(ends)
    wait_all(store(routed_sums(3), 1))
    wait_all(store(shared_sums, 0))
    wait_all(ends)


def ffn(tokens, dy, gu, dn, sgu, sdn, capacity):
    rows, width = dy.shape
    wide = tokens.shape[1]
    units = gu.shape[-1]
    outs = [(rows, width), (rows, wide)] + [a.shape for a in (gu, dn, sgu, sdn)]
    sizes = [
        ((rows, wide), BF), ((rows, width), BF), ((2, 4 * capacity, wide), BF), ((2, 4 * capacity, width), BF),
        ((2 * capacity, width), BF), ((2 * capacity, width), BF), ((2, 4 * capacity, rows // 2), BF),
        ((2, rows // 2, 4 * capacity), BF), ((2, 4 * capacity, 1), F32), ((2 * capacity, 1), F32),
        ((2, 3, width, units), BF), ((2, 3, width, units), BF),
        ((2 * capacity, units), BF), ((2 * capacity, units), BF), ((2 * capacity, units), BF),
        ((rows, units), BF), ((rows, units), BF), ((rows, units), BF), ((rows, width), BF), ((rows, wide), BF),
    ]
    sems = [(2,), (2, 3), (2, 3), (2,)]
    return pl.pallas_call(
        ffn_kernel,
        out_shape=[jax.ShapeDtypeStruct(shape, BF) for shape in outs],
        in_specs=[pl.BlockSpec(memory_space=pltpu.HBM)] * 6,
        out_specs=[pl.BlockSpec(memory_space=pltpu.HBM)] * 6,
        scratch_shapes=[pltpu.VMEM(*size) for size in sizes] + [pltpu.SemaphoreType.DMA(n) for n in sems],
        compiler_params=pltpu.CompilerParams(vmem_limit_bytes=62 * MIB),
    )(tokens, dy, gu, dn, sgu, sdn)


def back_kernel(
    gu, dn, sgu, sdn, part, attn_in, heads, out_w, up_q, up_kv, downs, query, keyval, rope, norms, qlat, kvlat, raw,
    resid, logits, pick_a, pick_b, grad, gains, cosine, sine, seg_col, seg_row,
    o_gu, o_dn, o_sgu, o_sdn, o_gout, o_gq, o_gkv, o_gdown, o_attn, o_resid, o_small,
    *rest,
):
    landing, rest = list(rest[:20]), rest[20:]
    scratch, (send, recv, here) = list(rest[:-3]), rest[-3:]
    spot, wire = Spot(), Wire(send, recv, here)
    greet(spot.rings() + [spot.along_y(1), spot.along_y(3), spot.core(), spot.far(), spot.diagonal()])
    own_rows, width = grad.shape
    groups = 4 * own_rows

    def take(count):
        taken, scratch[:] = scratch[:count], scratch[count:]
        return taken

    def unit(half, ref, order):
        rings = [take(3) + [landing.pop(0), landing.pop(0)] for _ in range(2)]
        return sum_unit(wire, spot, half, ref, order, rings)

    one = [unit(0, gu.at[pl.ds(0, 4)], "zx"), unit(1, gu.at[pl.ds(4, 4)], "zx")]
    two = [unit(0, dn, "xz"), unit(1, sgu, "xz"), unit(1, sdn, "xz")]

    def weights():
        yield from together(
            sum_stream(wire, spot, "zx", one, True), sum_stream(wire, spot, "xz", two, True)
        )
        moves = []
        places = (
            (one[0][2], o_gu.at[spot.yl, pl.ds(0, 4)]),
            (one[1][2], o_gu.at[spot.yl, pl.ds(4, 4)]),
            (two[0][2], o_dn.at[spot.yl]),
            (two[1][2], o_sgu.at[spot.yl]),
            (two[2][2], o_sdn.at[spot.yl]),
        )
        for total, place in places:
            moves += [wire.copy(total.at[:, 1 - spot.yl], place, spot.pair()), wire.keep(total.at[:, spot.yl], place)]
        yield
        wait_all(moves)

    tokens = take(5)
    (s_back, s_heads, s_wide, s_upq, s_upkv, s_query, s_keyval, s_rope, s_norms, s_qlat, s_kvlat, s_raw) = take(12)
    (s_normed, s_dres, s_dh, s_dhall, s_dheads, s_dq, s_dkv, s_accq, s_acck, s_dkn, s_dv, s_lat) = take(12)
    (s_swap, s_got, s_stage, s_attn, s_small) = take(5)
    t_scratch = take(3)
    s_part = tokens[1]
    sums = sum_y(wire, spot, part, s_back, *tokens)
    next(sums)
    ffn = weights()
    next(ffn)
    loads = [wire.keep(a, b) for a, b in ((heads, s_heads), (out_w, s_wide.at[:, pl.ds(0, 512)]))]
    others = [
        wire.keep(a, b)
        for a, b in (
            (query, s_query), (keyval, s_keyval), (rope, s_rope), (norms, s_norms), (qlat, s_qlat), (kvlat, s_kvlat),
            (up_q, s_upq), (up_kv, s_upkv), (raw.at[:, pl.ds(pl.multiple_of(spot.t * own_rows, 128), own_rows)], s_raw),
        )
    ]
    finish(sums)

    rows_f32 = gains[...].astype(F32)
    ffn_gain = rows_f32[9:10]
    dense = s_back[:, width : width + 16]
    scores = jax.nn.sigmoid(logits[...])
    first = jnp.sum(pick_a[...] * scores, axis=-1, keepdims=True)
    second = jnp.sum(pick_b[...] * scores, axis=-1, keepdims=True)
    both = first + second
    apart = jnp.sum((pick_a[...] - pick_b[...]) * dense, axis=-1, keepdims=True) * route_scale / both
    d_scores = (pick_a[...] * (second / both) - pick_b[...] * (first / both)) * apart
    d_logits = d_scores * scores * (1.0 - scores)
    s_normed[...] = dot(d_logits, rows_f32, "nn", lax.Precision.HIGHEST)
    s_small[0:1] = jnp.zeros((1, width), F32)

    def own_row(i):
        rows = at_tile(i, 16)
        values = resid[rows]
        scale = lax.rsqrt(jnp.mean(values * values, axis=-1, keepdims=True) + norm_eps)
        hat = values * scale
        grad_ffn = s_normed[rows] + s_back[rows, 0:width]
        s_small[0:1] += jnp.sum(grad_ffn * hat, axis=0, keepdims=True)
        weighted = grad_ffn * ffn_gain
        inner = scale * (weighted - hat * jnp.mean(weighted * hat, axis=-1, keepdims=True))
        total = grad[rows].astype(F32) + inner
        s_dres[rows] = total
        s_dh[rows] = total.astype(BF)
        s_normed[rows] = hat * ffn_gain

    loop(own_rows // 16, own_row)
    keeps = [wire.keep(s_dres, o_resid)]
    swap = gather_tp(wire, spot, s_dhall, s_dh)
    next(swap)
    next(swap)
    o_small[...] = dot(d_logits, s_normed[...], "tn", lax.Precision.HIGHEST)
    o_small[9:10] = s_small[0:1]
    finish(swap)

    wait_all(loads)

    def out_grads(i):
        lanes = at_tile(i, 512)
        s_stage[lanes, 0:512] = dot(flat(s_dhall[:, :, lanes]), s_heads[...], "tn").astype(BF)

    loop(4, out_grads)
    staged = wire.keep(s_stage.at[:, pl.ds(0, 512)], o_gout)

    def head_grads(i):
        s_dheads[at_tile(i, own_rows)] = dot(s_dhall[i], s_wide[:, 0:512]).astype(BF)

    loop(4, head_grads)
    wait_all(others)
    late = [wire.keep(attn_in.at[pl.ds(t * own_rows, own_rows)], s_dhall.at[t]) for t in range(4)]
    late.append(wire.keep(downs, s_wide))
    s_accq[...] = jnp.zeros_like(s_accq)
    s_acck[...] = jnp.zeros_like(s_acck)

    for head in range(4):
        nope, value = pl.ds(head * 256, 128), pl.ds(head * 256 + 128, 128)
        at = pl.ds(head * 128, 128)
        s_dkn[...] = jnp.zeros_like(s_dkn)
        s_dv[...] = jnp.zeros_like(s_dv)

        def attend(i, head=head, nope=nope, value=value, at=at):
            tile = at_tile(i, 256)
            places = lax.broadcasted_iota(jnp.int32, (256, groups), 0) + i * 256
            keys = lax.broadcasted_iota(jnp.int32, (256, groups), 1)
            allowed = (seg_col[tile] == seg_row[...]) & (keys <= places)
            front, back = head_lanes(s_query[tile, 512:640], head), head_lanes(s_query[tile, 640:768], head)
            scores = dot(s_query[tile, at], s_keyval[:, nope], "nt")
            scores += dot(front, s_rope[:, 0:128], "nt")
            scores += dot(back, s_rope[:, 128:256], "nt")
            scores = jnp.where(allowed, scores * (NOPE + ROPE) ** (-0.5), masked_score)
            probs = jnp.exp(scores - s_norms[tile, head : head + 1])
            d_head = s_dheads[tile, at]
            s_dv[...] += dot(probs.astype(BF), d_head, "tn")
            d_probs = dot(d_head, s_keyval[:, value], "nt")
            row_dot = jnp.sum(probs * d_probs, axis=-1, keepdims=True)
            d_scores = (probs * (d_probs - row_dot) * (NOPE + ROPE) ** (-0.5)).astype(BF)
            s_dq[tile, at] = dot(d_scores, s_keyval[:, nope]).astype(BF)
            s_accq[tile, 0:128] += head_lanes(dot(d_scores, s_rope[:, 0:128]), head)
            s_accq[tile, 128:256] += head_lanes(dot(d_scores, s_rope[:, 128:256]), head)
            s_dkn[...] += dot(d_scores, s_query[tile, at], "tn")
            s_acck[:, 0:128] += dot(d_scores, front, "tn")
            s_acck[:, 128:256] += dot(d_scores, back, "tn")

        loop(2, attend)
        s_dkv[:, nope] = s_dkn[...].astype(BF)
        s_dkv[:, value] = s_dv[...].astype(BF)
    next(ffn)

    row, lane = lane_grid(128, 128)
    fold_front = ((lane < 32) & (lane == lax.rem(row, 32))).astype(F32)
    fold_back = ((lane >= 32) & (lane < 64) & (lane - 32 == lax.rem(row, 32))).astype(F32)

    def unrotate(i):
        rows = at_tile(i, own_rows)
        c, s = cosine[rows], sine[rows]
        front, back = s_accq[rows, 0:128], s_accq[rows, 128:256]
        s_dq[rows, 512:640] = (front * c + back * s).astype(BF)
        s_dq[rows, 640:768] = (back * c - front * s).astype(BF)
        front, back = s_acck[rows, 0:128], s_acck[rows, 128:256]
        folded = dot(front * c + back * s, fold_front, "nn", lax.Precision.HIGHEST)
        folded += dot(back * c - front * s, fold_back, "nn", lax.Precision.HIGHEST)
        s_part[i, :, 2048:2176] = folded.astype(BF)
        for j in range(3):
            lanes = slice(j * 512, j * 512 + 512)
            s_part[i, :, lanes] = dot(s_dq[rows], s_upq[lanes], "nt").astype(BF)
        s_part[i, :, 1536:2048] = dot(s_dkv[rows], s_upkv[...], "nt").astype(BF)

    loop(4, unrotate)
    latents = sum_tp(wire, spot, s_part, s_lat, *t_scratch)
    next(latents)
    staged.wait()

    def q_grads(i):
        lanes = at_tile(i, 256)
        s_stage[lanes] = dot(s_qlat[:, lanes], s_dq[...], "tn").astype(BF)

    loop(6, q_grads)
    staged = wire.keep(s_stage.at[pl.ds(0, 1536)], o_gq)
    next(latents)

    def kv_grads(i):
        lanes = at_tile(i, 256)
        s_attn[lanes, 0:1024] = dot(s_kvlat[:, lanes], s_dkv[...], "tn").astype(BF)

    loop(2, kv_grads)
    staged_kv = wire.keep(s_attn.at[:, pl.ds(0, 1024)], o_gkv)
    finish(latents)

    gain = rows_f32[10:11]
    s_small[...] = jnp.zeros_like(s_small)

    def latent_row(i):
        rows = at_tile(i, 32)
        for cut, columns, start in ((slice(0, 384), 384, 0), (slice(384, 512), 128, 1536)):
            size = 4.0 * columns
            values = [s_raw[t, rows, cut].astype(F32) for t in range(4)]
            scale = lax.rsqrt(sum(jnp.sum(v * v, axis=-1, keepdims=True) for v in values) / size + norm_eps)
            hats = [v * scale for v in values]
            grads, weighted = [], []
            for t in range(4):
                at = slice(start + t * columns, start + (t + 1) * columns)
                grads.append(s_lat[rows, at])
                weighted.append(grads[t] * gain[:, at])
                s_small[0:1, at] += jnp.sum(grads[t] * hats[t], axis=0, keepdims=True)
            inner = sum(jnp.sum(w * h, axis=-1, keepdims=True) for w, h in zip(weighted, hats)) / size
            for t in range(4):
                s_swap[t, rows, cut] = (scale * (weighted[t] - hats[t] * inner)).astype(BF)
        folded = s_lat[rows, 2048:2176].astype(BF)
        for t in range(4):
            pick = ((row == t * 16 + lane) & (lane < 16)).astype(F32).astype(BF)
            s_swap[t, rows, 512:640] = dot(folded, pick).astype(BF)

    loop(own_rows // 32, latent_row)
    moves = [wire.keep(s_swap.at[spot.t], s_got.at[spot.t])]
    for yh, c, device in (
        (spot.yh, 1 - spot.c, spot.core()),
        (1 - spot.yh, spot.c, spot.far()),
        (1 - spot.yh, 1 - spot.c, spot.diagonal()),
    ):
        moves.append(wire.copy(s_swap.at[yh * 2 + c], s_got.at[spot.t], device))
    o_small[10:11] = s_small[0:1]
    s_small[0:1] = jnp.zeros((1, width), F32)
    wait_all(moves)
    wait_all(late)
    staged.wait()
    staged_kv.wait()
    next(ffn)

    def down_grads(i):
        lanes = at_tile(i, 512)
        s_stage[lanes, 0:640] = dot(flat(s_dhall[:, :, lanes]), flat(s_got[...]), "tn").astype(BF)

    loop(4, down_grads)
    staged = wire.keep(s_stage.at[:, pl.ds(0, 640)], o_gdown)

    def attn_grads(i):
        rows, lanes = lax.div(i, 4), at_tile(lax.rem(i, 4), 512)
        back = dot(s_got[rows], s_wide[lanes], "nt")
        s_attn[at_tile(rows, own_rows), lanes] = back.astype(BF)
        s_small[0:1, lanes] += jnp.sum(back * s_dhall[rows, :, lanes].astype(F32), axis=0, keepdims=True)

    loop(16, attn_grads)
    o_small[8:9] = s_small[0:1] / rows_f32[8:9]
    keeps.append(wire.keep(s_attn, o_attn))
    finish(ffn)
    staged.wait()
    wait_all(keeps)


def back(ffn_grads, part, saved, resid, logits, picks, grad, gains, cosine, sine, seg_col, seg_row):
    rows, width = grad.shape
    group = 4 * rows
    outs = [((2, a.shape[0]) + a.shape[4:], BF, "hbm") for a in ffn_grads]
    outs += [((2048, 512), BF, "hbm"), ((1536, 768), BF, "hbm"), ((512, 1024), BF, "hbm"), ((2048, 640), BF, "hbm")]
    outs += [((group, width), BF, "hbm"), ((rows, width), F32, "hbm"), ((16, width), F32, "vmem")]
    scratch = []
    tile = ffn_grads[0].shape[4:]
    for planes, order in ((4, "zx"), (4, "zx"), (4, "xz"), (2, "xz"), (1, "xz")):
        first = (planes, 2, 4) + tile if order == "zx" else (planes, 4, 2) + tile
        second = (planes, 2) + tile
        outs += [(first, BF, "hbm")] * 2 + [(second, BF, "hbm")] * 2
        scratch += [pltpu.VMEM(first, BF)] * 3 + [pltpu.VMEM(second, BF)] * 3
    columns = part.shape[-1]
    scratch += [pltpu.VMEM((4, rows, columns), BF)] * 2 + [pltpu.VMEM((rows, columns), BF)] * 3
    sizes = [
        ((rows, columns), F32), ((group, 512), BF), ((width, 640), BF), ((1536, 768), BF), ((512, 1024), BF),
        ((group, 768), BF), ((group, 1024), BF), ((group, 256), BF), ((group, 128), F32), ((group, 1536), BF),
        ((group, 512), BF), ((4, rows, 640), BF),
        ((rows, width), F32), ((rows, width), F32), ((rows, width), BF), ((4, rows, width), BF), ((group, 512), BF),
        ((group, 768), BF), ((group, 1024), BF), ((group, 256), F32), ((group, 256), F32), ((group, 128), F32),
        ((group, 128), F32), ((rows, columns), F32),
        ((4, rows, 640), BF), ((4, rows, 640), BF), ((width, 768), BF), ((group, width), BF), ((8, width), F32),
    ]
    scratch += [pltpu.VMEM(*size) for size in sizes] + tp_sum_scratch(rows, columns)
    return call(
        back_kernel, 1, outs, ["hbm"] * 18 + ["vmem"] * 10, scratch, 100, 90,
        tuple(ffn_grads) + (part,) + tuple(saved) + (resid, logits) + tuple(picks)
        + (grad, gains, cosine, sine, seg_col, seg_row),
        62,
    )[:11]


def last_kernel(downs, q_up, kv_up, out_t, part, moe, small, o_downs, o_q, o_kv, o_out, o_part, o_moe, o_small, *rest):
    scratch, (send, recv, here) = list(rest[:-3]), rest[-3:]
    spot, wire = Spot(), Wire(send, recv, here)
    greet(
        spot.rings()
        + [spot.along_x(2), spot.along_z(2), spot.along_y(1), spot.along_y(3)]
        + [spot.core(), spot.far(), spot.diagonal()]
    )

    def take(count):
        taken, scratch[:] = scratch[:count], scratch[count:]
        return taken

    def unit(half, ref, order):
        return sum_unit(wire, spot, half, ref, order, (take(5), take(5)))

    one = [unit(0, q_up, "zx"), unit(1, out_t, "zx")]
    two = [unit(0, downs, "xz"), unit(1, kv_up, "xz")]
    (got_q, got_out, got_downs, got_kv, rows), tokens, ring = take(5), take(3), take(5)
    s_small, s_buf = take(2)
    s_small[0] = small[...]

    def weights():
        yield from together(sum_stream(wire, spot, "zx", one), sum_stream(wire, spot, "xz", two))
        finals = (
            (two[0][2], got_downs, rows),
            (one[0][2], got_q, o_q),
            (one[1][2], got_out, o_out),
            (two[1][2], got_kv, o_kv),
        )
        moves = [wire.copy(total.at[:, 1 - spot.yl], got, spot.pair()) for total, got, _ in finals]
        yield
        swaps = []
        for made, (total, got, out) in zip(moves, finals):
            made.wait()
            add_into(out, total.at[0, spot.yl], got.at[0])
            if not swaps:
                cut = lambda t: rows.at[pl.ds(pl.multiple_of(t * 16, 16), 16)]
                swaps.append(wire.keep(cut(spot.t), o_downs.at[spot.t]))
                for yh, c, device in (
                    (spot.yh, 1 - spot.c, spot.core()),
                    (1 - spot.yh, spot.c, spot.far()),
                    (1 - spot.yh, 1 - spot.c, spot.diagonal()),
                ):
                    swaps.append(wire.copy(cut(yh * 2 + c), o_downs.at[spot.t], device))
        yield
        wait_all(swaps)

    finish(
        together(
            weights(),
            sum_tp(wire, spot, part, o_part, *tokens),
            all_sum_small(wire, spot, s_buf, s_small),
            sum_y(wire, spot, moe, o_moe, *ring),
        )
    )
    o_small[...] = s_small[5]


def last(downs, q_up, kv_up, out_t, part, moe, small):
    scratch, ends = [], []
    for a, order in ((q_up, "zx"), (out_t, "zx"), (downs, "xz"), (kv_up, "xz")):
        scratch += unit_scratch(1, order, *a.shape[-2:])
        ends.append(pltpu.VMEM((1,) + a.shape[-2:], BF))
    rows, columns = part.shape[1:]
    scratch += ends + [pltpu.VMEM(downs.shape[-2:], BF)] + tp_sum_scratch(rows, columns)
    scratch += [pltpu.VMEM((4, rows, columns), BF)] * 2 + [pltpu.VMEM((rows, columns), BF)] * 3
    scratch += [pltpu.VMEM((6,) + small.shape, F32), pltpu.VMEM((5, 3) + small.shape, F32)]
    outs = [((4, 16, downs.shape[-1]), BF, "hbm")]
    outs += [(a.shape[-2:], F32, "vmem") for a in (q_up, kv_up, out_t)]
    outs += [((rows, columns), F32, "vmem")] * 2 + [(small.shape, F32, "vmem")]
    return call(
        last_kernel, 2, outs, ["hbm"] * 4 + ["vmem", "hbm", "vmem"], scratch, 64, 32,
        (downs, q_up, kv_up, out_t, part, moe, small), 50,
    )


def rotary_tables(position):
    half_size = ROPE // 2
    inverse = theta_base ** (-(2.0 * jnp.arange(half_size, dtype=F32)) / ROPE)
    angles = position.astype(F32)[:, None] * inverse[None, :]
    return (jnp.cos(angles), jnp.sin(angles))


def packing(lengths, total_rows):
    positions = jnp.arange(total_rows, dtype=jnp.int32)
    endings = jnp.cumsum(lengths)
    segment = jnp.sum((positions[:, None] >= endings[None, :]).astype(jnp.int32), axis=1)
    starting = endings - lengths
    owner_mask = segment[:, None] == jnp.arange(lengths.shape[0], dtype=jnp.int32)[None, :]
    first_row = jnp.sum(jnp.where(owner_mask, starting[None, :], 0), axis=1)
    return (segment, positions - first_row)


def normalized(values):
    scale = lax.rsqrt(jnp.mean(values * values, axis=-1, keepdims=True) + norm_eps)
    return values * scale, scale


def norm_back(grad, gain, hat, scale):
    weighted = grad * gain
    return scale * (weighted - hat * jnp.mean(weighted * hat, axis=-1, keepdims=True))


def per_device(
    hidden_in,
    out_grad,
    attn_gain,
    q_down,
    q_gain,
    kv_down,
    kv_gain,
    q_up,
    kv_up,
    out_proj,
    ffn_gain,
    router,
    routed_gate_up,
    routed_down,
    shared_gate_up,
    shared_down,
    choices,
    seq_lens,
):
    local_rows, width = hidden_in.shape
    group_rows = choices.shape[0]
    tp_count = lax.axis_size("tp")
    tp_index = lax.axis_index("tp")
    y_lo = lax.rem(lax.div(lax.axis_index("fsdp"), 4), 2)
    head_count = HEADS // tp_count
    experts = router.shape[1]
    held = experts // 2
    capacity = 5 * group_rows * TOPK // (4 * experts)
    units = routed_gate_up.shape[3]
    row_shard = routed_gate_up.shape[1]
    q_cols = q_down.shape[1] // tp_count
    raw_cols = q_cols + kv_down.shape[1] // tp_count
    raw_pad = -raw_cols % 128
    small_at = raw_cols + raw_pad

    def own(array):
        return lax.dynamic_slice_in_dim(array, tp_index * local_rows, local_rows)

    down_rows = q_down.shape[0]
    devices = width // down_rows
    device = lax.axis_index("fsdp") * tp_count + tp_index
    rope_cols = ROPE // tp_count
    columns = jnp.concatenate(
        [
            q_down.reshape(down_rows, tp_count, q_cols),
            kv_down[:, :KVR].reshape(down_rows, tp_count, KVR // tp_count),
            kv_down[:, KVR:].reshape(down_rows, tp_count, rope_cols),
        ],
        axis=-1,
    ).transpose(1, 0, 2)
    downs = jnp.pad(columns, ((0, 0), (0, 0), (0, raw_pad)))
    half = ROPE // 2
    q_rows = q_up.reshape(-1, head_count, NOPE + ROPE)
    q_sent = jnp.concatenate(
        [
            q_rows[..., :NOPE].reshape(-1, head_count * NOPE),
            q_rows[..., NOPE : NOPE + half].reshape(-1, head_count * half),
            q_rows[..., NOPE + half :].reshape(-1, head_count * half),
        ],
        axis=1,
    )
    small = jnp.zeros((16, width), BF)
    vectors = jnp.concatenate([router.T, attn_gain[None], ffn_gain[None]], axis=0)
    small = lax.dynamic_update_slice(small, vectors, (0, device * down_rows))
    small = lax.dynamic_update_slice(small, q_gain[None], (experts + 2, device * q_gain.shape[0]))
    kv_at = q_down.shape[1] + device * kv_gain.shape[0]
    small = lax.dynamic_update_slice(small, kv_gain[None], (experts + 2, kv_at))
    send_gu = routed_gate_up.transpose(0, 2, 1, 3).reshape(2, held * 2, row_shard, units)
    send_dn = routed_down.transpose(0, 2, 1).reshape(2, held, row_shard, units)
    send_sgu = shared_gate_up.reshape(row_shard, 2, 2, units).transpose(2, 1, 0, 3)
    send_sdn = shared_down.T.reshape(row_shard, 2, units).transpose(1, 0, 2)[:, None]

    segment, position = packing(seq_lens[0], group_rows)
    cosine, sine_table = rotary_tables(position)
    cos_heads, sin_heads = jnp.tile(cosine, (1, head_count)), jnp.tile(sine_table, (1, head_count))
    picked = own(choices)
    lanes = jnp.arange(2 * experts, dtype=jnp.int32)
    pick_a, pick_b = ((picked[:, k : k + 1] == lanes[None]).astype(F32) for k in range(TOPK))
    pick_sent = sum((picked[:, k : k + 1] + experts == lanes[None]).astype(F32) for k in range(TOPK))

    (
        all_downs, all_q, all_kv, all_out, all_grad, wide_gu, wide_dn, wide_sgu, wide_sdn, tokens,
        attn_in, raw, group_query, group_keyval, query, keyval, rope, norms, heads_out, residual, logits,
        gains,
    ) = front(
        downs, q_sent, kv_up, out_proj.T, hidden_in, out_grad, (send_gu, send_dn, send_sgu, send_sdn), small,
        cos_heads, sin_heads, segment[:, None], segment[None, :], (pick_a, pick_b, pick_sent),
    )
    down_weight = all_downs.reshape(width, -1)
    up_query = all_q.reshape(-1, q_up.shape[1])
    up_keyval = all_kv.reshape(-1, kv_up.shape[1])
    out_weight = all_out.reshape(width, -1)
    planes = [a.reshape(a.shape[0], width, units) for a in (wide_gu, wide_dn, wide_sgu, wide_sdn)]
    moe_part, back_part, sum_gu, sum_dn, sum_sgu, sum_sdn = ffn(
        tokens.reshape(2 * group_rows, -1), all_grad.reshape(2 * group_rows, width), *planes, capacity
    )

    ring = (2, 2, 2, local_rows)
    blocks = (4, 2, 4, row_shard, units)
    own_gu, own_dn, own_sgu, own_sdn, grad_out, grad_q, grad_kv, grad_down, attn_back, grad_resid, small_grads = back(
        (
            sum_gu.reshape((held * 2,) + blocks),
            sum_dn.reshape((held,) + blocks),
            sum_sgu.reshape((2,) + blocks),
            sum_sdn.reshape((1,) + blocks),
        ),
        back_part.reshape(ring + (width + 128,)),
        (
            attn_in, heads_out, out_weight, up_query, up_keyval, down_weight, query, keyval, rope, norms, group_query,
            group_keyval, raw,
        ),
        residual, logits, (pick_a, pick_b), out_grad, gains, cos_heads, sin_heads, segment[:, None], segment[None, :],
    )

    def spread(array, like):
        return array.reshape((1, 4, 2, 4) + like.shape[-2:])

    got_downs, sum_up_query, sum_up_keyval, sum_out, attn_back_own, moe_own, small_sum = last(
        spread(grad_down, jnp.zeros((row_shard, grad_down.shape[1]))),
        spread(grad_q, q_up),
        spread(grad_kv, kv_up),
        spread(grad_out, out_proj.T),
        attn_back.reshape(tp_count, local_rows, width),
        moe_part.reshape(ring + (width,)),
        small_grads,
    )
    layer_out = (residual + moe_own).astype(BF)
    own_hat, own_scale = normalized(hidden_in.astype(F32))
    input_grad = grad_resid + norm_back(attn_back_own, gains[experts].astype(F32), own_hat, own_scale)
    got_downs = got_downs.astype(F32)
    sum_qdown = got_downs[..., :q_cols].transpose(1, 0, 2).reshape(down_rows, -1)
    kv_at = q_cols + KVR // tp_count
    sum_kvdown = jnp.concatenate(
        [
            got_downs[..., q_cols:kv_at].transpose(1, 0, 2).reshape(down_rows, -1),
            got_downs[..., kv_at:raw_cols].transpose(1, 0, 2).reshape(down_rows, -1),
        ],
        axis=-1,
    )
    nope_cols, half_cols = head_count * NOPE, head_count * half
    sum_up_query = jnp.concatenate(
        [
            sum_up_query[:, :nope_cols].reshape(-1, head_count, NOPE),
            sum_up_query[:, nope_cols : nope_cols + half_cols].reshape(-1, head_count, half),
            sum_up_query[:, nope_cols + half_cols :].reshape(-1, head_count, half),
        ],
        axis=-1,
    ).reshape(q_up.shape)

    def mine(row, at, count):
        return lax.dynamic_slice(small_sum, (row, at), (1, count))[0]

    rows_at = device * down_rows
    sum_router = lax.dynamic_slice(small_sum, (0, rows_at), (experts, down_rows)).T
    sum_wide_gu = own_gu.reshape(experts, 2, row_shard, units).transpose(0, 2, 1, 3).astype(F32)
    sum_wide_down = own_dn.reshape(experts, row_shard, units).transpose(0, 2, 1).astype(F32)
    sum_common_gu = own_sgu.transpose(2, 1, 0, 3).reshape(row_shard, 2, 2 * units).astype(F32)
    sum_common_down = own_sdn[:, 0].transpose(1, 0, 2).reshape(row_shard, 2 * units).T.astype(F32)
    q_rank = q_down.shape[1]
    return (
        layer_out,
        input_grad.astype(BF),
        mine(experts, rows_at, down_rows),
        sum_qdown,
        mine(experts + 2, device * q_gain.shape[0], q_gain.shape[0]),
        sum_kvdown,
        mine(experts + 2, q_rank + device * kv_gain.shape[0], kv_gain.shape[0]),
        sum_up_query,
        sum_up_keyval,
        sum_out.T,
        mine(experts + 1, rows_at, down_rows),
        sum_router,
        sum_wide_gu,
        sum_wide_down,
        sum_common_gu,
        sum_common_down,
    )


def solution(mesh):
    return jax.shard_map(
        per_device,
        mesh=mesh,
        in_specs=(
            P(("fsdp", "tp"), None),
            P(("fsdp", "tp"), None),
            P(("fsdp", "tp")),
            P(("fsdp", "tp"), None),
            P(("fsdp", "tp")),
            P(("fsdp", "tp"), None),
            P(("fsdp", "tp")),
            P("fsdp", "tp"),
            P("fsdp", "tp"),
            P("tp", "fsdp"),
            P(("fsdp", "tp")),
            P(("fsdp", "tp"), None),
            P(None, "fsdp", None, "tp"),
            P(None, "tp", "fsdp"),
            P("fsdp", None, "tp"),
            P("tp", "fsdp"),
            P("fsdp", None),
            P("fsdp", None),
        ),
        out_specs=(
            P(("fsdp", "tp"), None),
            P(("fsdp", "tp"), None),
            P(("fsdp", "tp")),
            P(("fsdp", "tp"), None),
            P(("fsdp", "tp")),
            P(("fsdp", "tp"), None),
            P(("fsdp", "tp")),
            P("fsdp", "tp"),
            P("fsdp", "tp"),
            P("tp", "fsdp"),
            P(("fsdp", "tp")),
            P(("fsdp", "tp"), None),
            P(None, "fsdp", None, "tp"),
            P(None, "tp", "fsdp"),
            P("fsdp", None, "tp"),
            P("tp", "fsdp"),
        ),
        check_vma=False,
    )
```

```python
import functools

import jax
import jax.numpy as jnp
from jax import lax
from jax.experimental import pallas as pl
from jax.experimental.pallas import tpu as pltpu
from jax.sharding import PartitionSpec as P

HEADS = 16
NOPE = 128
ROPE = 64
VDIM = 128
KVR = 512
TOPK = 2

theta_base = 50000.0
norm_eps = 1e-06
route_scale = 2.446
masked_score = -1e30

MESH = pl.DeviceIdType.MESH
BF = jnp.bfloat16
F32 = jnp.float32
MIB = 1 << 20


class Spot:
    def __init__(self):
        f, t = lax.axis_index("fsdp"), lax.axis_index("tp")
        self.t = t
        self.z, self.yl, self.x = lax.div(f, 8), lax.rem(lax.div(f, 4), 2), lax.rem(f, 4)
        self.yh, self.c = lax.div(t, 2), lax.rem(t, 2)
        self.y = self.yh * 2 + self.yl

    def at(self, z=None, yl=None, x=None, yh=None, c=None):
        z = self.z if z is None else z
        yl = self.yl if yl is None else yl
        x = self.x if x is None else x
        yh = self.yh if yh is None else yh
        c = self.c if c is None else c
        return ((z * 2 + yl) * 4 + x, yh * 2 + c)

    def along_x(self, by):
        return self.at(x=lax.rem(self.x + by, 4))

    def along_z(self, by):
        return self.at(z=lax.rem(self.z + by, 4))

    def along_y(self, by):
        y = lax.rem(self.y + by, 4)
        return self.at(yl=lax.rem(y, 2), yh=lax.div(y, 2))

    def pair(self):
        return self.at(yl=1 - self.yl)

    def core(self):
        return self.at(c=1 - self.c)

    def far(self):
        return self.at(yh=1 - self.yh)

    def diagonal(self):
        return self.at(yh=1 - self.yh, c=1 - self.c)

    def rings(self):
        return [self.along_x(1), self.along_x(3), self.along_z(1), self.along_z(3)]


def greet(devices):
    barrier = pltpu.get_barrier_semaphore()
    for device in devices:
        pl.semaphore_signal(barrier, inc=1, device_id=device, device_id_type=MESH)
    pl.semaphore_wait(barrier, len(devices))


class Wire:
    def __init__(self, send, recv, here):
        self.send, self.recv, self.here = send, recv, here
        self.sent = self.kept = 0

    def copy(self, source, target, device):
        made = pltpu.make_async_remote_copy(
            src_ref=source,
            dst_ref=target,
            send_sem=self.send.at[self.sent],
            recv_sem=self.recv.at[self.sent],
            device_id=device,
            device_id_type=MESH,
        )
        self.sent += 1
        made.start()
        return made

    def keep(self, source, target):
        made = pltpu.make_async_copy(source, target, self.here.at[self.kept])
        self.kept += 1
        made.start()
        return made


def wait_all(copies):
    for made in copies:
        made.wait()


def together(*parts):
    left = list(parts)
    while left:
        for part in list(left):
            if next(part, "over") == "over":
                left.remove(part)
        yield


def finish(part):
    for _ in part:
        pass


def add_into(target, *terms):
    lead, (rows, columns) = target.shape[:-2], target.shape[-2:]
    step = rows if rows * columns <= 49152 else 16
    pieces = rows // step
    count = pieces
    for size in lead:
        count *= size

    def body(i, carry):
        at = [pl.ds(pl.multiple_of(lax.rem(i, pieces) * step, 16), step)]
        i = lax.div(i, pieces)
        for size in reversed(lead):
            at.insert(0, lax.rem(i, size))
            i = lax.div(i, size)
        at = tuple(at)
        total = terms[0][at].astype(F32)
        for term in terms[1:]:
            total = total + term[at].astype(F32)
        target[at] = total.astype(target.dtype)
        return carry

    lax.fori_loop(0, count, body, 0)


def gather_ring(wire, pos, plus, minus, units):
    prev, following = lax.rem(pos + 3, 4), lax.rem(pos + 1, 4)
    mine = [unit[2] if len(unit) > 2 else unit[0](pos) for unit in units]
    right = [wire.copy(own, unit[0](pos), plus) for own, unit in zip(mine, units)]
    left = [wire.copy(own, unit[0](pos), minus) for own, unit in zip(mine, units)]
    yield
    wait_all(right)
    onward = [wire.copy(unit[0](prev), unit[0](prev), plus) for unit in units if unit[1] == 0]
    wait_all(left)
    onward += [wire.copy(unit[0](following), unit[0](following), minus) for unit in units if unit[1] == 1]
    yield
    wait_all(onward)


def sum_ring(wire, pos, plus, minus, units, staged=False):
    prev, following, across = lax.rem(pos + 3, 4), lax.rem(pos + 1, 4), lax.rem(pos + 2, 4)
    first, direct, last = [], [], []
    for half, view, between, own, through, from_left, from_right, loads in units:
        first.append(wire.copy(view(across), through, plus if half == 0 else minus))
    for half, view, between, own, through, from_left, from_right, loads in units:
        if half == 0:
            direct.append(wire.copy(view(prev), from_right, minus))
        else:
            direct.append(wire.copy(view(following), from_left, plus))
    yield
    for made, (half, view, between, own, through, from_left, from_right, loads) in zip(first, units):
        wait_all(loads)
        made.wait()
        add_into(between, between, through)
        if half == 0:
            last.append(wire.copy(between, from_left, plus))
        else:
            last.append(wire.copy(between, from_right, minus))
    yield
    for one, two, (half, view, between, own, through, from_left, from_right, loads) in zip(direct, last, units):
        one.wait()
        two.wait()
        if staged:
            wait_all([wire.keep(from_left, through), wire.keep(from_right, between)])
            add_into(own, own, through, between)
        else:
            add_into(own, own, from_left, from_right)


def gather_tp(wire, spot, out, source):
    across = wire.copy(source, out.at[spot.t], spot.far())
    own = wire.keep(source, out.at[spot.t])
    other = wire.copy(source, out.at[spot.t], spot.core())
    yield
    across.wait()
    there = (1 - spot.yh) * 2 + spot.c
    last = wire.copy(out.at[there], out.at[there], spot.core())
    yield
    own.wait()
    other.wait()
    last.wait()


def gather_y(wire, spot, out, source):
    def view(rows):
        return lambda y: out.at[lax.rem(y, 2), lax.div(y, 2), spot.c, rows]

    rows = source.shape[0] // 2
    own = wire.keep(source, out.at[spot.yl, spot.yh, spot.c])
    other = [own, wire.copy(source, out.at[spot.yl, spot.yh, spot.c], spot.core())]
    cuts = (pl.ds(0, rows), pl.ds(rows, rows))
    units = [(view(cut), half, source.at[cut]) for half, cut in enumerate(cuts)]
    yield from gather_ring(wire, spot.y, spot.along_y(1), spot.along_y(3), units)
    for by in (1, 2, 3):
        y = lax.rem(spot.y + by, 4)
        part = out.at[lax.rem(y, 2), lax.div(y, 2), spot.c]
        other.append(wire.copy(part, part, spot.core()))
    yield
    wait_all(other)


def sum_tp(wire, spot, source, out, got, held, last):
    cores = [wire.copy(source.at[yh * 2 + 1 - spot.c], got.at[yh], spot.core()) for yh in (0, 1)]
    yield
    wait_all(cores)
    there = 1 - spot.yh
    add_into(held, source.at[there * 2 + spot.c], got.at[there])
    across = wire.copy(held, last, spot.far())
    yield
    across.wait()
    add_into(out, source.at[spot.t], got.at[spot.yh], last)


def sum_y(wire, spot, source, out, got, held, through, from_left, from_right):
    cores = [wire.copy(source.at[y % 2, y // 2, 1 - spot.c], got.at[y], spot.core()) for y in range(4)]
    loads = [wire.keep(source.at[y % 2, y // 2, spot.c], held.at[y]) for y in range(4)]
    yield
    for y, made in enumerate(cores):
        made.wait()
        loads[y].wait()
        add_into(held.at[y], held.at[y], got.at[y])
    rows = out.shape[0] // 2
    following, prev = lax.rem(spot.y + 1, 4), lax.rem(spot.y + 3, 4)
    units = []
    for half in (0, 1):
        part = pl.ds(half * rows, rows)
        units.append(
            (
                half,
                lambda y, part=part: held.at[y, part],
                held.at[following if half == 0 else prev, part],
                held.at[spot.y, part],
                through.at[part],
                from_left.at[part],
                from_right.at[part],
                [],
            )
        )
    yield from sum_ring(wire, spot.y, spot.along_y(1), spot.along_y(3), units)
    add_into(out, held.at[spot.y])


def sum_unit(wire, spot, half, part, order, scratch):
    following, prev = (lambda p: lax.rem(p + 1, 4)), (lambda p: lax.rem(p + 3, 4))
    (between, own, through, from_left, from_right), (between2, own2, through2, from_left2, from_right2) = scratch
    near = following if half == 0 else prev
    if order == "zx":
        view, pos, pos2 = (lambda i: part.at[:, i]), spot.z, spot.x
        view2 = lambda i: own.at[:, :, i]
    else:
        view, pos, pos2 = (lambda i: part.at[:, :, :, i]), spot.x, spot.z
        view2 = lambda i: own.at[:, i]

    def loads():
        return [wire.keep(view(near(pos)), between), wire.keep(view(pos), own)]

    def loads2():
        return [wire.keep(view2(near(pos2)), between2), wire.keep(view2(pos2), own2)]

    one = lambda: (half, view, between, own, through, from_left, from_right, loads())
    two = lambda: (half, view2, between2, own2, through2, from_left2, from_right2, loads2())
    return one, two, own2


def sum_stream(wire, spot, order, units, staged=False):
    x = (spot.x, spot.along_x(1), spot.along_x(3))
    z = (spot.z, spot.along_z(1), spot.along_z(3))
    axes = (z, x) if order == "zx" else (x, z)
    yield from sum_ring(wire, *axes[0], [one() for one, _, _ in units], staged)
    yield from sum_ring(wire, *axes[1], [two() for _, two, _ in units], staged)


def unit_scratch(planes, order, rows, columns):
    first = (planes, 2, 4, rows, columns) if order == "zx" else (planes, 4, 2, rows, columns)
    second = (planes, 2, rows, columns)
    return [pltpu.VMEM(first, BF)] * 5 + [pltpu.VMEM(second, BF)] * 5


def call(kernel, number, outs, ins, scratch, copies, keeps, operands, vmem):
    space = {"hbm": pltpu.HBM, "vmem": pltpu.VMEM}
    return pl.pallas_call(
        kernel,
        out_shape=[jax.ShapeDtypeStruct(shape, dtype) for shape, dtype, _ in outs],
        in_specs=[pl.BlockSpec(memory_space=space[kind]) for kind in ins],
        out_specs=[pl.BlockSpec(memory_space=space[kind]) for _, _, kind in outs],
        scratch_shapes=list(scratch)
        + [
            pltpu.SemaphoreType.DMA((max(copies, 1),)),
            pltpu.SemaphoreType.DMA((max(copies, 1),)),
            pltpu.SemaphoreType.DMA((max(keeps, 1),)),
        ],
        compiler_params=pltpu.CompilerParams(
            collective_id=number, has_side_effects=True, vmem_limit_bytes=vmem * MIB
        ),
    )(*operands)


def tp_sum_scratch(rows, columns):
    return [pltpu.VMEM((2, rows, columns), BF), pltpu.VMEM((rows, columns), BF), pltpu.VMEM((rows, columns), BF)]


def dot(a, b, dims="nn", precision=None):
    left, right = {"nn": (1, 0), "nt": (1, 1), "tn": (0, 0)}[dims]
    return lax.dot_general(
        a, b, (((left,), (right,)), ((), ())), precision=precision, preferred_element_type=F32
    )


def loop(count, body):
    def step(i, carry):
        body(i)
        return carry

    lax.fori_loop(0, count, step, 0)


def at_tile(i, size):
    return pl.ds(pl.multiple_of(i * size, size), size)


def flat(block):
    return block.reshape(-1, block.shape[-1])


def lane_grid(rows, columns):
    return (
        lax.broadcasted_iota(jnp.int32, (rows, columns), 0),
        lax.broadcasted_iota(jnp.int32, (rows, columns), 1),
    )


def head_lanes(values, head):
    lanes = lax.broadcasted_iota(jnp.int32, (1, values.shape[1]), 1)
    return values * (lax.div(lanes, 32) == head).astype(F32).astype(values.dtype)


def all_sum_small(wire, spot, buffers, own):
    steps = (
        [spot.core()],
        [spot.far()],
        [spot.pair()],
        [spot.along_x(1), spot.along_x(2), spot.along_x(3)],
        [spot.along_z(1), spot.along_z(2), spot.along_z(3)],
    )
    for step, devices in enumerate(steps):
        moves = [wire.copy(own.at[step], buffers.at[step, i], device) for i, device in enumerate(devices)]
        yield
        wait_all(moves)
        total = own[step]
        for i in range(len(devices)):
            total = total + buffers[step, i]
        own[step + 1] = total


def ring_pair(wire, spot, first, second):
    x = (spot.x, spot.along_x(1), spot.along_x(3))
    z = (spot.z, spot.along_z(1), spot.along_z(3))

    def unit(part, place):
        ref, half, planes, rows = part[:4]
        lead = () if planes is None else (planes,)
        return (lambda i: ref.at[lead + place(i) + (rows,)], half) + tuple(part[4:])

    def stream(parts, one, place_one, two, place_two):
        yield from gather_ring(wire, *one, [unit(part, place_one) for part in parts])
        yield from gather_ring(wire, *two, [unit(part[:4], place_two) for part in parts])

    every = slice(None)
    yield from together(
        stream(first, x, lambda i: (spot.z, every, i), z, lambda i: (i, every, every)),
        stream(second, z, lambda i: (i, every, spot.x), x, lambda i: (every, every, i)),
    )


def front_kernel(
    downs, q_up, kv_up, out_t, hidden, grad, early, late, small, cosine, sine, seg_col, seg_row, pick_a, pick_b,
    pick_sent,
    o_downs, o_q, o_kv, o_out, o_grad, o_early, o_late, o_tokens,
    o_hat, o_raw, o_qhat, o_kvhat, o_query, o_keyval, o_rope, o_norm, o_heads, o_resid, o_logits, o_small,
    rows, s_downs, s_q, s_kv, s_out, s_hidden, s_hat, s_part, s_raw, s_qlat, s_kvlat, s_query, s_keyval, s_rope,
    s_norm, s_heads, s_attn, s_sum, s_resid, s_sent, s_small, s_buf, t_got, t_held, t_last,
    send, recv, here,
):
    spot, wire = Spot(), Wire(send, recv, here)
    greet(
        spot.rings()
        + [spot.along_x(2), spot.along_z(2), spot.along_y(1), spot.along_y(3)]
        + [spot.core(), spot.far(), spot.diagonal()]
    )
    groups, width = 4 * hidden.shape[0], hidden.shape[1]
    own_rows = hidden.shape[0]
    low, high, every = pl.ds(0, 32), pl.ds(32, 32), slice(None)

    def down_stream():
        mine = rows.at[pl.ds(pl.multiple_of(spot.t * 16, 16), 16)]
        swaps = [wire.keep(downs.at[spot.t], mine)]
        for yh, c, device in (
            (spot.yh, 1 - spot.c, spot.core()),
            (1 - spot.yh, spot.c, spot.far()),
            (1 - spot.yh, 1 - spot.c, spot.diagonal()),
        ):
            swaps.append(wire.copy(downs.at[yh * 2 + c], mine, device))
        yield
        wait_all(swaps)
        place = s_downs.at[spot.z, spot.yl, spot.x]
        moves = [wire.copy(rows, place, spot.pair()), wire.keep(rows, place)]
        yield
        wait_all(moves)
        quarters = [pl.ds(16 * k, 16) for k in range(4)]
        yield from ring_pair(
            wire,
            spot,
            [(s_downs, 0, None, quarters[0]), (s_downs, 1, None, quarters[1])],
            [(s_downs, 0, None, quarters[2]), (s_downs, 1, None, quarters[3])],
        )

    def rest_stream():
        moves = []
        for source, target in ((q_up, s_q), (kv_up, s_kv), (out_t, s_out)):
            place = target.at[spot.z, spot.yl, spot.x]
            moves += [wire.copy(source, place, spot.pair()), wire.keep(source, place)]
        yield
        wait_all(moves)
        yield from ring_pair(
            wire,
            spot,
            [(s_q, 0, None, pl.ds(0, 32)), (s_q, 1, None, pl.ds(32, 16))],
            [(s_out, 0, None, low), (s_out, 1, None, high), (s_kv, 1, None, every)],
        )

    def ffn_stream():
        moves = []
        for source, place in ((early, o_early.at[:, spot.z, spot.yl, spot.x]), (late, o_late.at[:, spot.yl])):
            moves += [wire.copy(source.at[1 - spot.yl], place, spot.pair()), wire.keep(source.at[spot.yl], place)]
        yield
        wait_all(moves)
        two = [pl.ds(2 * k, 2) for k in range(4)]
        yield from ring_pair(
            wire,
            spot,
            [(o_early, 0, two[0], every), (o_early, 1, two[1], every), (o_early, 0, pl.ds(8, 1), low)],
            [(o_early, 0, two[2], every), (o_early, 1, two[3], every), (o_early, 1, pl.ds(8, 1), high)],
        )

    first = down_stream()
    next(first)
    s_small[0] = small[...]
    smalls = all_sum_small(wire, spot, s_buf, s_small)
    next(smalls)
    hiddens = gather_tp(wire, spot, s_hidden, hidden)
    next(hiddens)
    rest = rest_stream()
    for _ in range(3):
        next(first)
        next(smalls)
    next(rest)
    next(hiddens)
    next(first)
    finish(smalls)
    finish(hiddens)
    next(rest)
    next(first)
    ffn = ffn_stream()
    next(ffn)
    gains = s_small[5].astype(F32)
    attn_gain, ffn_gain = gains[8:9], gains[9:10]
    latent_gain = gains[10:11]
    keeps = []

    def norm_rows(i):
        block, part = lax.div(i, 8), at_tile(lax.rem(i, 8), 16)
        values = s_hidden[block, part].astype(F32)
        scale = lax.rsqrt(jnp.mean(values * values, axis=-1, keepdims=True) + norm_eps)
        s_hat[at_tile(i, 16)] = (values * scale * attn_gain).astype(BF)

    loop(groups // 16, norm_rows)
    next(rest)
    finish(first)
    keeps += [wire.keep(s_downs, o_downs), wire.keep(s_hat, o_hat)]

    def down(i):
        j, k = lax.div(i, 2), lax.rem(i, 2)
        lanes = at_tile(j, 128)
        s_part[at_tile(k, 256), lanes] = dot(s_hat[at_tile(k, 256)], flat(s_downs[:, :, :, :, lanes])).astype(BF)

    loop(10, down)
    raws = gather_tp(wire, spot, s_raw, s_part)
    next(raws)
    next(rest)
    next(raws)
    next(rest)
    finish(raws)
    grads = gather_y(wire, spot, o_grad, grad)
    next(grads)
    keeps.append(wire.keep(s_raw, o_raw))

    row, lane = lane_grid(128, 128)
    low_pick = (row == lax.rem(lane, 16)) & (lax.rem(lane, 32) < 16)
    high_pick = (row == lax.rem(lane, 16)) & (lax.rem(lane, 32) >= 16)
    low_pick, high_pick = low_pick.astype(F32).astype(BF), high_pick.astype(F32).astype(BF)

    def latents(i):
        part = at_tile(i, 32)
        raw = [s_raw[t, part, 0:384].astype(F32) for t in range(4)]
        total = sum(jnp.sum(v * v, axis=-1, keepdims=True) for v in raw)
        scale = lax.rsqrt(total / 1536.0 + norm_eps)
        for t in range(4):
            s_qlat[part, t * 384 : t * 384 + 384] = (raw[t] * scale * latent_gain[:, t * 384 : t * 384 + 384]).astype(BF)
        raw = [s_raw[t, part, 384:512].astype(F32) for t in range(4)]
        total = sum(jnp.sum(v * v, axis=-1, keepdims=True) for v in raw)
        scale = lax.rsqrt(total / 512.0 + norm_eps)
        for t in range(4):
            gain = latent_gain[:, 1536 + t * 128 : 1664 + t * 128]
            s_kvlat[part, t * 128 : t * 128 + 128] = (raw[t] * scale * gain).astype(BF)
        front = dot(s_raw[0, part, 512:640], low_pick) + dot(s_raw[1, part, 512:640], high_pick)
        back = dot(s_raw[2, part, 512:640], low_pick) + dot(s_raw[3, part, 512:640], high_pick)
        c, s = cosine[part], sine[part]
        s_rope[part, 0:128] = (front * c - back * s).astype(BF)
        s_rope[part, 128:256] = (back * c + front * s).astype(BF)

    loop(groups // 32, latents)

    finish(rest)
    next(ffn)
    keeps += [wire.keep(a, b) for a, b in ((s_q, o_q), (s_kv, o_kv), (s_out, o_out))]

    def query(i):
        part = at_tile(i, 256)
        for j in range(2):
            lanes = pl.ds(j * 256, 256)
            s_query[part, lanes] = dot(s_qlat[part], flat(s_q[:, :, :, :, lanes])).astype(BF)
        both = dot(s_qlat[part], flat(s_q[:, :, :, :, 512:768]))
        front, back = both[:, 0:128], both[:, 128:256]
        c, s = cosine[part], sine[part]
        s_query[part, 512:640] = (front * c - back * s).astype(BF)
        s_query[part, 640:768] = (back * c + front * s).astype(BF)
        for j in range(4):
            lanes = pl.ds(j * 256, 256)
            s_keyval[part, lanes] = dot(s_kvlat[part], flat(s_kv[:, :, :, :, lanes])).astype(BF)

    loop(2, query)
    next(ffn)

    def attend(i):
        part = at_tile(i, 256)
        places = lax.broadcasted_iota(jnp.int32, (256, groups), 0) + i * 256
        keys = lax.broadcasted_iota(jnp.int32, (256, groups), 1)
        allowed = (seg_col[part] == seg_row[...]) & (keys <= places)
        norms = jnp.zeros((256, 128), F32)
        for head in range(4):
            scores = dot(s_query[part, head * 128 : head * 128 + 128], s_keyval[:, head * 256 : head * 256 + 128], "nt")
            scores += dot(head_lanes(s_query[part, 512:640], head), s_rope[:, 0:128], "nt")
            scores += dot(head_lanes(s_query[part, 640:768], head), s_rope[:, 128:256], "nt")
            scores = jnp.where(allowed, scores * (NOPE + ROPE) ** (-0.5), masked_score)
            peak = jnp.max(scores, axis=-1, keepdims=True)
            raised = jnp.exp(scores - peak)
            total = jnp.sum(raised, axis=-1, keepdims=True)
            probs = (raised / total).astype(BF)
            out = dot(probs, s_keyval[:, head * 256 + 128 : head * 256 + 256])
            s_heads[part, head * 128 : head * 128 + 128] = out.astype(BF)
            lanes = lax.broadcasted_iota(jnp.int32, (256, 128), 1)
            norms = jnp.where(lanes == head, peak + jnp.log(total), norms)
        s_norm[part] = norms

    loop(2, attend)
    next(ffn)
    next(grads)
    keeps += [
        wire.keep(a, b)
        for a, b in (
            (s_qlat, o_qhat), (s_kvlat, o_kvhat), (s_query, o_query), (s_keyval, o_keyval), (s_rope, o_rope),
            (s_norm, o_norm), (s_heads, o_heads),
        )
    ]

    def project(i):
        block, z = lax.div(i, 4), lax.rem(i, 4)
        s_attn[block, :, at_tile(z, 512)] = dot(s_heads[at_tile(block, own_rows)], flat(s_out[z]), "nt").astype(BF)

    loop(16, project)
    sums = sum_tp(wire, spot, s_attn, s_sum, t_got, t_held, t_last)
    finish(sums)

    def residual(i):
        part = at_tile(i, 16)
        values = s_hidden[spot.t, part].astype(F32) + s_sum[part]
        s_resid[part] = values
        scale = lax.rsqrt(jnp.mean(values * values, axis=-1, keepdims=True) + norm_eps)
        normed = values * scale * ffn_gain
        s_sent[part, 0:width] = normed.astype(BF)
        s_sum[part] = normed

    loop(own_rows // 16, residual)
    logits = dot(s_sum[...], gains, "nt", lax.Precision.HIGHEST)
    o_logits[...] = logits
    scores = jax.nn.sigmoid(logits)
    first = jnp.sum(pick_a[...] * scores, axis=-1, keepdims=True)
    second = jnp.sum(pick_b[...] * scores, axis=-1, keepdims=True)
    both = first + second
    dense = pick_a[...] * (route_scale * first / both) + pick_b[...] * (route_scale * second / both)
    s_sent[:, width : width + 128] = jnp.zeros((own_rows, 128), BF)
    s_sent[:, width : width + 16] = (dense + pick_sent[...]).astype(BF)
    o_small[...] = s_small[5]
    keeps.append(wire.keep(s_resid, o_resid))
    sents = gather_y(wire, spot, o_tokens, s_sent)
    next(sents)
    next(grads)
    next(sents)
    next(ffn)
    finish(together(sents, grads))
    finish(ffn)
    wait_all(keeps)


def front(downs, q_up, kv_up, out_t, hidden, grad, early, late, small, cosine, sine, seg_col, seg_row, picks):
    rows, width = hidden.shape
    group, columns = 4 * rows, downs.shape[-1]

    def spread(array):
        return (4, 2, 4) + array.shape[-2:]

    down_spread = (4, 2, 4, 64, columns)
    weights = [down_spread, spread(q_up), spread(kv_up), spread(out_t)]
    outs = [(shape, BF, "hbm") for shape in weights]
    outs.append(((2, 2, 2, rows, width), BF, "hbm"))
    outs.append(((early.shape[1], 4, 2, 4) + early.shape[2:], BF, "hbm"))
    outs.append(((late.shape[1], 2) + late.shape[2:], BF, "hbm"))
    outs.append(((2, 2, 2, rows, width + 128), BF, "hbm"))
    saved = [
        ((group, width), BF), ((4, group, columns), BF), ((group, 1536), BF),
        ((group, 512), BF), ((group, 768), BF), ((group, 1024), BF), ((group, 256), BF), ((group, 128), F32),
        ((group, 512), BF), ((rows, width), F32),
    ]
    outs += [(shape, dtype, "hbm") for shape, dtype in saved]
    outs += [((rows, 16), F32, "vmem"), (small.shape, small.dtype, "vmem")]
    scratch = [pltpu.VMEM((64, columns), BF)] + [pltpu.VMEM(shape, BF) for shape in weights]
    scratch += [
        pltpu.VMEM((4, rows, width), BF),
        pltpu.VMEM((group, width), BF),
        pltpu.VMEM((group, columns), BF),
        pltpu.VMEM((4, group, columns), BF),
        pltpu.VMEM((group, 1536), BF),
        pltpu.VMEM((group, 512), BF),
        pltpu.VMEM((group, 768), BF),
        pltpu.VMEM((group, 1024), BF),
        pltpu.VMEM((group, 256), BF),
        pltpu.VMEM((group, 128), F32),
        pltpu.VMEM((group, 512), BF),
        pltpu.VMEM((4, rows, width), BF),
        pltpu.VMEM((rows, width), F32),
        pltpu.VMEM((rows, width), F32),
        pltpu.VMEM((rows, width + 128), BF),
        pltpu.VMEM((6,) + small.shape, small.dtype),
        pltpu.VMEM((5, 3) + small.shape, small.dtype),
    ] + tp_sum_scratch(rows, width)
    return call(
        front_kernel, 0, outs, ["hbm"] * 8 + ["vmem"] * 8, scratch, 140, 40,
        (downs, q_up, kv_up, out_t, hidden, grad, early, late, small, cosine, sine, seg_col, seg_row) + tuple(picks),
        60,
    )


def swiglu_back(gate, up, d_hidden):
    bell = jax.nn.sigmoid(gate)
    silu = gate * bell
    return silu * up, d_hidden * up * bell * (1.0 + gate * (1.0 - bell)), d_hidden * silu


def ffn_kernel(
    tokens, dy, early, swapped, o_moe, o_back, o_early, o_late,
    s_tok, s_dy, s_in, s_dyr, s_x, s_dg, s_one, s_turned, s_gate, s_gb, s_w, s_late, s_g, s_h, s_d1, s_d2, s_ch, s_c1, s_c2,
    load, fetched, stored, done, send, recv, here,
):
    spot, wire = Spot(), Wire(send, recv, here)
    greet(spot.rings())
    capacity, slots, width = s_one.shape[1] // 4, s_one.shape[1], dy.shape[1]
    groups = s_tok.shape[0] // 2
    first = spot.yl * 4
    zs = 4
    step = width // zs

    def late_stream():
        kept = wire.keep(swapped, s_late.at[:, spot.z, :, spot.x])
        low, high, every = pl.ds(0, 32), pl.ds(32, 32), slice(None)

        def part(half, plane, rows):
            planes = pl.ds(plane, 1)
            return (s_late, half, planes, rows, swapped.at[planes, :, rows])

        rings = ring_pair(
            wire,
            spot,
            [part(0, 0, every), part(1, 1, every), part(0, 2, low), part(1, 2, high)],
            [part(0, 3, every), part(1, 4, every), part(0, 5, low), part(1, 5, high)],
        )
        next(rings)
        yield
        next(rings)
        kept.wait()
        yield
        yield from rings

    weights = late_stream()
    next(weights)

    slot_of = {0: 0, 1: 1, 2: 0, 4: 1, 3: 0}

    def fetch(e):
        slot = slot_of[e]
        return [pltpu.make_async_copy(early.at[3 * e + k], s_w.at[slot, k], fetched.at[slot, k]) for k in range(3)]

    def store(e):
        slot = slot_of[e]
        out = {3: o_late.at[pl.ds(0, 3)], 4: o_late.at[pl.ds(3, 3)]}.get(e)
        out = o_early.at[pl.ds(3 * e, 3)] if out is None else out
        return [pltpu.make_async_copy(s_g.at[slot, k], out.at[k], stored.at[slot, k]) for k in range(3)]

    def start(copies):
        for copy in copies:
            copy.start()

    loads = [pltpu.make_async_copy(tokens, s_tok, load.at[0]), pltpu.make_async_copy(dy, s_dy, load.at[1])]
    start(loads)
    start(fetch(0))
    loads[0].wait()

    row, lane = lane_grid(groups, groups)
    before = (row < lane).astype(F32).astype(BF)
    after = (lane < row).astype(F32).astype(BF)
    same = (lane == row).astype(F32).astype(BF)
    slot_row, _ = lane_grid(capacity, groups)
    turned_row, turned_lane = lane_grid(groups, slots)
    for g in range(2):
        extra = s_tok[g * groups : (g + 1) * groups, width : width + 128]
        flipped = dot(extra, same, "tn")
        gates = jnp.where(first == 0, flipped[0:4], flipped[4:8])
        masks = jnp.where(first == 0, flipped[8:12], flipped[12:16])
        padded = jnp.concatenate([masks, jnp.zeros((12, groups), F32)], axis=0)
        place = dot(padded.astype(BF), before)
        place = jnp.where(padded > 0, place, -1.0).astype(jnp.int32)
        for e in range(4):
            taken = place[e : e + 1] == slot_row
            rows = slice(e * capacity, (e + 1) * capacity)
            s_one[g, rows] = taken.astype(F32).astype(BF)
            s_gate[g, rows] = jnp.sum(jnp.where(taken, gates[e : e + 1], 0.0), axis=-1, keepdims=True)
        place = dot(after, extra)
        place = jnp.where(extra.astype(F32) > 0, place, -1.0)
        columns = jnp.where(first == 0, place[:, 8:12], place[:, 12:16]).astype(jnp.int32)
        wanted = jnp.full((groups, slots), -2, jnp.int32)
        for e in range(4):
            wanted = jnp.where(lax.div(turned_lane, capacity) == e, columns[:, e : e + 1], wanted)
        s_turned[g] = (wanted == lax.rem(turned_lane, capacity)).astype(F32).astype(BF)
    loads[1].wait()

    def dispatch(i):
        g, lanes = lax.div(i, zs), at_tile(lax.rem(i, zs), step)
        rows = at_tile(g, groups)
        s_in[g, :, lanes] = dot(s_one[g], s_tok[rows, lanes]).astype(BF)
        s_dyr[g, :, lanes] = dot(s_one[g], s_dy[rows, lanes]).astype(BF)

    loop(2 * zs, dispatch)
    next(weights)

    def expert(e, ahead, after_act, after_all):
        slot = slot_of[e]
        mine = pl.ds(e * capacity, capacity)
        if e < 3:
            wait_all(fetch(e))
        w_gate, w_up, w_down = (s_w.at[slot, k] if e < 3 else s_late.at[k] for k in range(3))
        if ahead is not None:
            start(fetch(ahead))

        def place(i):
            lanes = at_tile(i, step)
            for g in range(2):
                rows = slice(g * capacity, (g + 1) * capacity)
                s_x[rows, lanes] = s_in[g, mine, lanes]
                s_dg[rows, lanes] = (s_gate[g, mine] * s_dyr[g, mine, lanes].astype(F32)).astype(BF)

        loop(zs, place)
        gate, up = dot(s_x[...], flat(w_gate[...])), dot(s_x[...], flat(w_up[...]))
        hidden, d_gate, d_up = swiglu_back(gate, up, dot(s_dg[...], flat(w_down[...])))
        s_h[...], s_d1[...], s_d2[...] = hidden.astype(BF), d_gate.astype(BF), d_up.astype(BF)
        if after_act:
            next(weights)
        if e >= 2:
            wait_all(store({2: 0, 3: 2}[e]))

        def sums(i):
            lanes = at_tile(i, step)
            s_g[slot, 0, lanes] = dot(s_x[:, lanes], s_d1[...], "tn").astype(BF)
            s_g[slot, 1, lanes] = dot(s_x[:, lanes], s_d2[...], "tn").astype(BF)
            s_g[slot, 2, lanes] = dot(s_dg[:, lanes], s_h[...], "tn").astype(BF)

        loop(zs, sums)
        start(store(e))
        s_gb[...] = jnp.zeros_like(s_gb)

        def outward(i):
            lanes = at_tile(i, step)
            out = dot(s_h[...], flat(w_down[i]), "nt")
            back = dot(s_d1[...], flat(w_gate[i]), "nt") + dot(s_d2[...], flat(w_up[i]), "nt")
            for g in range(2):
                rows = slice(g * capacity, (g + 1) * capacity)
                s_gb[rows] += jnp.sum(out[rows] * s_dyr[g, mine, lanes].astype(F32), axis=-1, keepdims=True)
                s_dyr[g, mine, lanes] = (s_gate[g, mine] * out[rows]).astype(BF)
                s_in[g, mine, lanes] = back[rows].astype(BF)

        loop(zs, outward)
        extra_lane = lax.broadcasted_iota(jnp.int32, (capacity, 128), 1)
        for g in range(2):
            rows = slice(g * capacity, (g + 1) * capacity)
            s_in[g, mine, width : width + 128] = jnp.where(extra_lane == first + e, s_gb[rows], 0.0).astype(BF)
        if after_all:
            next(weights)

    expert(0, 1, True, False)
    expert(1, 2, False, False)
    expert(2, None, True, False)
    finish(weights)


    def common(i):
        rows = at_tile(i, 256)
        inputs = s_tok[rows, 0:width]
        gate, up = dot(inputs, flat(s_late[3])), dot(inputs, flat(s_late[4]))
        hidden, d_gate, d_up = swiglu_back(gate, up, dot(s_dy[rows], flat(s_late[5])))
        s_ch[rows], s_c1[rows], s_c2[rows] = hidden.astype(BF), d_gate.astype(BF), d_up.astype(BF)

    loop(2 * groups // 256, common)
    wait_all(store(1))

    def common_sums(i):
        lanes = at_tile(i, step)
        s_g[1, 0, lanes] = dot(s_tok[:, lanes], s_c1[...], "tn").astype(BF)
        s_g[1, 1, lanes] = dot(s_tok[:, lanes], s_c2[...], "tn").astype(BF)
        s_g[1, 2, lanes] = dot(s_dy[:, lanes], s_ch[...], "tn").astype(BF)

    loop(zs, common_sums)
    start(store(4))
    expert(3, None, False, False)

    def combine(i):
        g, z = lax.div(i, zs), lax.rem(i, zs)
        rows, lanes = at_tile(g, groups), at_tile(z, step)
        out = dot(s_ch[rows], flat(s_late[5, z]), "nt") + dot(s_turned[g], s_dyr[g, :, lanes])
        s_dy[rows, lanes] = out.astype(BF)
        back = dot(s_c1[rows], flat(s_late[3, z]), "nt") + dot(s_c2[rows], flat(s_late[4, z]), "nt")
        s_tok[rows, lanes] = (back + dot(s_turned[g], s_in[g, :, lanes])).astype(BF)

    loop(2 * zs, combine)
    for g in range(2):
        rows = slice(g * groups, (g + 1) * groups)
        s_tok[rows, width : width + 128] = dot(s_turned[g], s_in[g, :, width : width + 128]).astype(BF)
    ends = [pltpu.make_async_copy(s_dy, o_moe, done.at[0]), pltpu.make_async_copy(s_tok, o_back, done.at[1])]
    start(ends)
    wait_all(store(4))
    wait_all(store(3))
    wait_all(ends)


def ffn(tokens, dy, early, swapped, capacity):
    rows, width = dy.shape
    wide = tokens.shape[1]
    tile = early.shape[-2:]
    units = tile[1]
    outs = [(rows, width), (rows, wide), (early.shape[0], width, units), (swapped.shape[0], width, units)]
    sizes = [
        ((rows, wide), BF), ((rows, width), BF), ((2, 4 * capacity, wide), BF), ((2, 4 * capacity, width), BF),
        ((2 * capacity, width), BF), ((2 * capacity, width), BF), ((2, 4 * capacity, rows // 2), BF),
        ((2, rows // 2, 4 * capacity), BF), ((2, 4 * capacity, 1), F32), ((2 * capacity, 1), F32),
        ((2, 3, 4, 2, 4) + tile, BF), ((6, 4, 2, 4) + tile, BF), ((2, 3, width, units), BF),
        ((2 * capacity, units), BF), ((2 * capacity, units), BF), ((2 * capacity, units), BF),
        ((rows, units), BF), ((rows, units), BF), ((rows, units), BF),
    ]
    scratch = [pltpu.VMEM(*size) for size in sizes]
    scratch += [pltpu.SemaphoreType.DMA(n) for n in ((2,), (2, 3), (2, 3), (2,))]
    return call(
        ffn_kernel, 3, [(shape, BF, "hbm") for shape in outs], ["hbm"] * 4, scratch, 48, 1,
        (tokens, dy, early, swapped), 62,
    )


def back_kernel(
    early, late, part, attn_in, heads, out_w, up_q, up_kv, downs, query, keyval, rope, norms, qlat, kvlat, raw,
    resid, logits, pick_a, pick_b, grad, gains, cosine, sine, seg_col, seg_row,
    o_early, o_late, o_gout, o_gq, o_gkv, o_gdown, o_attn, o_resid, o_small,
    *rest,
):
    landing, rest = list(rest[:20]), rest[20:]
    scratch, (send, recv, here) = list(rest[:-3]), rest[-3:]
    spot, wire = Spot(), Wire(send, recv, here)
    greet(spot.rings() + [spot.along_y(1), spot.along_y(3), spot.core(), spot.far(), spot.diagonal()])
    own_rows, width = grad.shape
    groups = 4 * own_rows

    def take(count):
        taken, scratch[:] = scratch[:count], scratch[count:]
        return taken

    def unit(half, ref, order):
        rings = [take(3) + [landing.pop(0), landing.pop(0)] for _ in range(2)]
        return sum_unit(wire, spot, half, ref, order, rings)

    one = [unit(0, early.at[pl.ds(0, 4)], "zx"), unit(1, early.at[pl.ds(4, 4)], "zx")]
    two = [
        unit(0, late.at[pl.ds(0, 3)], "xz"),
        unit(1, late.at[pl.ds(3, 3)], "xz"),
        unit(0, early.at[pl.ds(8, 1)], "xz"),
    ]

    def weights():
        yield from together(
            sum_stream(wire, spot, "zx", one, True), sum_stream(wire, spot, "xz", two, True)
        )
        moves = []
        places = (
            (one[0][2], o_early.at[spot.yl, pl.ds(0, 4)]),
            (one[1][2], o_early.at[spot.yl, pl.ds(4, 4)]),
            (two[0][2], o_late.at[spot.yl, pl.ds(0, 3)]),
            (two[1][2], o_late.at[spot.yl, pl.ds(3, 3)]),
            (two[2][2], o_early.at[spot.yl, pl.ds(8, 1)]),
        )
        for total, place in places:
            moves += [wire.copy(total.at[:, 1 - spot.yl], place, spot.pair()), wire.keep(total.at[:, spot.yl], place)]
        yield
        wait_all(moves)

    tokens = take(5)
    (s_back, s_heads, s_wide, s_upq, s_upkv, s_query, s_keyval, s_rope, s_norms, s_qlat, s_kvlat, s_raw) = take(12)
    (s_normed, s_dres, s_dh, s_dhall, s_dheads, s_dq, s_dkv, s_accq, s_acck, s_dkn, s_dv, s_lat) = take(12)
    (s_swap, s_got, s_stage, s_attn, s_small) = take(5)
    t_scratch = take(3)
    s_part = tokens[1]
    sums = sum_y(wire, spot, part, s_back, *tokens)
    next(sums)
    ffn = weights()
    next(ffn)
    loads = [wire.keep(a, b) for a, b in ((heads, s_heads), (out_w, s_wide.at[:, pl.ds(0, 512)]))]
    others = [
        wire.keep(a, b)
        for a, b in (
            (query, s_query), (keyval, s_keyval), (rope, s_rope), (norms, s_norms), (qlat, s_qlat), (kvlat, s_kvlat),
            (up_q, s_upq), (up_kv, s_upkv), (raw.at[:, pl.ds(pl.multiple_of(spot.t * own_rows, 128), own_rows)], s_raw),
        )
    ]
    finish(sums)

    rows_f32 = gains[...].astype(F32)
    ffn_gain = rows_f32[9:10]
    dense = s_back[:, width : width + 16]
    scores = jax.nn.sigmoid(logits[...])
    first = jnp.sum(pick_a[...] * scores, axis=-1, keepdims=True)
    second = jnp.sum(pick_b[...] * scores, axis=-1, keepdims=True)
    both = first + second
    apart = jnp.sum((pick_a[...] - pick_b[...]) * dense, axis=-1, keepdims=True) * route_scale / both
    d_scores = (pick_a[...] * (second / both) - pick_b[...] * (first / both)) * apart
    d_logits = d_scores * scores * (1.0 - scores)
    s_normed[...] = dot(d_logits, rows_f32, "nn", lax.Precision.HIGHEST)
    s_small[0:1] = jnp.zeros((1, width), F32)

    def own_row(i):
        rows = at_tile(i, 16)
        values = resid[rows]
        scale = lax.rsqrt(jnp.mean(values * values, axis=-1, keepdims=True) + norm_eps)
        hat = values * scale
        grad_ffn = s_normed[rows] + s_back[rows, 0:width]
        s_small[0:1] += jnp.sum(grad_ffn * hat, axis=0, keepdims=True)
        weighted = grad_ffn * ffn_gain
        inner = scale * (weighted - hat * jnp.mean(weighted * hat, axis=-1, keepdims=True))
        total = grad[rows].astype(F32) + inner
        s_dres[rows] = total
        s_dh[rows] = total.astype(BF)
        s_normed[rows] = hat * ffn_gain

    loop(own_rows // 16, own_row)
    keeps = [wire.keep(s_dres, o_resid)]
    swap = gather_tp(wire, spot, s_dhall, s_dh)
    next(swap)
    next(swap)
    o_small[...] = dot(d_logits, s_normed[...], "tn", lax.Precision.HIGHEST)
    o_small[9:10] = s_small[0:1]
    finish(swap)

    wait_all(loads)

    def out_grads(i):
        lanes = at_tile(i, 512)
        s_stage[lanes, 0:512] = dot(flat(s_dhall[:, :, lanes]), s_heads[...], "tn").astype(BF)

    loop(4, out_grads)
    staged = wire.keep(s_stage.at[:, pl.ds(0, 512)], o_gout)

    def head_grads(i):
        s_dheads[at_tile(i, own_rows)] = dot(s_dhall[i], s_wide[:, 0:512]).astype(BF)

    loop(4, head_grads)
    wait_all(others)
    late = [wire.keep(attn_in.at[pl.ds(t * own_rows, own_rows)], s_dhall.at[t]) for t in range(4)]
    late.append(wire.keep(downs, s_wide))
    s_accq[...] = jnp.zeros_like(s_accq)
    s_acck[...] = jnp.zeros_like(s_acck)

    for head in range(4):
        nope, value = pl.ds(head * 256, 128), pl.ds(head * 256 + 128, 128)
        at = pl.ds(head * 128, 128)
        s_dkn[...] = jnp.zeros_like(s_dkn)
        s_dv[...] = jnp.zeros_like(s_dv)

        def attend(i, head=head, nope=nope, value=value, at=at):
            tile = at_tile(i, 256)
            places = lax.broadcasted_iota(jnp.int32, (256, groups), 0) + i * 256
            keys = lax.broadcasted_iota(jnp.int32, (256, groups), 1)
            allowed = (seg_col[tile] == seg_row[...]) & (keys <= places)
            front, back = head_lanes(s_query[tile, 512:640], head), head_lanes(s_query[tile, 640:768], head)
            scores = dot(s_query[tile, at], s_keyval[:, nope], "nt")
            scores += dot(front, s_rope[:, 0:128], "nt")
            scores += dot(back, s_rope[:, 128:256], "nt")
            scores = jnp.where(allowed, scores * (NOPE + ROPE) ** (-0.5), masked_score)
            probs = jnp.exp(scores - s_norms[tile, head : head + 1])
            d_head = s_dheads[tile, at]
            s_dv[...] += dot(probs.astype(BF), d_head, "tn")
            d_probs = dot(d_head, s_keyval[:, value], "nt")
            row_dot = jnp.sum(probs * d_probs, axis=-1, keepdims=True)
            d_scores = (probs * (d_probs - row_dot) * (NOPE + ROPE) ** (-0.5)).astype(BF)
            s_dq[tile, at] = dot(d_scores, s_keyval[:, nope]).astype(BF)
            s_accq[tile, 0:128] += head_lanes(dot(d_scores, s_rope[:, 0:128]), head)
            s_accq[tile, 128:256] += head_lanes(dot(d_scores, s_rope[:, 128:256]), head)
            s_dkn[...] += dot(d_scores, s_query[tile, at], "tn")
            s_acck[:, 0:128] += dot(d_scores, front, "tn")
            s_acck[:, 128:256] += dot(d_scores, back, "tn")

        loop(2, attend)
        s_dkv[:, nope] = s_dkn[...].astype(BF)
        s_dkv[:, value] = s_dv[...].astype(BF)
    next(ffn)

    row, lane = lane_grid(128, 128)
    fold_front = ((lane < 32) & (lane == lax.rem(row, 32))).astype(F32)
    fold_back = ((lane >= 32) & (lane < 64) & (lane - 32 == lax.rem(row, 32))).astype(F32)

    def unrotate(i):
        rows = at_tile(i, own_rows)
        c, s = cosine[rows], sine[rows]
        front, back = s_accq[rows, 0:128], s_accq[rows, 128:256]
        s_dq[rows, 512:640] = (front * c + back * s).astype(BF)
        s_dq[rows, 640:768] = (back * c - front * s).astype(BF)
        front, back = s_acck[rows, 0:128], s_acck[rows, 128:256]
        folded = dot(front * c + back * s, fold_front, "nn", lax.Precision.HIGHEST)
        folded += dot(back * c - front * s, fold_back, "nn", lax.Precision.HIGHEST)
        s_part[i, :, 2048:2176] = folded.astype(BF)
        for j in range(3):
            lanes = slice(j * 512, j * 512 + 512)
            s_part[i, :, lanes] = dot(s_dq[rows], s_upq[lanes], "nt").astype(BF)
        s_part[i, :, 1536:2048] = dot(s_dkv[rows], s_upkv[...], "nt").astype(BF)

    loop(4, unrotate)
    latents = sum_tp(wire, spot, s_part, s_lat, *t_scratch)
    next(latents)
    staged.wait()

    def q_grads(i):
        lanes = at_tile(i, 256)
        s_stage[lanes] = dot(s_qlat[:, lanes], s_dq[...], "tn").astype(BF)

    loop(6, q_grads)
    staged = wire.keep(s_stage.at[pl.ds(0, 1536)], o_gq)
    next(latents)

    def kv_grads(i):
        lanes = at_tile(i, 256)
        s_attn[lanes, 0:1024] = dot(s_kvlat[:, lanes], s_dkv[...], "tn").astype(BF)

    loop(2, kv_grads)
    staged_kv = wire.keep(s_attn.at[:, pl.ds(0, 1024)], o_gkv)
    finish(latents)

    gain = rows_f32[10:11]
    s_small[...] = jnp.zeros_like(s_small)

    def latent_row(i):
        rows = at_tile(i, 32)
        for cut, columns, start in ((slice(0, 384), 384, 0), (slice(384, 512), 128, 1536)):
            size = 4.0 * columns
            values = [s_raw[t, rows, cut].astype(F32) for t in range(4)]
            scale = lax.rsqrt(sum(jnp.sum(v * v, axis=-1, keepdims=True) for v in values) / size + norm_eps)
            hats = [v * scale for v in values]
            grads, weighted = [], []
            for t in range(4):
                at = slice(start + t * columns, start + (t + 1) * columns)
                grads.append(s_lat[rows, at])
                weighted.append(grads[t] * gain[:, at])
                s_small[0:1, at] += jnp.sum(grads[t] * hats[t], axis=0, keepdims=True)
            inner = sum(jnp.sum(w * h, axis=-1, keepdims=True) for w, h in zip(weighted, hats)) / size
            for t in range(4):
                s_swap[t, rows, cut] = (scale * (weighted[t] - hats[t] * inner)).astype(BF)
        folded = s_lat[rows, 2048:2176].astype(BF)
        for t in range(4):
            pick = ((row == t * 16 + lane) & (lane < 16)).astype(F32).astype(BF)
            s_swap[t, rows, 512:640] = dot(folded, pick).astype(BF)

    loop(own_rows // 32, latent_row)
    moves = [wire.keep(s_swap.at[spot.t], s_got.at[spot.t])]
    for yh, c, device in (
        (spot.yh, 1 - spot.c, spot.core()),
        (1 - spot.yh, spot.c, spot.far()),
        (1 - spot.yh, 1 - spot.c, spot.diagonal()),
    ):
        moves.append(wire.copy(s_swap.at[yh * 2 + c], s_got.at[spot.t], device))
    o_small[10:11] = s_small[0:1]
    s_small[0:1] = jnp.zeros((1, width), F32)
    wait_all(moves)
    wait_all(late)
    staged.wait()
    staged_kv.wait()
    next(ffn)

    def down_grads(i):
        lanes = at_tile(i, 512)
        s_stage[lanes, 0:640] = dot(flat(s_dhall[:, :, lanes]), flat(s_got[...]), "tn").astype(BF)

    loop(4, down_grads)
    staged = wire.keep(s_stage.at[:, pl.ds(0, 640)], o_gdown)

    def attn_grads(i):
        rows, lanes = lax.div(i, 4), at_tile(lax.rem(i, 4), 512)
        back = dot(s_got[rows], s_wide[lanes], "nt")
        s_attn[at_tile(rows, own_rows), lanes] = back.astype(BF)
        s_small[0:1, lanes] += jnp.sum(back * s_dhall[rows, :, lanes].astype(F32), axis=0, keepdims=True)

    loop(16, attn_grads)
    o_small[8:9] = s_small[0:1] / rows_f32[8:9]
    keeps.append(wire.keep(s_attn, o_attn))
    finish(ffn)
    staged.wait()
    wait_all(keeps)


def back(ffn_grads, part, saved, resid, logits, picks, grad, gains, cosine, sine, seg_col, seg_row):
    rows, width = grad.shape
    group = 4 * rows
    outs = [((2, a.shape[0]) + a.shape[4:], BF, "hbm") for a in ffn_grads]
    outs += [((2048, 512), BF, "hbm"), ((1536, 768), BF, "hbm"), ((512, 1024), BF, "hbm"), ((2048, 640), BF, "hbm")]
    outs += [((group, width), BF, "hbm"), ((rows, width), F32, "hbm"), ((16, width), F32, "vmem")]
    scratch = []
    tile = ffn_grads[0].shape[4:]
    for planes, order in ((4, "zx"), (4, "zx"), (3, "xz"), (3, "xz"), (1, "xz")):
        first = (planes, 2, 4) + tile if order == "zx" else (planes, 4, 2) + tile
        second = (planes, 2) + tile
        outs += [(first, BF, "hbm")] * 2 + [(second, BF, "hbm")] * 2
        scratch += [pltpu.VMEM(first, BF)] * 3 + [pltpu.VMEM(second, BF)] * 3
    columns = part.shape[-1]
    scratch += [pltpu.VMEM((4, rows, columns), BF)] * 2 + [pltpu.VMEM((rows, columns), BF)] * 3
    sizes = [
        ((rows, columns), F32), ((group, 512), BF), ((width, 640), BF), ((1536, 768), BF), ((512, 1024), BF),
        ((group, 768), BF), ((group, 1024), BF), ((group, 256), BF), ((group, 128), F32), ((group, 1536), BF),
        ((group, 512), BF), ((4, rows, 640), BF),
        ((rows, width), F32), ((rows, width), F32), ((rows, width), BF), ((4, rows, width), BF), ((group, 512), BF),
        ((group, 768), BF), ((group, 1024), BF), ((group, 256), F32), ((group, 256), F32), ((group, 128), F32),
        ((group, 128), F32), ((rows, columns), F32),
        ((4, rows, 640), BF), ((4, rows, 640), BF), ((width, 768), BF), ((group, width), BF), ((8, width), F32),
    ]
    scratch += [pltpu.VMEM(*size) for size in sizes] + tp_sum_scratch(rows, columns)
    return call(
        back_kernel, 1, outs, ["hbm"] * 16 + ["vmem"] * 10, scratch, 100, 90,
        tuple(ffn_grads) + (part,) + tuple(saved) + (resid, logits) + tuple(picks)
        + (grad, gains, cosine, sine, seg_col, seg_row),
        62,
    )[:9]


def last_kernel(downs, q_up, kv_up, out_t, part, moe, small, o_downs, o_q, o_kv, o_out, o_part, o_moe, o_small, *rest):
    scratch, (send, recv, here) = list(rest[:-3]), rest[-3:]
    spot, wire = Spot(), Wire(send, recv, here)
    greet(
        spot.rings()
        + [spot.along_x(2), spot.along_z(2), spot.along_y(1), spot.along_y(3)]
        + [spot.core(), spot.far(), spot.diagonal()]
    )

    def take(count):
        taken, scratch[:] = scratch[:count], scratch[count:]
        return taken

    def unit(half, ref, order):
        return sum_unit(wire, spot, half, ref, order, (take(5), take(5)))

    one = [unit(0, q_up, "zx"), unit(1, out_t, "zx")]
    two = [unit(0, downs, "xz"), unit(1, kv_up, "xz")]
    (got_q, got_out, got_downs, got_kv, rows), tokens, ring = take(5), take(3), take(5)
    s_small, s_buf = take(2)
    s_small[0] = small[...]

    def weights():
        yield from together(sum_stream(wire, spot, "zx", one), sum_stream(wire, spot, "xz", two))
        finals = (
            (two[0][2], got_downs, rows),
            (one[0][2], got_q, o_q),
            (one[1][2], got_out, o_out),
            (two[1][2], got_kv, o_kv),
        )
        moves = [wire.copy(total.at[:, 1 - spot.yl], got, spot.pair()) for total, got, _ in finals]
        yield
        swaps = []
        for made, (total, got, out) in zip(moves, finals):
            made.wait()
            add_into(out, total.at[0, spot.yl], got.at[0])
            if not swaps:
                cut = lambda t: rows.at[pl.ds(pl.multiple_of(t * 16, 16), 16)]
                swaps.append(wire.keep(cut(spot.t), o_downs.at[spot.t]))
                for yh, c, device in (
                    (spot.yh, 1 - spot.c, spot.core()),
                    (1 - spot.yh, spot.c, spot.far()),
                    (1 - spot.yh, 1 - spot.c, spot.diagonal()),
                ):
                    swaps.append(wire.copy(cut(yh * 2 + c), o_downs.at[spot.t], device))
        yield
        wait_all(swaps)

    finish(
        together(
            weights(),
            sum_tp(wire, spot, part, o_part, *tokens),
            all_sum_small(wire, spot, s_buf, s_small),
            sum_y(wire, spot, moe, o_moe, *ring),
        )
    )
    o_small[...] = s_small[5]


def last(downs, q_up, kv_up, out_t, part, moe, small):
    scratch, ends = [], []
    for a, order in ((q_up, "zx"), (out_t, "zx"), (downs, "xz"), (kv_up, "xz")):
        scratch += unit_scratch(1, order, *a.shape[-2:])
        ends.append(pltpu.VMEM((1,) + a.shape[-2:], BF))
    rows, columns = part.shape[1:]
    scratch += ends + [pltpu.VMEM(downs.shape[-2:], BF)] + tp_sum_scratch(rows, columns)
    scratch += [pltpu.VMEM((4, rows, columns), BF)] * 2 + [pltpu.VMEM((rows, columns), BF)] * 3
    scratch += [pltpu.VMEM((6,) + small.shape, F32), pltpu.VMEM((5, 3) + small.shape, F32)]
    outs = [((4, 16, downs.shape[-1]), BF, "hbm")]
    outs += [(a.shape[-2:], F32, "vmem") for a in (q_up, kv_up, out_t)]
    outs += [((rows, columns), F32, "vmem")] * 2 + [(small.shape, F32, "vmem")]
    return call(
        last_kernel, 2, outs, ["hbm"] * 4 + ["vmem", "hbm", "vmem"], scratch, 64, 32,
        (downs, q_up, kv_up, out_t, part, moe, small), 50,
    )


def rotary_tables(position):
    half_size = ROPE // 2
    inverse = theta_base ** (-(2.0 * jnp.arange(half_size, dtype=F32)) / ROPE)
    angles = position.astype(F32)[:, None] * inverse[None, :]
    return (jnp.cos(angles), jnp.sin(angles))


def packing(lengths, total_rows):
    positions = jnp.arange(total_rows, dtype=jnp.int32)
    endings = jnp.cumsum(lengths)
    segment = jnp.sum((positions[:, None] >= endings[None, :]).astype(jnp.int32), axis=1)
    starting = endings - lengths
    owner_mask = segment[:, None] == jnp.arange(lengths.shape[0], dtype=jnp.int32)[None, :]
    first_row = jnp.sum(jnp.where(owner_mask, starting[None, :], 0), axis=1)
    return (segment, positions - first_row)


def normalized(values):
    scale = lax.rsqrt(jnp.mean(values * values, axis=-1, keepdims=True) + norm_eps)
    return values * scale, scale


def norm_back(grad, gain, hat, scale):
    weighted = grad * gain
    return scale * (weighted - hat * jnp.mean(weighted * hat, axis=-1, keepdims=True))


def per_device(
    hidden_in,
    out_grad,
    attn_gain,
    q_down,
    q_gain,
    kv_down,
    kv_gain,
    q_up,
    kv_up,
    out_proj,
    ffn_gain,
    router,
    routed_gate_up,
    routed_down,
    shared_gate_up,
    shared_down,
    choices,
    seq_lens,
):
    local_rows, width = hidden_in.shape
    group_rows = choices.shape[0]
    tp_count = lax.axis_size("tp")
    tp_index = lax.axis_index("tp")
    y_lo = lax.rem(lax.div(lax.axis_index("fsdp"), 4), 2)
    head_count = HEADS // tp_count
    experts = router.shape[1]
    held = experts // 2
    capacity = 5 * group_rows * TOPK // (4 * experts)
    units = routed_gate_up.shape[3]
    row_shard = routed_gate_up.shape[1]
    q_cols = q_down.shape[1] // tp_count
    raw_cols = q_cols + kv_down.shape[1] // tp_count
    raw_pad = -raw_cols % 128
    small_at = raw_cols + raw_pad

    def own(array):
        return lax.dynamic_slice_in_dim(array, tp_index * local_rows, local_rows)

    down_rows = q_down.shape[0]
    devices = width // down_rows
    device = lax.axis_index("fsdp") * tp_count + tp_index
    rope_cols = ROPE // tp_count
    columns = jnp.concatenate(
        [
            q_down.reshape(down_rows, tp_count, q_cols),
            kv_down[:, :KVR].reshape(down_rows, tp_count, KVR // tp_count),
            kv_down[:, KVR:].reshape(down_rows, tp_count, rope_cols),
        ],
        axis=-1,
    ).transpose(1, 0, 2)
    downs = jnp.pad(columns, ((0, 0), (0, 0), (0, raw_pad)))
    half = ROPE // 2
    q_rows = q_up.reshape(-1, head_count, NOPE + ROPE)
    q_sent = jnp.concatenate(
        [
            q_rows[..., :NOPE].reshape(-1, head_count * NOPE),
            q_rows[..., NOPE : NOPE + half].reshape(-1, head_count * half),
            q_rows[..., NOPE + half :].reshape(-1, head_count * half),
        ],
        axis=1,
    )
    small = jnp.zeros((16, width), BF)
    vectors = jnp.concatenate([router.T, attn_gain[None], ffn_gain[None]], axis=0)
    small = lax.dynamic_update_slice(small, vectors, (0, device * down_rows))
    small = lax.dynamic_update_slice(small, q_gain[None], (experts + 2, device * q_gain.shape[0]))
    kv_at = q_down.shape[1] + device * kv_gain.shape[0]
    small = lax.dynamic_update_slice(small, kv_gain[None], (experts + 2, kv_at))
    gate_up = routed_gate_up.transpose(0, 2, 1, 3)
    down_t = routed_down.transpose(0, 2, 1)[:, None]
    routed = jnp.concatenate([gate_up, down_t], axis=1).reshape(2, held, 3, row_shard, units)
    shared = jnp.concatenate(
        [
            shared_gate_up.reshape(row_shard, 2, 2, units).transpose(2, 1, 0, 3),
            shared_down.T.reshape(row_shard, 2, units).transpose(1, 0, 2)[:, None],
        ],
        axis=1,
    )
    early = routed[:, : held - 1].reshape(2, 3 * (held - 1), row_shard, units)
    late = jnp.concatenate([routed[:, held - 1], shared], axis=1)

    segment, position = packing(seq_lens[0], group_rows)
    cosine, sine_table = rotary_tables(position)
    cos_heads, sin_heads = jnp.tile(cosine, (1, head_count)), jnp.tile(sine_table, (1, head_count))
    picked = own(choices)
    lanes = jnp.arange(2 * experts, dtype=jnp.int32)
    pick_a, pick_b = ((picked[:, k : k + 1] == lanes[None]).astype(F32) for k in range(TOPK))
    pick_sent = sum((picked[:, k : k + 1] + experts == lanes[None]).astype(F32) for k in range(TOPK))

    (
        all_downs, all_q, all_kv, all_out, all_grad, wide_early, swapped_late, tokens,
        attn_in, raw, group_query, group_keyval, query, keyval, rope, norms, heads_out, residual, logits,
        gains,
    ) = front(
        downs, q_sent, kv_up, out_proj.T, hidden_in, out_grad, early, late, small,
        cos_heads, sin_heads, segment[:, None], segment[None, :], (pick_a, pick_b, pick_sent),
    )
    down_weight = all_downs.reshape(width, -1)
    up_query = all_q.reshape(-1, q_up.shape[1])
    up_keyval = all_kv.reshape(-1, kv_up.shape[1])
    out_weight = all_out.reshape(width, -1)
    moe_part, back_part, sum_early, sum_late = ffn(
        tokens.reshape(2 * group_rows, -1), all_grad.reshape(2 * group_rows, width), wide_early, swapped_late, capacity
    )

    ring = (2, 2, 2, local_rows)
    blocks = (4, 2, 4, row_shard, units)
    own_early, own_late, grad_out, grad_q, grad_kv, grad_down, attn_back, grad_resid, small_grads = back(
        (sum_early.reshape((-1,) + blocks), sum_late.reshape((-1,) + blocks)),
        back_part.reshape(ring + (width + 128,)),
        (
            attn_in, heads_out, out_weight, up_query, up_keyval, down_weight, query, keyval, rope, norms, group_query,
            group_keyval, raw,
        ),
        residual, logits, (pick_a, pick_b), out_grad, gains, cos_heads, sin_heads, segment[:, None], segment[None, :],
    )

    def spread(array, like):
        return array.reshape((1, 4, 2, 4) + like.shape[-2:])

    got_downs, sum_up_query, sum_up_keyval, sum_out, attn_back_own, moe_own, small_sum = last(
        spread(grad_down, jnp.zeros((row_shard, grad_down.shape[1]))),
        spread(grad_q, q_up),
        spread(grad_kv, kv_up),
        spread(grad_out, out_proj.T),
        attn_back.reshape(tp_count, local_rows, width),
        moe_part.reshape(ring + (width,)),
        small_grads,
    )
    layer_out = (residual + moe_own).astype(BF)
    own_hat, own_scale = normalized(hidden_in.astype(F32))
    input_grad = grad_resid + norm_back(attn_back_own, gains[experts].astype(F32), own_hat, own_scale)
    got_downs = got_downs.astype(F32)
    sum_qdown = got_downs[..., :q_cols].transpose(1, 0, 2).reshape(down_rows, -1)
    kv_at = q_cols + KVR // tp_count
    sum_kvdown = jnp.concatenate(
        [
            got_downs[..., q_cols:kv_at].transpose(1, 0, 2).reshape(down_rows, -1),
            got_downs[..., kv_at:raw_cols].transpose(1, 0, 2).reshape(down_rows, -1),
        ],
        axis=-1,
    )
    nope_cols, half_cols = head_count * NOPE, head_count * half
    sum_up_query = jnp.concatenate(
        [
            sum_up_query[:, :nope_cols].reshape(-1, head_count, NOPE),
            sum_up_query[:, nope_cols : nope_cols + half_cols].reshape(-1, head_count, half),
            sum_up_query[:, nope_cols + half_cols :].reshape(-1, head_count, half),
        ],
        axis=-1,
    ).reshape(q_up.shape)

    def mine(row, at, count):
        return lax.dynamic_slice(small_sum, (row, at), (1, count))[0]

    rows_at = device * down_rows
    sum_router = lax.dynamic_slice(small_sum, (0, rows_at), (experts, down_rows)).T
    own_routed = jnp.concatenate([own_early, own_late[:, :3]], axis=1).reshape(experts, 3, row_shard, units)
    sum_wide_gu = own_routed[:, :2].transpose(0, 2, 1, 3).astype(F32)
    sum_wide_down = own_routed[:, 2].transpose(0, 2, 1).astype(F32)
    sum_common_gu = own_late[:, 3:5].transpose(2, 1, 0, 3).reshape(row_shard, 2, 2 * units).astype(F32)
    sum_common_down = own_late[:, 5].transpose(1, 0, 2).reshape(row_shard, 2 * units).T.astype(F32)
    q_rank = q_down.shape[1]
    return (
        layer_out,
        input_grad.astype(BF),
        mine(experts, rows_at, down_rows),
        sum_qdown,
        mine(experts + 2, device * q_gain.shape[0], q_gain.shape[0]),
        sum_kvdown,
        mine(experts + 2, q_rank + device * kv_gain.shape[0], kv_gain.shape[0]),
        sum_up_query,
        sum_up_keyval,
        sum_out.T,
        mine(experts + 1, rows_at, down_rows),
        sum_router,
        sum_wide_gu,
        sum_wide_down,
        sum_common_gu,
        sum_common_down,
    )


def solution(mesh):
    return jax.shard_map(
        per_device,
        mesh=mesh,
        in_specs=(
            P(("fsdp", "tp"), None),
            P(("fsdp", "tp"), None),
            P(("fsdp", "tp")),
            P(("fsdp", "tp"), None),
            P(("fsdp", "tp")),
            P(("fsdp", "tp"), None),
            P(("fsdp", "tp")),
            P("fsdp", "tp"),
            P("fsdp", "tp"),
            P("tp", "fsdp"),
            P(("fsdp", "tp")),
            P(("fsdp", "tp"), None),
            P(None, "fsdp", None, "tp"),
            P(None, "tp", "fsdp"),
            P("fsdp", None, "tp"),
            P("tp", "fsdp"),
            P("fsdp", None),
            P("fsdp", None),
        ),
        out_specs=(
            P(("fsdp", "tp"), None),
            P(("fsdp", "tp"), None),
            P(("fsdp", "tp")),
            P(("fsdp", "tp"), None),
            P(("fsdp", "tp")),
            P(("fsdp", "tp"), None),
            P(("fsdp", "tp")),
            P("fsdp", "tp"),
            P("fsdp", "tp"),
            P("tp", "fsdp"),
            P(("fsdp", "tp")),
            P(("fsdp", "tp"), None),
            P(None, "fsdp", None, "tp"),
            P(None, "tp", "fsdp"),
            P("fsdp", None, "tp"),
            P("tp", "fsdp"),
        ),
        check_vma=False,
    )
```

```python
import functools

import jax
import jax.numpy as jnp
from jax import lax
from jax.experimental import pallas as pl
from jax.experimental.pallas import tpu as pltpu
from jax.sharding import PartitionSpec as P

HEADS = 16
NOPE = 128
ROPE = 64
VDIM = 128
KVR = 512
TOPK = 2

theta_base = 50000.0
norm_eps = 1e-06
route_scale = 2.446
masked_score = -1e30

MESH = pl.DeviceIdType.MESH
BF = jnp.bfloat16
F32 = jnp.float32
MIB = 1 << 20


class Spot:
    def __init__(self):
        f, t = lax.axis_index("fsdp"), lax.axis_index("tp")
        self.t = t
        self.z, self.yl, self.x = lax.div(f, 8), lax.rem(lax.div(f, 4), 2), lax.rem(f, 4)
        self.yh, self.c = lax.div(t, 2), lax.rem(t, 2)
        self.y = self.yh * 2 + self.yl

    def at(self, z=None, yl=None, x=None, yh=None, c=None):
        z = self.z if z is None else z
        yl = self.yl if yl is None else yl
        x = self.x if x is None else x
        yh = self.yh if yh is None else yh
        c = self.c if c is None else c
        return ((z * 2 + yl) * 4 + x, yh * 2 + c)

    def along_x(self, by):
        return self.at(x=lax.rem(self.x + by, 4))

    def along_z(self, by):
        return self.at(z=lax.rem(self.z + by, 4))

    def along_y(self, by):
        y = lax.rem(self.y + by, 4)
        return self.at(yl=lax.rem(y, 2), yh=lax.div(y, 2))

    def pair(self):
        return self.at(yl=1 - self.yl)

    def core(self):
        return self.at(c=1 - self.c)

    def far(self):
        return self.at(yh=1 - self.yh)

    def diagonal(self):
        return self.at(yh=1 - self.yh, c=1 - self.c)

    def rings(self):
        return [self.along_x(1), self.along_x(3), self.along_z(1), self.along_z(3)]


def greet(devices):
    barrier = pltpu.get_barrier_semaphore()
    for device in devices:
        pl.semaphore_signal(barrier, inc=1, device_id=device, device_id_type=MESH)
    pl.semaphore_wait(barrier, len(devices))


class Wire:
    def __init__(self, send, recv, here):
        self.send, self.recv, self.here = send, recv, here
        self.sent = self.kept = 0

    def copy(self, source, target, device):
        made = pltpu.make_async_remote_copy(
            src_ref=source,
            dst_ref=target,
            send_sem=self.send.at[self.sent],
            recv_sem=self.recv.at[self.sent],
            device_id=device,
            device_id_type=MESH,
        )
        self.sent += 1
        made.start()
        return made

    def keep(self, source, target):
        made = pltpu.make_async_copy(source, target, self.here.at[self.kept])
        self.kept += 1
        made.start()
        return made


def wait_all(copies):
    for made in copies:
        made.wait()


def together(*parts):
    left = list(parts)
    while left:
        for part in list(left):
            if next(part, "over") == "over":
                left.remove(part)
        yield


def finish(part):
    for _ in part:
        pass


def add_into(target, *terms):
    lead, (rows, columns) = target.shape[:-2], target.shape[-2:]
    step = rows if rows * columns <= 49152 else 16
    pieces = rows // step
    count = pieces
    for size in lead:
        count *= size

    def body(i, carry):
        at = [pl.ds(pl.multiple_of(lax.rem(i, pieces) * step, 16), step)]
        i = lax.div(i, pieces)
        for size in reversed(lead):
            at.insert(0, lax.rem(i, size))
            i = lax.div(i, size)
        at = tuple(at)
        total = terms[0][at].astype(F32)
        for term in terms[1:]:
            total = total + term[at].astype(F32)
        target[at] = total.astype(target.dtype)
        return carry

    lax.fori_loop(0, count, body, 0)


def gather_ring(wire, pos, plus, minus, units):
    prev, following = lax.rem(pos + 3, 4), lax.rem(pos + 1, 4)
    mine = [unit[2] if len(unit) > 2 else unit[0](pos) for unit in units]
    right = [wire.copy(own, unit[0](pos), plus) for own, unit in zip(mine, units)]
    left = [wire.copy(own, unit[0](pos), minus) for own, unit in zip(mine, units)]
    yield
    wait_all(right)
    onward = [wire.copy(unit[0](prev), unit[0](prev), plus) for unit in units if unit[1] == 0]
    wait_all(left)
    onward += [wire.copy(unit[0](following), unit[0](following), minus) for unit in units if unit[1] == 1]
    yield
    wait_all(onward)


def sum_ring(wire, pos, plus, minus, units, staged=False):
    prev, following, across = lax.rem(pos + 3, 4), lax.rem(pos + 1, 4), lax.rem(pos + 2, 4)
    first, direct, last = [], [], []
    for half, view, between, own, through, from_left, from_right, loads in units:
        first.append(wire.copy(view(across), through, plus if half == 0 else minus))
    for half, view, between, own, through, from_left, from_right, loads in units:
        if half == 0:
            direct.append(wire.copy(view(prev), from_right, minus))
        else:
            direct.append(wire.copy(view(following), from_left, plus))
    yield
    for made, (half, view, between, own, through, from_left, from_right, loads) in zip(first, units):
        wait_all(loads)
        made.wait()
        add_into(between, between, through)
        if half == 0:
            last.append(wire.copy(between, from_left, plus))
        else:
            last.append(wire.copy(between, from_right, minus))
    yield
    for one, two, (half, view, between, own, through, from_left, from_right, loads) in zip(direct, last, units):
        one.wait()
        two.wait()
        if staged:
            wait_all([wire.keep(from_left, through), wire.keep(from_right, between)])
            add_into(own, own, through, between)
        else:
            add_into(own, own, from_left, from_right)


def gather_tp(wire, spot, out, source):
    across = wire.copy(source, out.at[spot.t], spot.far())
    own = wire.keep(source, out.at[spot.t])
    other = wire.copy(source, out.at[spot.t], spot.core())
    yield
    across.wait()
    there = (1 - spot.yh) * 2 + spot.c
    last = wire.copy(out.at[there], out.at[there], spot.core())
    yield
    own.wait()
    other.wait()
    last.wait()


def gather_y(wire, spot, out, source):
    def view(rows):
        return lambda y: out.at[lax.rem(y, 2), lax.div(y, 2), spot.c, rows]

    rows = source.shape[0] // 2
    own = wire.keep(source, out.at[spot.yl, spot.yh, spot.c])
    other = [own, wire.copy(source, out.at[spot.yl, spot.yh, spot.c], spot.core())]
    cuts = (pl.ds(0, rows), pl.ds(rows, rows))
    units = [(view(cut), half, source.at[cut]) for half, cut in enumerate(cuts)]
    yield from gather_ring(wire, spot.y, spot.along_y(1), spot.along_y(3), units)
    for by in (1, 2, 3):
        y = lax.rem(spot.y + by, 4)
        part = out.at[lax.rem(y, 2), lax.div(y, 2), spot.c]
        other.append(wire.copy(part, part, spot.core()))
    yield
    wait_all(other)


def sum_tp(wire, spot, source, out, got, held, last):
    cores = [wire.copy(source.at[yh * 2 + 1 - spot.c], got.at[yh], spot.core()) for yh in (0, 1)]
    yield
    wait_all(cores)
    there = 1 - spot.yh
    add_into(held, source.at[there * 2 + spot.c], got.at[there])
    across = wire.copy(held, last, spot.far())
    yield
    across.wait()
    add_into(out, source.at[spot.t], got.at[spot.yh], last)


def sum_y(wire, spot, source, out, got, held, through, from_left, from_right):
    cores = [wire.copy(source.at[y % 2, y // 2, 1 - spot.c], got.at[y], spot.core()) for y in range(4)]
    loads = [wire.keep(source.at[y % 2, y // 2, spot.c], held.at[y]) for y in range(4)]
    yield
    for y, made in enumerate(cores):
        made.wait()
        loads[y].wait()
        add_into(held.at[y], held.at[y], got.at[y])
    rows = out.shape[0] // 2
    following, prev = lax.rem(spot.y + 1, 4), lax.rem(spot.y + 3, 4)
    units = []
    for half in (0, 1):
        part = pl.ds(half * rows, rows)
        units.append(
            (
                half,
                lambda y, part=part: held.at[y, part],
                held.at[following if half == 0 else prev, part],
                held.at[spot.y, part],
                through.at[part],
                from_left.at[part],
                from_right.at[part],
                [],
            )
        )
    yield from sum_ring(wire, spot.y, spot.along_y(1), spot.along_y(3), units)
    add_into(out, held.at[spot.y])


def sum_unit(wire, spot, half, part, order, scratch):
    following, prev = (lambda p: lax.rem(p + 1, 4)), (lambda p: lax.rem(p + 3, 4))
    (between, own, through, from_left, from_right), (between2, own2, through2, from_left2, from_right2) = scratch
    near = following if half == 0 else prev
    if order == "zx":
        view, pos, pos2 = (lambda i: part.at[:, i]), spot.z, spot.x
        view2 = lambda i: own.at[:, :, i]
    else:
        view, pos, pos2 = (lambda i: part.at[:, :, :, i]), spot.x, spot.z
        view2 = lambda i: own.at[:, i]

    def loads():
        return [wire.keep(view(near(pos)), between), wire.keep(view(pos), own)]

    def loads2():
        return [wire.keep(view2(near(pos2)), between2), wire.keep(view2(pos2), own2)]

    one = lambda: (half, view, between, own, through, from_left, from_right, loads())
    two = lambda: (half, view2, between2, own2, through2, from_left2, from_right2, loads2())
    return one, two, own2


def sum_chain(wire, spot, order, unit, after, staged=False):
    one, two, total = unit
    x = (spot.x, spot.along_x(1), spot.along_x(3))
    z = (spot.z, spot.along_z(1), spot.along_z(3))
    axes = (z, x) if order == "zx" else (x, z)
    yield from sum_ring(wire, *axes[0], [one()], staged)
    yield from sum_ring(wire, *axes[1], [two()], staged)
    yield from after(total)


def unit_scratch(planes, order, rows, columns):
    first = (planes, 2, 4, rows, columns) if order == "zx" else (planes, 4, 2, rows, columns)
    second = (planes, 2, rows, columns)
    return [pltpu.VMEM(first, BF)] * 5 + [pltpu.VMEM(second, BF)] * 5


def call(kernel, number, outs, ins, scratch, copies, keeps, operands, vmem):
    space = {"hbm": pltpu.HBM, "vmem": pltpu.VMEM}
    return pl.pallas_call(
        kernel,
        out_shape=[jax.ShapeDtypeStruct(shape, dtype) for shape, dtype, _ in outs],
        in_specs=[pl.BlockSpec(memory_space=space[kind]) for kind in ins],
        out_specs=[pl.BlockSpec(memory_space=space[kind]) for _, _, kind in outs],
        scratch_shapes=list(scratch)
        + [
            pltpu.SemaphoreType.DMA((max(copies, 1),)),
            pltpu.SemaphoreType.DMA((max(copies, 1),)),
            pltpu.SemaphoreType.DMA((max(keeps, 1),)),
        ],
        compiler_params=pltpu.CompilerParams(
            collective_id=number, has_side_effects=True, vmem_limit_bytes=vmem * MIB
        ),
    )(*operands)


def tp_sum_scratch(rows, columns):
    return [pltpu.VMEM((2, rows, columns), BF), pltpu.VMEM((rows, columns), BF), pltpu.VMEM((rows, columns), BF)]


def dot(a, b, dims="nn", precision=None):
    left, right = {"nn": (1, 0), "nt": (1, 1), "tn": (0, 0)}[dims]
    return lax.dot_general(
        a, b, (((left,), (right,)), ((), ())), precision=precision, preferred_element_type=F32
    )


def loop(count, body):
    def step(i, carry):
        body(i)
        return carry

    lax.fori_loop(0, count, step, 0)


def at_tile(i, size):
    return pl.ds(pl.multiple_of(i * size, size), size)


def flat(block):
    return block.reshape(-1, block.shape[-1])


def lane_grid(rows, columns):
    return (
        lax.broadcasted_iota(jnp.int32, (rows, columns), 0),
        lax.broadcasted_iota(jnp.int32, (rows, columns), 1),
    )


def head_lanes(values, head):
    lanes = lax.broadcasted_iota(jnp.int32, (1, values.shape[1]), 1)
    return values * (lax.div(lanes, 32) == head).astype(F32).astype(values.dtype)


def all_sum_small(wire, spot, buffers, own):
    steps = (
        [spot.core()],
        [spot.far()],
        [spot.pair()],
        [spot.along_x(1), spot.along_x(2), spot.along_x(3)],
        [spot.along_z(1), spot.along_z(2), spot.along_z(3)],
    )
    for step, devices in enumerate(steps):
        moves = [wire.copy(own.at[step], buffers.at[step, i], device) for i, device in enumerate(devices)]
        yield
        wait_all(moves)
        total = own[step]
        for i in range(len(devices)):
            total = total + buffers[step, i]
        own[step + 1] = total


def ring_pair(wire, spot, first, second):
    x = (spot.x, spot.along_x(1), spot.along_x(3))
    z = (spot.z, spot.along_z(1), spot.along_z(3))

    def unit(part, place):
        ref, half, planes, rows = part[:4]
        lead = () if planes is None else (planes,)
        return (lambda i: ref.at[lead + place(i) + (rows,)], half) + tuple(part[4:])

    def stream(parts, one, place_one, two, place_two):
        yield from gather_ring(wire, *one, [unit(part, place_one) for part in parts])
        yield from gather_ring(wire, *two, [unit(part[:4], place_two) for part in parts])

    every = slice(None)
    yield from together(
        stream(first, x, lambda i: (spot.z, every, i), z, lambda i: (i, every, every)),
        stream(second, z, lambda i: (i, every, spot.x), x, lambda i: (every, every, i)),
    )


def front_kernel(
    downs, q_up, kv_up, out_t, hidden, grad, early, late, small, cosine, sine, seg_col, seg_row, pick_a, pick_b,
    pick_sent,
    o_downs, o_q, o_kv, o_out, o_grad, o_early, o_late, o_tokens,
    o_hat, o_raw, o_qhat, o_kvhat, o_query, o_keyval, o_rope, o_norm, o_heads, o_resid, o_logits, o_small,
    rows, s_downs, s_q, s_kv, s_out, s_hidden, s_hat, s_part, s_raw, s_qlat, s_kvlat, s_query, s_keyval, s_rope,
    s_norm, s_heads, s_attn, s_sum, s_resid, s_sent, s_small, s_buf, t_got, t_held, t_last,
    send, recv, here,
):
    spot, wire = Spot(), Wire(send, recv, here)
    greet(
        spot.rings()
        + [spot.along_x(2), spot.along_z(2), spot.along_y(1), spot.along_y(3)]
        + [spot.core(), spot.far(), spot.diagonal()]
    )
    groups, width = 4 * hidden.shape[0], hidden.shape[1]
    own_rows = hidden.shape[0]
    low, high, every = pl.ds(0, 32), pl.ds(32, 32), slice(None)

    def down_stream():
        mine = rows.at[pl.ds(pl.multiple_of(spot.t * 16, 16), 16)]
        swaps = [wire.keep(downs.at[spot.t], mine)]
        for yh, c, device in (
            (spot.yh, 1 - spot.c, spot.core()),
            (1 - spot.yh, spot.c, spot.far()),
            (1 - spot.yh, 1 - spot.c, spot.diagonal()),
        ):
            swaps.append(wire.copy(downs.at[yh * 2 + c], mine, device))
        yield
        wait_all(swaps)
        place = s_downs.at[spot.z, spot.yl, spot.x]
        moves = [wire.copy(rows, place, spot.pair()), wire.keep(rows, place)]
        yield
        wait_all(moves)
        quarters = [pl.ds(16 * k, 16) for k in range(4)]
        yield from ring_pair(
            wire,
            spot,
            [(s_downs, 0, None, quarters[0]), (s_downs, 1, None, quarters[1])],
            [(s_downs, 0, None, quarters[2]), (s_downs, 1, None, quarters[3])],
        )

    def rest_stream():
        moves = []
        for source, target in ((q_up, s_q), (kv_up, s_kv), (out_t, s_out)):
            place = target.at[spot.z, spot.yl, spot.x]
            moves += [wire.copy(source, place, spot.pair()), wire.keep(source, place)]
        yield
        wait_all(moves)
        yield from ring_pair(
            wire,
            spot,
            [(s_q, 0, None, pl.ds(0, 32)), (s_q, 1, None, pl.ds(32, 16))],
            [(s_out, 0, None, low), (s_out, 1, None, high), (s_kv, 1, None, every)],
        )

    def ffn_stream():
        moves = []
        for source, place in ((early, o_early.at[:, spot.z, spot.yl, spot.x]), (late, o_late.at[:, spot.yl])):
            moves += [wire.copy(source.at[1 - spot.yl], place, spot.pair()), wire.keep(source.at[spot.yl], place)]
        yield
        wait_all(moves)
        two = [pl.ds(2 * k, 2) for k in range(4)]
        yield from ring_pair(
            wire,
            spot,
            [(o_early, 0, two[0], every), (o_early, 1, two[1], every), (o_early, 0, pl.ds(8, 1), low)],
            [(o_early, 0, two[2], every), (o_early, 1, two[3], every), (o_early, 1, pl.ds(8, 1), high)],
        )

    first = down_stream()
    next(first)
    s_small[0] = small[...]
    smalls = all_sum_small(wire, spot, s_buf, s_small)
    next(smalls)
    hiddens = gather_tp(wire, spot, s_hidden, hidden)
    next(hiddens)
    rest = rest_stream()
    for _ in range(3):
        next(first)
        next(smalls)
    next(rest)
    next(hiddens)
    next(first)
    finish(smalls)
    finish(hiddens)
    next(rest)
    next(first)
    ffn = ffn_stream()
    next(ffn)
    gains = s_small[5].astype(F32)
    attn_gain, ffn_gain = gains[8:9], gains[9:10]
    latent_gain = gains[10:11]
    keeps = []

    def norm_rows(i):
        block, part = lax.div(i, 8), at_tile(lax.rem(i, 8), 16)
        values = s_hidden[block, part].astype(F32)
        scale = lax.rsqrt(jnp.mean(values * values, axis=-1, keepdims=True) + norm_eps)
        s_hat[at_tile(i, 16)] = (values * scale * attn_gain).astype(BF)

    loop(groups // 16, norm_rows)
    next(rest)
    finish(first)
    keeps += [wire.keep(s_downs, o_downs), wire.keep(s_hat, o_hat)]

    def down(i):
        j, k = lax.div(i, 2), lax.rem(i, 2)
        lanes = at_tile(j, 128)
        s_part[at_tile(k, 256), lanes] = dot(s_hat[at_tile(k, 256)], flat(s_downs[:, :, :, :, lanes])).astype(BF)

    loop(10, down)
    raws = gather_tp(wire, spot, s_raw, s_part)
    next(raws)
    next(rest)
    next(raws)
    next(rest)
    finish(raws)
    next(ffn)
    grads = gather_y(wire, spot, o_grad, grad)
    next(grads)
    keeps.append(wire.keep(s_raw, o_raw))

    row, lane = lane_grid(128, 128)
    low_pick = (row == lax.rem(lane, 16)) & (lax.rem(lane, 32) < 16)
    high_pick = (row == lax.rem(lane, 16)) & (lax.rem(lane, 32) >= 16)
    low_pick, high_pick = low_pick.astype(F32).astype(BF), high_pick.astype(F32).astype(BF)

    def latents(i):
        part = at_tile(i, 32)
        raw = [s_raw[t, part, 0:384].astype(F32) for t in range(4)]
        total = sum(jnp.sum(v * v, axis=-1, keepdims=True) for v in raw)
        scale = lax.rsqrt(total / 1536.0 + norm_eps)
        for t in range(4):
            s_qlat[part, t * 384 : t * 384 + 384] = (raw[t] * scale * latent_gain[:, t * 384 : t * 384 + 384]).astype(BF)
        raw = [s_raw[t, part, 384:512].astype(F32) for t in range(4)]
        total = sum(jnp.sum(v * v, axis=-1, keepdims=True) for v in raw)
        scale = lax.rsqrt(total / 512.0 + norm_eps)
        for t in range(4):
            gain = latent_gain[:, 1536 + t * 128 : 1664 + t * 128]
            s_kvlat[part, t * 128 : t * 128 + 128] = (raw[t] * scale * gain).astype(BF)
        front = dot(s_raw[0, part, 512:640], low_pick) + dot(s_raw[1, part, 512:640], high_pick)
        back = dot(s_raw[2, part, 512:640], low_pick) + dot(s_raw[3, part, 512:640], high_pick)
        c, s = cosine[part], sine[part]
        s_rope[part, 0:128] = (front * c - back * s).astype(BF)
        s_rope[part, 128:256] = (back * c + front * s).astype(BF)

    loop(groups // 32, latents)

    finish(rest)
    keeps += [wire.keep(a, b) for a, b in ((s_q, o_q), (s_kv, o_kv), (s_out, o_out))]

    def query(i):
        part = at_tile(i, 256)
        for j in range(2):
            lanes = pl.ds(j * 256, 256)
            s_query[part, lanes] = dot(s_qlat[part], flat(s_q[:, :, :, :, lanes])).astype(BF)
        both = dot(s_qlat[part], flat(s_q[:, :, :, :, 512:768]))
        front, back = both[:, 0:128], both[:, 128:256]
        c, s = cosine[part], sine[part]
        s_query[part, 512:640] = (front * c - back * s).astype(BF)
        s_query[part, 640:768] = (back * c + front * s).astype(BF)
        for j in range(4):
            lanes = pl.ds(j * 256, 256)
            s_keyval[part, lanes] = dot(s_kvlat[part], flat(s_kv[:, :, :, :, lanes])).astype(BF)

    loop(2, query)
    next(ffn)

    def attend(i):
        part = at_tile(i, 256)
        places = lax.broadcasted_iota(jnp.int32, (256, groups), 0) + i * 256
        keys = lax.broadcasted_iota(jnp.int32, (256, groups), 1)
        allowed = (seg_col[part] == seg_row[...]) & (keys <= places)
        norms = jnp.zeros((256, 128), F32)
        for head in range(4):
            scores = dot(s_query[part, head * 128 : head * 128 + 128], s_keyval[:, head * 256 : head * 256 + 128], "nt")
            scores += dot(head_lanes(s_query[part, 512:640], head), s_rope[:, 0:128], "nt")
            scores += dot(head_lanes(s_query[part, 640:768], head), s_rope[:, 128:256], "nt")
            scores = jnp.where(allowed, scores * (NOPE + ROPE) ** (-0.5), masked_score)
            peak = jnp.max(scores, axis=-1, keepdims=True)
            raised = jnp.exp(scores - peak)
            total = jnp.sum(raised, axis=-1, keepdims=True)
            probs = (raised / total).astype(BF)
            out = dot(probs, s_keyval[:, head * 256 + 128 : head * 256 + 256])
            s_heads[part, head * 128 : head * 128 + 128] = out.astype(BF)
            lanes = lax.broadcasted_iota(jnp.int32, (256, 128), 1)
            norms = jnp.where(lanes == head, peak + jnp.log(total), norms)
        s_norm[part] = norms

    loop(2, attend)
    next(ffn)
    next(grads)
    keeps += [
        wire.keep(a, b)
        for a, b in (
            (s_qlat, o_qhat), (s_kvlat, o_kvhat), (s_query, o_query), (s_keyval, o_keyval), (s_rope, o_rope),
            (s_norm, o_norm), (s_heads, o_heads),
        )
    ]

    def project(i):
        block, z = lax.div(i, 4), lax.rem(i, 4)
        s_attn[block, :, at_tile(z, 512)] = dot(s_heads[at_tile(block, own_rows)], flat(s_out[z]), "nt").astype(BF)

    loop(16, project)
    sums = sum_tp(wire, spot, s_attn, s_sum, t_got, t_held, t_last)
    finish(sums)

    def residual(i):
        part = at_tile(i, 16)
        values = s_hidden[spot.t, part].astype(F32) + s_sum[part]
        s_resid[part] = values
        scale = lax.rsqrt(jnp.mean(values * values, axis=-1, keepdims=True) + norm_eps)
        normed = values * scale * ffn_gain
        s_sent[part, 0:width] = normed.astype(BF)
        s_sum[part] = normed

    loop(own_rows // 16, residual)
    logits = dot(s_sum[...], gains, "nt", lax.Precision.HIGHEST)
    o_logits[...] = logits
    scores = jax.nn.sigmoid(logits)
    first = jnp.sum(pick_a[...] * scores, axis=-1, keepdims=True)
    second = jnp.sum(pick_b[...] * scores, axis=-1, keepdims=True)
    both = first + second
    dense = pick_a[...] * (route_scale * first / both) + pick_b[...] * (route_scale * second / both)
    s_sent[:, width : width + 128] = jnp.zeros((own_rows, 128), BF)
    s_sent[:, width : width + 16] = (dense + pick_sent[...]).astype(BF)
    o_small[...] = s_small[5]
    keeps.append(wire.keep(s_resid, o_resid))
    sents = gather_y(wire, spot, o_tokens, s_sent)
    next(sents)
    next(grads)
    next(sents)
    next(ffn)
    finish(together(sents, grads))
    finish(ffn)
    wait_all(keeps)


def front(downs, q_up, kv_up, out_t, hidden, grad, early, late, small, cosine, sine, seg_col, seg_row, picks):
    rows, width = hidden.shape
    group, columns = 4 * rows, downs.shape[-1]

    def spread(array):
        return (4, 2, 4) + array.shape[-2:]

    down_spread = (4, 2, 4, 64, columns)
    weights = [down_spread, spread(q_up), spread(kv_up), spread(out_t)]
    outs = [(shape, BF, "hbm") for shape in weights]
    outs.append(((2, 2, 2, rows, width), BF, "hbm"))
    outs.append(((early.shape[1], 4, 2, 4) + early.shape[2:], BF, "hbm"))
    outs.append(((late.shape[1], 2) + late.shape[2:], BF, "hbm"))
    outs.append(((2, 2, 2, rows, width + 128), BF, "hbm"))
    saved = [
        ((group, width), BF), ((4, group, columns), BF), ((group, 1536), BF),
        ((group, 512), BF), ((group, 768), BF), ((group, 1024), BF), ((group, 256), BF), ((group, 128), F32),
        ((group, 512), BF), ((rows, width), F32),
    ]
    outs += [(shape, dtype, "hbm") for shape, dtype in saved]
    outs += [((rows, 16), F32, "vmem"), (small.shape, small.dtype, "vmem")]
    scratch = [pltpu.VMEM((64, columns), BF)] + [pltpu.VMEM(shape, BF) for shape in weights]
    scratch += [
        pltpu.VMEM((4, rows, width), BF),
        pltpu.VMEM((group, width), BF),
        pltpu.VMEM((group, columns), BF),
        pltpu.VMEM((4, group, columns), BF),
        pltpu.VMEM((group, 1536), BF),
        pltpu.VMEM((group, 512), BF),
        pltpu.VMEM((group, 768), BF),
        pltpu.VMEM((group, 1024), BF),
        pltpu.VMEM((group, 256), BF),
        pltpu.VMEM((group, 128), F32),
        pltpu.VMEM((group, 512), BF),
        pltpu.VMEM((4, rows, width), BF),
        pltpu.VMEM((rows, width), F32),
        pltpu.VMEM((rows, width), F32),
        pltpu.VMEM((rows, width + 128), BF),
        pltpu.VMEM((6,) + small.shape, small.dtype),
        pltpu.VMEM((5, 3) + small.shape, small.dtype),
    ] + tp_sum_scratch(rows, width)
    return call(
        front_kernel, 0, outs, ["hbm"] * 4 + ["vmem"] * 12, scratch, 140, 40,
        (downs, q_up, kv_up, out_t, hidden, grad, early, late, small, cosine, sine, seg_col, seg_row) + tuple(picks),
        60,
    )


def swiglu_back(gate, up, d_hidden):
    bell = jax.nn.sigmoid(gate)
    silu = gate * bell
    return silu * up, d_hidden * up * bell * (1.0 + gate * (1.0 - bell)), d_hidden * silu


def ffn_kernel(
    tokens, dy, early, swapped, o_moe, o_back, o_early, o_late,
    s_tok, s_dy, s_in, s_dyr, s_x, s_dg, s_one, s_turned, s_gate, s_gb, s_w, s_late, s_g, s_h, s_d1, s_d2, s_ch, s_c1, s_c2,
    load, fetched, stored, done, send, recv, here,
):
    spot, wire = Spot(), Wire(send, recv, here)
    greet(spot.rings())
    capacity, slots, width = s_one.shape[1] // 4, s_one.shape[1], dy.shape[1]
    groups = s_tok.shape[0] // 2
    first = spot.yl * 4
    zs = 4
    step = width // zs

    def late_stream():
        kept = wire.keep(swapped, s_late.at[:, spot.z, :, spot.x])
        low, high, every = pl.ds(0, 32), pl.ds(32, 32), slice(None)

        def part(half, plane, rows):
            planes = pl.ds(plane, 1)
            return (s_late, half, planes, rows, swapped.at[planes, :, rows])

        rings = ring_pair(
            wire,
            spot,
            [part(0, 0, every), part(1, 1, every), part(0, 2, low), part(1, 2, high)],
            [part(0, 3, every), part(1, 4, every), part(0, 5, low), part(1, 5, high)],
        )
        next(rings)
        yield
        next(rings)
        kept.wait()
        yield
        yield from rings

    weights = late_stream()
    next(weights)

    slot_of = {0: 0, 1: 1, 2: 0, 4: 1, 3: 0}

    def fetch(e):
        slot = slot_of[e]
        return [pltpu.make_async_copy(early.at[3 * e + k], s_w.at[slot, k], fetched.at[slot, k]) for k in range(3)]

    def store(e):
        slot = slot_of[e]
        out = {3: o_late.at[pl.ds(0, 3)], 4: o_late.at[pl.ds(3, 3)]}.get(e)
        out = o_early.at[pl.ds(3 * e, 3)] if out is None else out
        return [pltpu.make_async_copy(s_g.at[slot, k], out.at[k], stored.at[slot, k]) for k in range(3)]

    def start(copies):
        for copy in copies:
            copy.start()

    loads = [pltpu.make_async_copy(tokens, s_tok, load.at[0]), pltpu.make_async_copy(dy, s_dy, load.at[1])]
    start(loads)
    start(fetch(0))
    loads[0].wait()

    row, lane = lane_grid(groups, groups)
    before = (row < lane).astype(F32).astype(BF)
    after = (lane < row).astype(F32).astype(BF)
    same = (lane == row).astype(F32).astype(BF)
    slot_row, _ = lane_grid(capacity, groups)
    turned_row, turned_lane = lane_grid(groups, slots)
    for g in range(2):
        extra = s_tok[g * groups : (g + 1) * groups, width : width + 128]
        flipped = dot(extra, same, "tn")
        gates = jnp.where(first == 0, flipped[0:4], flipped[4:8])
        masks = jnp.where(first == 0, flipped[8:12], flipped[12:16])
        padded = jnp.concatenate([masks, jnp.zeros((12, groups), F32)], axis=0)
        place = dot(padded.astype(BF), before)
        place = jnp.where(padded > 0, place, -1.0).astype(jnp.int32)
        for e in range(4):
            taken = place[e : e + 1] == slot_row
            rows = slice(e * capacity, (e + 1) * capacity)
            s_one[g, rows] = taken.astype(F32).astype(BF)
            s_gate[g, rows] = jnp.sum(jnp.where(taken, gates[e : e + 1], 0.0), axis=-1, keepdims=True)
        place = dot(after, extra)
        place = jnp.where(extra.astype(F32) > 0, place, -1.0)
        columns = jnp.where(first == 0, place[:, 8:12], place[:, 12:16]).astype(jnp.int32)
        wanted = jnp.full((groups, slots), -2, jnp.int32)
        for e in range(4):
            wanted = jnp.where(lax.div(turned_lane, capacity) == e, columns[:, e : e + 1], wanted)
        s_turned[g] = (wanted == lax.rem(turned_lane, capacity)).astype(F32).astype(BF)
    loads[1].wait()

    def dispatch(i):
        g, lanes = lax.div(i, zs), at_tile(lax.rem(i, zs), step)
        rows = at_tile(g, groups)
        s_in[g, :, lanes] = dot(s_one[g], s_tok[rows, lanes]).astype(BF)
        s_dyr[g, :, lanes] = dot(s_one[g], s_dy[rows, lanes]).astype(BF)

    loop(2 * zs, dispatch)
    next(weights)

    def expert(e, ahead, after_act, after_all):
        slot = slot_of[e]
        mine = pl.ds(e * capacity, capacity)
        if e < 3:
            wait_all(fetch(e))
        w_gate, w_up, w_down = (s_w.at[slot, k] if e < 3 else s_late.at[k] for k in range(3))
        if ahead is not None:
            start(fetch(ahead))

        def place(i):
            lanes = at_tile(i, step)
            for g in range(2):
                rows = slice(g * capacity, (g + 1) * capacity)
                s_x[rows, lanes] = s_in[g, mine, lanes]
                s_dg[rows, lanes] = (s_gate[g, mine] * s_dyr[g, mine, lanes].astype(F32)).astype(BF)

        loop(zs, place)
        gate, up = dot(s_x[...], flat(w_gate[...])), dot(s_x[...], flat(w_up[...]))
        hidden, d_gate, d_up = swiglu_back(gate, up, dot(s_dg[...], flat(w_down[...])))
        s_h[...], s_d1[...], s_d2[...] = hidden.astype(BF), d_gate.astype(BF), d_up.astype(BF)
        if after_act:
            next(weights)
        if e >= 2:
            wait_all(store({2: 0, 3: 2}[e]))

        def sums(i):
            lanes = at_tile(i, step)
            s_g[slot, 0, lanes] = dot(s_x[:, lanes], s_d1[...], "tn").astype(BF)
            s_g[slot, 1, lanes] = dot(s_x[:, lanes], s_d2[...], "tn").astype(BF)
            s_g[slot, 2, lanes] = dot(s_dg[:, lanes], s_h[...], "tn").astype(BF)

        loop(zs, sums)
        start(store(e))
        s_gb[...] = jnp.zeros_like(s_gb)

        def outward(i):
            lanes = at_tile(i, step)
            out = dot(s_h[...], flat(w_down[i]), "nt")
            back = dot(s_d1[...], flat(w_gate[i]), "nt") + dot(s_d2[...], flat(w_up[i]), "nt")
            for g in range(2):
                rows = slice(g * capacity, (g + 1) * capacity)
                s_gb[rows] += jnp.sum(out[rows] * s_dyr[g, mine, lanes].astype(F32), axis=-1, keepdims=True)
                s_dyr[g, mine, lanes] = (s_gate[g, mine] * out[rows]).astype(BF)
                s_in[g, mine, lanes] = back[rows].astype(BF)

        loop(zs, outward)
        extra_lane = lax.broadcasted_iota(jnp.int32, (capacity, 128), 1)
        for g in range(2):
            rows = slice(g * capacity, (g + 1) * capacity)
            s_in[g, mine, width : width + 128] = jnp.where(extra_lane == first + e, s_gb[rows], 0.0).astype(BF)
        if after_all:
            next(weights)

    expert(0, 1, True, False)
    expert(1, 2, False, False)
    expert(2, None, True, False)
    finish(weights)


    def common(i):
        rows = at_tile(i, 256)
        inputs = s_tok[rows, 0:width]
        gate, up = dot(inputs, flat(s_late[3])), dot(inputs, flat(s_late[4]))
        hidden, d_gate, d_up = swiglu_back(gate, up, dot(s_dy[rows], flat(s_late[5])))
        s_ch[rows], s_c1[rows], s_c2[rows] = hidden.astype(BF), d_gate.astype(BF), d_up.astype(BF)

    loop(2 * groups // 256, common)
    wait_all(store(1))

    def common_sums(i):
        lanes = at_tile(i, step)
        s_g[1, 0, lanes] = dot(s_tok[:, lanes], s_c1[...], "tn").astype(BF)
        s_g[1, 1, lanes] = dot(s_tok[:, lanes], s_c2[...], "tn").astype(BF)
        s_g[1, 2, lanes] = dot(s_dy[:, lanes], s_ch[...], "tn").astype(BF)

    loop(zs, common_sums)
    start(store(4))
    expert(3, None, False, False)

    def combine(i):
        g, z = lax.div(i, zs), lax.rem(i, zs)
        rows, lanes = at_tile(g, groups), at_tile(z, step)
        out = dot(s_ch[rows], flat(s_late[5, z]), "nt") + dot(s_turned[g], s_dyr[g, :, lanes])
        s_dy[rows, lanes] = out.astype(BF)
        back = dot(s_c1[rows], flat(s_late[3, z]), "nt") + dot(s_c2[rows], flat(s_late[4, z]), "nt")
        s_tok[rows, lanes] = (back + dot(s_turned[g], s_in[g, :, lanes])).astype(BF)

    loop(2 * zs, combine)
    for g in range(2):
        rows = slice(g * groups, (g + 1) * groups)
        s_tok[rows, width : width + 128] = dot(s_turned[g], s_in[g, :, width : width + 128]).astype(BF)
    ends = [pltpu.make_async_copy(s_dy, o_moe, done.at[0]), pltpu.make_async_copy(s_tok, o_back, done.at[1])]
    start(ends)
    wait_all(store(4))
    wait_all(store(3))
    wait_all(ends)


def ffn(tokens, dy, early, swapped, capacity):
    rows, width = dy.shape
    wide = tokens.shape[1]
    tile = early.shape[-2:]
    units = tile[1]
    outs = [(rows, width), (rows, wide), (early.shape[0], width, units), (swapped.shape[0], width, units)]
    sizes = [
        ((rows, wide), BF), ((rows, width), BF), ((2, 4 * capacity, wide), BF), ((2, 4 * capacity, width), BF),
        ((2 * capacity, width), BF), ((2 * capacity, width), BF), ((2, 4 * capacity, rows // 2), BF),
        ((2, rows // 2, 4 * capacity), BF), ((2, 4 * capacity, 1), F32), ((2 * capacity, 1), F32),
        ((2, 3, 4, 2, 4) + tile, BF), ((6, 4, 2, 4) + tile, BF), ((2, 3, width, units), BF),
        ((2 * capacity, units), BF), ((2 * capacity, units), BF), ((2 * capacity, units), BF),
        ((rows, units), BF), ((rows, units), BF), ((rows, units), BF),
    ]
    scratch = [pltpu.VMEM(*size) for size in sizes]
    scratch += [pltpu.SemaphoreType.DMA(n) for n in ((2,), (2, 3), (2, 3), (2,))]
    return call(
        ffn_kernel, 3, [(shape, BF, "hbm") for shape in outs], ["hbm"] * 4, scratch, 48, 1,
        (tokens, dy, early, swapped), 62,
    )


def back_kernel(
    early, late, part, attn_in, heads, out_w, up_q, up_kv, downs, query, keyval, rope, norms, qlat, kvlat, raw,
    resid, logits, pick_a, pick_b, grad, gains, cosine, sine, seg_col, seg_row,
    o_early, o_late, o_gout, o_gq, o_gkv, o_gdown, o_attn, o_resid, o_small, o_q, o_kv, o_out,
    *rest,
):
    landing, rest = list(rest[:32]), rest[32:]
    scratch, (send, recv, here) = list(rest[:-3]), rest[-3:]
    spot, wire = Spot(), Wire(send, recv, here)
    greet(spot.rings() + [spot.along_y(1), spot.along_y(3), spot.core(), spot.far(), spot.diagonal()])
    own_rows, width = grad.shape
    groups = 4 * own_rows

    def take(count):
        taken, scratch[:] = scratch[:count], scratch[count:]
        return taken

    def unit(half, ref, order):
        rings = [take(3) + [landing.pop(0), landing.pop(0)] for _ in range(2)]
        return sum_unit(wire, spot, half, ref, order, rings)

    def swap_to(place):
        def after(total):
            moves = [wire.copy(total.at[:, 1 - spot.yl], place, spot.pair()), wire.keep(total.at[:, spot.yl], place)]
            yield
            wait_all(moves)

        return after

    def sum_to(got, out):
        def after(total):
            move = wire.copy(total.at[:, 1 - spot.yl], got, spot.pair())
            yield
            move.wait()
            add_into(out, total.at[0, spot.yl], got.at[0])

        return after

    chains = []
    for half, source, out, planes, order in (
        (0, early, o_early, pl.ds(0, 4), "zx"),
        (0, late, o_late, pl.ds(0, 3), "xz"),
        (1, early, o_early, pl.ds(4, 4), "zx"),
        (1, late, o_late, pl.ds(3, 3), "xz"),
        (0, early, o_early, pl.ds(8, 1), "xz"),
    ):
        made = unit(half, source.at[planes], order)
        chains.append(sum_chain(wire, spot, order, made, swap_to(out.at[spot.yl, planes]), True))
    unit_q, unit_kv, unit_out = unit(0, o_gq, "zx"), unit(1, o_gkv, "xz"), unit(0, o_gout, "xz")
    got_q, got_kv, got_out = take(3)
    tokens = take(5)
    (s_back, s_heads, s_wide, s_upq, s_upkv, s_query, s_keyval, s_rope, s_norms, s_qlat, s_kvlat, s_raw) = take(12)
    (s_normed, s_dh, s_dhall, s_dheads, s_accq, s_acck, s_dkn, s_dv) = take(8)
    s_resid, s_lat = s_back.at[:, pl.ds(0, width)], s_back
    s_flow, q_at = tokens[0], 1024
    (s_swap, s_got, s_stage, s_attn, s_small) = take(5)
    t_scratch = take(3)
    s_part = tokens[1]
    sums = sum_y(wire, spot, part, s_back, *tokens)
    next(sums)
    ffn = together(*chains)
    next(ffn)
    loads = [wire.keep(a, b) for a, b in ((heads, s_heads), (out_w, s_wide.at[:, pl.ds(0, 512)]))]
    others = [
        wire.keep(a, b)
        for a, b in (
            (query, s_query), (keyval, s_keyval), (rope, s_rope), (norms, s_norms), (qlat, s_qlat), (kvlat, s_kvlat),
            (up_q, s_upq), (up_kv, s_upkv), (raw.at[:, pl.ds(pl.multiple_of(spot.t * own_rows, 128), own_rows)], s_raw),
        )
    ]
    finish(sums)

    rows_f32 = gains[...].astype(F32)
    ffn_gain = rows_f32[9:10]
    dense = s_back[:, width : width + 16]
    scores = jax.nn.sigmoid(logits[...])
    first = jnp.sum(pick_a[...] * scores, axis=-1, keepdims=True)
    second = jnp.sum(pick_b[...] * scores, axis=-1, keepdims=True)
    both = first + second
    apart = jnp.sum((pick_a[...] - pick_b[...]) * dense, axis=-1, keepdims=True) * route_scale / both
    d_scores = (pick_a[...] * (second / both) - pick_b[...] * (first / both)) * apart
    d_logits = d_scores * scores * (1.0 - scores)
    s_normed[...] = dot(d_logits, rows_f32, "nn", lax.Precision.HIGHEST)
    s_small[0:1] = jnp.zeros((1, width), F32)

    def own_row(i):
        rows = at_tile(i, 16)
        values = resid[rows]
        scale = lax.rsqrt(jnp.mean(values * values, axis=-1, keepdims=True) + norm_eps)
        hat = values * scale
        grad_ffn = s_normed[rows] + s_back[rows, 0:width]
        s_small[0:1] += jnp.sum(grad_ffn * hat, axis=0, keepdims=True)
        weighted = grad_ffn * ffn_gain
        inner = scale * (weighted - hat * jnp.mean(weighted * hat, axis=-1, keepdims=True))
        total = grad[rows].astype(F32) + inner
        s_resid[rows] = total
        s_dh[rows] = total.astype(BF)
        s_normed[rows] = hat * ffn_gain

    loop(own_rows // 16, own_row)
    keeps = []
    resid_kept = wire.keep(s_resid, o_resid)
    swap = gather_tp(wire, spot, s_dhall, s_dh)
    next(swap)
    next(swap)
    o_small[...] = dot(d_logits, s_normed[...], "tn", lax.Precision.HIGHEST)
    o_small[9:10] = s_small[0:1]
    finish(swap)

    wait_all(loads)

    def out_grads(i):
        lanes = at_tile(i, 512)
        block = dot(flat(s_dhall[:, :, lanes]), s_heads[...], "tn").astype(BF)
        s_stage[i, :, :, :, 0:512] = block.reshape(2, 4, 64, 512)

    loop(4, out_grads)
    staged = wire.keep(s_stage.at[:, :, :, :, pl.ds(0, 512)], o_gout.at[0])
    chain_out = sum_chain(wire, spot, "xz", unit_out, sum_to(got_out, o_out), True)

    def head_grads(i):
        s_dheads[at_tile(i, own_rows)] = dot(s_dhall[i], s_wide[:, 0:512]).astype(BF)

    loop(4, head_grads)
    wait_all(others)
    late_loads = [wire.keep(attn_in.at[pl.ds(t * own_rows, own_rows)], s_dhall.at[t]) for t in range(4)]
    late_loads.append(wire.keep(downs, s_wide))
    s_accq[...] = jnp.zeros_like(s_accq)
    s_acck[...] = jnp.zeros_like(s_acck)

    for head in range(4):
        nope, value = pl.ds(head * 256, 128), pl.ds(head * 256 + 128, 128)
        at = pl.ds(head * 128, 128)
        s_dkn[...] = jnp.zeros_like(s_dkn)
        s_dv[...] = jnp.zeros_like(s_dv)

        def attend(i, head=head, nope=nope, value=value, at=at):
            tile = at_tile(i, 256)
            places = lax.broadcasted_iota(jnp.int32, (256, groups), 0) + i * 256
            keys = lax.broadcasted_iota(jnp.int32, (256, groups), 1)
            allowed = (seg_col[tile] == seg_row[...]) & (keys <= places)
            front, back = head_lanes(s_query[tile, 512:640], head), head_lanes(s_query[tile, 640:768], head)
            scores = dot(s_query[tile, at], s_keyval[:, nope], "nt")
            scores += dot(front, s_rope[:, 0:128], "nt")
            scores += dot(back, s_rope[:, 128:256], "nt")
            scores = jnp.where(allowed, scores * (NOPE + ROPE) ** (-0.5), masked_score)
            probs = jnp.exp(scores - s_norms[tile, head : head + 1])
            d_head = s_dheads[tile, at]
            s_dv[...] += dot(probs.astype(BF), d_head, "tn")
            d_probs = dot(d_head, s_keyval[:, value], "nt")
            row_dot = jnp.sum(probs * d_probs, axis=-1, keepdims=True)
            d_scores = (probs * (d_probs - row_dot) * (NOPE + ROPE) ** (-0.5)).astype(BF)
            d_query = dot(d_scores, s_keyval[:, nope]).astype(BF)
            s_flow[pl.ds(2 * i, 2), :, pl.ds(q_at + head * 128, 128)] = d_query.reshape(2, own_rows, 128)
            s_accq[tile, 0:128] += head_lanes(dot(d_scores, s_rope[:, 0:128]), head)
            s_accq[tile, 128:256] += head_lanes(dot(d_scores, s_rope[:, 128:256]), head)
            s_dkn[...] += dot(d_scores, s_query[tile, at], "tn")
            s_acck[:, 0:128] += dot(d_scores, front, "tn")
            s_acck[:, 128:256] += dot(d_scores, back, "tn")

        loop(2, attend)
        s_flow[:, :, nope] = s_dkn[...].astype(BF).reshape(4, own_rows, 128)
        s_flow[:, :, value] = s_dv[...].astype(BF).reshape(4, own_rows, 128)
    next(ffn)

    row, lane = lane_grid(128, 128)
    fold_front = ((lane < 32) & (lane == lax.rem(row, 32))).astype(F32)
    fold_back = ((lane >= 32) & (lane < 64) & (lane - 32 == lax.rem(row, 32))).astype(F32)

    def unrotate(i):
        rows = at_tile(i, own_rows)
        c, s = cosine[rows], sine[rows]
        front, back = s_accq[rows, 0:128], s_accq[rows, 128:256]
        s_flow[i, :, q_at + 512 : q_at + 640] = (front * c + back * s).astype(BF)
        s_flow[i, :, q_at + 640 : q_at + 768] = (back * c - front * s).astype(BF)
        front, back = s_acck[rows, 0:128], s_acck[rows, 128:256]
        folded = dot(front * c + back * s, fold_front, "nn", lax.Precision.HIGHEST)
        folded += dot(back * c - front * s, fold_back, "nn", lax.Precision.HIGHEST)
        s_part[i, :, 2048:2176] = folded.astype(BF)
        for j in range(3):
            lanes = slice(j * 512, j * 512 + 512)
            s_part[i, :, lanes] = dot(s_flow[i, :, q_at : q_at + 768], s_upq[lanes], "nt").astype(BF)
        s_part[i, :, 1536:2048] = dot(s_flow[i, :, 0:1024], s_upkv[...], "nt").astype(BF)

    loop(4, unrotate)
    resid_kept.wait()
    latents = sum_tp(wire, spot, s_part, s_lat, *t_scratch)
    next(latents)
    staged.wait()
    next(chain_out)

    def q_grads(i):
        block = dot(s_qlat[:, at_tile(i, 384)], flat(s_flow[:, :, q_at : q_at + 768]), "tn").astype(BF)
        s_stage[i, :, :, 0:48] = block.reshape(2, 4, 48, 768)

    loop(4, q_grads)
    staged = wire.keep(s_stage.at[:, :, :, pl.ds(0, 48)], o_gq.at[0])
    next(latents)

    def kv_grads(i):
        block = dot(s_kvlat[:, at_tile(i, 128)], flat(s_flow[:, :, 0:1024]), "tn").astype(BF)
        s_attn[i, :, :, :, 0:1024] = block.reshape(2, 4, 16, 1024)

    loop(4, kv_grads)
    staged_kv = wire.keep(s_attn.at[:, :, :, :, pl.ds(0, 1024)], o_gkv.at[0])
    finish(latents)

    gain = rows_f32[10:11]
    s_small[...] = jnp.zeros_like(s_small)

    def latent_row(i):
        rows = at_tile(i, 32)
        for cut, columns, start in ((slice(0, 384), 384, 0), (slice(384, 512), 128, 1536)):
            size = 4.0 * columns
            values = [s_raw[t, rows, cut].astype(F32) for t in range(4)]
            scale = lax.rsqrt(sum(jnp.sum(v * v, axis=-1, keepdims=True) for v in values) / size + norm_eps)
            hats = [v * scale for v in values]
            grads, weighted = [], []
            for t in range(4):
                at = slice(start + t * columns, start + (t + 1) * columns)
                grads.append(s_lat[rows, at])
                weighted.append(grads[t] * gain[:, at])
                s_small[0:1, at] += jnp.sum(grads[t] * hats[t], axis=0, keepdims=True)
            inner = sum(jnp.sum(w * h, axis=-1, keepdims=True) for w, h in zip(weighted, hats)) / size
            for t in range(4):
                s_swap[t, rows, cut] = (scale * (weighted[t] - hats[t] * inner)).astype(BF)
        folded = s_lat[rows, 2048:2176].astype(BF)
        for t in range(4):
            pick = ((row == t * 16 + lane) & (lane < 16)).astype(F32).astype(BF)
            s_swap[t, rows, 512:640] = dot(folded, pick).astype(BF)

    loop(own_rows // 32, latent_row)
    moves = [wire.keep(s_swap.at[spot.t], s_got.at[spot.t])]
    for yh, c, device in (
        (spot.yh, 1 - spot.c, spot.core()),
        (1 - spot.yh, spot.c, spot.far()),
        (1 - spot.yh, 1 - spot.c, spot.diagonal()),
    ):
        moves.append(wire.copy(s_swap.at[yh * 2 + c], s_got.at[spot.t], device))
    o_small[10:11] = s_small[0:1]
    s_small[0:1] = jnp.zeros((1, width), F32)
    wait_all(moves)
    wait_all(late_loads)
    staged.wait()
    staged_kv.wait()
    next(ffn)
    heads_left = [
        chain_out,
        sum_chain(wire, spot, "zx", unit_q, sum_to(got_q, o_q), True),
        sum_chain(wire, spot, "xz", unit_kv, sum_to(got_kv, o_kv), True),
    ]
    head_sums = together(*heads_left)
    next(head_sums)

    def down_grads(i):
        lanes = at_tile(i, 512)
        block = dot(flat(s_dhall[:, :, lanes]), flat(s_got[...]), "tn").astype(BF)
        s_stage[i, :, :, :, 0:640] = block.reshape(2, 4, 64, 640)

    loop(4, down_grads)
    staged = wire.keep(s_stage.at[:, :, :, :, pl.ds(0, 640)], o_gdown)

    def attn_grads(i):
        rows, lanes = lax.div(i, 4), at_tile(lax.rem(i, 4), 512)
        back = dot(s_got[rows], s_wide[lanes], "nt")
        s_attn[rows, :, :, :, lanes] = back.astype(BF).reshape(2, 4, 16, 512)
        s_small[0:1, lanes] += jnp.sum(back * s_dhall[rows, :, lanes].astype(F32), axis=0, keepdims=True)

    loop(16, attn_grads)
    o_small[8:9] = s_small[0:1] / rows_f32[8:9]
    keeps.append(wire.keep(s_attn, o_attn))
    finish(together(ffn, head_sums))
    staged.wait()
    wait_all(keeps)


def back(ffn_grads, part, saved, resid, logits, picks, grad, gains, cosine, sine, seg_col, seg_row):
    rows, width = grad.shape
    group = 4 * rows
    outs = [((2, a.shape[0]) + a.shape[4:], BF, "hbm") for a in ffn_grads]
    spread = [(1, 4, 2, 4) + block for block in ((64, 512), (48, 768), (16, 1024))]
    outs += [(shape, BF, "hbm") for shape in spread + [(4, 2, 4, 64, 640), (4, 2, 4, 16, width)]]
    outs += [ ((rows, width), F32, "hbm"), ((16, width), F32, "vmem")]
    head_tiles = [(48, 768), (16, 1024), (64, 512)]
    outs += [(shape, F32, "vmem") for shape in head_tiles]
    scratch = []
    tile = ffn_grads[0].shape[4:]
    units = [(4, "zx", tile), (3, "xz", tile), (4, "zx", tile), (3, "xz", tile), (1, "xz", tile)]
    units += [(1, order, shape) for order, shape in zip(("zx", "xz", "xz"), head_tiles)]
    for planes, order, block in units:
        first = (planes, 2, 4) + block if order == "zx" else (planes, 4, 2) + block
        second = (planes, 2) + block
        outs += [(first, BF, "hbm")] * 2 + [(second, BF, "hbm")] * 2
        scratch += [pltpu.VMEM(first, BF)] * 3 + [pltpu.VMEM(second, BF)] * 3
    scratch += [pltpu.VMEM((1,) + shape, BF) for shape in head_tiles]
    columns = part.shape[-1]
    scratch += [pltpu.VMEM((4, rows, columns), BF)] * 2 + [pltpu.VMEM((rows, columns), BF)] * 3
    sizes = [
        ((rows, columns), F32), ((group, 512), BF), ((width, 640), BF), ((1536, 768), BF), ((512, 1024), BF),
        ((group, 768), BF), ((group, 1024), BF), ((group, 256), BF), ((group, 128), F32), ((group, 1536), BF),
        ((group, 512), BF), ((4, rows, 640), BF),
        ((rows, width), F32), ((rows, width), BF), ((4, rows, width), BF), ((group, 512), BF),
        ((group, 256), F32), ((group, 256), F32), ((group, 128), F32), ((group, 128), F32),
        ((4, rows, 640), BF), ((4, rows, 640), BF), ((4, 2, 4, 64, 768), BF), ((4, 2, 4, 16, width), BF), ((8, width), F32),
    ]
    scratch += [pltpu.VMEM(*size) for size in sizes] + tp_sum_scratch(rows, columns)
    return call(
        back_kernel, 1, outs, ["hbm"] * 16 + ["vmem"] * 10, scratch, 120, 120,
        tuple(ffn_grads) + (part,) + tuple(saved) + (resid, logits) + tuple(picks)
        + (grad, gains, cosine, sine, seg_col, seg_row),
        63,
    )[:12]


def last_kernel(downs, part, moe, small, o_downs, o_part, o_moe, o_small, *rest):
    scratch, (send, recv, here) = list(rest[:-3]), rest[-3:]
    spot, wire = Spot(), Wire(send, recv, here)
    greet(
        spot.rings()
        + [spot.along_x(2), spot.along_z(2), spot.along_y(1), spot.along_y(3)]
        + [spot.core(), spot.far(), spot.diagonal()]
    )

    def take(count):
        taken, scratch[:] = scratch[:count], scratch[count:]
        return taken

    def chain(half, columns, order):
        got, rows = take(2)
        cut = lambda t: rows.at[pl.ds(pl.multiple_of(t * 16, 16), 16)]

        def after(total):
            move = wire.copy(total.at[:, 1 - spot.yl], got, spot.pair())
            yield
            move.wait()
            add_into(rows, total.at[0, spot.yl], got.at[0])
            swaps = [wire.keep(cut(spot.t), o_downs.at[spot.t, :, columns])]
            for yh, c, device in (
                (spot.yh, 1 - spot.c, spot.core()),
                (1 - spot.yh, spot.c, spot.far()),
                (1 - spot.yh, 1 - spot.c, spot.diagonal()),
            ):
                swaps.append(wire.copy(cut(yh * 2 + c), o_downs.at[spot.t, :, columns], device))
            yield
            wait_all(swaps)

        made = sum_unit(wire, spot, half, downs.at[:, :, :, :, :, columns], order, (take(5), take(5)))
        return sum_chain(wire, spot, order, made, after)

    tokens, ring = take(3), take(5)
    s_small, s_buf = take(2)
    s_small[0] = small[...]
    cuts = last_cuts(downs.shape[-1])
    finish(
        together(
            *[chain(half, pl.ds(start, size), order) for half, start, size, order in cuts],
            sum_tp(wire, spot, part, o_part, *tokens),
            all_sum_small(wire, spot, s_buf, s_small),
            sum_y(wire, spot, moe, o_moe, *ring),
        )
    )
    o_small[...] = s_small[5]


def last_cuts(columns):
    return ((0, 0, 128, "zx"), (1, 128, 128, "zx"), (0, 256, 128, "xz"), (1, 384, columns - 384, "xz"))


def last(downs, part, moe, small):
    rows, columns = part.shape[1:]
    scratch = tp_sum_scratch(rows, columns)
    scratch += [pltpu.VMEM((4, rows, columns), BF)] * 2 + [pltpu.VMEM((rows, columns), BF)] * 3
    scratch += [pltpu.VMEM((6,) + small.shape, F32), pltpu.VMEM((5, 3) + small.shape, F32)]
    height = downs.shape[-2]
    for _, _, size, order in last_cuts(downs.shape[-1]):
        scratch += [pltpu.VMEM((1, height, size), BF), pltpu.VMEM((height, size), BF)]
        scratch += unit_scratch(1, order, height, size)
    outs = [((4, 16, downs.shape[-1]), BF, "hbm")]
    outs += [((rows, columns), F32, "vmem")] * 2 + [(small.shape, F32, "vmem")]
    return call(
        last_kernel, 2, outs, ["hbm", "vmem", "hbm", "vmem"], scratch, 72, 32, (downs, part, moe, small), 50
    )


def rotary_tables(position):
    half_size = ROPE // 2
    inverse = theta_base ** (-(2.0 * jnp.arange(half_size, dtype=F32)) / ROPE)
    angles = position.astype(F32)[:, None] * inverse[None, :]
    return (jnp.cos(angles), jnp.sin(angles))


def packing(lengths, total_rows):
    positions = jnp.arange(total_rows, dtype=jnp.int32)
    endings = jnp.cumsum(lengths)
    segment = jnp.sum((positions[:, None] >= endings[None, :]).astype(jnp.int32), axis=1)
    starting = endings - lengths
    owner_mask = segment[:, None] == jnp.arange(lengths.shape[0], dtype=jnp.int32)[None, :]
    first_row = jnp.sum(jnp.where(owner_mask, starting[None, :], 0), axis=1)
    return (segment, positions - first_row)


def normalized(values):
    scale = lax.rsqrt(jnp.mean(values * values, axis=-1, keepdims=True) + norm_eps)
    return values * scale, scale


def norm_back(grad, gain, hat, scale):
    weighted = grad * gain
    return scale * (weighted - hat * jnp.mean(weighted * hat, axis=-1, keepdims=True))


def per_device(
    hidden_in,
    out_grad,
    attn_gain,
    q_down,
    q_gain,
    kv_down,
    kv_gain,
    q_up,
    kv_up,
    out_proj,
    ffn_gain,
    router,
    routed_gate_up,
    routed_down,
    shared_gate_up,
    shared_down,
    choices,
    seq_lens,
):
    local_rows, width = hidden_in.shape
    group_rows = choices.shape[0]
    tp_count = lax.axis_size("tp")
    tp_index = lax.axis_index("tp")
    y_lo = lax.rem(lax.div(lax.axis_index("fsdp"), 4), 2)
    head_count = HEADS // tp_count
    experts = router.shape[1]
    held = experts // 2
    capacity = 5 * group_rows * TOPK // (4 * experts)
    units = routed_gate_up.shape[3]
    row_shard = routed_gate_up.shape[1]
    q_cols = q_down.shape[1] // tp_count
    raw_cols = q_cols + kv_down.shape[1] // tp_count
    raw_pad = -raw_cols % 128
    small_at = raw_cols + raw_pad

    def own(array):
        return lax.dynamic_slice_in_dim(array, tp_index * local_rows, local_rows)

    down_rows = q_down.shape[0]
    devices = width // down_rows
    device = lax.axis_index("fsdp") * tp_count + tp_index
    rope_cols = ROPE // tp_count
    columns = jnp.concatenate(
        [
            q_down.reshape(down_rows, tp_count, q_cols),
            kv_down[:, :KVR].reshape(down_rows, tp_count, KVR // tp_count),
            kv_down[:, KVR:].reshape(down_rows, tp_count, rope_cols),
        ],
        axis=-1,
    ).transpose(1, 0, 2)
    downs = jnp.pad(columns, ((0, 0), (0, 0), (0, raw_pad)))
    half = ROPE // 2
    q_rows = q_up.reshape(-1, head_count, NOPE + ROPE)
    q_sent = jnp.concatenate(
        [
            q_rows[..., :NOPE].reshape(-1, head_count * NOPE),
            q_rows[..., NOPE : NOPE + half].reshape(-1, head_count * half),
            q_rows[..., NOPE + half :].reshape(-1, head_count * half),
        ],
        axis=1,
    )
    small = jnp.zeros((16, width), BF)
    vectors = jnp.concatenate([router.T, attn_gain[None], ffn_gain[None]], axis=0)
    small = lax.dynamic_update_slice(small, vectors, (0, device * down_rows))
    small = lax.dynamic_update_slice(small, q_gain[None], (experts + 2, device * q_gain.shape[0]))
    kv_at = q_down.shape[1] + device * kv_gain.shape[0]
    small = lax.dynamic_update_slice(small, kv_gain[None], (experts + 2, kv_at))
    gate_up = routed_gate_up.transpose(0, 2, 1, 3)
    down_t = routed_down.transpose(0, 2, 1)[:, None]
    routed = jnp.concatenate([gate_up, down_t], axis=1).reshape(2, held, 3, row_shard, units)
    shared = jnp.concatenate(
        [
            shared_gate_up.reshape(row_shard, 2, 2, units).transpose(2, 1, 0, 3),
            shared_down.T.reshape(row_shard, 2, units).transpose(1, 0, 2)[:, None],
        ],
        axis=1,
    )
    early = routed[:, : held - 1].reshape(2, 3 * (held - 1), row_shard, units)
    late = jnp.concatenate([routed[:, held - 1], shared], axis=1)

    segment, position = packing(seq_lens[0], group_rows)
    cosine, sine_table = rotary_tables(position)
    cos_heads, sin_heads = jnp.tile(cosine, (1, head_count)), jnp.tile(sine_table, (1, head_count))
    picked = own(choices)
    lanes = jnp.arange(2 * experts, dtype=jnp.int32)
    pick_a, pick_b = ((picked[:, k : k + 1] == lanes[None]).astype(F32) for k in range(TOPK))
    pick_sent = sum((picked[:, k : k + 1] + experts == lanes[None]).astype(F32) for k in range(TOPK))

    (
        all_downs, all_q, all_kv, all_out, all_grad, wide_early, swapped_late, tokens,
        attn_in, raw, group_query, group_keyval, query, keyval, rope, norms, heads_out, residual, logits,
        gains,
    ) = front(
        downs, q_sent, kv_up, out_proj.T, hidden_in, out_grad, early, late, small,
        cos_heads, sin_heads, segment[:, None], segment[None, :], (pick_a, pick_b, pick_sent),
    )
    down_weight = all_downs.reshape(width, -1)
    up_query = all_q.reshape(-1, q_up.shape[1])
    up_keyval = all_kv.reshape(-1, kv_up.shape[1])
    out_weight = all_out.reshape(width, -1)
    moe_part, back_part, sum_early, sum_late = ffn(
        tokens.reshape(2 * group_rows, -1), all_grad.reshape(2 * group_rows, width), wide_early, swapped_late, capacity
    )

    ring = (2, 2, 2, local_rows)
    blocks = (4, 2, 4, row_shard, units)
    (
        own_early, own_late, _, _, _, grad_down, attn_back, grad_resid, small_grads, sum_up_query, sum_up_keyval, sum_out,
    ) = back(
        (sum_early.reshape((-1,) + blocks), sum_late.reshape((-1,) + blocks)),
        back_part.reshape(ring + (width + 128,)),
        (
            attn_in, heads_out, out_weight, up_query, up_keyval, down_weight, query, keyval, rope, norms, group_query,
            group_keyval, raw,
        ),
        residual, logits, (pick_a, pick_b), out_grad, gains, cos_heads, sin_heads, segment[:, None], segment[None, :],
    )

    got_downs, attn_back_own, moe_own, small_sum = last(
        grad_down.reshape(1, 4, 2, 4, row_shard, -1),
        attn_back.reshape(tp_count, local_rows, width),
        moe_part.reshape(ring + (width,)),
        small_grads,
    )
    layer_out = (residual + moe_own).astype(BF)
    own_hat, own_scale = normalized(hidden_in.astype(F32))
    input_grad = grad_resid + norm_back(attn_back_own, gains[experts].astype(F32), own_hat, own_scale)
    got_downs = got_downs.astype(F32)
    sum_qdown = got_downs[..., :q_cols].transpose(1, 0, 2).reshape(down_rows, -1)
    kv_at = q_cols + KVR // tp_count
    sum_kvdown = jnp.concatenate(
        [
            got_downs[..., q_cols:kv_at].transpose(1, 0, 2).reshape(down_rows, -1),
            got_downs[..., kv_at:raw_cols].transpose(1, 0, 2).reshape(down_rows, -1),
        ],
        axis=-1,
    )
    nope_cols, half_cols = head_count * NOPE, head_count * half
    sum_up_query = jnp.concatenate(
        [
            sum_up_query[:, :nope_cols].reshape(-1, head_count, NOPE),
            sum_up_query[:, nope_cols : nope_cols + half_cols].reshape(-1, head_count, half),
            sum_up_query[:, nope_cols + half_cols :].reshape(-1, head_count, half),
        ],
        axis=-1,
    ).reshape(q_up.shape)

    def mine(row, at, count):
        return lax.dynamic_slice(small_sum, (row, at), (1, count))[0]

    rows_at = device * down_rows
    sum_router = lax.dynamic_slice(small_sum, (0, rows_at), (experts, down_rows)).T
    own_routed = jnp.concatenate([own_early, own_late[:, :3]], axis=1).reshape(experts, 3, row_shard, units)
    sum_wide_gu = own_routed[:, :2].transpose(0, 2, 1, 3).astype(F32)
    sum_wide_down = own_routed[:, 2].transpose(0, 2, 1).astype(F32)
    sum_common_gu = own_late[:, 3:5].transpose(2, 1, 0, 3).reshape(row_shard, 2, 2 * units).astype(F32)
    sum_common_down = own_late[:, 5].transpose(1, 0, 2).reshape(row_shard, 2 * units).T.astype(F32)
    q_rank = q_down.shape[1]
    return (
        layer_out,
        input_grad.astype(BF),
        mine(experts, rows_at, down_rows),
        sum_qdown,
        mine(experts + 2, device * q_gain.shape[0], q_gain.shape[0]),
        sum_kvdown,
        mine(experts + 2, q_rank + device * kv_gain.shape[0], kv_gain.shape[0]),
        sum_up_query,
        sum_up_keyval,
        sum_out.T,
        mine(experts + 1, rows_at, down_rows),
        sum_router,
        sum_wide_gu,
        sum_wide_down,
        sum_common_gu,
        sum_common_down,
    )


def solution(mesh):
    return jax.shard_map(
        per_device,
        mesh=mesh,
        in_specs=(
            P(("fsdp", "tp"), None),
            P(("fsdp", "tp"), None),
            P(("fsdp", "tp")),
            P(("fsdp", "tp"), None),
            P(("fsdp", "tp")),
            P(("fsdp", "tp"), None),
            P(("fsdp", "tp")),
            P("fsdp", "tp"),
            P("fsdp", "tp"),
            P("tp", "fsdp"),
            P(("fsdp", "tp")),
            P(("fsdp", "tp"), None),
            P(None, "fsdp", None, "tp"),
            P(None, "tp", "fsdp"),
            P("fsdp", None, "tp"),
            P("tp", "fsdp"),
            P("fsdp", None),
            P("fsdp", None),
        ),
        out_specs=(
            P(("fsdp", "tp"), None),
            P(("fsdp", "tp"), None),
            P(("fsdp", "tp")),
            P(("fsdp", "tp"), None),
            P(("fsdp", "tp")),
            P(("fsdp", "tp"), None),
            P(("fsdp", "tp")),
            P("fsdp", "tp"),
            P("fsdp", "tp"),
            P("tp", "fsdp"),
            P(("fsdp", "tp")),
            P(("fsdp", "tp"), None),
            P(None, "fsdp", None, "tp"),
            P(None, "tp", "fsdp"),
            P("fsdp", None, "tp"),
            P("tp", "fsdp"),
        ),
        check_vma=False,
    )
```

```python
import functools

import jax
import jax.numpy as jnp
from jax import lax
from jax.experimental import pallas as pl
from jax.experimental.pallas import tpu as pltpu
from jax.sharding import PartitionSpec as P

HEADS = 16
NOPE = 128
ROPE = 64
VDIM = 128
KVR = 512
TOPK = 2

theta_base = 50000.0
norm_eps = 1e-06
route_scale = 2.446
masked_score = -1e30

MESH = pl.DeviceIdType.MESH
BF = jnp.bfloat16
F32 = jnp.float32
MIB = 1 << 20


class Spot:
    def __init__(self):
        f, t = lax.axis_index("fsdp"), lax.axis_index("tp")
        self.t = t
        self.z, self.yl, self.x = lax.div(f, 8), lax.rem(lax.div(f, 4), 2), lax.rem(f, 4)
        self.yh, self.c = lax.div(t, 2), lax.rem(t, 2)
        self.y = self.yh * 2 + self.yl

    def at(self, z=None, yl=None, x=None, yh=None, c=None):
        z = self.z if z is None else z
        yl = self.yl if yl is None else yl
        x = self.x if x is None else x
        yh = self.yh if yh is None else yh
        c = self.c if c is None else c
        return ((z * 2 + yl) * 4 + x, yh * 2 + c)

    def along_x(self, by):
        return self.at(x=lax.rem(self.x + by, 4))

    def along_z(self, by):
        return self.at(z=lax.rem(self.z + by, 4))

    def along_y(self, by):
        y = lax.rem(self.y + by, 4)
        return self.at(yl=lax.rem(y, 2), yh=lax.div(y, 2))

    def pair(self):
        return self.at(yl=1 - self.yl)

    def core(self):
        return self.at(c=1 - self.c)

    def far(self):
        return self.at(yh=1 - self.yh)

    def diagonal(self):
        return self.at(yh=1 - self.yh, c=1 - self.c)

    def rings(self):
        return [self.along_x(1), self.along_x(3), self.along_z(1), self.along_z(3)]


def greet(devices):
    barrier = pltpu.get_barrier_semaphore()
    for device in devices:
        pl.semaphore_signal(barrier, inc=1, device_id=device, device_id_type=MESH)
    pl.semaphore_wait(barrier, len(devices))


class Wire:
    def __init__(self, send, recv, here):
        self.send, self.recv, self.here = send, recv, here
        self.sent = self.kept = 0

    def copy(self, source, target, device):
        made = pltpu.make_async_remote_copy(
            src_ref=source,
            dst_ref=target,
            send_sem=self.send.at[self.sent],
            recv_sem=self.recv.at[self.sent],
            device_id=device,
            device_id_type=MESH,
        )
        self.sent += 1
        made.start()
        return made

    def keep(self, source, target):
        made = pltpu.make_async_copy(source, target, self.here.at[self.kept])
        self.kept += 1
        made.start()
        return made


def wait_all(copies):
    for made in copies:
        made.wait()


def together(*parts):
    left = list(parts)
    while left:
        for part in list(left):
            if next(part, "over") == "over":
                left.remove(part)
        yield


def finish(part):
    for _ in part:
        pass


def add_into(target, *terms):
    lead, (rows, columns) = target.shape[:-2], target.shape[-2:]
    step = rows if rows * columns <= 49152 else 16
    pieces = rows // step
    count = pieces
    for size in lead:
        count *= size

    def body(i, carry):
        at = [pl.ds(pl.multiple_of(lax.rem(i, pieces) * step, 16), step)]
        i = lax.div(i, pieces)
        for size in reversed(lead):
            at.insert(0, lax.rem(i, size))
            i = lax.div(i, size)
        at = tuple(at)
        total = terms[0][at].astype(F32)
        for term in terms[1:]:
            total = total + term[at].astype(F32)
        target[at] = total.astype(target.dtype)
        return carry

    lax.fori_loop(0, count, body, 0)


def gather_ring(wire, pos, plus, minus, units):
    prev, following = lax.rem(pos + 3, 4), lax.rem(pos + 1, 4)
    mine = [unit[2] if len(unit) > 2 else unit[0](pos) for unit in units]
    right = [wire.copy(own, unit[0](pos), plus) for own, unit in zip(mine, units)]
    left = [wire.copy(own, unit[0](pos), minus) for own, unit in zip(mine, units)]
    yield
    wait_all(right)
    onward = [wire.copy(unit[0](prev), unit[0](prev), plus) for unit in units if unit[1] == 0]
    wait_all(left)
    onward += [wire.copy(unit[0](following), unit[0](following), minus) for unit in units if unit[1] == 1]
    yield
    wait_all(onward)


def sum_ring(wire, pos, plus, minus, units, staged=False):
    prev, following, across = lax.rem(pos + 3, 4), lax.rem(pos + 1, 4), lax.rem(pos + 2, 4)
    first, direct, last = [], [], []
    for half, view, between, own, through, from_left, from_right, loads in units:
        first.append(wire.copy(view(across), through, plus if half == 0 else minus))
    for half, view, between, own, through, from_left, from_right, loads in units:
        if half == 0:
            direct.append(wire.copy(view(prev), from_right, minus))
        else:
            direct.append(wire.copy(view(following), from_left, plus))
    yield
    for made, (half, view, between, own, through, from_left, from_right, loads) in zip(first, units):
        wait_all(loads)
        made.wait()
        add_into(between, between, through)
        if half == 0:
            last.append(wire.copy(between, from_left, plus))
        else:
            last.append(wire.copy(between, from_right, minus))
    yield
    for one, two, (half, view, between, own, through, from_left, from_right, loads) in zip(direct, last, units):
        one.wait()
        two.wait()
        if staged:
            wait_all([wire.keep(from_left, through), wire.keep(from_right, between)])
            add_into(own, own, through, between)
        else:
            add_into(own, own, from_left, from_right)


def gather_tp(wire, spot, out, source):
    across = wire.copy(source, out.at[spot.t], spot.far())
    own = wire.keep(source, out.at[spot.t])
    other = wire.copy(source, out.at[spot.t], spot.core())
    yield
    across.wait()
    there = (1 - spot.yh) * 2 + spot.c
    last = wire.copy(out.at[there], out.at[there], spot.core())
    yield
    own.wait()
    other.wait()
    last.wait()


def gather_y(wire, spot, out, source):
    def view(rows):
        return lambda y: out.at[lax.rem(y, 2), lax.div(y, 2), spot.c, rows]

    rows = source.shape[0] // 2
    own = wire.keep(source, out.at[spot.yl, spot.yh, spot.c])
    other = [own, wire.copy(source, out.at[spot.yl, spot.yh, spot.c], spot.core())]
    cuts = (pl.ds(0, rows), pl.ds(rows, rows))
    units = [(view(cut), half, source.at[cut]) for half, cut in enumerate(cuts)]
    yield from gather_ring(wire, spot.y, spot.along_y(1), spot.along_y(3), units)
    for by in (1, 2, 3):
        y = lax.rem(spot.y + by, 4)
        part = out.at[lax.rem(y, 2), lax.div(y, 2), spot.c]
        other.append(wire.copy(part, part, spot.core()))
    yield
    wait_all(other)


def sum_tp(wire, spot, source, out, got, held, last):
    cores = [wire.copy(source.at[yh * 2 + 1 - spot.c], got.at[yh], spot.core()) for yh in (0, 1)]
    yield
    wait_all(cores)
    there = 1 - spot.yh
    add_into(held, source.at[there * 2 + spot.c], got.at[there])
    across = wire.copy(held, last, spot.far())
    yield
    across.wait()
    add_into(out, source.at[spot.t], got.at[spot.yh], last)


def sum_y(wire, spot, source, out, got, held, through, from_left, from_right):
    cores = [wire.copy(source.at[y % 2, y // 2, 1 - spot.c], got.at[y], spot.core()) for y in range(4)]
    loads = [wire.keep(source.at[y % 2, y // 2, spot.c], held.at[y]) for y in range(4)]
    yield
    for y, made in enumerate(cores):
        made.wait()
        loads[y].wait()
        add_into(held.at[y], held.at[y], got.at[y])
    rows = out.shape[0] // 2
    following, prev = lax.rem(spot.y + 1, 4), lax.rem(spot.y + 3, 4)
    units = []
    for half in (0, 1):
        part = pl.ds(half * rows, rows)
        units.append(
            (
                half,
                lambda y, part=part: held.at[y, part],
                held.at[following if half == 0 else prev, part],
                held.at[spot.y, part],
                through.at[part],
                from_left.at[part],
                from_right.at[part],
                [],
            )
        )
    yield from sum_ring(wire, spot.y, spot.along_y(1), spot.along_y(3), units)
    add_into(out, held.at[spot.y])


def sum_unit(wire, spot, half, part, order, scratch):
    following, prev = (lambda p: lax.rem(p + 1, 4)), (lambda p: lax.rem(p + 3, 4))
    (between, own, through, from_left, from_right), (between2, own2, through2, from_left2, from_right2) = scratch
    near = following if half == 0 else prev
    if order == "zx":
        view, pos, pos2 = (lambda i: part.at[:, i]), spot.z, spot.x
        view2 = lambda i: own.at[:, :, i]
    else:
        view, pos, pos2 = (lambda i: part.at[:, :, :, i]), spot.x, spot.z
        view2 = lambda i: own.at[:, i]

    def loads():
        return [wire.keep(view(near(pos)), between), wire.keep(view(pos), own)]

    def loads2():
        return [wire.keep(view2(near(pos2)), between2), wire.keep(view2(pos2), own2)]

    one = lambda: (half, view, between, own, through, from_left, from_right, loads())
    two = lambda: (half, view2, between2, own2, through2, from_left2, from_right2, loads2())
    return one, two, own2


def sum_chain(wire, spot, order, unit, after, staged=False):
    one, two, total = unit
    x = (spot.x, spot.along_x(1), spot.along_x(3))
    z = (spot.z, spot.along_z(1), spot.along_z(3))
    axes = (z, x) if order == "zx" else (x, z)
    yield from sum_ring(wire, *axes[0], [one()], staged)
    yield from sum_ring(wire, *axes[1], [two()], staged)
    yield from after(total)


def unit_scratch(planes, order, rows, columns):
    first = (planes, 2, 4, rows, columns) if order == "zx" else (planes, 4, 2, rows, columns)
    second = (planes, 2, rows, columns)
    return [pltpu.VMEM(first, BF)] * 5 + [pltpu.VMEM(second, BF)] * 5


def call(kernel, number, outs, ins, scratch, copies, keeps, operands, vmem):
    space = {"hbm": pltpu.HBM, "vmem": pltpu.VMEM}
    return pl.pallas_call(
        kernel,
        out_shape=[jax.ShapeDtypeStruct(shape, dtype) for shape, dtype, _ in outs],
        in_specs=[pl.BlockSpec(memory_space=space[kind]) for kind in ins],
        out_specs=[pl.BlockSpec(memory_space=space[kind]) for _, _, kind in outs],
        scratch_shapes=list(scratch)
        + [
            pltpu.SemaphoreType.DMA((max(copies, 1),)),
            pltpu.SemaphoreType.DMA((max(copies, 1),)),
            pltpu.SemaphoreType.DMA((max(keeps, 1),)),
        ],
        compiler_params=pltpu.CompilerParams(
            collective_id=number, has_side_effects=True, vmem_limit_bytes=vmem * MIB
        ),
    )(*operands)


def tp_sum_scratch(rows, columns):
    return [pltpu.VMEM((2, rows, columns), BF), pltpu.VMEM((rows, columns), BF), pltpu.VMEM((rows, columns), BF)]


def dot(a, b, dims="nn", precision=None):
    left, right = {"nn": (1, 0), "nt": (1, 1), "tn": (0, 0)}[dims]
    return lax.dot_general(
        a, b, (((left,), (right,)), ((), ())), precision=precision, preferred_element_type=F32
    )


def loop(count, body):
    def step(i, carry):
        body(i)
        return carry

    lax.fori_loop(0, count, step, 0)


def at_tile(i, size):
    return pl.ds(pl.multiple_of(i * size, size), size)


def flat(block):
    return block.reshape(-1, block.shape[-1])


def lane_grid(rows, columns):
    return (
        lax.broadcasted_iota(jnp.int32, (rows, columns), 0),
        lax.broadcasted_iota(jnp.int32, (rows, columns), 1),
    )


def head_lanes(values, head):
    lanes = lax.broadcasted_iota(jnp.int32, (1, values.shape[1]), 1)
    return values * (lax.div(lanes, 32) == head).astype(F32).astype(values.dtype)


def all_sum_small(wire, spot, buffers, own):
    steps = (
        [spot.core()],
        [spot.far()],
        [spot.pair()],
        [spot.along_x(1), spot.along_x(2), spot.along_x(3)],
        [spot.along_z(1), spot.along_z(2), spot.along_z(3)],
    )
    for step, devices in enumerate(steps):
        moves = [wire.copy(own.at[step], buffers.at[step, i], device) for i, device in enumerate(devices)]
        yield
        wait_all(moves)
        total = own[step]
        for i in range(len(devices)):
            total = total + buffers[step, i]
        own[step + 1] = total


def ring_pair(wire, spot, first, second):
    x = (spot.x, spot.along_x(1), spot.along_x(3))
    z = (spot.z, spot.along_z(1), spot.along_z(3))

    def unit(part, place):
        ref, half, planes, rows = part[:4]
        lead = () if planes is None else (planes,)
        return (lambda i: ref.at[lead + place(i) + (rows,)], half) + tuple(part[4:])

    def stream(parts, one, place_one, two, place_two):
        yield from gather_ring(wire, *one, [unit(part, place_one) for part in parts])
        yield from gather_ring(wire, *two, [unit(part[:4], place_two) for part in parts])

    every = slice(None)
    yield from together(
        stream(first, x, lambda i: (spot.z, every, i), z, lambda i: (i, every, every)),
        stream(second, z, lambda i: (i, every, spot.x), x, lambda i: (every, every, i)),
    )


def front_kernel(
    downs, q_up, kv_up, out_t, hidden, grad, early, late, small, cosine, sine, seg_col, seg_row, pick_a, pick_b,
    pick_sent,
    o_downs, o_q, o_kv, o_out, o_grad, o_early, o_late, o_tokens,
    o_hat, o_raw, o_qhat, o_kvhat, o_query, o_keyval, o_rope, o_norm, o_heads, o_resid, o_logits, o_small,
    rows, s_downs, s_q, s_kv, s_out, s_hidden, s_hat, s_part, s_raw, s_qlat, s_kvlat, s_query, s_keyval, s_rope,
    s_norm, s_heads, s_attn, s_sum, s_resid, s_sent, s_small, s_buf, t_got, t_held, t_last,
    send, recv, here,
):
    spot, wire = Spot(), Wire(send, recv, here)
    greet(
        spot.rings()
        + [spot.along_x(2), spot.along_z(2), spot.along_y(1), spot.along_y(3)]
        + [spot.core(), spot.far(), spot.diagonal()]
    )
    groups, width = 4 * hidden.shape[0], hidden.shape[1]
    own_rows = hidden.shape[0]
    low, high, every = pl.ds(0, 32), pl.ds(32, 32), slice(None)

    def down_stream():
        mine = rows.at[pl.ds(pl.multiple_of(spot.t * 16, 16), 16)]
        swaps = [wire.keep(downs.at[spot.t], mine)]
        for yh, c, device in (
            (spot.yh, 1 - spot.c, spot.core()),
            (1 - spot.yh, spot.c, spot.far()),
            (1 - spot.yh, 1 - spot.c, spot.diagonal()),
        ):
            swaps.append(wire.copy(downs.at[yh * 2 + c], mine, device))
        yield
        wait_all(swaps)
        place = s_downs.at[spot.z, spot.yl, spot.x]
        moves = [wire.copy(rows, place, spot.pair()), wire.keep(rows, place)]
        yield
        wait_all(moves)
        quarters = [pl.ds(16 * k, 16) for k in range(4)]
        yield from ring_pair(
            wire,
            spot,
            [(s_downs, 0, None, quarters[0]), (s_downs, 1, None, quarters[1])],
            [(s_downs, 0, None, quarters[2]), (s_downs, 1, None, quarters[3])],
        )

    def rest_stream():
        moves = []
        for source, target in ((q_up, s_q), (kv_up, s_kv), (out_t, s_out)):
            place = target.at[spot.z, spot.yl, spot.x]
            moves += [wire.copy(source, place, spot.pair()), wire.keep(source, place)]
        yield
        wait_all(moves)
        yield from ring_pair(
            wire,
            spot,
            [(s_q, 0, None, pl.ds(0, 32)), (s_q, 1, None, pl.ds(32, 16))],
            [(s_out, 0, None, low), (s_out, 1, None, high), (s_kv, 1, None, every)],
        )

    def ffn_stream():
        moves = []
        for source, place in ((early, o_early.at[:, spot.z, spot.yl, spot.x]), (late, o_late.at[:, spot.yl])):
            moves += [wire.copy(source.at[1 - spot.yl], place, spot.pair()), wire.keep(source.at[spot.yl], place)]
        yield
        wait_all(moves)
        two = [pl.ds(2 * k, 2) for k in range(4)]
        yield from ring_pair(
            wire,
            spot,
            [(o_early, 0, two[0], every), (o_early, 1, two[1], every), (o_early, 0, pl.ds(8, 1), low)],
            [(o_early, 0, two[2], every), (o_early, 1, two[3], every), (o_early, 1, pl.ds(8, 1), high)],
        )

    first = down_stream()
    next(first)
    s_small[0] = small[...]
    smalls = all_sum_small(wire, spot, s_buf, s_small)
    next(smalls)
    hiddens = gather_tp(wire, spot, s_hidden, hidden)
    next(hiddens)
    rest = rest_stream()
    for _ in range(3):
        next(first)
        next(smalls)
    next(rest)
    next(hiddens)
    next(first)
    finish(smalls)
    finish(hiddens)
    next(rest)
    next(first)
    ffn = ffn_stream()
    next(ffn)
    gains = s_small[5].astype(F32)
    attn_gain, ffn_gain = gains[8:9], gains[9:10]
    latent_gain = gains[10:11]
    keeps = []

    def norm_rows(i):
        block, part = lax.div(i, 8), at_tile(lax.rem(i, 8), 16)
        values = s_hidden[block, part].astype(F32)
        scale = lax.rsqrt(jnp.mean(values * values, axis=-1, keepdims=True) + norm_eps)
        s_hat[at_tile(i, 16)] = (values * scale * attn_gain).astype(BF)

    loop(groups // 16, norm_rows)
    next(rest)
    finish(first)
    keeps += [wire.keep(s_downs, o_downs), wire.keep(s_hat, o_hat)]

    def down(i):
        j, k = lax.div(i, 2), lax.rem(i, 2)
        lanes = at_tile(j, 128)
        s_part[at_tile(k, 256), lanes] = dot(s_hat[at_tile(k, 256)], flat(s_downs[:, :, :, :, lanes])).astype(BF)

    loop(10, down)
    raws = gather_tp(wire, spot, s_raw, s_part)
    next(raws)
    next(rest)
    next(raws)
    next(rest)
    finish(raws)
    next(ffn)
    grads = gather_y(wire, spot, o_grad, grad)
    next(grads)
    keeps.append(wire.keep(s_raw, o_raw))

    row, lane = lane_grid(128, 128)
    low_pick = (row == lax.rem(lane, 16)) & (lax.rem(lane, 32) < 16)
    high_pick = (row == lax.rem(lane, 16)) & (lax.rem(lane, 32) >= 16)
    low_pick, high_pick = low_pick.astype(F32).astype(BF), high_pick.astype(F32).astype(BF)

    def latents(i):
        part = at_tile(i, 32)
        raw = [s_raw[t, part, 0:384].astype(F32) for t in range(4)]
        total = sum(jnp.sum(v * v, axis=-1, keepdims=True) for v in raw)
        scale = lax.rsqrt(total / 1536.0 + norm_eps)
        for t in range(4):
            s_qlat[part, t * 384 : t * 384 + 384] = (raw[t] * scale * latent_gain[:, t * 384 : t * 384 + 384]).astype(BF)
        raw = [s_raw[t, part, 384:512].astype(F32) for t in range(4)]
        total = sum(jnp.sum(v * v, axis=-1, keepdims=True) for v in raw)
        scale = lax.rsqrt(total / 512.0 + norm_eps)
        for t in range(4):
            gain = latent_gain[:, 1536 + t * 128 : 1664 + t * 128]
            s_kvlat[part, t * 128 : t * 128 + 128] = (raw[t] * scale * gain).astype(BF)
        front = dot(s_raw[0, part, 512:640], low_pick) + dot(s_raw[1, part, 512:640], high_pick)
        back = dot(s_raw[2, part, 512:640], low_pick) + dot(s_raw[3, part, 512:640], high_pick)
        c, s = cosine[part], sine[part]
        s_rope[part, 0:128] = (front * c - back * s).astype(BF)
        s_rope[part, 128:256] = (back * c + front * s).astype(BF)

    loop(groups // 32, latents)

    finish(rest)
    keeps += [wire.keep(a, b) for a, b in ((s_q, o_q), (s_kv, o_kv), (s_out, o_out))]

    def query(i):
        part = at_tile(i, 256)
        for j in range(2):
            lanes = pl.ds(j * 256, 256)
            s_query[part, lanes] = dot(s_qlat[part], flat(s_q[:, :, :, :, lanes])).astype(BF)
        both = dot(s_qlat[part], flat(s_q[:, :, :, :, 512:768]))
        front, back = both[:, 0:128], both[:, 128:256]
        c, s = cosine[part], sine[part]
        s_query[part, 512:640] = (front * c - back * s).astype(BF)
        s_query[part, 640:768] = (back * c + front * s).astype(BF)
        for j in range(4):
            lanes = pl.ds(j * 256, 256)
            s_keyval[part, lanes] = dot(s_kvlat[part], flat(s_kv[:, :, :, :, lanes])).astype(BF)

    loop(2, query)
    next(ffn)

    def attend(i):
        part = at_tile(i, 256)
        places = lax.broadcasted_iota(jnp.int32, (256, groups), 0) + i * 256
        keys = lax.broadcasted_iota(jnp.int32, (256, groups), 1)
        allowed = (seg_col[part] == seg_row[...]) & (keys <= places)
        norms = jnp.zeros((256, 128), F32)
        for head in range(4):
            scores = dot(s_query[part, head * 128 : head * 128 + 128], s_keyval[:, head * 256 : head * 256 + 128], "nt")
            scores += dot(head_lanes(s_query[part, 512:640], head), s_rope[:, 0:128], "nt")
            scores += dot(head_lanes(s_query[part, 640:768], head), s_rope[:, 128:256], "nt")
            scores = jnp.where(allowed, scores * (NOPE + ROPE) ** (-0.5), masked_score)
            peak = jnp.max(scores, axis=-1, keepdims=True)
            raised = jnp.exp(scores - peak)
            total = jnp.sum(raised, axis=-1, keepdims=True)
            probs = (raised / total).astype(BF)
            out = dot(probs, s_keyval[:, head * 256 + 128 : head * 256 + 256])
            s_heads[part, head * 128 : head * 128 + 128] = out.astype(BF)
            lanes = lax.broadcasted_iota(jnp.int32, (256, 128), 1)
            norms = jnp.where(lanes == head, peak + jnp.log(total), norms)
        s_norm[part] = norms

    loop(2, attend)
    next(ffn)
    next(grads)
    keeps += [
        wire.keep(a, b)
        for a, b in (
            (s_qlat, o_qhat), (s_kvlat, o_kvhat), (s_query, o_query), (s_keyval, o_keyval), (s_rope, o_rope),
            (s_norm, o_norm), (s_heads, o_heads),
        )
    ]

    def project(i):
        block, z = lax.div(i, 4), lax.rem(i, 4)
        s_attn[block, :, at_tile(z, 512)] = dot(s_heads[at_tile(block, own_rows)], flat(s_out[z]), "nt").astype(BF)

    loop(16, project)
    sums = sum_tp(wire, spot, s_attn, s_sum, t_got, t_held, t_last)
    finish(sums)

    def residual(i):
        part = at_tile(i, 16)
        values = s_hidden[spot.t, part].astype(F32) + s_sum[part]
        s_resid[part] = values
        scale = lax.rsqrt(jnp.mean(values * values, axis=-1, keepdims=True) + norm_eps)
        normed = values * scale * ffn_gain
        s_sent[part, 0:width] = normed.astype(BF)
        s_sum[part] = normed

    loop(own_rows // 16, residual)
    logits = dot(s_sum[...], gains, "nt", lax.Precision.HIGHEST)
    o_logits[...] = logits
    scores = jax.nn.sigmoid(logits)
    first = jnp.sum(pick_a[...] * scores, axis=-1, keepdims=True)
    second = jnp.sum(pick_b[...] * scores, axis=-1, keepdims=True)
    both = first + second
    dense = pick_a[...] * (route_scale * first / both) + pick_b[...] * (route_scale * second / both)
    s_sent[:, width : width + 128] = jnp.zeros((own_rows, 128), BF)
    s_sent[:, width : width + 16] = (dense + pick_sent[...]).astype(BF)
    o_small[...] = s_small[5]
    keeps.append(wire.keep(s_resid, o_resid))
    sents = gather_y(wire, spot, o_tokens, s_sent)
    next(sents)
    next(grads)
    next(sents)
    next(ffn)
    finish(together(sents, grads))
    finish(ffn)
    wait_all(keeps)


def front(downs, q_up, kv_up, out_t, hidden, grad, early, late, small, cosine, sine, seg_col, seg_row, picks):
    rows, width = hidden.shape
    group, columns = 4 * rows, downs.shape[-1]

    def spread(array):
        return (4, 2, 4) + array.shape[-2:]

    down_spread = (4, 2, 4, 64, columns)
    weights = [down_spread, spread(q_up), spread(kv_up), spread(out_t)]
    outs = [(shape, BF, "hbm") for shape in weights]
    outs.append(((2, 2, 2, rows, width), BF, "hbm"))
    outs.append(((early.shape[1], 4, 2, 4) + early.shape[2:], BF, "hbm"))
    outs.append(((late.shape[1], 2) + late.shape[2:], BF, "hbm"))
    outs.append(((2, 2, 2, rows, width + 128), BF, "hbm"))
    saved = [
        ((group, width), BF), ((4, group, columns), BF), ((group, 1536), BF),
        ((group, 512), BF), ((group, 768), BF), ((group, 1024), BF), ((group, 256), BF), ((group, 128), F32),
        ((group, 512), BF), ((rows, width), F32),
    ]
    outs += [(shape, dtype, "hbm") for shape, dtype in saved]
    outs += [((rows, 16), F32, "vmem"), (small.shape, small.dtype, "vmem")]
    scratch = [pltpu.VMEM((64, columns), BF)] + [pltpu.VMEM(shape, BF) for shape in weights]
    scratch += [
        pltpu.VMEM((4, rows, width), BF),
        pltpu.VMEM((group, width), BF),
        pltpu.VMEM((group, columns), BF),
        pltpu.VMEM((4, group, columns), BF),
        pltpu.VMEM((group, 1536), BF),
        pltpu.VMEM((group, 512), BF),
        pltpu.VMEM((group, 768), BF),
        pltpu.VMEM((group, 1024), BF),
        pltpu.VMEM((group, 256), BF),
        pltpu.VMEM((group, 128), F32),
        pltpu.VMEM((group, 512), BF),
        pltpu.VMEM((4, rows, width), BF),
        pltpu.VMEM((rows, width), F32),
        pltpu.VMEM((rows, width), F32),
        pltpu.VMEM((rows, width + 128), BF),
        pltpu.VMEM((6,) + small.shape, small.dtype),
        pltpu.VMEM((5, 3) + small.shape, small.dtype),
    ] + tp_sum_scratch(rows, width)
    return call(
        front_kernel, 0, outs, ["hbm"] * 4 + ["vmem"] * 12, scratch, 140, 40,
        (downs, q_up, kv_up, out_t, hidden, grad, early, late, small, cosine, sine, seg_col, seg_row) + tuple(picks),
        60,
    )


def swiglu_back(gate, up, d_hidden):
    bell = jax.nn.sigmoid(gate)
    silu = gate * bell
    return silu * up, d_hidden * up * bell * (1.0 + gate * (1.0 - bell)), d_hidden * silu


def ffn_kernel(
    tokens, dy, early, swapped, o_moe, o_back, o_early, o_late,
    s_tok, s_dy, s_in, s_dyr, s_x, s_dg, s_one, s_turned, s_gate, s_gb, s_w, s_late, s_g, s_h, s_d1, s_d2, s_ch, s_c1, s_c2,
    load, fetched, stored, done, send, recv, here,
):
    spot, wire = Spot(), Wire(send, recv, here)
    greet(spot.rings())
    capacity, slots, width = s_one.shape[1] // 4, s_one.shape[1], dy.shape[1]
    groups = s_tok.shape[0] // 2
    first = spot.yl * 4
    zs = 4
    step = width // zs

    def late_stream():
        kept = wire.keep(swapped, s_late.at[:, spot.z, :, spot.x])
        low, high, every = pl.ds(0, 32), pl.ds(32, 32), slice(None)

        def part(half, plane, rows):
            planes = pl.ds(plane, 1)
            return (s_late, half, planes, rows, swapped.at[planes, :, rows])

        rings = ring_pair(
            wire,
            spot,
            [part(0, 0, every), part(1, 1, every), part(0, 2, low), part(1, 2, high)],
            [part(0, 3, every), part(1, 4, every), part(0, 5, low), part(1, 5, high)],
        )
        next(rings)
        yield
        next(rings)
        kept.wait()
        yield
        yield from rings

    weights = late_stream()
    next(weights)

    slot_of = {0: 0, 1: 1, 2: 0, 4: 1, 3: 0}

    def fetch(e):
        slot = slot_of[e]
        return [pltpu.make_async_copy(early.at[3 * e + k], s_w.at[slot, k], fetched.at[slot, k]) for k in range(3)]

    def store(e):
        slot = slot_of[e]
        out = {3: o_late.at[pl.ds(0, 3)], 4: o_late.at[pl.ds(3, 3)]}.get(e)
        out = o_early.at[pl.ds(3 * e, 3)] if out is None else out
        return [pltpu.make_async_copy(s_g.at[slot, k], out.at[k], stored.at[slot, k]) for k in range(3)]

    def start(copies):
        for copy in copies:
            copy.start()

    loads = [pltpu.make_async_copy(tokens, s_tok, load.at[0]), pltpu.make_async_copy(dy, s_dy, load.at[1])]
    start(loads)
    start(fetch(0))
    loads[0].wait()

    row, lane = lane_grid(groups, groups)
    before = (row < lane).astype(F32).astype(BF)
    after = (lane < row).astype(F32).astype(BF)
    same = (lane == row).astype(F32).astype(BF)
    slot_row, _ = lane_grid(capacity, groups)
    turned_row, turned_lane = lane_grid(groups, slots)
    for g in range(2):
        extra = s_tok[g * groups : (g + 1) * groups, width : width + 128]
        flipped = dot(extra, same, "tn")
        gates = jnp.where(first == 0, flipped[0:4], flipped[4:8])
        masks = jnp.where(first == 0, flipped[8:12], flipped[12:16])
        padded = jnp.concatenate([masks, jnp.zeros((12, groups), F32)], axis=0)
        place = dot(padded.astype(BF), before)
        place = jnp.where(padded > 0, place, -1.0).astype(jnp.int32)
        for e in range(4):
            taken = place[e : e + 1] == slot_row
            rows = slice(e * capacity, (e + 1) * capacity)
            s_one[g, rows] = taken.astype(F32).astype(BF)
            s_gate[g, rows] = jnp.sum(jnp.where(taken, gates[e : e + 1], 0.0), axis=-1, keepdims=True)
        place = dot(after, extra)
        place = jnp.where(extra.astype(F32) > 0, place, -1.0)
        columns = jnp.where(first == 0, place[:, 8:12], place[:, 12:16]).astype(jnp.int32)
        wanted = jnp.full((groups, slots), -2, jnp.int32)
        for e in range(4):
            wanted = jnp.where(lax.div(turned_lane, capacity) == e, columns[:, e : e + 1], wanted)
        s_turned[g] = (wanted == lax.rem(turned_lane, capacity)).astype(F32).astype(BF)
    loads[1].wait()
    next(weights)

    def dispatch(i):
        g, lanes = lax.div(i, zs), at_tile(lax.rem(i, zs), step)
        rows = at_tile(g, groups)
        s_in[g, :, lanes] = dot(s_one[g], s_tok[rows, lanes]).astype(BF)
        s_dyr[g, :, lanes] = dot(s_one[g], s_dy[rows, lanes]).astype(BF)

    loop(2 * zs, dispatch)
    next(weights)

    def expert(e, ahead, after_act, after_all):
        slot = slot_of[e]
        mine = pl.ds(e * capacity, capacity)
        if e < 3:
            wait_all(fetch(e))
        w_gate, w_up, w_down = (s_w.at[slot, k] if e < 3 else s_late.at[k] for k in range(3))
        if ahead is not None:
            start(fetch(ahead))

        def place(i):
            lanes = at_tile(i, step)
            for g in range(2):
                rows = slice(g * capacity, (g + 1) * capacity)
                s_x[rows, lanes] = s_in[g, mine, lanes]
                s_dg[rows, lanes] = (s_gate[g, mine] * s_dyr[g, mine, lanes].astype(F32)).astype(BF)

        loop(zs, place)
        gate, up = dot(s_x[...], flat(w_gate[...])), dot(s_x[...], flat(w_up[...]))
        hidden, d_gate, d_up = swiglu_back(gate, up, dot(s_dg[...], flat(w_down[...])))
        s_h[...], s_d1[...], s_d2[...] = hidden.astype(BF), d_gate.astype(BF), d_up.astype(BF)
        if after_act:
            next(weights)
        if e >= 2:
            wait_all(store({2: 0, 3: 2}[e]))

        def sums(i):
            lanes = at_tile(i, step)
            s_g[slot, 0, lanes] = dot(s_x[:, lanes], s_d1[...], "tn").astype(BF)
            s_g[slot, 1, lanes] = dot(s_x[:, lanes], s_d2[...], "tn").astype(BF)
            s_g[slot, 2, lanes] = dot(s_dg[:, lanes], s_h[...], "tn").astype(BF)

        loop(zs, sums)
        start(store(e))
        s_gb[...] = jnp.zeros_like(s_gb)

        def outward(i):
            lanes = at_tile(i, step)
            out = dot(s_h[...], flat(w_down[i]), "nt")
            back = dot(s_d1[...], flat(w_gate[i]), "nt") + dot(s_d2[...], flat(w_up[i]), "nt")
            for g in range(2):
                rows = slice(g * capacity, (g + 1) * capacity)
                s_gb[rows] += jnp.sum(out[rows] * s_dyr[g, mine, lanes].astype(F32), axis=-1, keepdims=True)
                s_dyr[g, mine, lanes] = (s_gate[g, mine] * out[rows]).astype(BF)
                s_in[g, mine, lanes] = back[rows].astype(BF)

        loop(zs, outward)
        extra_lane = lax.broadcasted_iota(jnp.int32, (capacity, 128), 1)
        for g in range(2):
            rows = slice(g * capacity, (g + 1) * capacity)
            s_in[g, mine, width : width + 128] = jnp.where(extra_lane == first + e, s_gb[rows], 0.0).astype(BF)
        if after_all:
            next(weights)

    expert(0, 1, False, False)
    expert(1, 2, False, True)
    expert(2, None, False, False)
    finish(weights)


    def common(i):
        rows = at_tile(i, 256)
        inputs = s_tok[rows, 0:width]
        gate, up = dot(inputs, flat(s_late[3])), dot(inputs, flat(s_late[4]))
        hidden, d_gate, d_up = swiglu_back(gate, up, dot(s_dy[rows], flat(s_late[5])))
        s_ch[rows], s_c1[rows], s_c2[rows] = hidden.astype(BF), d_gate.astype(BF), d_up.astype(BF)

    loop(2 * groups // 256, common)
    wait_all(store(1))

    def common_sums(i):
        lanes = at_tile(i, step)
        s_g[1, 0, lanes] = dot(s_tok[:, lanes], s_c1[...], "tn").astype(BF)
        s_g[1, 1, lanes] = dot(s_tok[:, lanes], s_c2[...], "tn").astype(BF)
        s_g[1, 2, lanes] = dot(s_dy[:, lanes], s_ch[...], "tn").astype(BF)

    loop(zs, common_sums)
    start(store(4))
    expert(3, None, False, False)

    def combine(i):
        g, z = lax.div(i, zs), lax.rem(i, zs)
        rows, lanes = at_tile(g, groups), at_tile(z, step)
        out = dot(s_ch[rows], flat(s_late[5, z]), "nt") + dot(s_turned[g], s_dyr[g, :, lanes])
        s_dy[rows, lanes] = out.astype(BF)
        back = dot(s_c1[rows], flat(s_late[3, z]), "nt") + dot(s_c2[rows], flat(s_late[4, z]), "nt")
        s_tok[rows, lanes] = (back + dot(s_turned[g], s_in[g, :, lanes])).astype(BF)

    loop(2 * zs, combine)
    for g in range(2):
        rows = slice(g * groups, (g + 1) * groups)
        s_tok[rows, width : width + 128] = dot(s_turned[g], s_in[g, :, width : width + 128]).astype(BF)
    ends = [pltpu.make_async_copy(s_dy, o_moe, done.at[0]), pltpu.make_async_copy(s_tok, o_back, done.at[1])]
    start(ends)
    wait_all(store(4))
    wait_all(store(3))
    wait_all(ends)


def ffn(tokens, dy, early, swapped, capacity):
    rows, width = dy.shape
    wide = tokens.shape[1]
    tile = early.shape[-2:]
    units = tile[1]
    outs = [(rows, width), (rows, wide), (early.shape[0], width, units), (swapped.shape[0], width, units)]
    sizes = [
        ((rows, wide), BF), ((rows, width), BF), ((2, 4 * capacity, wide), BF), ((2, 4 * capacity, width), BF),
        ((2 * capacity, width), BF), ((2 * capacity, width), BF), ((2, 4 * capacity, rows // 2), BF),
        ((2, rows // 2, 4 * capacity), BF), ((2, 4 * capacity, 1), F32), ((2 * capacity, 1), F32),
        ((2, 3, 4, 2, 4) + tile, BF), ((6, 4, 2, 4) + tile, BF), ((2, 3, width, units), BF),
        ((2 * capacity, units), BF), ((2 * capacity, units), BF), ((2 * capacity, units), BF),
        ((rows, units), BF), ((rows, units), BF), ((rows, units), BF),
    ]
    scratch = [pltpu.VMEM(*size) for size in sizes]
    scratch += [pltpu.SemaphoreType.DMA(n) for n in ((2,), (2, 3), (2, 3), (2,))]
    return call(
        ffn_kernel, 3, [(shape, BF, "hbm") for shape in outs], ["hbm"] * 4, scratch, 48, 1,
        (tokens, dy, early, swapped), 62,
    )


EARLY_PARTS = ((0, 0, 2, "zx"), (0, 4, 2, "xz"), (1, 2, 2, "zx"), (1, 6, 2, "xz"), (0, 8, 1, "xz"))
LATE_PARTS = ((0, 0, 1, "zx"), (0, 3, 2, "xz"), (1, 1, 2, "zx"), (1, 5, 1, "xz"))


def back_kernel(
    early, late, part, moe, attn_in, heads, out_w, up_q, up_kv, downs, query, keyval, rope, norms, qlat, kvlat, raw,
    resid, logits, pick_a, pick_b, grad, gains, cosine, sine, seg_col, seg_row,
    o_early, o_late, o_gout, o_gq, o_gkv, o_gdown, o_attn, o_resid, o_small, o_moe,
    *rest,
):
    landing, rest = list(rest[:36]), rest[36:]
    scratch, (send, recv, here) = list(rest[:-3]), rest[-3:]
    spot, wire = Spot(), Wire(send, recv, here)
    greet(spot.rings() + [spot.along_y(1), spot.along_y(3), spot.core(), spot.far(), spot.diagonal()])
    own_rows, width = grad.shape
    groups = 4 * own_rows

    def take(count):
        taken, scratch[:] = scratch[:count], scratch[count:]
        return taken

    def unit(half, ref, order):
        rings = [take(3) + [landing.pop(0), landing.pop(0)] for _ in range(2)]
        return sum_unit(wire, spot, half, ref, order, rings)

    def swap_to(place):
        def after(total):
            moves = [wire.copy(total.at[:, 1 - spot.yl], place, spot.pair()), wire.keep(total.at[:, spot.yl], place)]
            yield
            wait_all(moves)

        return after

    def chains(source, out, parts):
        for half, start, count, order in parts:
            planes = pl.ds(start, count)
            made = unit(half, source.at[planes], order)
            yield sum_chain(wire, spot, order, made, swap_to(out.at[spot.yl, planes]), True)

    early_chains = list(chains(early, o_early, EARLY_PARTS))
    late_chains = list(chains(late, o_late, LATE_PARTS))
    ring = take(4)
    tokens = take(5)
    (s_back, s_heads, s_wide, s_upq, s_upkv, s_query, s_keyval, s_rope, s_norms, s_qlat, s_kvlat, s_raw) = take(12)
    (s_normed, s_dh, s_dhall, s_dheads, s_accq, s_acck, s_dkn, s_dv) = take(8)
    s_resid, s_lat = s_back.at[:, pl.ds(0, width)], s_back
    s_flow, q_at = tokens[0], 1024
    (s_swap, s_got, s_stage, s_attn, s_small) = take(5)
    t_scratch = take(3)
    s_part = tokens[1]
    sums = sum_y(wire, spot, part, s_back, *tokens)
    next(sums)
    ffn = together(*early_chains)
    next(ffn)
    loads = [wire.keep(a, b) for a, b in ((heads, s_heads), (out_w, s_wide.at[:, pl.ds(0, 512)]))]
    others = [
        wire.keep(a, b)
        for a, b in (
            (query, s_query), (keyval, s_keyval), (rope, s_rope), (norms, s_norms), (qlat, s_qlat), (kvlat, s_kvlat),
            (up_q, s_upq), (up_kv, s_upkv), (raw.at[:, pl.ds(pl.multiple_of(spot.t * own_rows, 128), own_rows)], s_raw),
        )
    ]
    finish(sums)

    rows_f32 = gains[...].astype(F32)
    ffn_gain = rows_f32[9:10]
    dense = s_back[:, width : width + 16]
    scores = jax.nn.sigmoid(logits[...])
    first = jnp.sum(pick_a[...] * scores, axis=-1, keepdims=True)
    second = jnp.sum(pick_b[...] * scores, axis=-1, keepdims=True)
    both = first + second
    apart = jnp.sum((pick_a[...] - pick_b[...]) * dense, axis=-1, keepdims=True) * route_scale / both
    d_scores = (pick_a[...] * (second / both) - pick_b[...] * (first / both)) * apart
    d_logits = d_scores * scores * (1.0 - scores)
    s_normed[...] = dot(d_logits, rows_f32, "nn", lax.Precision.HIGHEST)
    s_small[0:1] = jnp.zeros((1, width), F32)

    def own_row(i):
        rows = at_tile(i, 16)
        values = resid[rows]
        scale = lax.rsqrt(jnp.mean(values * values, axis=-1, keepdims=True) + norm_eps)
        hat = values * scale
        grad_ffn = s_normed[rows] + s_back[rows, 0:width]
        s_small[0:1] += jnp.sum(grad_ffn * hat, axis=0, keepdims=True)
        weighted = grad_ffn * ffn_gain
        inner = scale * (weighted - hat * jnp.mean(weighted * hat, axis=-1, keepdims=True))
        total = grad[rows].astype(F32) + inner
        s_resid[rows] = total
        s_dh[rows] = total.astype(BF)
        s_normed[rows] = hat * ffn_gain

    loop(own_rows // 16, own_row)
    keeps = []
    resid_kept = wire.keep(s_resid, o_resid)
    swap = gather_tp(wire, spot, s_dhall, s_dh)
    next(swap)
    next(ffn)
    next(swap)
    o_small[...] = dot(d_logits, s_normed[...], "tn", lax.Precision.HIGHEST)
    o_small[9:10] = s_small[0:1]
    finish(swap)

    wait_all(loads)

    def out_grads(i):
        lanes = at_tile(i, 512)
        block = dot(flat(s_dhall[:, :, lanes]), s_heads[...], "tn").astype(BF)
        s_stage[i, :, :, :, 0:512] = block.reshape(2, 4, 64, 512)

    loop(4, out_grads)
    staged = wire.keep(s_stage.at[:, :, :, :, pl.ds(0, 512)], o_gout.at[0])

    def head_grads(i):
        s_dheads[at_tile(i, own_rows)] = dot(s_dhall[i], s_wide[:, 0:512]).astype(BF)

    loop(4, head_grads)
    wait_all(others)
    late_loads = [wire.keep(attn_in.at[pl.ds(t * own_rows, own_rows)], s_dhall.at[t]) for t in range(4)]
    late_loads.append(wire.keep(downs, s_wide))
    s_accq[...] = jnp.zeros_like(s_accq)
    s_acck[...] = jnp.zeros_like(s_acck)

    for head in range(4):
        nope, value = pl.ds(head * 256, 128), pl.ds(head * 256 + 128, 128)
        at = pl.ds(head * 128, 128)
        s_dkn[...] = jnp.zeros_like(s_dkn)
        s_dv[...] = jnp.zeros_like(s_dv)

        def attend(i, head=head, nope=nope, value=value, at=at):
            tile = at_tile(i, 256)
            places = lax.broadcasted_iota(jnp.int32, (256, groups), 0) + i * 256
            keys = lax.broadcasted_iota(jnp.int32, (256, groups), 1)
            allowed = (seg_col[tile] == seg_row[...]) & (keys <= places)
            front, back = head_lanes(s_query[tile, 512:640], head), head_lanes(s_query[tile, 640:768], head)
            scores = dot(s_query[tile, at], s_keyval[:, nope], "nt")
            scores += dot(front, s_rope[:, 0:128], "nt")
            scores += dot(back, s_rope[:, 128:256], "nt")
            scores = jnp.where(allowed, scores * (NOPE + ROPE) ** (-0.5), masked_score)
            probs = jnp.exp(scores - s_norms[tile, head : head + 1])
            d_head = s_dheads[tile, at]
            s_dv[...] += dot(probs.astype(BF), d_head, "tn")
            d_probs = dot(d_head, s_keyval[:, value], "nt")
            row_dot = jnp.sum(probs * d_probs, axis=-1, keepdims=True)
            d_scores = (probs * (d_probs - row_dot) * (NOPE + ROPE) ** (-0.5)).astype(BF)
            d_query = dot(d_scores, s_keyval[:, nope]).astype(BF)
            s_flow[pl.ds(2 * i, 2), :, pl.ds(q_at + head * 128, 128)] = d_query.reshape(2, own_rows, 128)
            s_accq[tile, 0:128] += head_lanes(dot(d_scores, s_rope[:, 0:128]), head)
            s_accq[tile, 128:256] += head_lanes(dot(d_scores, s_rope[:, 128:256]), head)
            s_dkn[...] += dot(d_scores, s_query[tile, at], "tn")
            s_acck[:, 0:128] += dot(d_scores, front, "tn")
            s_acck[:, 128:256] += dot(d_scores, back, "tn")

        loop(2, attend)
        s_flow[:, :, nope] = s_dkn[...].astype(BF).reshape(4, own_rows, 128)
        s_flow[:, :, value] = s_dv[...].astype(BF).reshape(4, own_rows, 128)
    next(ffn)
    late_ffn = together(*late_chains)
    next(late_ffn)

    row, lane = lane_grid(128, 128)
    fold_front = ((lane < 32) & (lane == lax.rem(row, 32))).astype(F32)
    fold_back = ((lane >= 32) & (lane < 64) & (lane - 32 == lax.rem(row, 32))).astype(F32)

    def unrotate(i):
        rows = at_tile(i, own_rows)
        c, s = cosine[rows], sine[rows]
        front, back = s_accq[rows, 0:128], s_accq[rows, 128:256]
        s_flow[i, :, q_at + 512 : q_at + 640] = (front * c + back * s).astype(BF)
        s_flow[i, :, q_at + 640 : q_at + 768] = (back * c - front * s).astype(BF)
        front, back = s_acck[rows, 0:128], s_acck[rows, 128:256]
        folded = dot(front * c + back * s, fold_front, "nn", lax.Precision.HIGHEST)
        folded += dot(back * c - front * s, fold_back, "nn", lax.Precision.HIGHEST)
        s_part[i, :, 2048:2176] = folded.astype(BF)
        for j in range(3):
            lanes = slice(j * 512, j * 512 + 512)
            s_part[i, :, lanes] = dot(s_flow[i, :, q_at : q_at + 768], s_upq[lanes], "nt").astype(BF)
        s_part[i, :, 1536:2048] = dot(s_flow[i, :, 0:1024], s_upkv[...], "nt").astype(BF)

    loop(4, unrotate)
    resid_kept.wait()
    latents = sum_tp(wire, spot, s_part, s_lat, *t_scratch)
    next(latents)
    staged.wait()

    def q_grads(i):
        block = dot(s_qlat[:, at_tile(i, 384)], flat(s_flow[:, :, q_at : q_at + 768]), "tn").astype(BF)
        s_stage[i, :, :, 0:48] = block.reshape(2, 4, 48, 768)

    loop(4, q_grads)
    staged = wire.keep(s_stage.at[:, :, :, pl.ds(0, 48)], o_gq.at[0])
    next(ffn)
    next(latents)

    def kv_grads(i):
        block = dot(s_kvlat[:, at_tile(i, 128)], flat(s_flow[:, :, 0:1024]), "tn").astype(BF)
        s_attn[i, :, :, :, 0:1024] = block.reshape(2, 4, 16, 1024)

    loop(4, kv_grads)
    staged_kv = wire.keep(s_attn.at[:, :, :, :, pl.ds(0, 1024)], o_gkv.at[0])
    finish(latents)

    gain = rows_f32[10:11]
    s_small[...] = jnp.zeros_like(s_small)

    def latent_row(i):
        rows = at_tile(i, 32)
        for cut, columns, start in ((slice(0, 384), 384, 0), (slice(384, 512), 128, 1536)):
            size = 4.0 * columns
            values = [s_raw[t, rows, cut].astype(F32) for t in range(4)]
            scale = lax.rsqrt(sum(jnp.sum(v * v, axis=-1, keepdims=True) for v in values) / size + norm_eps)
            hats = [v * scale for v in values]
            grads, weighted = [], []
            for t in range(4):
                at = slice(start + t * columns, start + (t + 1) * columns)
                grads.append(s_lat[rows, at])
                weighted.append(grads[t] * gain[:, at])
                s_small[0:1, at] += jnp.sum(grads[t] * hats[t], axis=0, keepdims=True)
            inner = sum(jnp.sum(w * h, axis=-1, keepdims=True) for w, h in zip(weighted, hats)) / size
            for t in range(4):
                s_swap[t, rows, cut] = (scale * (weighted[t] - hats[t] * inner)).astype(BF)
        folded = s_lat[rows, 2048:2176].astype(BF)
        for t in range(4):
            pick = ((row == t * 16 + lane) & (lane < 16)).astype(F32).astype(BF)
            s_swap[t, rows, 512:640] = dot(folded, pick).astype(BF)

    loop(own_rows // 32, latent_row)
    moves = [wire.keep(s_swap.at[spot.t], s_got.at[spot.t])]
    for yh, c, device in (
        (spot.yh, 1 - spot.c, spot.core()),
        (1 - spot.yh, spot.c, spot.far()),
        (1 - spot.yh, 1 - spot.c, spot.diagonal()),
    ):
        moves.append(wire.copy(s_swap.at[yh * 2 + c], s_got.at[spot.t], device))
    o_small[10:11] = s_small[0:1]
    s_small[0:1] = jnp.zeros((1, width), F32)
    wait_all(moves)
    wait_all(late_loads)
    staged.wait()
    staged_kv.wait()
    next(late_ffn)
    next(ffn)
    s_moe = s_lat.at[:, pl.ds(0, width)]
    moes = sum_y(wire, spot, moe, s_moe, ring[0], s_part.at[:, :, pl.ds(0, width)], *ring[1:])
    next(moes)

    def down_grads(i):
        lanes = at_tile(i, 512)
        block = dot(flat(s_dhall[:, :, lanes]), flat(s_got[...]), "tn").astype(BF)
        s_stage[i, :, :, :, 0:640] = block.reshape(2, 4, 64, 640)

    loop(4, down_grads)
    staged = wire.keep(s_stage.at[:, :, :, :, pl.ds(0, 640)], o_gdown)

    def attn_grads(i):
        rows, lanes = lax.div(i, 4), at_tile(lax.rem(i, 4), 512)
        back = dot(s_got[rows], s_wide[lanes], "nt")
        s_attn[rows, :, :, :, lanes] = back.astype(BF).reshape(2, 4, 16, 512)
        s_small[0:1, lanes] += jnp.sum(back * s_dhall[rows, :, lanes].astype(F32), axis=0, keepdims=True)

    loop(16, attn_grads)
    o_small[8:9] = s_small[0:1] / rows_f32[8:9]
    keeps.append(wire.keep(s_attn, o_attn))
    next(late_ffn)
    finish(ffn)
    next(moes)
    finish(together(late_ffn, moes))
    keeps.append(wire.keep(s_moe, o_moe))
    staged.wait()
    wait_all(keeps)


def back(ffn_grads, part, moe, saved, resid, logits, picks, grad, gains, cosine, sine, seg_col, seg_row):
    rows, width = grad.shape
    group = 4 * rows
    outs = [((2, a.shape[0]) + a.shape[4:], BF, "hbm") for a in ffn_grads]
    spread = [(1, 4, 2, 4) + block for block in ((64, 512), (48, 768), (16, 1024))]
    outs += [(shape, BF, "hbm") for shape in spread + [(4, 2, 4, 64, 640), (4, 2, 4, 16, width)]]
    outs += [ ((rows, width), F32, "hbm"), ((16, width), F32, "vmem")]
    outs.append(((rows, width), F32, "hbm"))
    scratch = []
    tile = ffn_grads[0].shape[4:]
    units = [(count, order, tile) for _, _, count, order in EARLY_PARTS + LATE_PARTS]
    for planes, order, block in units:
        first = (planes, 2, 4) + block if order == "zx" else (planes, 4, 2) + block
        second = (planes, 2) + block
        outs += [(first, BF, "hbm")] * 2 + [(second, BF, "hbm")] * 2
        scratch += [pltpu.VMEM(first, BF)] * 3 + [pltpu.VMEM(second, BF)] * 3
    scratch += [pltpu.VMEM((4, rows, width), BF)] + [pltpu.VMEM((rows, width), BF)] * 3
    columns = part.shape[-1]
    scratch += [pltpu.VMEM((4, rows, columns), BF)] * 2 + [pltpu.VMEM((rows, columns), BF)] * 3
    sizes = [
        ((rows, columns), F32), ((group, 512), BF), ((width, 640), BF), ((1536, 768), BF), ((512, 1024), BF),
        ((group, 768), BF), ((group, 1024), BF), ((group, 256), BF), ((group, 128), F32), ((group, 1536), BF),
        ((group, 512), BF), ((4, rows, 640), BF),
        ((rows, width), F32), ((rows, width), BF), ((4, rows, width), BF), ((group, 512), BF),
        ((group, 256), F32), ((group, 256), F32), ((group, 128), F32), ((group, 128), F32),
        ((4, rows, 640), BF), ((4, rows, 640), BF), ((4, 2, 4, 64, 768), BF), ((4, 2, 4, 16, width), BF), ((8, width), F32),
    ]
    scratch += [pltpu.VMEM(*size) for size in sizes] + tp_sum_scratch(rows, columns)
    return call(
        back_kernel, 1, outs, ["hbm"] * 17 + ["vmem"] * 10, scratch, 110, 130,
        tuple(ffn_grads) + (part, moe) + tuple(saved) + (resid, logits) + tuple(picks)
        + (grad, gains, cosine, sine, seg_col, seg_row),
        63,
    )[:10]


def last_kernel(downs, q_up, kv_up, out_t, part, small, o_downs, o_q, o_kv, o_out, o_part, o_small, *rest):
    scratch, (send, recv, here) = list(rest[:-3]), rest[-3:]
    spot, wire = Spot(), Wire(send, recv, here)
    greet(
        spot.rings()
        + [spot.along_x(2), spot.along_z(2), spot.pair()]
        + [spot.core(), spot.far(), spot.diagonal()]
    )

    def take(count):
        taken, scratch[:] = scratch[:count], scratch[count:]
        return taken

    def chain(half, ref, order, out):
        made = sum_unit(wire, spot, half, ref, order, (take(5), take(5)))
        (got,) = take(1)
        rows = out if out is not None else take(1)[0]
        cut = lambda t: rows.at[pl.ds(pl.multiple_of(t * 16, 16), 16)]

        def after(total):
            move = wire.copy(total.at[:, 1 - spot.yl], got, spot.pair())
            yield
            move.wait()
            add_into(rows, total.at[0, spot.yl], got.at[0])
            if out is None:
                swaps = [wire.keep(cut(spot.t), o_downs.at[spot.t])]
                for yh, c, device in (
                    (spot.yh, 1 - spot.c, spot.core()),
                    (1 - spot.yh, spot.c, spot.far()),
                    (1 - spot.yh, 1 - spot.c, spot.diagonal()),
                ):
                    swaps.append(wire.copy(cut(yh * 2 + c), o_downs.at[spot.t], device))
                yield
                wait_all(swaps)

        return sum_chain(wire, spot, order, made, after)

    chains = [chain(0, downs, "xz", None), chain(0, q_up, "zx", o_q), chain(1, out_t, "zx", o_out)]
    chains.append(chain(1, kv_up, "xz", o_kv))
    tokens = take(3)
    s_small, s_buf = take(2)
    s_small[0] = small[...]
    finish(together(*chains, all_sum_small(wire, spot, s_buf, s_small), sum_tp(wire, spot, part, o_part, *tokens)))
    o_small[...] = s_small[5]


def last(downs, q_up, kv_up, out_t, part, small):
    scratch = []
    for a, order in ((downs, "xz"), (q_up, "zx"), (out_t, "zx"), (kv_up, "xz")):
        block = a.shape[-2:]
        scratch += unit_scratch(1, order, *block) + [pltpu.VMEM((1,) + block, BF)]
        if a is downs:
            scratch.append(pltpu.VMEM(block, BF))
    rows, columns = part.shape[1:]
    scratch += tp_sum_scratch(rows, columns)
    scratch += [pltpu.VMEM((6,) + small.shape, F32), pltpu.VMEM((5, 3) + small.shape, F32)]
    outs = [((4, 16, downs.shape[-1]), BF, "hbm")]
    outs += [(a.shape[-2:], F32, "vmem") for a in (q_up, kv_up, out_t)]
    outs += [((rows, columns), F32, "vmem"), (small.shape, F32, "vmem")]
    return call(
        last_kernel, 2, outs, ["hbm"] * 4 + ["vmem"] * 2, scratch, 64, 32, (downs, q_up, kv_up, out_t, part, small), 50
    )


def rotary_tables(position):
    half_size = ROPE // 2
    inverse = theta_base ** (-(2.0 * jnp.arange(half_size, dtype=F32)) / ROPE)
    angles = position.astype(F32)[:, None] * inverse[None, :]
    return (jnp.cos(angles), jnp.sin(angles))


def packing(lengths, total_rows):
    positions = jnp.arange(total_rows, dtype=jnp.int32)
    endings = jnp.cumsum(lengths)
    segment = jnp.sum((positions[:, None] >= endings[None, :]).astype(jnp.int32), axis=1)
    starting = endings - lengths
    owner_mask = segment[:, None] == jnp.arange(lengths.shape[0], dtype=jnp.int32)[None, :]
    first_row = jnp.sum(jnp.where(owner_mask, starting[None, :], 0), axis=1)
    return (segment, positions - first_row)


def normalized(values):
    scale = lax.rsqrt(jnp.mean(values * values, axis=-1, keepdims=True) + norm_eps)
    return values * scale, scale


def norm_back(grad, gain, hat, scale):
    weighted = grad * gain
    return scale * (weighted - hat * jnp.mean(weighted * hat, axis=-1, keepdims=True))


def per_device(
    hidden_in,
    out_grad,
    attn_gain,
    q_down,
    q_gain,
    kv_down,
    kv_gain,
    q_up,
    kv_up,
    out_proj,
    ffn_gain,
    router,
    routed_gate_up,
    routed_down,
    shared_gate_up,
    shared_down,
    choices,
    seq_lens,
):
    local_rows, width = hidden_in.shape
    group_rows = choices.shape[0]
    tp_count = lax.axis_size("tp")
    tp_index = lax.axis_index("tp")
    y_lo = lax.rem(lax.div(lax.axis_index("fsdp"), 4), 2)
    head_count = HEADS // tp_count
    experts = router.shape[1]
    held = experts // 2
    capacity = 5 * group_rows * TOPK // (4 * experts)
    units = routed_gate_up.shape[3]
    row_shard = routed_gate_up.shape[1]
    q_cols = q_down.shape[1] // tp_count
    raw_cols = q_cols + kv_down.shape[1] // tp_count
    raw_pad = -raw_cols % 128
    small_at = raw_cols + raw_pad

    def own(array):
        return lax.dynamic_slice_in_dim(array, tp_index * local_rows, local_rows)

    down_rows = q_down.shape[0]
    devices = width // down_rows
    device = lax.axis_index("fsdp") * tp_count + tp_index
    rope_cols = ROPE // tp_count
    columns = jnp.concatenate(
        [
            q_down.reshape(down_rows, tp_count, q_cols),
            kv_down[:, :KVR].reshape(down_rows, tp_count, KVR // tp_count),
            kv_down[:, KVR:].reshape(down_rows, tp_count, rope_cols),
        ],
        axis=-1,
    ).transpose(1, 0, 2)
    downs = jnp.pad(columns, ((0, 0), (0, 0), (0, raw_pad)))
    half = ROPE // 2
    q_rows = q_up.reshape(-1, head_count, NOPE + ROPE)
    q_sent = jnp.concatenate(
        [
            q_rows[..., :NOPE].reshape(-1, head_count * NOPE),
            q_rows[..., NOPE : NOPE + half].reshape(-1, head_count * half),
            q_rows[..., NOPE + half :].reshape(-1, head_count * half),
        ],
        axis=1,
    )
    small = jnp.zeros((16, width), BF)
    vectors = jnp.concatenate([router.T, attn_gain[None], ffn_gain[None]], axis=0)
    small = lax.dynamic_update_slice(small, vectors, (0, device * down_rows))
    small = lax.dynamic_update_slice(small, q_gain[None], (experts + 2, device * q_gain.shape[0]))
    kv_at = q_down.shape[1] + device * kv_gain.shape[0]
    small = lax.dynamic_update_slice(small, kv_gain[None], (experts + 2, kv_at))
    gate_up = routed_gate_up.transpose(0, 2, 1, 3)
    down_t = routed_down.transpose(0, 2, 1)[:, None]
    routed = jnp.concatenate([gate_up, down_t], axis=1).reshape(2, held, 3, row_shard, units)
    shared = jnp.concatenate(
        [
            shared_gate_up.reshape(row_shard, 2, 2, units).transpose(2, 1, 0, 3),
            shared_down.T.reshape(row_shard, 2, units).transpose(1, 0, 2)[:, None],
        ],
        axis=1,
    )
    early = routed[:, : held - 1].reshape(2, 3 * (held - 1), row_shard, units)
    late = jnp.concatenate([routed[:, held - 1], shared], axis=1)

    segment, position = packing(seq_lens[0], group_rows)
    cosine, sine_table = rotary_tables(position)
    cos_heads, sin_heads = jnp.tile(cosine, (1, head_count)), jnp.tile(sine_table, (1, head_count))
    picked = own(choices)
    lanes = jnp.arange(2 * experts, dtype=jnp.int32)
    pick_a, pick_b = ((picked[:, k : k + 1] == lanes[None]).astype(F32) for k in range(TOPK))
    pick_sent = sum((picked[:, k : k + 1] + experts == lanes[None]).astype(F32) for k in range(TOPK))

    (
        all_downs, all_q, all_kv, all_out, all_grad, wide_early, swapped_late, tokens,
        attn_in, raw, group_query, group_keyval, query, keyval, rope, norms, heads_out, residual, logits,
        gains,
    ) = front(
        downs, q_sent, kv_up, out_proj.T, hidden_in, out_grad, early, late, small,
        cos_heads, sin_heads, segment[:, None], segment[None, :], (pick_a, pick_b, pick_sent),
    )
    down_weight = all_downs.reshape(width, -1)
    up_query = all_q.reshape(-1, q_up.shape[1])
    up_keyval = all_kv.reshape(-1, kv_up.shape[1])
    out_weight = all_out.reshape(width, -1)
    moe_part, back_part, sum_early, sum_late = ffn(
        tokens.reshape(2 * group_rows, -1), all_grad.reshape(2 * group_rows, width), wide_early, swapped_late, capacity
    )

    ring = (2, 2, 2, local_rows)
    blocks = (4, 2, 4, row_shard, units)
    own_early, own_late, grad_out, grad_q, grad_kv, grad_down, attn_back, grad_resid, small_grads, moe_own = back(
        (sum_early.reshape((-1,) + blocks), sum_late.reshape((-1,) + blocks)),
        back_part.reshape(ring + (width + 128,)),
        moe_part.reshape(ring + (width,)),
        (
            attn_in, heads_out, out_weight, up_query, up_keyval, down_weight, query, keyval, rope, norms, group_query,
            group_keyval, raw,
        ),
        residual, logits, (pick_a, pick_b), out_grad, gains, cos_heads, sin_heads, segment[:, None], segment[None, :],
    )

    got_downs, sum_up_query, sum_up_keyval, sum_out, attn_back_own, small_sum = last(
        grad_down[None], grad_q, grad_kv, grad_out, attn_back.reshape(tp_count, local_rows, width), small_grads
    )
    layer_out = (residual + moe_own).astype(BF)
    own_hat, own_scale = normalized(hidden_in.astype(F32))
    input_grad = grad_resid + norm_back(attn_back_own, gains[experts].astype(F32), own_hat, own_scale)
    got_downs = got_downs.astype(F32)
    sum_qdown = got_downs[..., :q_cols].transpose(1, 0, 2).reshape(down_rows, -1)
    kv_at = q_cols + KVR // tp_count
    sum_kvdown = jnp.concatenate(
        [
            got_downs[..., q_cols:kv_at].transpose(1, 0, 2).reshape(down_rows, -1),
            got_downs[..., kv_at:raw_cols].transpose(1, 0, 2).reshape(down_rows, -1),
        ],
        axis=-1,
    )
    nope_cols, half_cols = head_count * NOPE, head_count * half
    sum_up_query = jnp.concatenate(
        [
            sum_up_query[:, :nope_cols].reshape(-1, head_count, NOPE),
            sum_up_query[:, nope_cols : nope_cols + half_cols].reshape(-1, head_count, half),
            sum_up_query[:, nope_cols + half_cols :].reshape(-1, head_count, half),
        ],
        axis=-1,
    ).reshape(q_up.shape)

    def mine(row, at, count):
        return lax.dynamic_slice(small_sum, (row, at), (1, count))[0]

    rows_at = device * down_rows
    sum_router = lax.dynamic_slice(small_sum, (0, rows_at), (experts, down_rows)).T
    own_routed = jnp.concatenate([own_early, own_late[:, :3]], axis=1).reshape(experts, 3, row_shard, units)
    sum_wide_gu = own_routed[:, :2].transpose(0, 2, 1, 3).astype(F32)
    sum_wide_down = own_routed[:, 2].transpose(0, 2, 1).astype(F32)
    sum_common_gu = own_late[:, 3:5].transpose(2, 1, 0, 3).reshape(row_shard, 2, 2 * units).astype(F32)
    sum_common_down = own_late[:, 5].transpose(1, 0, 2).reshape(row_shard, 2 * units).T.astype(F32)
    q_rank = q_down.shape[1]
    return (
        layer_out,
        input_grad.astype(BF),
        mine(experts, rows_at, down_rows),
        sum_qdown,
        mine(experts + 2, device * q_gain.shape[0], q_gain.shape[0]),
        sum_kvdown,
        mine(experts + 2, q_rank + device * kv_gain.shape[0], kv_gain.shape[0]),
        sum_up_query,
        sum_up_keyval,
        sum_out.T,
        mine(experts + 1, rows_at, down_rows),
        sum_router,
        sum_wide_gu,
        sum_wide_down,
        sum_common_gu,
        sum_common_down,
    )


def solution(mesh):
    return jax.shard_map(
        per_device,
        mesh=mesh,
        in_specs=(
            P(("fsdp", "tp"), None),
            P(("fsdp", "tp"), None),
            P(("fsdp", "tp")),
            P(("fsdp", "tp"), None),
            P(("fsdp", "tp")),
            P(("fsdp", "tp"), None),
            P(("fsdp", "tp")),
            P("fsdp", "tp"),
            P("fsdp", "tp"),
            P("tp", "fsdp"),
            P(("fsdp", "tp")),
            P(("fsdp", "tp"), None),
            P(None, "fsdp", None, "tp"),
            P(None, "tp", "fsdp"),
            P("fsdp", None, "tp"),
            P("tp", "fsdp"),
            P("fsdp", None),
            P("fsdp", None),
        ),
        out_specs=(
            P(("fsdp", "tp"), None),
            P(("fsdp", "tp"), None),
            P(("fsdp", "tp")),
            P(("fsdp", "tp"), None),
            P(("fsdp", "tp")),
            P(("fsdp", "tp"), None),
            P(("fsdp", "tp")),
            P("fsdp", "tp"),
            P("fsdp", "tp"),
            P("tp", "fsdp"),
            P(("fsdp", "tp")),
            P(("fsdp", "tp"), None),
            P(None, "fsdp", None, "tp"),
            P(None, "tp", "fsdp"),
            P("fsdp", None, "tp"),
            P("tp", "fsdp"),
        ),
        check_vma=False,
    )
```
